32 devices in a mesh: seq: 8 (over y, x, core), head: 4 (over z).
Axes of the slice: x: 2, y: 2, z: 4, core: 2. Of those that a mesh axis runs over, the one named last changes fastest.
Arguments:
- tokens: bfloat16 [1536, 2048], P('seq'), may hold values from -6 to 6
- cotangent: bfloat16 [1536, 2048], P('seq'), may hold values from -6 to 6
- owners: int32 [2, 8], replicated, may hold values from 0 to 7, as said below
- master: float32 [4, 8, 772, 2048], P('head', 'seq'), may hold values from -0.110485435 to 0.110485435
- first_moment: float32 [4, 8, 772, 2048], P('head', 'seq'), may hold values from -176.36326 to 176.36326
- second_moment: float32 [4, 8, 772, 2048], P('head', 'seq'), may hold values from 45.6192 to 6635.52
- eigenbases: float32 [4, 8, 16, 128, 128], P('head', 'seq'), may hold values from -1 to 1, as said below
- norm_gains: float32 [2, 2048], P(None, 'seq'), may hold values from 0.5 to 1.5
- gain_first: float32 [2, 2048], P(None, 'seq'), may hold values from -160 to 160
- gain_second: float32 [2, 2048], P(None, 'seq'), may hold values from 307.2 to 6144
Outputs:
- block_out: bfloat16 [1536, 2048], P('seq', 'head')
- input_grad: float32 [1536, 2048], P('seq')
- weight_grad: float32 [4, 8, 772, 2048], P('head', 'seq')
- first_new: float32 [4, 8, 772, 2048], P('head', 'seq')
- second_new: float32 [4, 8, 772, 2048], P('head', 'seq')
- master_new: float32 [4, 8, 772, 2048], P('head', 'seq')
- weights_new: bfloat16 [4, 8, 772, 2048], P('head', 'seq')
- gain_grad: float32 [2, 2048], P(None, 'seq')
- gain_first_new: float32 [2, 2048], P(None, 'seq')
- gain_second_new: float32 [2, 2048], P(None, 'seq')
- gain_new: float32 [2, 2048], P(None, 'seq')
The draws below stay inside these ranges and needn't reach their ends.
Inputs may be any that keep to these rules, and one draw needn't show every extreme that they name: `owners`: row 0 names, for each attention row block j, the seq index of its owner; row 1 the same for feed-forward row blocks; each row is a permutation. `eigenbases`: each [128, 128] matrix is orthogonal.
All inputs are finite; a program needn't handle non-finite values.
Results may differ from the reference program's by a relative error of at most 0.015.
Values may be sent and summed in bfloat16 or wider, within the bound.
A program may use at most 256 MiB of HBM per device.

```python
import math
import jax
import jax.numpy as jnp
from jax import lax

D = 2048
HEADS = 16
HEAD_DIM = 128
FF = 5504
WINDOW = 1024
TOK_DEV = 192
ROT_BLOCK = 128
ADAM_STEP = 5
TOKENS = 1536
HEAD_SHARE = 512
FFN_SHARE = 1376
ATT_SLAB = 256
FFN_SLAB = 516
SLAB_ROWS = 772
BLOCKS_ROT = 16
N_SEQ = 8
N_HEAD = 4


def owner_table(key):
    base_key = jax.random.fold_in(key, 101)
    first_row = jax.random.permutation(jax.random.fold_in(base_key, 1), N_SEQ)
    second_row = jax.random.permutation(jax.random.fold_in(base_key, 2), N_SEQ)
    return jnp.stack([first_row, second_row]).astype(jnp.int32)


def inverse_order_drawn(owner_row):
    places = jnp.arange(owner_row.shape[0], dtype=jnp.int32)
    matches = (owner_row[:, None] == places[None, :]).astype(jnp.int32)
    return jnp.sum(matches * places[:, None], axis=0).astype(jnp.int32)


def slab_kinds(key):
    owner_rows = owner_table(key)
    slab_attn = inverse_order_drawn(owner_rows[0])
    slab_ffn = inverse_order_drawn(owner_rows[1])
    attn_kind = (slab_attn[:, None] * ATT_SLAB + jnp.arange(ATT_SLAB, dtype=jnp.int32)[None, :]) // HEAD_SHARE
    ffn_kind = 4 + (slab_ffn[:, None] * FFN_SLAB + jnp.arange(FFN_SLAB, dtype=jnp.int32)[None, :]) // FFN_SHARE
    return jnp.concatenate([attn_kind, ffn_kind], axis=1)


def pick_table(kinds, table):
    matches = (kinds[..., None] == jnp.arange(7, dtype=jnp.int32)).astype(jnp.float32)
    return jnp.sum(matches * jnp.array(table, jnp.float32), axis=-1)


def grad_spreads():
    root_tokens = math.sqrt(TOKENS)
    return [0.9 * root_tokens, 0.9 * root_tokens, 0.9 * root_tokens, 0.9 * root_tokens, 0.3 * root_tokens, 0.3 * root_tokens, 0.5 * root_tokens]


def draw_owners(key, part):
    return owner_table(key)


def draw_master(key, part):
    kinds = slab_kinds(key)
    key = jax.random.fold_in(key, 5)
    wide = D ** (-0.5)
    spreads = pick_table(kinds, [wide, wide, wide, wide, wide, wide, FF ** (-0.5)])
    noise = jax.random.truncated_normal(key, -5.0, 5.0, (N_HEAD, N_SEQ, SLAB_ROWS, D), jnp.float32)
    return noise * spreads[None, :, :, None]


def draw_first_moment(key, part):
    kinds = slab_kinds(key)
    key = jax.random.fold_in(key, 6)
    spreads = pick_table(kinds, grad_spreads())
    noise = jax.random.truncated_normal(key, -5.0, 5.0, (N_HEAD, N_SEQ, SLAB_ROWS, D), jnp.float32)
    return noise * spreads[None, :, :, None]


def draw_second_moment(key, part):
    kinds = slab_kinds(key)
    key = jax.random.fold_in(key, 7)
    spreads = pick_table(kinds, grad_spreads())
    factors = jnp.exp(jax.random.uniform(key, (N_HEAD, N_SEQ, SLAB_ROWS, D), jnp.float32, math.log(0.5), math.log(8.0)))
    return 2.0 / 3.0 * factors * (spreads * spreads)[None, :, :, None]


def draw_eigenbases(key, part):
    key = jax.random.fold_in(key, 9)
    sign_key, vector_key = jax.random.split(key)
    lead_shape = (N_HEAD, N_SEQ, BLOCKS_ROT, ROT_BLOCK)
    signs = jax.random.rademacher(sign_key, lead_shape, jnp.float32)
    vectors = jax.random.normal(vector_key, lead_shape, jnp.float32)
    places = jnp.arange(ROT_BLOCK, dtype=jnp.float32)
    cosines = jnp.cos(math.pi * places[:, None] * (places[None, :] + 0.5) / ROT_BLOCK) * math.sqrt(2.0 / ROT_BLOCK)
    cosines = jnp.where(places[:, None] == 0.0, cosines * math.sqrt(0.5), cosines)
    signed = signs[..., :, None] * cosines
    weighted = jnp.einsum('...m,mk->...k', vectors * signs, cosines)
    lengths = jnp.sum(vectors * vectors, axis=-1, keepdims=True)
    return signed - 2.0 * vectors[..., :, None] * weighted[..., None, :] / lengths[..., None]


def levels(stream_key, extent, shards, low, high):
    factor_of = 1.0
    for position, shards_of in shards:
        heights = jax.random.uniform(jax.random.fold_in(jax.random.fold_in(stream_key, 6), position), (shards_of,), jnp.float32, low / len(shards), high / len(shards))
        factor_of = factor_of * jnp.repeat(jnp.exp(heights), extent[position] // shards_of).reshape((-1,) + (1,) * (len(extent) - 1 - position))
    return factor_of


def bell_draw(own_key, shape, scale, bound, pieces=(), kind=jnp.bfloat16):
    values = jax.random.normal(own_key, shape, jnp.float32) * scale
    if len(pieces) > 0:
        values = levels(own_key, shape, pieces, -0.22, 0.18) * values
    return jnp.clip(values, min=-bound, max=bound).astype(kind)


def setup_inputs(seed: int = 0) -> dict:
    splits = jax.random.split(jax.random.key(seed), 11)
    tokens = bell_draw(splits[0], (TOKENS, D), 1.0, 6.0, ((0, 8),))
    cotangent = bell_draw(splits[1], (TOKENS, D), 1.0, 6.0, ((0, 8),))
    owners = draw_owners(jax.random.fold_in(splits[10], 71), 0)
    master = draw_master(jax.random.fold_in(splits[10], 71), 0)
    first_moment = draw_first_moment(jax.random.fold_in(splits[10], 71), 0)
    second_moment = draw_second_moment(jax.random.fold_in(splits[10], 71), 0)
    eigenbases = draw_eigenbases(jax.random.fold_in(splits[10], 71), 0)
    norm_gains = jnp.clip(1.0 + 0.1 * jax.random.normal(splits[7], (2, D), jnp.float32), 0.5, 1.5)
    gain_first = bell_draw(splits[8], (2, D), (0.7 * TOKENS ** 0.5), 160.0, ((1, 8),), jnp.float32)
    gain_second = jnp.clip(jnp.exp(math.log(6144.0) - 2.9957322 * jax.random.uniform(splits[9], (2, D), jnp.float32) ** levels(splits[9], (2, D), ((1, 8),), -0.2, 0.2)), 307.2, 6144.0)
    return dict(tokens=tokens, cotangent=cotangent, owners=owners, master=master, first_moment=first_moment, second_moment=second_moment, eigenbases=eigenbases, norm_gains=norm_gains, gain_first=gain_first, gain_second=gain_second)


EPS_NORM = 1e-05
BETA_FIRST = 0.5
BETA_SECOND = 0.6
ADAM_EPS = 1e-08
DECAY_RATE = 0.1
GAIN_RATE = 0.25
ROPE_BASE = 10000.0
NEGATIVE = -1e+30
PRECISE = lax.Precision.HIGHEST

@jax.custom_vjp
def low(v):
    return lax.optimization_barrier(v.astype(jnp.bfloat16)).astype(jnp.float32)

@jax.custom_vjp
def low_back(v):
    return v

def low_keep(v):
    return (low(v), None)

def low_pass(kept, grad):
    return (grad,)

def back_keep(v):
    return (v, None)

def back_low(kept, grad):
    return (low(grad),)
low.defvjp(low_keep, low_pass)
low_back.defvjp(back_keep, back_low)

def inverse_order(owner_row):
    places = jnp.arange(owner_row.shape[0], dtype=jnp.int32)
    matches = (owner_row[:, None] == places[None, :]).astype(jnp.int32)
    return lax.optimization_barrier(jnp.sum(matches * places[:, None], axis=0)).astype(jnp.int32)

def kind_rates(kinds, width):
    wide = width ** (-0.5)
    spreads = jnp.array([wide, wide, wide, wide, wide, wide, FF ** (-0.5)], jnp.float32)
    matches = (kinds[..., None] == jnp.arange(7, dtype=jnp.int32)).astype(jnp.float32)
    return 0.5 * lax.optimization_barrier(jnp.sum(matches * spreads, axis=-1))

def angles(positions):
    half_dim = HEAD_DIM // 2
    frequencies = ROPE_BASE ** (-jnp.arange(half_dim, dtype=jnp.float32) / half_dim)
    turning = positions[:, None] * frequencies[None, :]
    return (jnp.cos(turning)[:, None, :], jnp.sin(turning)[:, None, :])

def rotate(vectors, cosine, sine):
    half_dim = vectors.shape[-1] // 2
    former = vectors[..., :half_dim]
    latter = vectors[..., half_dim:]
    return jnp.concatenate([former * cosine - latter * sine, latter * cosine + former * sine], axis=-1)

def inverse_rms(vectors):
    return lax.rsqrt(lax.optimization_barrier(jnp.mean(vectors * vectors, axis=-1, keepdims=True)) + EPS_NORM)

def attend(query_rows, key_rows, value_rows):
    padding = jnp.zeros((WINDOW, HEADS, HEAD_DIM), jnp.float32)
    key_padded = jnp.concatenate([padding, key_rows], axis=0)
    value_padded = jnp.concatenate([padding, value_rows], axis=0)
    row_ids = jnp.arange(TOK_DEV, dtype=jnp.int32)[:, None]
    col_ids = jnp.arange(WINDOW + TOK_DEV, dtype=jnp.int32)[None, :]
    score_scale = HEAD_DIM ** (-0.5)

    def one_block(block_index):
        start = (block_index * TOK_DEV).astype(jnp.int32)
        block_query = lax.dynamic_slice_in_dim(query_rows, start, TOK_DEV, 0)
        block_key = lax.dynamic_slice_in_dim(key_padded, start, WINDOW + TOK_DEV, 0)
        block_value = lax.dynamic_slice_in_dim(value_padded, start, WINDOW + TOK_DEV, 0)
        raw = low_back(jnp.einsum('thd,chd->htc', block_query, block_key, precision=PRECISE))
        allowed = (col_ids > row_ids) & (col_ids <= row_ids + WINDOW) & (start - WINDOW + col_ids >= 0)
        scores = jnp.where(allowed[None], raw * score_scale, NEGATIVE)
        row_top = lax.optimization_barrier(jnp.max(scores, axis=-1, keepdims=True))
        exp_scores = jnp.exp(scores - row_top)
        soft_low = low(exp_scores / lax.optimization_barrier(jnp.sum(exp_scores, axis=-1, keepdims=True)))
        return jnp.einsum('htc,chd->thd', soft_low, block_value, precision=PRECISE)
    blocks = lax.map(jax.checkpoint(one_block), jnp.arange(N_SEQ, dtype=jnp.int32))
    return blocks.reshape(TOKENS, HEADS, HEAD_DIM)

def forward(inputs, attn_rows, ffn_rows, gains_low):
    head_share = D // N_HEAD
    ffn_share = FF // N_HEAD
    branch_scale = (WINDOW / 3.0) ** 0.5

    def part_rows(stacked, place, share):
        return stacked[:, place * share:(place + 1) * share].reshape(N_HEAD * share, D)
    w_query = part_rows(attn_rows, 0, head_share)
    w_key = part_rows(attn_rows, 1, head_share)
    w_value = part_rows(attn_rows, 2, head_share)
    w_out = part_rows(attn_rows, 3, head_share)
    w_gate = part_rows(ffn_rows, 0, ffn_share)
    w_up = part_rows(ffn_rows, 1, ffn_share)
    w_down = part_rows(ffn_rows, 2, ffn_share)
    cosine, sine = angles(jnp.arange(TOKENS, dtype=jnp.float32))
    head_shape = (TOKENS, HEADS, HEAD_DIM)
    normed_one = low(inputs * inverse_rms(inputs) * gains_low[0])

    def project(weight_rows):
        return jnp.dot(normed_one, weight_rows.T, precision=PRECISE)
    query_rows = low(rotate(low_back(project(w_query)).reshape(head_shape), cosine, sine))
    key_rows = low(rotate(low_back(project(w_key)).reshape(head_shape), cosine, sine))
    value_rows = low(low_back(project(w_value))).reshape(head_shape)
    attended = low(low_back(attend(query_rows, key_rows, value_rows).reshape(TOKENS, D)))
    hidden_one = inputs + low_back(branch_scale * jnp.dot(attended, w_out, precision=PRECISE))
    normed_two = low(hidden_one * inverse_rms(hidden_one) * gains_low[1])
    gate_pre = low_back(jnp.dot(normed_two, w_gate.T, precision=PRECISE))
    up_pre = low_back(jnp.dot(normed_two, w_up.T, precision=PRECISE))
    hidden_low = low(jax.nn.silu(gate_pre) * up_pre)
    return hidden_one + jnp.dot(hidden_low, w_down, precision=PRECISE)

def reference(tokens, cotangent, owners, master, first_moment, second_moment, eigenbases, norm_gains, gain_first, gain_second):
    head_share = D // N_HEAD
    ffn_share = FF // N_HEAD
    attn_slab = 4 * D // (N_HEAD * N_SEQ)
    ffn_slab = 3 * FF // (N_HEAD * N_SEQ)
    master_low = lax.optimization_barrier(master.astype(jnp.bfloat16)).astype(jnp.float32)
    gains_low = lax.optimization_barrier(norm_gains.astype(jnp.bfloat16)).astype(jnp.float32)
    attn_rows = jnp.take(master_low[:, :, :attn_slab], owners[0], axis=1).reshape(N_HEAD, 4 * head_share, D)
    ffn_rows = jnp.take(master_low[:, :, attn_slab:], owners[1], axis=1).reshape(N_HEAD, 3 * ffn_share, D)
    inputs = tokens.astype(jnp.float32)
    output_full, pullback = jax.vjp(forward, inputs, attn_rows, ffn_rows, gains_low)
    input_grad, attn_grad, ffn_grad, gain_grad = pullback(cotangent.astype(jnp.float32))
    inverse_attn = inverse_order(owners[0])
    inverse_ffn = inverse_order(owners[1])
    weight_grad = jnp.concatenate([jnp.take(attn_grad.reshape(N_HEAD, N_SEQ, attn_slab, D), inverse_attn, axis=1), jnp.take(ffn_grad.reshape(N_HEAD, N_SEQ, ffn_slab, D), inverse_ffn, axis=1)], axis=2)
    block_size = eigenbases.shape[-1]
    split_shape = (N_HEAD, N_SEQ, attn_slab + ffn_slab, D // block_size, block_size)
    turned = jnp.einsum('hprbk,hpbkl->hprbl', weight_grad.reshape(split_shape), eigenbases, precision=PRECISE).reshape(weight_grad.shape)
    first_new = BETA_FIRST * first_moment + (1.0 - BETA_FIRST) * turned
    second_new = BETA_SECOND * second_moment + (1.0 - BETA_SECOND) * turned * turned
    adam_dir = first_new / (1.0 - BETA_FIRST ** ADAM_STEP) / (jnp.sqrt(second_new / (1.0 - BETA_SECOND ** ADAM_STEP)) + ADAM_EPS)
    backward_dir = jnp.einsum('hprbl,hpbkl->hprbk', adam_dir.reshape(split_shape), eigenbases, precision=PRECISE).reshape(weight_grad.shape)
    attn_kinds = (inverse_attn[:, None] * attn_slab + jnp.arange(attn_slab, dtype=jnp.int32)[None, :]) // head_share
    ffn_kinds = 4 + (inverse_ffn[:, None] * ffn_slab + jnp.arange(ffn_slab, dtype=jnp.int32)[None, :]) // ffn_share
    row_rates = kind_rates(jnp.concatenate([attn_kinds, ffn_kinds], axis=1), D)[None, :, :, None]
    master_new = master - row_rates * (backward_dir + DECAY_RATE * master)
    gain_first_new = BETA_FIRST * gain_first + (1.0 - BETA_FIRST) * gain_grad
    gain_second_new = BETA_SECOND * gain_second + (1.0 - BETA_SECOND) * gain_grad * gain_grad
    gain_new = norm_gains - GAIN_RATE * (gain_first_new / (1.0 - BETA_FIRST ** ADAM_STEP)) / (jnp.sqrt(gain_second_new / (1.0 - BETA_SECOND ** ADAM_STEP)) + ADAM_EPS)
    return (output_full.astype(jnp.bfloat16), input_grad, weight_grad, first_new, second_new, master_new, master_new.astype(jnp.bfloat16), gain_grad, gain_first_new, gain_second_new, gain_new)
```

```python
import functools

import jax
import jax.numpy as jnp
from jax import lax
from jax.experimental import pallas as pl
from jax.experimental.pallas import tpu as pltpu
from jax.sharding import PartitionSpec as P

HEADS = 16
HEAD_DIM = 128
FF = 5504
WINDOW = 1024
ADAM_STEP = 5


EPS_NORM = 1e-05
BETA_FIRST = 0.5
BETA_SECOND = 0.6
ADAM_EPS = 1e-08
DECAY_RATE = 0.1
GAIN_RATE = 0.25
ROPE_BASE = 10000.0
NEGATIVE = -1e30
PRECISE = lax.Precision.HIGHEST

BF16 = jnp.bfloat16
F32 = jnp.float32


def passed_along(shard, axis, by):
    devices = lax.axis_size(axis)
    pairs = [(i, i + by) for i in range(devices) if 0 <= i + by < devices]
    return lax.ppermute(shard, axis, pairs)


def inverse_order(owner_row):
    places = jnp.arange(owner_row.shape[0], dtype=jnp.int32)
    matches = (owner_row[:, None] == places[None, :]).astype(jnp.int32)
    return jnp.sum(matches * places[:, None], axis=0)


def kind_rates(kinds, width):
    wide = width ** (-0.5)
    spreads = jnp.array([wide, wide, wide, wide, wide, wide, FF ** (-0.5)], jnp.float32)
    matches = (kinds[..., None] == jnp.arange(7, dtype=jnp.int32)).astype(jnp.float32)
    return 0.5 * jnp.sum(matches * spreads, axis=-1)


def angles(positions):
    half_dim = HEAD_DIM // 2
    frequencies = ROPE_BASE ** (-jnp.arange(half_dim, dtype=jnp.float32) / half_dim)
    turning = positions[:, None] * frequencies[None, :]
    return (jnp.cos(turning)[:, None, :], jnp.sin(turning)[:, None, :])


def rotate(vectors, cosine, sine):
    half_dim = vectors.shape[-1] // 2
    former = vectors[..., :half_dim]
    latter = vectors[..., half_dim:]
    return jnp.concatenate(
        [former * cosine - latter * sine, latter * cosine + former * sine], axis=-1
    )


def inverse_rms(vectors):
    return lax.rsqrt(jnp.mean(vectors * vectors, axis=-1, keepdims=True) + EPS_NORM)


def norm_back(grad_normed, inputs, rms_values, gain_row):
    weighted = grad_normed * gain_row
    inner = jnp.mean(weighted * inputs, axis=-1, keepdims=True)
    input_part = rms_values * weighted - inputs * rms_values**3 * inner
    return (input_part, jnp.sum(grad_normed * inputs * rms_values, axis=0))


def any_mesh(
    tokens,
    cotangent,
    owners,
    master,
    first_moment,
    second_moment,
    eigenbases,
    norm_gains,
    gain_first,
    gain_second,
):
    tok_rows, width = tokens.shape
    seq_devices = lax.axis_size("seq")
    head_devices = lax.axis_size("head")
    seq_place = lax.axis_index("seq")
    head_place = lax.axis_index("head")
    slab_rows = master.shape[2]
    attn_slab = 4 * width // (head_devices * seq_devices)
    ffn_slab = slab_rows - attn_slab
    head_width = width // head_devices
    ffn_width = FF // head_devices
    local_heads = HEADS // head_devices
    score_scale = HEAD_DIM ** (-0.5)
    branch_scale = (WINDOW / 3.0) ** 0.5
    inverse_attn = inverse_order(owners[0])
    inverse_ffn = inverse_order(owners[1])
    master_low = master[0, 0].astype(jnp.bfloat16)
    gathered, gains_all = (
        lax.all_gather(master_low, "seq", axis=0, tiled=True),
        lax.all_gather(norm_gains.astype(jnp.bfloat16), "seq", axis=1, tiled=True),
    )
    gathered = gathered.reshape(seq_devices, slab_rows, width)
    attn_rows = jnp.take(gathered[:, :attn_slab], owners[0], axis=0).reshape(4 * head_width, width)
    ffn_rows = jnp.take(gathered[:, attn_slab:], owners[1], axis=0).reshape(3 * ffn_width, width)
    w_query = attn_rows[:head_width]
    w_key = attn_rows[head_width : 2 * head_width]
    w_value = attn_rows[2 * head_width : 3 * head_width]
    w_out = attn_rows[3 * head_width :]
    w_gate = ffn_rows[:ffn_width]
    w_up = ffn_rows[ffn_width : 2 * ffn_width]
    w_down = ffn_rows[2 * ffn_width :]
    gain_one = gains_all[0].astype(jnp.float32)
    gain_two = gains_all[1].astype(jnp.float32)
    inputs = tokens.astype(jnp.float32)
    rms_one = inverse_rms(inputs)
    normed_one = (inputs * rms_one * gain_one).astype(jnp.bfloat16)
    positions = (seq_place * tok_rows + jnp.arange(tok_rows, dtype=jnp.int32)).astype(jnp.float32)
    cosine, sine = angles(positions)
    head_shape = (tok_rows, local_heads, HEAD_DIM)

    def project(weight_rows):
        return jnp.einsum("td,id->ti", normed_one, weight_rows, preferred_element_type=jnp.float32)

    queries = rotate(project(w_query).reshape(head_shape), cosine, sine).astype(jnp.bfloat16)
    keys_own = rotate(project(w_key).reshape(head_shape), cosine, sine).astype(jnp.bfloat16)
    values_own = project(w_value).reshape(head_shape).astype(jnp.bfloat16)
    hop_total = -(-WINDOW // tok_rows)
    hop_sizes = [
        min(tok_rows, WINDOW - (hop_index - 1) * tok_rows) for hop_index in range(1, hop_total + 1)
    ]
    halo_keys = []
    halo_values = []
    for hop_index in range(hop_total, 0, -1):
        hop_rows = hop_sizes[hop_index - 1]
        far_keys, far_values = passed_along(
            (keys_own[tok_rows - hop_rows :], values_own[tok_rows - hop_rows :]), "seq", hop_index
        )
        halo_keys.append(far_keys)
        halo_values.append(far_values)
    keys_all = jnp.concatenate(halo_keys + [keys_own], axis=0)
    values_all = jnp.concatenate(halo_values + [values_own], axis=0)
    row_ids = jnp.arange(tok_rows, dtype=jnp.int32)[:, None]
    col_ids = jnp.arange(WINDOW + tok_rows, dtype=jnp.int32)[None, :]
    allowed = (
        (col_ids > row_ids)
        & (col_ids <= row_ids + WINDOW)
        & (seq_place * tok_rows - WINDOW + col_ids >= 0)
    )

    def scores_of():
        raw = jnp.einsum("thd,chd->htc", queries, keys_all, preferred_element_type=jnp.float32)
        return jnp.where(allowed[None], raw * score_scale, NEGATIVE)

    scores = scores_of()
    row_top = jnp.max(scores, axis=-1, keepdims=True)
    exp_scores = jnp.exp(scores - row_top)
    exp_total = jnp.sum(exp_scores, axis=-1, keepdims=True)
    soft_low = (exp_scores / exp_total).astype(jnp.bfloat16)
    log_total = row_top + jnp.log(exp_total)
    attended = jnp.einsum("htc,chd->thd", soft_low, values_all, preferred_element_type=jnp.float32)
    attended_low = attended.reshape(tok_rows, head_width).astype(jnp.bfloat16)
    attn_part = branch_scale * jnp.dot(attended_low, w_out, preferred_element_type=jnp.float32)
    hidden_one = inputs + lax.psum(attn_part, "head")
    rms_two = inverse_rms(hidden_one)
    normed_two = (hidden_one * rms_two * gain_two).astype(jnp.bfloat16)
    gate_pre = jnp.einsum("td,fd->tf", normed_two, w_gate, preferred_element_type=jnp.float32)
    up_pre = jnp.einsum("td,fd->tf", normed_two, w_up, preferred_element_type=jnp.float32)
    sigma = jax.nn.sigmoid(gate_pre)
    hidden_low = (gate_pre * sigma * up_pre).astype(jnp.bfloat16)
    ffn_part = jnp.dot(hidden_low, w_down, preferred_element_type=jnp.float32)
    ffn_share = lax.psum_scatter(ffn_part, "head", scatter_dimension=1, tiled=True)
    share_width = width // head_devices
    residual_share = lax.dynamic_slice_in_dim(hidden_one, head_place * share_width, share_width, 1)
    block_out = (residual_share + ffn_share).astype(jnp.bfloat16)
    grad_out_f = cotangent.astype(jnp.float32)
    hidden_grad = jnp.einsum("td,fd->tf", cotangent, w_down, preferred_element_type=jnp.float32)
    silu_grad = sigma * (1.0 + gate_pre * (1.0 - sigma))
    gate_grad = (hidden_grad * up_pre * silu_grad).astype(jnp.bfloat16)
    up_grad = (hidden_grad * gate_pre * sigma).astype(jnp.bfloat16)
    down_grad = jnp.einsum("tf,td->fd", hidden_low, cotangent, preferred_element_type=jnp.float32)
    gate_w_grad = jnp.einsum("tf,td->fd", gate_grad, normed_two, preferred_element_type=jnp.float32)
    up_w_grad = jnp.einsum("tf,td->fd", up_grad, normed_two, preferred_element_type=jnp.float32)
    ffn_rows_grad = jnp.concatenate([gate_w_grad, up_w_grad, down_grad], axis=0)
    ffn_owner = jnp.take(ffn_rows_grad.reshape(seq_devices, ffn_slab, width), inverse_ffn, axis=0)
    normed_two_part = jnp.einsum(
        "tf,fd->td", gate_grad, w_gate, preferred_element_type=jnp.float32
    ) + jnp.einsum("tf,fd->td", up_grad, w_up, preferred_element_type=jnp.float32)
    normed_two_share = lax.psum_scatter(normed_two_part, "head", scatter_dimension=1, tiled=True)
    normed_two_grad = lax.all_gather(normed_two_share, "head", axis=1, tiled=True)
    back_two, gain_two_grad = norm_back(normed_two_grad, hidden_one, rms_two, gain_two)
    hidden_one_grad = grad_out_f + back_two
    hidden_grad_low = hidden_one_grad.astype(jnp.bfloat16)
    attended_grad = branch_scale * jnp.einsum(
        "td,id->ti", hidden_grad_low, w_out, preferred_element_type=jnp.float32
    )
    attended_grad = attended_grad.reshape(head_shape).astype(jnp.bfloat16)
    soft_again = jnp.exp(scores_of() - log_total)
    soft_grad = jnp.einsum(
        "thd,chd->htc", attended_grad, values_all, preferred_element_type=jnp.float32
    )
    inner_sum = jnp.sum(soft_again * soft_grad, axis=-1, keepdims=True)
    score_grad = (soft_again * (soft_grad - inner_sum) * score_scale).astype(jnp.bfloat16)
    query_grad_turned = jnp.einsum(
        "htc,chd->thd", score_grad, keys_all, preferred_element_type=jnp.float32
    )
    key_grad_all = jnp.einsum(
        "htc,thd->chd", score_grad, queries, preferred_element_type=jnp.float32
    )
    value_grad_all = jnp.einsum(
        "htc,thd->chd", soft_low, attended_grad, preferred_element_type=jnp.float32
    )
    key_grad_own = key_grad_all[WINDOW:]
    value_grad_own = value_grad_all[WINDOW:]
    start_at = 0
    for hop_index in range(hop_total, 0, -1):
        hop_rows = hop_sizes[hop_index - 1]
        back_keys, back_values = passed_along(
            (
                key_grad_all[start_at : start_at + hop_rows],
                value_grad_all[start_at : start_at + hop_rows],
            ),
            "seq",
            -hop_index,
        )
        key_grad_own = key_grad_own.at[tok_rows - hop_rows :].add(back_keys)
        value_grad_own = value_grad_own.at[tok_rows - hop_rows :].add(back_values)
        start_at = start_at + hop_rows
    query_grad = (
        rotate(query_grad_turned, cosine, -sine).reshape(tok_rows, head_width).astype(jnp.bfloat16)
    )
    key_grad = (
        rotate(key_grad_own, cosine, -sine).reshape(tok_rows, head_width).astype(jnp.bfloat16)
    )
    value_grad = value_grad_own.reshape(tok_rows, head_width).astype(jnp.bfloat16)

    def input_part(row_grad, weight_rows):
        return jnp.einsum("ti,id->td", row_grad, weight_rows, preferred_element_type=jnp.float32)

    normed_one_part = (
        input_part(query_grad, w_query)
        + input_part(key_grad, w_key)
        + input_part(value_grad, w_value)
    )
    normed_one_share = lax.psum_scatter(normed_one_part, "head", scatter_dimension=1, tiled=True)
    normed_one_grad = lax.all_gather(
        normed_one_share.astype(jnp.bfloat16), "head", axis=1, tiled=True
    ).astype(normed_one_share.dtype)
    back_one, gain_one_grad = norm_back(normed_one_grad, inputs, rms_one, gain_one)
    input_grad = hidden_one_grad + back_one
    gain_grads = jnp.stack([gain_one_grad, gain_two_grad])

    def rows_grad(row_grad):
        return jnp.einsum("ti,td->id", row_grad, normed_one, preferred_element_type=jnp.float32)

    out_w_grad = branch_scale * jnp.einsum(
        "ti,td->id", attended_low, hidden_grad_low, preferred_element_type=jnp.float32
    )
    attn_rows_grad = jnp.concatenate(
        [rows_grad(query_grad), rows_grad(key_grad), rows_grad(value_grad), out_w_grad], axis=0
    )
    attn_owner = jnp.take(
        attn_rows_grad.reshape(seq_devices, attn_slab, width), inverse_attn, axis=0
    )
    owner_rows = jnp.concatenate([attn_owner, ffn_owner], axis=1).reshape(
        seq_devices * slab_rows, width
    )
    reduced, gain_reduced = (
        lax.psum_scatter(owner_rows, "seq", scatter_dimension=0, tiled=True),
        lax.psum_scatter(gain_grads, "seq", scatter_dimension=1, tiled=True),
    )
    attn_kinds = (
        inverse_attn[seq_place] * attn_slab + jnp.arange(attn_slab, dtype=jnp.int32)
    ) // head_width
    ffn_kinds = (
        4 + (inverse_ffn[seq_place] * ffn_slab + jnp.arange(ffn_slab, dtype=jnp.int32)) // ffn_width
    )
    row_rates = kind_rates(jnp.concatenate([attn_kinds, ffn_kinds]), width)[:, None]
    basis = eigenbases[0, 0]
    block_size = basis.shape[-1]
    split_shape = (slab_rows, width // block_size, block_size)
    turned = jnp.einsum(
        "rbk,bkl->rbl", reduced.reshape(split_shape), basis, precision=PRECISE
    ).reshape(slab_rows, width)
    first_new = BETA_FIRST * first_moment[0, 0] + (1.0 - BETA_FIRST) * turned
    second_new = BETA_SECOND * second_moment[0, 0] + (1.0 - BETA_SECOND) * turned * turned
    adam_dir = (
        first_new
        / (1.0 - BETA_FIRST**ADAM_STEP)
        / (jnp.sqrt(second_new / (1.0 - BETA_SECOND**ADAM_STEP)) + ADAM_EPS)
    )
    backward_dir = jnp.einsum(
        "rbl,bkl->rbk", adam_dir.reshape(split_shape), basis, precision=PRECISE
    ).reshape(slab_rows, width)
    master_old = master[0, 0]
    master_new = master_old - row_rates * (backward_dir + DECAY_RATE * master_old)
    gain_first_new = BETA_FIRST * gain_first + (1.0 - BETA_FIRST) * gain_reduced
    gain_second_new = BETA_SECOND * gain_second + (1.0 - BETA_SECOND) * gain_reduced * gain_reduced
    gain_new = norm_gains - GAIN_RATE * (gain_first_new / (1.0 - BETA_FIRST**ADAM_STEP)) / (
        jnp.sqrt(gain_second_new / (1.0 - BETA_SECOND**ADAM_STEP)) + ADAM_EPS
    )
    return (
        block_out,
        input_grad,
        reduced[None, None],
        first_new[None, None],
        second_new[None, None],
        master_new[None, None],
        master_new.astype(jnp.bfloat16)[None, None],
        gain_reduced,
        gain_first_new,
        gain_second_new,
        gain_new,
    )


SLAB = 516
PAD = 528
HALF = 1024
QUART = 512
UNITS = 1376
NT = (((1,), (1,)), ((), ()))
TN = (((0,), (0,)), ((), ()))


def hop(value, axis, mask):
    return lax.ppermute(value, axis, [(i, i ^ mask) for i in range(lax.axis_size(axis))])


def gather_plane(top, low):
    x_top, y_low = hop(top, "seq", 2), hop(low, "seq", 4)
    x_low, y_top = hop(low, "seq", 2), hop(top, "seq", 4)
    d_top, d_low = hop(x_top, "seq", 4), hop(y_low, "seq", 2)
    out = [None] * 8
    for place, pair in zip((0, 2, 4, 6), ((top, low), (x_top, x_low), (y_top, y_low), (d_top, d_low))):
        out[place] = pair
        out[place | 1] = tuple(hop(part, "seq", 1) for part in pair)
    return out


def line_sum(pieces):
    got = [hop(pieces[m], "head", m) for m in (1, 2, 3)]
    total = (pieces[0] + got[0].astype(F32) + got[1].astype(F32) + got[2].astype(F32)).astype(BF16)
    return [total] + [hop(total, "head", m) for m in (1, 2, 3)]


VM = pl.BlockSpec(memory_space=pltpu.VMEM)
SM = pl.BlockSpec(memory_space=pltpu.SMEM)
HB = pl.BlockSpec(memory_space=pl.ANY)


def shape(rows, columns, dtype=BF16):
    return jax.ShapeDtypeStruct((rows, columns), dtype)


def call(kernel, outs, specs, args, scratch=(), flops=0, moved=0, out_specs=None, grid=None):
    extra = {} if grid is None else {"grid": grid}
    return pl.pallas_call(
        kernel,
        out_shape=outs,
        in_specs=specs,
        out_specs=[VM] * len(outs) if out_specs is None else out_specs,
        scratch_shapes=list(scratch),
        compiler_params=pltpu.CompilerParams(vmem_limit_bytes=56 * 2**20),
        cost_estimate=pl.CostEstimate(flops=flops, bytes_accessed=moved, transcendentals=0),
        **extra,
    )(*args)


def flat(pairs):
    return [part for pair in pairs for part in pair]


def fetch_slab(order, j, refs, dst, sem):
    for m in range(8):

        @pl.when(order[j] == m)
        def _():
            pltpu.make_async_copy(refs[2 * m], dst.at[0], sem.at[0]).start()
            pltpu.make_async_copy(refs[2 * m + 1], dst.at[1], sem.at[1]).start()


def wait_slab(refs, dst, sem):
    pltpu.make_async_copy(refs[0], dst.at[0], sem.at[0]).wait()
    pltpu.make_async_copy(refs[1], dst.at[1], sem.at[1]).wait()


def cast_attn_kernel(master, low_l, low_r):
    low_l[...] = master[:, :HALF].astype(BF16)
    low_r[...] = master[:, HALF:].astype(BF16)


def cast_attn(master):
    block = pl.BlockSpec((256, HALF), lambda i: (0, 0))
    return call(
        cast_attn_kernel,
        [shape(256, HALF)] * 2,
        [pl.BlockSpec((256, 2 * HALF), lambda i: (0, 0))],
        [master],
        out_specs=[block] * 2,
        grid=(1,),
        moved=3 * 2**20,
    )


def cast_ffn_kernel(master, *rest):
    low_l, low_r = rest[-2:]
    row = pl.program_id(0) * 128 + lax.broadcasted_iota(jnp.int32, (128, 1), 0)
    kept = jnp.where(row < SLAB, master[...], 0.0).astype(BF16)
    low_l[...] = kept[:, :HALF]
    low_r[...] = kept[:, HALF:]


def cast_ffn(master, after):
    block = pl.BlockSpec((128, HALF), lambda i: (i, 0))
    return call(
        cast_ffn_kernel,
        [shape(PAD, HALF)] * 2,
        [pl.BlockSpec((128, 2 * HALF), lambda i: (i + 2, 0))] + [HB] * len(after),
        [master, *after],
        out_specs=[block] * 2,
        grid=(5,),
        moved=6 * 2**20,
    )


def root_of(values):
    return lax.rsqrt(jnp.mean(values * values, axis=-1, keepdims=True) + EPS_NORM)


def norm_one_kernel(tokens, gains, out_l, out_r):
    x = tokens[...].astype(F32)
    normed = (x * root_of(x) * gains[0:1, :]).astype(BF16)
    out_l[...] = normed[:, :HALF]
    out_r[...] = normed[:, HALF:]


def norm_one(tokens, gains):
    rows = tokens.shape[0]
    return call(norm_one_kernel, [shape(rows, HALF)] * 2, [VM, VM], [tokens, gains], moved=2**21)


def later_kernel(a_l, a_r, dy, *rest):
    out = rest[-4:]
    out[0][...] = a_l[...]
    out[1][...] = a_r[...]
    out[2][...] = dy[:, :HALF]
    out[3][...] = dy[:, HALF:]


def later(a_l, a_r, dy, after):
    rows = dy.shape[0]
    return call(
        later_kernel,
        [shape(rows, HALF)] * 4,
        [VM] * 3 + [HB] * len(after),
        [a_l, a_r, dy, *after],
        moved=2**22,
    )


def turn(values, cosine, sine):
    parts = []
    for h in range(values.shape[1] // HEAD_DIM):
        v = values[:, h * HEAD_DIM : (h + 1) * HEAD_DIM]
        parts.append(v * cosine + pltpu.roll(v, HEAD_DIM // 2, 1) * sine)
    return parts


def qkv_kernel(order, a_l, a_r, cosine, sine, *rest):
    refs, (q_l, q_r, k, v), (slab, sems) = rest[:16], rest[16:20], rest[20:]
    for j in range(6):
        fetch_slab(order, j, refs, slab.at[j], sems.at[j])
    for j in range(6):
        wait_slab(refs, slab.at[j], sems.at[j])
        made = lax.dot_general(a_l[...], slab[j, 0], NT, preferred_element_type=F32)
        made += lax.dot_general(a_r[...], slab[j, 1], NT, preferred_element_type=F32)
        if j < 4:
            made = turn(made, cosine[...], sine[...])
        else:
            made = [made[:, :HEAD_DIM], made[:, HEAD_DIM:]]
        for i, part in enumerate(made):
            if j < 2:
                (q_l, q_r)[j][:, i * HEAD_DIM : (i + 1) * HEAD_DIM] = part.astype(BF16)
            else:
                at = (2 * (j % 2) + i) * HEAD_DIM
                (k, v)[j // 2 - 1][:, at : at + HEAD_DIM] = part.astype(BF16)


def qkv(order, a_l, a_r, cosine, sine, pieces):
    rows = a_l.shape[0]
    return call(
        qkv_kernel,
        [shape(rows, 256)] * 2 + [shape(rows, QUART)] * 2,
        [SM] + [VM] * 4 + [HB] * 16,
        [order, a_l, a_r, cosine, sine, *flat(pieces)],
        [pltpu.VMEM((6, 2, 256, HALF), BF16), pltpu.SemaphoreType.DMA((6, 2))],
        flops=2 * rows * 1536 * 2048,
        moved=9 * 2**20,
    )


def quarter_out(place, full, outs):
    for m in range(4):
        at = pl.multiple_of((place[1] ^ m) * QUART, QUART)
        outs[m][...] = full[:, pl.ds(at, QUART)].astype(outs[m].dtype)


def quarter_in(place, pieces, full):
    for m in range(4):
        at = pl.multiple_of((place[1] ^ m) * QUART, QUART)
        full[:, pl.ds(at, QUART)] = pieces[m][...].astype(full.dtype)


def quarter_shapes(rows):
    return [shape(rows, QUART, F32)] + [shape(rows, QUART)] * 3


def attend_kernel(rows, scale, branch, place, order, q_l, q_r, where_k, *rest):
    keys, values, refs = rest[:8], rest[8:16], rest[16:32]
    (o_low, o_wide, stats, *parts) = rest[32:39]
    kcat, vcat, slab, total, sems, wsems = rest[39:]
    copies = []
    for m in range(8):
        copies.append(pltpu.make_async_copy(keys[m], kcat.at[pl.ds(m * rows, rows)], sems.at[0, m]))
        copies.append(pltpu.make_async_copy(values[m], vcat.at[pl.ds(m * rows, rows)], sems.at[1, m]))
    for copy in copies:
        copy.start()
    for j in (0, 1):
        fetch_slab(order, 6 + j, refs, slab.at[j], wsems.at[j])
    for copy in copies:
        copy.wait()
    at_q = place[0] * rows + lax.broadcasted_iota(jnp.int32, (rows, 1), 0)
    at_k = where_k[0:1, :]
    allowed = (at_k > at_q - WINDOW) & (at_k <= at_q)
    lane = lax.broadcasted_iota(jnp.int32, (rows, HEAD_DIM), 1)
    stat = jnp.zeros((rows, HEAD_DIM), F32)
    for h in range(4):
        cut = slice(h * HEAD_DIM, (h + 1) * HEAD_DIM)
        q = (q_l, q_r)[h // 2][:, (h % 2) * HEAD_DIM : (h % 2 + 1) * HEAD_DIM]
        s = lax.dot_general(q, kcat[:, cut], NT, preferred_element_type=F32)
        s = jnp.where(allowed, s * scale, NEGATIVE)
        top = jnp.max(s, axis=-1, keepdims=True)
        e = jnp.exp(s - top)
        sums = jnp.sum(e, axis=-1, keepdims=True)
        soft = (e / sums).astype(BF16)
        o = jnp.dot(soft, vcat[:, cut], preferred_element_type=F32)
        o_wide[:, cut] = o
        o_low[:, cut] = o.astype(BF16)
        stat = jnp.where(lane == h, top + jnp.log(sums), stat)
    stats[...] = stat
    for j in (0, 1):
        wait_slab(refs, slab.at[j], wsems.at[j])
    for side in (0, 1):
        made = jnp.dot(o_low[:, :256], slab[0, side], preferred_element_type=F32)
        made += jnp.dot(o_low[:, 256:], slab[1, side], preferred_element_type=F32)
        total[:, side * HALF : (side + 1) * HALF] = branch * made
    quarter_out(place, total, parts)


def attend(place, order, q_l, q_r, where_k, kv, pieces, scale, branch):
    rows = q_l.shape[0]
    return call(
        functools.partial(attend_kernel, rows, scale, branch),
        [shape(rows, QUART), shape(rows, QUART, F32), shape(rows, HEAD_DIM, F32)] + quarter_shapes(rows),
        [SM, SM, VM, VM, VM] + [HB] * 32,
        [place, order, q_l, q_r, where_k, *[p[0] for p in kv], *[p[1] for p in kv], *flat(pieces)],
        [
            pltpu.VMEM((8 * rows, QUART), BF16),
            pltpu.VMEM((8 * rows, QUART), BF16),
            pltpu.VMEM((2, 2, 256, HALF), BF16),
            pltpu.VMEM((rows, 2 * HALF), F32),
            pltpu.SemaphoreType.DMA((2, 8)),
            pltpu.SemaphoreType.DMA((2, 2)),
        ],
        flops=4 * 2 * 2 * rows * 8 * rows * 128 * 4,
        moved=12 * 2**20,
    )


def norm_two_kernel(place, tokens, gains, s0, s1, s2, s3, h_out, out_l, out_r):
    quarter_in(place, (s0, s1, s2, s3), h_out)
    h = h_out[...] + tokens[...].astype(F32)
    h_out[...] = h
    normed = (h * root_of(h) * gains[1:2, :]).astype(BF16)
    out_l[...] = normed[:, :HALF]
    out_r[...] = normed[:, HALF:]


def norm_two(place, tokens, gains, sums):
    rows = tokens.shape[0]
    return call(
        norm_two_kernel,
        [shape(rows, 2 * HALF, F32)] + [shape(rows, HALF)] * 2,
        [SM] + [VM] * 6,
        [place, tokens, gains, *sums],
        moved=4 * 2**20,
    )


def ffn_kernel(rows, place, order, inverse, a_l, a_r, dy, *rest):
    refs, sent, rest = rest[:16], rest[16:24], rest[24:]
    n_parts, b_parts = rest[:4], rest[4:8]
    slab, made, cut, n_sum, b_sum, sems = rest[8:]
    for j in range(8):
        fetch_slab(order, j, refs, slab.at[j], sems.at[j])
    dy_l, dy_r = dy[:, :HALF], dy[:, HALF:]

    def through(j, left, right):
        out = lax.dot_general(slab[j, 0], left, NT, preferred_element_type=F32)
        return out + lax.dot_general(slab[j, 1], right, NT, preferred_element_type=F32)

    made[pl.ds(8 * SLAB, 16), :] = jnp.zeros((16, rows), F32)
    for j in range(8):
        wait_slab(refs, slab.at[j], sems.at[j])
        if j < 5:
            out = through(j, a_l[...], a_r[...])
        elif j > 5:
            out = through(j, dy_l, dy_r)
        else:
            row = lax.broadcasted_iota(jnp.int32, (PAD, 1), 0)
            out = jnp.where(
                row < 2 * UNITS - 5 * SLAB, through(j, a_l[...], a_r[...]), through(j, dy_l, dy_r)
            )
        made[pl.ds(j * SLAB, PAD), :] = out

    def mix(i, _):
        at = pl.multiple_of(i * 32, 8)
        gate = made[pl.ds(at, 32), :]
        up = made[pl.ds(UNITS + at, 32), :]
        back = made[pl.ds(2 * UNITS + at, 32), :]
        sigma = 1.0 / (1.0 + jnp.exp(-gate))
        silu = gate * sigma
        made[pl.ds(at, 32), :] = back * up * (sigma * (1.0 + gate * (1.0 - sigma)))
        made[pl.ds(UNITS + at, 32), :] = back * silu
        made[pl.ds(2 * UNITS + at, 32), :] = silu * up
        return 0

    lax.fori_loop(0, UNITS // 32, mix, 0)
    for j in range(8):
        cut[j] = made[pl.ds(j * SLAB, PAD), :].astype(BF16)
    for m in range(8):
        sent[m][...] = cut[inverse[place[0] ^ m]]
    row = lax.broadcasted_iota(jnp.int32, (PAD, 1), 0)
    for side in (0, 1):
        columns = slice(side * HALF, (side + 1) * HALF)
        for total, kinds in ((n_sum, range(0, 6)), (b_sum, range(5, 8))):
            for j in kinds:
                z = cut[j]
                if j == 5:
                    first = row < 2 * UNITS - 5 * SLAB
                    z = jnp.where(first if total is n_sum else ~first, z, jnp.zeros_like(z))
                out = lax.dot_general(z, slab[j, side], TN, preferred_element_type=F32)
                total[:, columns] = out if j == kinds[0] else total[:, columns] + out
    quarter_out(place, n_sum, n_parts)
    quarter_out(place, b_sum, b_parts)


def ffn(place, order, inverse, a_l, a_r, dy, pieces):
    rows = dy.shape[0]
    return call(
        functools.partial(ffn_kernel, rows),
        [shape(PAD, rows)] * 8 + quarter_shapes(rows) * 2,
        [SM] * 3 + [VM] * 3 + [HB] * 16,
        [place, order, inverse, a_l, a_r, dy, *flat(pieces)],
        [
            pltpu.VMEM((8, 2, PAD, HALF), BF16),
            pltpu.VMEM((8 * SLAB + 16, rows), F32),
            pltpu.VMEM((8, PAD, rows), BF16),
            pltpu.VMEM((rows, 2 * HALF), F32),
            pltpu.VMEM((rows, 2 * HALF), F32),
            pltpu.SemaphoreType.DMA((8, 2)),
        ],
        flops=2 * 2 * rows * 8 * PAD * 2048,
        moved=20 * 2**20,
    )


def back_two_kernel(rows, branch, place, order, dy, h_in, gains, o_wide, stats, *rest):
    sums, refs = rest[:4], rest[4:20]
    d_out, low_l, low_r, gain_out, do_l, do_r = rest[20:26]
    slab, full, stat_l, stat_r, sems = rest[26:]
    for j in (0, 1):
        fetch_slab(order, 6 + j, refs, slab.at[j], sems.at[j])
    quarter_in(place, sums, full)
    normed_grad = full[...]
    h = h_in[...]
    root = root_of(h)
    gain_out[...] = jnp.sum(normed_grad * h * root, axis=0, keepdims=True)
    weighted = normed_grad * gains[1:2, :]
    inner = jnp.mean(weighted * h, axis=-1, keepdims=True)
    grad = dy[...].astype(F32) + root * weighted - h * (root * root * root) * inner
    d_out[...] = grad
    low = grad.astype(BF16)
    low_l[...] = low[:, :HALF]
    low_r[...] = low[:, HALF:]
    lane = lax.broadcasted_iota(jnp.int32, (rows, HEAD_DIM), 1)
    for j, (do, stat) in enumerate(((do_l, stat_l), (do_r, stat_r))):
        wait_slab(refs, slab.at[j], sems.at[j])
        made = lax.dot_general(low_l[...], slab[j, 0], NT, preferred_element_type=F32)
        made += lax.dot_general(low_r[...], slab[j, 1], NT, preferred_element_type=F32)
        made = (branch * made).astype(BF16)
        do[pl.ds(0, rows), :] = made
        lines = jnp.zeros((rows, HEAD_DIM), F32)
        for i in (0, 1):
            h_at = 2 * j + i
            cut = slice(h_at * HEAD_DIM, (h_at + 1) * HEAD_DIM)
            delta = jnp.sum(
                made[:, i * HEAD_DIM : (i + 1) * HEAD_DIM].astype(F32) * o_wide[:, cut], axis=-1, keepdims=True
            )
            top = stats[:, h_at : h_at + 1]
            for at, value in ((i, top), (2 + i, delta)):
                for step in range(3):
                    part = value.astype(BF16).astype(F32)
                    value = value - part
                    lines = jnp.where(lane == 4 * step + at, part, lines)
        stat[pl.ds(0, rows), :] = lines
        stat[pl.ds(rows, 256 - rows), :] = jnp.zeros((256 - rows, HEAD_DIM), F32)
        do[pl.ds(rows, 16), :] = stat[...].T[:16, :].astype(BF16)


def back_two(place, order, dy, h, gains, o_wide, stats, sums, pieces, branch):
    rows = dy.shape[0]
    return call(
        functools.partial(back_two_kernel, rows, branch),
        [shape(rows, 2 * HALF, F32), shape(rows, HALF), shape(rows, HALF), shape(1, 2 * HALF, F32)]
        + [shape(rows + 16, 256)] * 2,
        [SM, SM] + [VM] * 9 + [HB] * 16,
        [place, order, dy, h, gains, o_wide, stats, *sums, *flat(pieces)],
        [
            pltpu.VMEM((2, 2, 256, HALF), BF16),
            pltpu.VMEM((rows, 2 * HALF), F32),
            pltpu.VMEM((256, HEAD_DIM), F32),
            pltpu.VMEM((256, HEAD_DIM), F32),
            pltpu.SemaphoreType.DMA((2, 2)),
        ],
        flops=2 * rows * 512 * 2048,
        moved=9 * 2**20,
    )


def attend_back_kernel(rows, scale, place, order, inverse, cosine, sine, o_low, *rest):
    qs, keys, values, dos, refs = rest[:16], rest[16:24], rest[24:32], rest[32:48], rest[48:64]
    sent, parts = rest[64:72], rest[72:76]
    qcat, kcat, vcat, docat, slab, dq, dk, dv, groups, total, sems, wsems = rest[76:]
    copies = []
    for m in range(8):
        copies.append(pltpu.make_async_copy(keys[m], kcat.at[m], sems.at[0, m]))
        copies.append(pltpu.make_async_copy(values[m], vcat.at[m], sems.at[1, m]))
        for side in (0, 1):
            copies.append(pltpu.make_async_copy(qs[2 * m + side], qcat.at[m, side], sems.at[2 + side, m]))
            copies.append(pltpu.make_async_copy(dos[2 * m + side], docat.at[m, side], sems.at[4 + side, m]))
    for copy in copies:
        copy.start()
    for j in range(6):
        fetch_slab(order, j, refs, slab.at[j], wsems.at[j])
    for copy in copies:
        copy.wait()
    dq[...] = jnp.zeros_like(dq)
    dk[...] = jnp.zeros_like(dk)
    dv[...] = jnp.zeros_like(dv)
    me = place[0]
    reach = -(-WINDOW // rows)
    down = lax.broadcasted_iota(jnp.int32, (rows, rows), 0)
    along = lax.broadcasted_iota(jnp.int32, (rows, rows), 1)

    def head_cut(h):
        return h // 2, slice((h % 2) * HEAD_DIM, (h % 2 + 1) * HEAD_DIM), slice(h * HEAD_DIM, (h + 1) * HEAD_DIM)

    def sums_of(lines, at):
        return lines[at : at + 1] + lines[4 + at : 5 + at] + lines[8 + at : 9 + at]

    def lines_of(m, side):
        return docat[m, side, pl.ds(rows, 16), :].astype(F32)

    own = []
    for side in (0, 1):
        lines = lines_of(0, side)
        whole = lines[0:4] + lines[4:8] + lines[8:12]
        own.append(jnp.concatenate([whole, jnp.zeros((124, 256), F32)], axis=0).T[:rows, :])

    def step(m, _):
        apart = me - (me ^ m)

        @pl.when((apart >= 0) & (apart <= reach))
        def _():
            ahead = apart * rows + down - along
            allowed = (ahead >= 0) & (ahead < WINDOW)
            for h in range(4):
                side, two, cut = head_cut(h)
                k, do = kcat[m, :, cut], docat[0, side, pl.ds(0, rows), two]
                s = lax.dot_general(qcat[0, side, :, two], k, NT, preferred_element_type=F32)
                p = jnp.where(allowed, jnp.exp(s * scale - own[side][:, h % 2 : h % 2 + 1]), 0.0)
                dp = lax.dot_general(do, vcat[m, :, cut], NT, preferred_element_type=F32)
                ds = (p * (dp - own[side][:, 2 + h % 2 : 3 + h % 2]) * scale).astype(BF16)
                dq[:, cut] += jnp.dot(ds, k, preferred_element_type=F32)

        @pl.when((apart <= 0) & (apart >= -reach))
        def _():
            ahead = along - down - apart * rows
            allowed = (ahead >= 0) & (ahead < WINDOW)
            for side in (0, 1):
                lines = lines_of(m, side)
                for i in (0, 1):
                    side, two, cut = head_cut(2 * side + i)
                    q, do = qcat[m, side, :, two], docat[m, side, pl.ds(0, rows), two]
                    top, delta = sums_of(lines, i)[:, :rows], sums_of(lines, 2 + i)[:, :rows]
                    s = lax.dot_general(kcat[0, :, cut], q, NT, preferred_element_type=F32)
                    p = jnp.where(allowed, jnp.exp(s * scale - top), 0.0)
                    dv[:, cut] += jnp.dot(p.astype(BF16), do, preferred_element_type=F32)
                    dp = lax.dot_general(vcat[0, :, cut], do, NT, preferred_element_type=F32)
                    ds = (p * (dp - delta) * scale).astype(BF16)
                    dk[:, cut] += jnp.dot(ds, q, preferred_element_type=F32)

        return 0

    lax.fori_loop(0, 8, step, 0)
    for j in range(8):
        cut = slice((j % 2) * 256, (j % 2 + 1) * 256)
        if j < 4:
            made = turn((dq, dk)[j // 2][:, cut], cosine[...], -sine[...])
            for i in (0, 1):
                groups[j, :, i * HEAD_DIM : (i + 1) * HEAD_DIM] = made[i].astype(BF16)
        elif j < 6:
            groups[j] = dv[:, cut].astype(BF16)
        else:
            groups[j] = o_low[:, cut]
    for m in range(8):
        sent[m][...] = groups[inverse[me ^ m]]
    for j in range(6):
        wait_slab(refs, slab.at[j], wsems.at[j])
        for side in (0, 1):
            out = jnp.dot(groups[j], slab[j, side], preferred_element_type=F32)
            columns = slice(side * HALF, (side + 1) * HALF)
            total[:, columns] = out if j == 0 else total[:, columns] + out
    quarter_out(place, total, parts)


def attend_back(place, order, inverse, cosine, sine, o_low, qs, kv, dos, pieces, scale):
    rows = o_low.shape[0]
    return call(
        functools.partial(attend_back_kernel, rows, scale),
        [shape(rows, 256)] * 8 + quarter_shapes(rows),
        [SM] * 3 + [VM] * 3 + [HB] * 64,
        [place, order, inverse, cosine, sine, o_low]
        + flat(qs) + [p[0] for p in kv] + [p[1] for p in kv] + flat(dos) + flat(pieces),
        [
            pltpu.VMEM((8, 2, rows, 256), BF16),
            pltpu.VMEM((8, rows, QUART), BF16),
            pltpu.VMEM((8, rows, QUART), BF16),
            pltpu.VMEM((8, 2, rows + 16, 256), BF16),
            pltpu.VMEM((6, 2, 256, HALF), BF16),
            pltpu.VMEM((rows, QUART), F32),
            pltpu.VMEM((rows, QUART), F32),
            pltpu.VMEM((rows, QUART), F32),
            pltpu.VMEM((8, rows, 256), BF16),
            pltpu.VMEM((rows, 2 * HALF), F32),
            pltpu.SemaphoreType.DMA((6, 8)),
            pltpu.SemaphoreType.DMA((6, 2)),
        ],
        flops=3 * 10**9,
        moved=20 * 2**20,
    )


def back_one_kernel(place, tokens, d_in, gains, s0, s1, s2, s3, out, gain_out, full):
    quarter_in(place, (s0, s1, s2, s3), full)
    normed_grad = full[...]
    x = tokens[...].astype(F32)
    root = root_of(x)
    gain_out[...] = jnp.sum(normed_grad * x * root, axis=0, keepdims=True)
    weighted = normed_grad * gains[0:1, :]
    inner = jnp.mean(weighted * x, axis=-1, keepdims=True)
    out[...] = d_in[...] + root * weighted - x * (root * root * root) * inner


def back_one(place, tokens, d_in, gains, sums):
    rows = tokens.shape[0]
    return call(
        back_one_kernel,
        [shape(rows, 2 * HALF, F32), shape(1, 2 * HALF, F32)],
        [SM] + [VM] * 7,
        [place, tokens, d_in, gains, *sums],
        [pltpu.VMEM((rows, 2 * HALF), F32)],
        moved=5 * 2**20,
    )


TILE = 256


def update_kernel(rows, branch, slabs, *rest):
    zs, gs, rest = rest[:8], rest[8:16], rest[16:]
    acts, rest = [rest[16 * i : 16 * i + 16] for i in range(4)], rest[64:]
    basis, first, second, master = rest[:4]
    grad, first_new, second_new, master_new, low_new = rest[4:9]
    turned_g, act, = rest[9:]
    tile = pl.program_id(0)
    a_slab, f_slab = slabs[0], slabs[1]

    @pl.when(tile == 0)
    def _():
        for m in range(8):
            turned_g[:, m * rows : (m + 1) * rows] = gs[m][...].T

    def take(kind):
        for m in range(8):
            for side in (0, 1):

                @pl.when((tile >= 4) == (side == 1))
                def _():
                    act[pl.ds(m * rows, rows), :] = acts[kind][2 * m + side][...]

    def ffn_rows():
        total = jnp.dot(zs[0][...], act[pl.ds(0, rows), :], preferred_element_type=F32)
        for m in range(1, 8):
            total += jnp.dot(zs[m][...], act[pl.ds(m * rows, rows), :], preferred_element_type=F32)
        return total[:SLAB]

    @pl.when(a_slab < 6)
    def _():
        take(0)
        grad[pl.ds(0, 256), :] = jnp.dot(turned_g[...], act[...], preferred_element_type=F32)

    @pl.when(a_slab >= 6)
    def _():
        take(3)
        grad[pl.ds(0, 256), :] = branch * jnp.dot(turned_g[...], act[...], preferred_element_type=F32)

    @pl.when(f_slab <= 5)
    def _():
        take(1)
        grad[pl.ds(256, SLAB), :] = ffn_rows()

    @pl.when(f_slab > 5)
    def _():
        take(2)
        grad[pl.ds(256, SLAB), :] = ffn_rows()

    first_of_down = 2 * UNITS - f_slab * SLAB

    @pl.when(f_slab == 5)
    def _():
        take(2)
        row = lax.broadcasted_iota(jnp.int32, (SLAB, 1), 0)
        grad[pl.ds(256, SLAB), :] = jnp.where(row < first_of_down, grad[pl.ds(256, SLAB), :], ffn_rows())

    row = lax.broadcasted_iota(jnp.int32, (256 + SLAB, 1), 0)
    rate = jnp.where((row < 256) | (row - 256 < first_of_down), 0.5 * (2 * HALF) ** (-0.5), 0.5 * FF ** (-0.5))
    for b in range(TILE // HEAD_DIM):
        cut = slice(b * HEAD_DIM, (b + 1) * HEAD_DIM)
        turned = jnp.dot(grad[:, cut], basis[b], precision=PRECISE, preferred_element_type=F32)
        one = BETA_FIRST * first[:, cut] + (1.0 - BETA_FIRST) * turned
        two = BETA_SECOND * second[:, cut] + (1.0 - BETA_SECOND) * turned * turned
        first_new[:, cut] = one
        second_new[:, cut] = two
        adam = (one / (1.0 - BETA_FIRST**ADAM_STEP)) / (
            jnp.sqrt(two / (1.0 - BETA_SECOND**ADAM_STEP)) + ADAM_EPS
        )
        back = lax.dot_general(adam, basis[b], NT, precision=PRECISE, preferred_element_type=F32)
        old = master[:, cut]
        new = old - rate * (back + DECAY_RATE * old)
        master_new[:, cut] = new
        low_new[:, cut] = new.astype(BF16)


def update(slabs, zs, gs, acts, basis, first, second, master, branch):
    rows = gs[0].shape[0]
    height, width = master.shape

    def whole(array):
        return pl.BlockSpec(array.shape, lambda i: (0,) * array.ndim)

    left = pl.BlockSpec((rows, TILE), lambda i: (0, jnp.minimum(i, HALF // TILE - 1)))
    right = pl.BlockSpec((rows, TILE), lambda i: (0, jnp.maximum(i - HALF // TILE, 0)))
    tall = pl.BlockSpec((height, TILE), lambda i: (0, i))
    per = TILE // HEAD_DIM
    return call(
        functools.partial(update_kernel, rows, branch),
        [jax.ShapeDtypeStruct(master.shape, F32)] * 4 + [jax.ShapeDtypeStruct(master.shape, BF16)],
        [SM]
        + [whole(z) for z in zs]
        + [whole(g) for g in gs]
        + [left, right] * 32
        + [pl.BlockSpec((per, HEAD_DIM, HEAD_DIM), lambda i: (i, 0, 0))]
        + [tall] * 3,
        [slabs, *zs, *gs, *[part for pairs in acts for part in flat(pairs)], basis, first, second, master],
        [pltpu.VMEM((256, 8 * rows), BF16), pltpu.VMEM((8 * rows, TILE), BF16)],
        out_specs=[tall] * 5,
        grid=(width // TILE,),
        flops=2 * 8 * rows * height * width,
        moved=70 * 2**20,
    )


def plane_mesh(
    tokens,
    cotangent,
    owners,
    master,
    first_moment,
    second_moment,
    eigenbases,
    norm_gains,
    gain_first,
    gain_second,
):
    rows, width = tokens.shape
    me, line = lax.axis_index("seq"), lax.axis_index("head")
    scale = HEAD_DIM ** (-0.5)
    branch = (WINDOW / 3.0) ** 0.5
    place = jnp.stack([me, line]).astype(jnp.int32)
    inverse_attn, inverse_ffn = inverse_order(owners[0]), inverse_order(owners[1])
    order_attn, order_ffn = owners[0] ^ me, owners[1] ^ me
    slabs = jnp.stack([inverse_attn[me], inverse_ffn[me]]).astype(jnp.int32)
    old = master[0, 0]
    attn = gather_plane(*cast_attn(old))
    gains = lax.all_gather(norm_gains.astype(BF16), "seq", axis=1, tiled=True).astype(F32)
    ffn_all = gather_plane(*cast_ffn(old, attn[6]))
    a_l, a_r = norm_one(tokens, gains)
    cosine, sine = angles((me * rows + jnp.arange(rows, dtype=jnp.int32)).astype(F32))
    cosine, sine = cosine[:, 0, :], sine[:, 0, :]
    cosine = jnp.concatenate([cosine, cosine], axis=1)
    sine = jnp.concatenate([-sine, sine], axis=1)
    q_l, q_r, k, v = qkv(order_attn, a_l, a_r, cosine, sine, attn)
    kv = gather_plane(k, v)
    sources = me ^ jnp.arange(8, dtype=jnp.int32)
    where_k = (sources[:, None] * rows + jnp.arange(rows, dtype=jnp.int32)[None, :]).reshape(1, 8 * rows)
    where_k = jnp.broadcast_to(where_k, (8, 8 * rows))
    o_low, o_wide, stats, *parts = attend(
        place, order_attn, q_l, q_r, where_k, kv, attn, scale, branch
    )
    h, b_l, b_r = norm_two(place, tokens, gains, line_sum(parts))
    made = ffn(place, order_ffn, inverse_ffn, b_l, b_r, cotangent, ffn_all)
    sent_ffn, n_parts, b_parts = made[:8], made[8:12], made[12:]
    n_sums = line_sum(n_parts)
    d_one, d_l, d_r, gain_two, do_l, do_r = back_two(
        place, order_attn, cotangent, h, gains, o_wide, stats, n_sums, attn, branch
    )
    qs = gather_plane(q_l, q_r)
    dos = gather_plane(do_l, do_r)
    *sent_attn, p0, p1, p2, p3 = attend_back(
        place, order_attn, inverse_attn, cosine, sine, o_low, qs, kv, dos, attn, scale
    )
    input_grad, gain_one = back_one(place, tokens, d_one, gains, line_sum([p0, p1, p2, p3]))
    late = later(a_l, a_r, cotangent, ffn_all[6])
    acts = [gather_plane(*late[:2]), gather_plane(b_l, b_r), gather_plane(*late[2:]), gather_plane(d_l, d_r)]
    zs = [sent_ffn[0]] + [hop(sent_ffn[m], "seq", m) for m in range(1, 8)]
    gs = [sent_attn[0]] + [hop(sent_attn[m], "seq", m) for m in range(1, 8)]
    grad, first_new, second_new, master_new, low_new = update(
        slabs, zs, gs, acts, eigenbases[0, 0], first_moment[0, 0], second_moment[0, 0], old, branch
    )
    got = [hop(b_parts[m], "head", m) for m in (1, 2, 3)]
    kept = lax.dynamic_slice_in_dim(h, line * QUART, QUART, 1)
    block_out = kept + b_parts[0] + got[0].astype(F32) + got[1].astype(F32) + got[2].astype(F32)
    gain_parts = jnp.concatenate([gain_one, gain_two], axis=0)
    share = width // 8
    gain_grad = lax.dynamic_slice_in_dim(gain_parts, me * share, share, 1)
    for m in range(1, 8):
        gain_grad += hop(lax.dynamic_slice_in_dim(gain_parts, (me ^ m) * share, share, 1), "seq", m)
    gain_first_new = BETA_FIRST * gain_first + (1.0 - BETA_FIRST) * gain_grad
    gain_second_new = BETA_SECOND * gain_second + (1.0 - BETA_SECOND) * gain_grad * gain_grad
    gain_new = norm_gains - GAIN_RATE * (gain_first_new / (1.0 - BETA_FIRST**ADAM_STEP)) / (
        jnp.sqrt(gain_second_new / (1.0 - BETA_SECOND**ADAM_STEP)) + ADAM_EPS
    )
    return (
        block_out.astype(BF16),
        input_grad,
        grad[None, None],
        first_new[None, None],
        second_new[None, None],
        master_new[None, None],
        low_new[None, None],
        gain_grad,
        gain_first_new,
        gain_second_new,
        gain_new,
    )


def solution(mesh):
    in_specs = (
        P("seq", None),
        P("seq", None),
        P(),
        P("head", "seq", None, None),
        P("head", "seq", None, None),
        P("head", "seq", None, None),
        P("head", "seq", None, None, None),
        P(None, "seq"),
        P(None, "seq"),
        P(None, "seq"),
    )
    out_specs = (
        P("seq", "head"),
        P("seq", None),
        P("head", "seq", None, None),
        P("head", "seq", None, None),
        P("head", "seq", None, None),
        P("head", "seq", None, None),
        P("head", "seq", None, None),
        P(None, "seq"),
        P(None, "seq"),
        P(None, "seq"),
        P(None, "seq"),
    )
    plane = mesh.shape["seq"] == 8 and mesh.shape["head"] == 4
    return jax.shard_map(
        plane_mesh if plane else any_mesh, mesh=mesh, in_specs=in_specs, out_specs=out_specs, check_vma=False
    )
```

```python
import functools

import jax
import jax.numpy as jnp
from jax import lax
from jax.experimental import pallas as pl
from jax.experimental.pallas import tpu as pltpu
from jax.sharding import PartitionSpec as P

HEADS = 16
HEAD_DIM = 128
FF = 5504
WINDOW = 1024
ADAM_STEP = 5


EPS_NORM = 1e-05
BETA_FIRST = 0.5
BETA_SECOND = 0.6
ADAM_EPS = 1e-08
DECAY_RATE = 0.1
GAIN_RATE = 0.25
ROPE_BASE = 10000.0
NEGATIVE = -1e30
PRECISE = lax.Precision.HIGHEST

BF16 = jnp.bfloat16
F32 = jnp.float32


def passed_along(shard, axis, by):
    devices = lax.axis_size(axis)
    pairs = [(i, i + by) for i in range(devices) if 0 <= i + by < devices]
    return lax.ppermute(shard, axis, pairs)


def inverse_order(owner_row):
    places = jnp.arange(owner_row.shape[0], dtype=jnp.int32)
    matches = (owner_row[:, None] == places[None, :]).astype(jnp.int32)
    return jnp.sum(matches * places[:, None], axis=0)


def kind_rates(kinds, width):
    wide = width ** (-0.5)
    spreads = jnp.array([wide, wide, wide, wide, wide, wide, FF ** (-0.5)], jnp.float32)
    matches = (kinds[..., None] == jnp.arange(7, dtype=jnp.int32)).astype(jnp.float32)
    return 0.5 * jnp.sum(matches * spreads, axis=-1)


def angles(positions):
    half_dim = HEAD_DIM // 2
    frequencies = ROPE_BASE ** (-jnp.arange(half_dim, dtype=jnp.float32) / half_dim)
    turning = positions[:, None] * frequencies[None, :]
    return (jnp.cos(turning)[:, None, :], jnp.sin(turning)[:, None, :])


def rotate(vectors, cosine, sine):
    half_dim = vectors.shape[-1] // 2
    former = vectors[..., :half_dim]
    latter = vectors[..., half_dim:]
    return jnp.concatenate(
        [former * cosine - latter * sine, latter * cosine + former * sine], axis=-1
    )


def inverse_rms(vectors):
    return lax.rsqrt(jnp.mean(vectors * vectors, axis=-1, keepdims=True) + EPS_NORM)


def norm_back(grad_normed, inputs, rms_values, gain_row):
    weighted = grad_normed * gain_row
    inner = jnp.mean(weighted * inputs, axis=-1, keepdims=True)
    input_part = rms_values * weighted - inputs * rms_values**3 * inner
    return (input_part, jnp.sum(grad_normed * inputs * rms_values, axis=0))


def any_mesh(
    tokens,
    cotangent,
    owners,
    master,
    first_moment,
    second_moment,
    eigenbases,
    norm_gains,
    gain_first,
    gain_second,
):
    tok_rows, width = tokens.shape
    seq_devices = lax.axis_size("seq")
    head_devices = lax.axis_size("head")
    seq_place = lax.axis_index("seq")
    head_place = lax.axis_index("head")
    slab_rows = master.shape[2]
    attn_slab = 4 * width // (head_devices * seq_devices)
    ffn_slab = slab_rows - attn_slab
    head_width = width // head_devices
    ffn_width = FF // head_devices
    local_heads = HEADS // head_devices
    score_scale = HEAD_DIM ** (-0.5)
    branch_scale = (WINDOW / 3.0) ** 0.5
    inverse_attn = inverse_order(owners[0])
    inverse_ffn = inverse_order(owners[1])
    master_low = master[0, 0].astype(jnp.bfloat16)
    gathered, gains_all = (
        lax.all_gather(master_low, "seq", axis=0, tiled=True),
        lax.all_gather(norm_gains.astype(jnp.bfloat16), "seq", axis=1, tiled=True),
    )
    gathered = gathered.reshape(seq_devices, slab_rows, width)
    attn_rows = jnp.take(gathered[:, :attn_slab], owners[0], axis=0).reshape(4 * head_width, width)
    ffn_rows = jnp.take(gathered[:, attn_slab:], owners[1], axis=0).reshape(3 * ffn_width, width)
    w_query = attn_rows[:head_width]
    w_key = attn_rows[head_width : 2 * head_width]
    w_value = attn_rows[2 * head_width : 3 * head_width]
    w_out = attn_rows[3 * head_width :]
    w_gate = ffn_rows[:ffn_width]
    w_up = ffn_rows[ffn_width : 2 * ffn_width]
    w_down = ffn_rows[2 * ffn_width :]
    gain_one = gains_all[0].astype(jnp.float32)
    gain_two = gains_all[1].astype(jnp.float32)
    inputs = tokens.astype(jnp.float32)
    rms_one = inverse_rms(inputs)
    normed_one = (inputs * rms_one * gain_one).astype(jnp.bfloat16)
    positions = (seq_place * tok_rows + jnp.arange(tok_rows, dtype=jnp.int32)).astype(jnp.float32)
    cosine, sine = angles(positions)
    head_shape = (tok_rows, local_heads, HEAD_DIM)

    def project(weight_rows):
        return jnp.einsum("td,id->ti", normed_one, weight_rows, preferred_element_type=jnp.float32)

    queries = rotate(project(w_query).reshape(head_shape), cosine, sine).astype(jnp.bfloat16)
    keys_own = rotate(project(w_key).reshape(head_shape), cosine, sine).astype(jnp.bfloat16)
    values_own = project(w_value).reshape(head_shape).astype(jnp.bfloat16)
    hop_total = -(-WINDOW // tok_rows)
    hop_sizes = [
        min(tok_rows, WINDOW - (hop_index - 1) * tok_rows) for hop_index in range(1, hop_total + 1)
    ]
    halo_keys = []
    halo_values = []
    for hop_index in range(hop_total, 0, -1):
        hop_rows = hop_sizes[hop_index - 1]
        far_keys, far_values = passed_along(
            (keys_own[tok_rows - hop_rows :], values_own[tok_rows - hop_rows :]), "seq", hop_index
        )
        halo_keys.append(far_keys)
        halo_values.append(far_values)
    keys_all = jnp.concatenate(halo_keys + [keys_own], axis=0)
    values_all = jnp.concatenate(halo_values + [values_own], axis=0)
    row_ids = jnp.arange(tok_rows, dtype=jnp.int32)[:, None]
    col_ids = jnp.arange(WINDOW + tok_rows, dtype=jnp.int32)[None, :]
    allowed = (
        (col_ids > row_ids)
        & (col_ids <= row_ids + WINDOW)
        & (seq_place * tok_rows - WINDOW + col_ids >= 0)
    )

    def scores_of():
        raw = jnp.einsum("thd,chd->htc", queries, keys_all, preferred_element_type=jnp.float32)
        return jnp.where(allowed[None], raw * score_scale, NEGATIVE)

    scores = scores_of()
    row_top = jnp.max(scores, axis=-1, keepdims=True)
    exp_scores = jnp.exp(scores - row_top)
    exp_total = jnp.sum(exp_scores, axis=-1, keepdims=True)
    soft_low = (exp_scores / exp_total).astype(jnp.bfloat16)
    log_total = row_top + jnp.log(exp_total)
    attended = jnp.einsum("htc,chd->thd", soft_low, values_all, preferred_element_type=jnp.float32)
    attended_low = attended.reshape(tok_rows, head_width).astype(jnp.bfloat16)
    attn_part = branch_scale * jnp.dot(attended_low, w_out, preferred_element_type=jnp.float32)
    hidden_one = inputs + lax.psum(attn_part, "head")
    rms_two = inverse_rms(hidden_one)
    normed_two = (hidden_one * rms_two * gain_two).astype(jnp.bfloat16)
    gate_pre = jnp.einsum("td,fd->tf", normed_two, w_gate, preferred_element_type=jnp.float32)
    up_pre = jnp.einsum("td,fd->tf", normed_two, w_up, preferred_element_type=jnp.float32)
    sigma = jax.nn.sigmoid(gate_pre)
    hidden_low = (gate_pre * sigma * up_pre).astype(jnp.bfloat16)
    ffn_part = jnp.dot(hidden_low, w_down, preferred_element_type=jnp.float32)
    ffn_share = lax.psum_scatter(ffn_part, "head", scatter_dimension=1, tiled=True)
    share_width = width // head_devices
    residual_share = lax.dynamic_slice_in_dim(hidden_one, head_place * share_width, share_width, 1)
    block_out = (residual_share + ffn_share).astype(jnp.bfloat16)
    grad_out_f = cotangent.astype(jnp.float32)
    hidden_grad = jnp.einsum("td,fd->tf", cotangent, w_down, preferred_element_type=jnp.float32)
    silu_grad = sigma * (1.0 + gate_pre * (1.0 - sigma))
    gate_grad = (hidden_grad * up_pre * silu_grad).astype(jnp.bfloat16)
    up_grad = (hidden_grad * gate_pre * sigma).astype(jnp.bfloat16)
    down_grad = jnp.einsum("tf,td->fd", hidden_low, cotangent, preferred_element_type=jnp.float32)
    gate_w_grad = jnp.einsum("tf,td->fd", gate_grad, normed_two, preferred_element_type=jnp.float32)
    up_w_grad = jnp.einsum("tf,td->fd", up_grad, normed_two, preferred_element_type=jnp.float32)
    ffn_rows_grad = jnp.concatenate([gate_w_grad, up_w_grad, down_grad], axis=0)
    ffn_owner = jnp.take(ffn_rows_grad.reshape(seq_devices, ffn_slab, width), inverse_ffn, axis=0)
    normed_two_part = jnp.einsum(
        "tf,fd->td", gate_grad, w_gate, preferred_element_type=jnp.float32
    ) + jnp.einsum("tf,fd->td", up_grad, w_up, preferred_element_type=jnp.float32)
    normed_two_share = lax.psum_scatter(normed_two_part, "head", scatter_dimension=1, tiled=True)
    normed_two_grad = lax.all_gather(normed_two_share, "head", axis=1, tiled=True)
    back_two, gain_two_grad = norm_back(normed_two_grad, hidden_one, rms_two, gain_two)
    hidden_one_grad = grad_out_f + back_two
    hidden_grad_low = hidden_one_grad.astype(jnp.bfloat16)
    attended_grad = branch_scale * jnp.einsum(
        "td,id->ti", hidden_grad_low, w_out, preferred_element_type=jnp.float32
    )
    attended_grad = attended_grad.reshape(head_shape).astype(jnp.bfloat16)
    soft_again = jnp.exp(scores_of() - log_total)
    soft_grad = jnp.einsum(
        "thd,chd->htc", attended_grad, values_all, preferred_element_type=jnp.float32
    )
    inner_sum = jnp.sum(soft_again * soft_grad, axis=-1, keepdims=True)
    score_grad = (soft_again * (soft_grad - inner_sum) * score_scale).astype(jnp.bfloat16)
    query_grad_turned = jnp.einsum(
        "htc,chd->thd", score_grad, keys_all, preferred_element_type=jnp.float32
    )
    key_grad_all = jnp.einsum(
        "htc,thd->chd", score_grad, queries, preferred_element_type=jnp.float32
    )
    value_grad_all = jnp.einsum(
        "htc,thd->chd", soft_low, attended_grad, preferred_element_type=jnp.float32
    )
    key_grad_own = key_grad_all[WINDOW:]
    value_grad_own = value_grad_all[WINDOW:]
    start_at = 0
    for hop_index in range(hop_total, 0, -1):
        hop_rows = hop_sizes[hop_index - 1]
        back_keys, back_values = passed_along(
            (
                key_grad_all[start_at : start_at + hop_rows],
                value_grad_all[start_at : start_at + hop_rows],
            ),
            "seq",
            -hop_index,
        )
        key_grad_own = key_grad_own.at[tok_rows - hop_rows :].add(back_keys)
        value_grad_own = value_grad_own.at[tok_rows - hop_rows :].add(back_values)
        start_at = start_at + hop_rows
    query_grad = (
        rotate(query_grad_turned, cosine, -sine).reshape(tok_rows, head_width).astype(jnp.bfloat16)
    )
    key_grad = (
        rotate(key_grad_own, cosine, -sine).reshape(tok_rows, head_width).astype(jnp.bfloat16)
    )
    value_grad = value_grad_own.reshape(tok_rows, head_width).astype(jnp.bfloat16)

    def input_part(row_grad, weight_rows):
        return jnp.einsum("ti,id->td", row_grad, weight_rows, preferred_element_type=jnp.float32)

    normed_one_part = (
        input_part(query_grad, w_query)
        + input_part(key_grad, w_key)
        + input_part(value_grad, w_value)
    )
    normed_one_share = lax.psum_scatter(normed_one_part, "head", scatter_dimension=1, tiled=True)
    normed_one_grad = lax.all_gather(
        normed_one_share.astype(jnp.bfloat16), "head", axis=1, tiled=True
    ).astype(normed_one_share.dtype)
    back_one, gain_one_grad = norm_back(normed_one_grad, inputs, rms_one, gain_one)
    input_grad = hidden_one_grad + back_one
    gain_grads = jnp.stack([gain_one_grad, gain_two_grad])

    def rows_grad(row_grad):
        return jnp.einsum("ti,td->id", row_grad, normed_one, preferred_element_type=jnp.float32)

    out_w_grad = branch_scale * jnp.einsum(
        "ti,td->id", attended_low, hidden_grad_low, preferred_element_type=jnp.float32
    )
    attn_rows_grad = jnp.concatenate(
        [rows_grad(query_grad), rows_grad(key_grad), rows_grad(value_grad), out_w_grad], axis=0
    )
    attn_owner = jnp.take(
        attn_rows_grad.reshape(seq_devices, attn_slab, width), inverse_attn, axis=0
    )
    owner_rows = jnp.concatenate([attn_owner, ffn_owner], axis=1).reshape(
        seq_devices * slab_rows, width
    )
    reduced, gain_reduced = (
        lax.psum_scatter(owner_rows, "seq", scatter_dimension=0, tiled=True),
        lax.psum_scatter(gain_grads, "seq", scatter_dimension=1, tiled=True),
    )
    attn_kinds = (
        inverse_attn[seq_place] * attn_slab + jnp.arange(attn_slab, dtype=jnp.int32)
    ) // head_width
    ffn_kinds = (
        4 + (inverse_ffn[seq_place] * ffn_slab + jnp.arange(ffn_slab, dtype=jnp.int32)) // ffn_width
    )
    row_rates = kind_rates(jnp.concatenate([attn_kinds, ffn_kinds]), width)[:, None]
    basis = eigenbases[0, 0]
    block_size = basis.shape[-1]
    split_shape = (slab_rows, width // block_size, block_size)
    turned = jnp.einsum(
        "rbk,bkl->rbl", reduced.reshape(split_shape), basis, precision=PRECISE
    ).reshape(slab_rows, width)
    first_new = BETA_FIRST * first_moment[0, 0] + (1.0 - BETA_FIRST) * turned
    second_new = BETA_SECOND * second_moment[0, 0] + (1.0 - BETA_SECOND) * turned * turned
    adam_dir = (
        first_new
        / (1.0 - BETA_FIRST**ADAM_STEP)
        / (jnp.sqrt(second_new / (1.0 - BETA_SECOND**ADAM_STEP)) + ADAM_EPS)
    )
    backward_dir = jnp.einsum(
        "rbl,bkl->rbk", adam_dir.reshape(split_shape), basis, precision=PRECISE
    ).reshape(slab_rows, width)
    master_old = master[0, 0]
    master_new = master_old - row_rates * (backward_dir + DECAY_RATE * master_old)
    gain_first_new = BETA_FIRST * gain_first + (1.0 - BETA_FIRST) * gain_reduced
    gain_second_new = BETA_SECOND * gain_second + (1.0 - BETA_SECOND) * gain_reduced * gain_reduced
    gain_new = norm_gains - GAIN_RATE * (gain_first_new / (1.0 - BETA_FIRST**ADAM_STEP)) / (
        jnp.sqrt(gain_second_new / (1.0 - BETA_SECOND**ADAM_STEP)) + ADAM_EPS
    )
    return (
        block_out,
        input_grad,
        reduced[None, None],
        first_new[None, None],
        second_new[None, None],
        master_new[None, None],
        master_new.astype(jnp.bfloat16)[None, None],
        gain_reduced,
        gain_first_new,
        gain_second_new,
        gain_new,
    )


SLAB = 516
PAD = 528
HALF = 1024
QUART = 512
UNITS = 1376
NT = (((1,), (1,)), ((), ()))
TN = (((0,), (0,)), ((), ()))


def hop(value, axis, mask):
    return lax.ppermute(value, axis, [(i, i ^ mask) for i in range(lax.axis_size(axis))])


def gather_plane(top, low):
    x_top, y_low = hop(top, "seq", 2), hop(low, "seq", 4)
    x_low, y_top = hop(low, "seq", 2), hop(top, "seq", 4)
    d_top, d_low = hop(x_top, "seq", 4), hop(y_low, "seq", 2)
    out = [None] * 8
    for place, pair in zip((0, 2, 4, 6), ((top, low), (x_top, x_low), (y_top, y_low), (d_top, d_low))):
        out[place] = pair
        out[place | 1] = tuple(hop(part, "seq", 1) for part in pair)
    return out


def line_sum(pieces):
    got = [hop(pieces[m], "head", m) for m in (1, 2, 3)]
    total = (pieces[0] + got[0].astype(F32) + got[1].astype(F32) + got[2].astype(F32)).astype(BF16)
    return [total] + [hop(total, "head", m) for m in (1, 2, 3)]


VM = pl.BlockSpec(memory_space=pltpu.VMEM)
SM = pl.BlockSpec(memory_space=pltpu.SMEM)
HB = pl.BlockSpec(memory_space=pl.ANY)


def shape(rows, columns, dtype=BF16):
    return jax.ShapeDtypeStruct((rows, columns), dtype)


def call(kernel, outs, specs, args, scratch=(), flops=0, moved=0, out_specs=None, grid=None):
    extra = {} if grid is None else {"grid": grid}
    return pl.pallas_call(
        kernel,
        out_shape=outs,
        in_specs=specs,
        out_specs=[VM] * len(outs) if out_specs is None else out_specs,
        scratch_shapes=list(scratch),
        compiler_params=pltpu.CompilerParams(vmem_limit_bytes=56 * 2**20),
        cost_estimate=pl.CostEstimate(flops=flops, bytes_accessed=moved, transcendentals=0),
        name=getattr(kernel, "func", kernel).__name__,
        **extra,
    )(*args)


def flat(pairs):
    return [part for pair in pairs for part in pair]


def fetch_slab(order, j, pieces, dst, sem):
    copy = pltpu.make_async_copy(pieces.at[order[j], :, pl.ds(0, 256)], dst, sem)
    copy.start()
    return copy


def gate_kernel(*refs):
    pass


def gate(values, after):
    count = len(values)
    out = pl.pallas_call(
        gate_kernel,
        out_shape=[jax.ShapeDtypeStruct(v.shape, v.dtype) for v in values],
        in_specs=[HB] * (count + len(after)),
        out_specs=[HB] * count,
        input_output_aliases={i: i for i in range(count)},
        cost_estimate=pl.CostEstimate(flops=0, bytes_accessed=1024, transcendentals=0),
    )(*values, *after)
    return list(out)


def root_of(values):
    return lax.rsqrt(jnp.mean(values * values, axis=-1, keepdims=True) + EPS_NORM)


def turn(values, cosine, sine):
    parts = []
    for h in range(values.shape[1] // HEAD_DIM):
        v = values[:, h * HEAD_DIM : (h + 1) * HEAD_DIM]
        parts.append(v * cosine + pltpu.roll(v, HEAD_DIM // 2, 1) * sine)
    return parts


def quarter_out(place, full, outs):
    for m in range(4):
        at = pl.multiple_of((place[1] ^ m) * QUART, QUART)
        outs[m][...] = full[:, pl.ds(at, QUART)].astype(outs[m].dtype)


def quarter_in(place, pieces, full):
    for m in range(4):
        at = pl.multiple_of((place[1] ^ m) * QUART, QUART)
        full[:, pl.ds(at, QUART)] = pieces[m][...].astype(full.dtype)


def quarter_shapes(rows):
    return [shape(rows, QUART, F32)] + [shape(rows, QUART)] * 3


MESH = pl.DeviceIdType.MESH


def flip(index, mask):
    for bit in (1, 2, 4):
        if mask & bit:
            index = index + bit - 2 * bit * lax.rem(lax.div(index, bit), 2)
    return index


class Plane:
    def __init__(self, at, sent, got, me, line):
        self.at, self.sent, self.got, self.me, self.line = at, sent, got, me, line

    def copy(self, src, dst, side, hop_mask):
        return pltpu.make_async_remote_copy(
            src_ref=self.at(src, side),
            dst_ref=self.at(dst, side),
            send_sem=self.sent.at[dst, side],
            recv_sem=self.got.at[dst, side],
            device_id=(flip(self.me, hop_mask), self.line),
            device_id_type=MESH,
        )

    def start(self):
        for mask, side in ((2, 0), (4, 1), (2, 1), (4, 0)):
            self.copy(0, mask, side, mask).start()
        for side in (0, 1):
            self.copy(0, 1, side, 1).start()

    def arrive(self, mask, side):
        self.copy(mask, mask, side, 1).wait_recv()

    def twin(self, mask, side):
        self.copy(mask, mask + 1, side, 1).start()

    def relay_first(self):
        for mask, side in ((2, 0), (4, 1)):
            self.arrive(mask, side)
            self.copy(mask, 6, side, 6 - mask).start()
            self.twin(mask, side)

    def relay_second(self):
        for mask, side in ((2, 1), (4, 0)):
            self.arrive(mask, side)
            self.twin(mask, side)

    def relay_last(self):
        for side in (0, 1):
            self.arrive(6, side)
            self.twin(6, side)

    def finish(self):
        for mask in (1, 3, 5, 7):
            for side in (0, 1):
                self.arrive(mask, side)

    def drain(self):
        for mask in range(1, 8):
            for side in (0, 1):
                self.copy(0, mask, side, 1).wait_send()


def line_copy(src, dst, sent, got, m, me, line):
    return pltpu.make_async_remote_copy(
        src_ref=src,
        dst_ref=dst,
        send_sem=sent.at[m],
        recv_sem=got.at[m],
        device_id=(me, flip(line, m)),
        device_id_type=MESH,
    )


def greet(me, line, plane_masks, line_masks):
    barrier = pltpu.get_barrier_semaphore()
    for mask in plane_masks:
        pl.semaphore_signal(barrier, inc=1, device_id=(flip(me, mask), line), device_id_type=MESH)
    for mask in line_masks:
        pl.semaphore_signal(barrier, inc=1, device_id=(me, flip(line, mask)), device_id_type=MESH)
    return lambda: pl.semaphore_wait(barrier, len(plane_masks) + len(line_masks))


def front_kernel(
    rows, scale, branch,
    order_a, order_f, inverse_f, tokens, dy, own_gains, cosine, sine, master,
    a_low, gains, b_low, h_out, o_low, o_wide, stats, kcat, vcat, qcat, w_out, sent, n_parts, b_parts,
    wide, w_a, w_f, made, cut, total, z_out, z_in, z_sum, work,
    sem_w, sem_o, a_sent, a_got, f_sent, f_got, k_sent, k_got, q_sent, q_got, z_sems,
):
    me, line = lax.axis_index("seq"), lax.axis_index("head")
    ready = greet(me, line, (1, 2, 4), (1, 2, 3))
    w_a_plane = Plane(lambda m, s: w_a.at[m, s], a_sent, a_got, me, line)
    w_f_plane = Plane(lambda m, s: w_f.at[m, s], f_sent, f_got, me, line)
    kv_plane = Plane(lambda m, s: (kcat, vcat)[s].at[pl.ds(m * rows, rows)], k_sent, k_got, me, line)
    q_plane = Plane(lambda m, s: qcat.at[m, s], q_sent, q_got, me, line)

    load = pltpu.make_async_copy(master.at[pl.ds(0, 256), 0, :], wide.at[pl.ds(0, 256)], sem_w.at[0])
    load.start()
    w_a[0, 0, pl.ds(256, 16), :] = jnp.zeros((16, HALF), BF16)
    w_a[0, 1, pl.ds(256, 16), :] = jnp.zeros((16, HALF), BF16)
    w_a[0, 1, 256:258, 0:256] = own_gains[...].astype(BF16)
    load.wait()
    for side in (0, 1):
        w_a[0, side, pl.ds(0, 256), :] = wide[pl.ds(0, 256), side * HALF : (side + 1) * HALF].astype(BF16)
    load = pltpu.make_async_copy(master.at[pl.ds(256, SLAB), 0, :], wide, sem_w.at[1])
    load.start()
    ready()
    w_a_plane.start()
    load.wait()
    for side in (0, 1):
        columns = slice(side * HALF, (side + 1) * HALF)
        w_f[0, side, pl.ds(0, 512), :] = wide[pl.ds(0, 512), columns].astype(BF16)
        last = jnp.concatenate([wide[512:SLAB, columns], jnp.zeros((PAD - SLAB, HALF), F32)], axis=0)
        w_f[0, side, pl.ds(512, 16), :] = last.astype(BF16)
    w_a_plane.relay_first()
    w_a_plane.relay_second()
    w_a_plane.relay_last()
    w_f_plane.start()
    w_a_plane.finish()
    keep = pltpu.make_async_copy(w_a, w_out, sem_o.at[0])
    keep.start()

    for m in range(8):
        at = pl.multiple_of(flip(me, m) * 256, 256)
        gains[:, pl.ds(at, 256)] = w_a[m, 1, 256:258, 0:256].astype(F32)
    x = tokens[...].astype(F32)
    normed = (x * root_of(x) * gains[0:1, :]).astype(BF16)
    for side in (0, 1):
        a_low[side] = normed[:, side * HALF : (side + 1) * HALF]
    for j in (2, 3, 4, 5, 0, 1):
        out = lax.dot_general(a_low[0], w_a[order_a[j], 0, pl.ds(0, 256), :], NT, preferred_element_type=F32)
        out += lax.dot_general(a_low[1], w_a[order_a[j], 1, pl.ds(0, 256), :], NT, preferred_element_type=F32)
        if j < 4:
            parts = turn(out, cosine[...], sine[...])
        else:
            parts = [out[:, :HEAD_DIM], out[:, HEAD_DIM:]]
        for i, part in enumerate(parts):
            if j < 2:
                qcat[0, j, :, i * HEAD_DIM : (i + 1) * HEAD_DIM] = part.astype(BF16)
            else:
                at = (2 * (j % 2) + i) * HEAD_DIM
                (kcat, vcat)[j // 2 - 1][pl.ds(0, rows), at : at + HEAD_DIM] = part.astype(BF16)
        if j == 5:
            kv_plane.start()
    kv_plane.relay_first()
    kv_plane.relay_second()
    kv_plane.relay_last()
    q_plane.start()
    kv_plane.finish()

    at_q = me * rows + lax.broadcasted_iota(jnp.int32, (rows, 1), 0)
    along = lax.broadcasted_iota(jnp.int32, (1, rows), 1)
    lane = lax.broadcasted_iota(jnp.int32, (rows, HEAD_DIM), 1)
    stat = jnp.zeros((rows, HEAD_DIM), F32)
    for h in range(4):
        columns = slice(h * HEAD_DIM, (h + 1) * HEAD_DIM)
        q = qcat[0, h // 2, :, (h % 2) * HEAD_DIM : (h % 2 + 1) * HEAD_DIM]
        top = jnp.full((rows, 1), NEGATIVE, F32)
        for m in range(8):
            ahead = at_q - (flip(me, m) * rows + along)
            s = lax.dot_general(q, kcat[pl.ds(m * rows, rows), columns], NT, preferred_element_type=F32)
            s = jnp.where((ahead >= 0) & (ahead < WINDOW), s * scale, NEGATIVE)
            work[m] = s
            top = jnp.maximum(top, jnp.max(s, axis=-1, keepdims=True))
        sums = jnp.zeros((rows, 1), F32)
        for m in range(8):
            e = jnp.exp(work[m] - top)
            work[m] = e
            sums += jnp.sum(e, axis=-1, keepdims=True)
        share = 1.0 / sums
        o = jnp.zeros((rows, HEAD_DIM), F32)
        for m in range(8):
            soft = (work[m] * share).astype(BF16)
            o += jnp.dot(soft, vcat[pl.ds(m * rows, rows), columns], preferred_element_type=F32)
        o_wide[:, columns] = o
        o_low[:, columns] = o.astype(BF16)
        stat = jnp.where(lane == h, top + jnp.log(sums), stat)
    stats[...] = stat
    for side in (0, 1):
        out = jnp.dot(o_low[:, :256], w_a[order_a[6], side, pl.ds(0, 256), :], preferred_element_type=F32)
        out += jnp.dot(o_low[:, 256:], w_a[order_a[7], side, pl.ds(0, 256), :], preferred_element_type=F32)
        total[:, side * HALF : (side + 1) * HALF] = branch * out

    def quarter(m):
        return pl.ds(pl.multiple_of(flip(line, m) * QUART, QUART), QUART)

    def piece(m):
        return line_copy(z_out.at[m], z_in.at[m], z_sems.at[0], z_sems.at[1], m, me, line)

    def whole(m):
        return line_copy(z_sum.at[0], z_sum.at[m], z_sems.at[2], z_sems.at[3], m, me, line)

    for m in (3, 2, 1):
        z_out[m] = total[:, quarter(m)].astype(BF16)
        piece(m).start()
    w_f_plane.relay_first()
    for m in (1, 2, 3):
        piece(m).wait_recv()
    summed = total[:, quarter(0)]
    for m in (1, 2, 3):
        summed += z_in[m].astype(F32)
    z_sum[0] = summed.astype(BF16)
    for m in (3, 2, 1):
        whole(m).start()
    w_f_plane.relay_second()
    q_plane.relay_first()
    q_plane.relay_second()
    q_plane.relay_last()
    for m in (1, 2, 3):
        whole(m).wait_recv()

    for m in range(4):
        h_out[:, quarter(m)] = z_sum[m].astype(F32)
    h = h_out[...] + tokens[...].astype(F32)
    h_out[...] = h
    normed = (h * root_of(h) * gains[1:2, :]).astype(BF16)
    for side in (0, 1):
        b_low[side] = normed[:, side * HALF : (side + 1) * HALF]
    w_f_plane.relay_last()
    w_f_plane.finish()

    def through(j, left, right):
        out = lax.dot_general(w_f[order_f[j], 0], left, NT, preferred_element_type=F32)
        return out + lax.dot_general(w_f[order_f[j], 1], right, NT, preferred_element_type=F32)

    made[pl.ds(8 * SLAB, 16), :] = jnp.zeros((16, rows), F32)
    row = lax.broadcasted_iota(jnp.int32, (PAD, 1), 0)
    gate_rows = row < 2 * UNITS - 5 * SLAB
    for j in range(8):
        if j < 5:
            out = through(j, b_low[0], b_low[1])
        elif j > 5:
            out = through(j, dy[:, :HALF], dy[:, HALF:])
        else:
            out = jnp.where(gate_rows, through(j, b_low[0], b_low[1]), through(j, dy[:, :HALF], dy[:, HALF:]))
        made[pl.ds(j * SLAB, PAD), :] = out

    def mix(i, _):
        at = pl.multiple_of(i * 32, 8)
        gate = made[pl.ds(at, 32), :]
        up = made[pl.ds(UNITS + at, 32), :]
        back = made[pl.ds(2 * UNITS + at, 32), :]
        sigma = 1.0 / (1.0 + jnp.exp(-gate))
        silu = gate * sigma
        made[pl.ds(at, 32), :] = back * up * (sigma * (1.0 + gate * (1.0 - sigma)))
        made[pl.ds(UNITS + at, 32), :] = back * silu
        made[pl.ds(2 * UNITS + at, 32), :] = silu * up
        return 0

    lax.fori_loop(0, UNITS // 32, mix, 0)
    for j in range(8):
        cut[j] = made[pl.ds(j * SLAB, PAD), :].astype(BF16)
    for m in range(8):
        sent[m] = cut[inverse_f[flip(me, m)]]
    for parts, kinds in ((n_parts, range(0, 6)), (b_parts, range(5, 8))):
        for side in (0, 1):
            columns = slice(side * HALF, (side + 1) * HALF)
            for j in kinds:
                z = cut[j]
                if j == 5:
                    z = jnp.where(gate_rows if parts is n_parts else ~gate_rows, z, jnp.zeros_like(z))
                out = lax.dot_general(z, w_f[order_f[j], side], TN, preferred_element_type=F32)
                total[:, columns] = out if j == kinds[0] else total[:, columns] + out
        for m in range(4):
            parts[m] = total[:, quarter(m)]

    q_plane.finish()
    for plane in (w_a_plane, w_f_plane, kv_plane, q_plane):
        plane.drain()
    for m in (1, 2, 3):
        piece(m).wait_send()
        whole(m).wait_send()
    keep.wait()


def front(order_a, order_f, inverse_f, tokens, dy, own_gains, cosine, sine, master, scale, branch):
    rows = tokens.shape[0]
    array = jax.ShapeDtypeStruct
    outs = [
        array((2, rows, HALF), BF16),
        array((2, 2 * HALF), F32),
        array((2, rows, HALF), BF16),
        array((rows, 2 * HALF), F32),
        array((rows, QUART), BF16),
        array((rows, QUART), F32),
        array((rows, HEAD_DIM), F32),
        array((8 * rows, QUART), BF16),
        array((8 * rows, QUART), BF16),
        array((8, 2, rows, 256), BF16),
        array((8, 2, 272, HALF), BF16),
        array((8, PAD, rows), BF16),
        array((4, rows, QUART), F32),
        array((4, rows, QUART), F32),
    ]
    out_specs = [VM] * len(outs)
    out_specs[10] = HB
    dma = pltpu.SemaphoreType.DMA
    return pl.pallas_call(
        functools.partial(front_kernel, rows, scale, branch),
        out_shape=outs,
        in_specs=[SM] * 3 + [VM] * 5 + [HB],
        out_specs=out_specs,
        scratch_shapes=[
            pltpu.VMEM((SLAB, 2 * HALF), F32),
            pltpu.VMEM((8, 2, 272, HALF), BF16),
            pltpu.VMEM((8, 2, PAD, HALF), BF16),
            pltpu.VMEM((8 * SLAB + 16, rows), F32),
            pltpu.VMEM((8, PAD, rows), BF16),
            pltpu.VMEM((rows, 2 * HALF), F32),
            pltpu.VMEM((4, rows, QUART), BF16),
            pltpu.VMEM((4, rows, QUART), BF16),
            pltpu.VMEM((4, rows, QUART), BF16),
            pltpu.VMEM((8, rows, rows), F32),
            dma((2,)),
            dma((1,)),
        ]
        + [dma((8, 2))] * 8
        + [dma((4, 4))],
        compiler_params=pltpu.CompilerParams(
            collective_id=0, has_side_effects=True, vmem_limit_bytes=62 * 2**20
        ),
        cost_estimate=pl.CostEstimate(flops=10**10, bytes_accessed=30 * 2**20, transcendentals=0),
        name="front",
    )(order_a, order_f, inverse_f, tokens, dy, own_gains, cosine, sine, master)


def back_two_kernel(rows, branch, place, order, dy, h_in, gains, o_wide, stats, s0, s1, s2, s3, pieces, *rest):
    sums = (s0, s1, s2, s3)
    d_out, low_l, low_r, gain_out, do_l, do_r = rest[:6]
    slab, full, stat_l, stat_r, sems = rest[6:]
    copies = [fetch_slab(order, 6 + j, pieces, slab.at[j], sems.at[j]) for j in (0, 1)]
    quarter_in(place, sums, full)
    normed_grad = full[...]
    h = h_in[...]
    root = root_of(h)
    gain_out[...] = jnp.sum(normed_grad * h * root, axis=0, keepdims=True)
    weighted = normed_grad * gains[1:2, :]
    inner = jnp.mean(weighted * h, axis=-1, keepdims=True)
    grad = dy[...].astype(F32) + root * weighted - h * (root * root * root) * inner
    d_out[...] = grad
    low = grad.astype(BF16)
    low_l[...] = low[:, :HALF]
    low_r[...] = low[:, HALF:]
    lane = lax.broadcasted_iota(jnp.int32, (rows, HEAD_DIM), 1)
    for j, (do, stat) in enumerate(((do_l, stat_l), (do_r, stat_r))):
        copies[j].wait()
        made = lax.dot_general(low_l[...], slab[j, 0], NT, preferred_element_type=F32)
        made += lax.dot_general(low_r[...], slab[j, 1], NT, preferred_element_type=F32)
        made = (branch * made).astype(BF16)
        do[pl.ds(0, rows), :] = made
        lines = jnp.zeros((rows, HEAD_DIM), F32)
        for i in (0, 1):
            h_at = 2 * j + i
            cut = slice(h_at * HEAD_DIM, (h_at + 1) * HEAD_DIM)
            delta = jnp.sum(
                made[:, i * HEAD_DIM : (i + 1) * HEAD_DIM].astype(F32) * o_wide[:, cut], axis=-1, keepdims=True
            )
            top = stats[:, h_at : h_at + 1]
            for at, value in ((i, top), (2 + i, delta)):
                for step in range(3):
                    part = value.astype(BF16).astype(F32)
                    value = value - part
                    lines = jnp.where(lane == 4 * step + at, part, lines)
        stat[pl.ds(0, rows), :] = lines
        stat[pl.ds(rows, 256 - rows), :] = jnp.zeros((256 - rows, HEAD_DIM), F32)
        do[pl.ds(rows, 16), :] = stat[...].T[:16, :].astype(BF16)


def back_two(place, order, dy, h, gains, o_wide, stats, sums, pieces, branch):
    rows = dy.shape[0]
    return call(
        functools.partial(back_two_kernel, rows, branch),
        [shape(rows, 2 * HALF, F32), shape(rows, HALF), shape(rows, HALF), shape(1, 2 * HALF, F32)]
        + [shape(rows + 16, 256)] * 2,
        [SM, SM] + [VM] * 9 + [HB],
        [place, order, dy, h, gains, o_wide, stats, *sums, pieces],
        [
            pltpu.VMEM((2, 2, 256, HALF), BF16),
            pltpu.VMEM((rows, 2 * HALF), F32),
            pltpu.VMEM((256, HEAD_DIM), F32),
            pltpu.VMEM((256, HEAD_DIM), F32),
            pltpu.SemaphoreType.DMA((2,)),
        ],
        flops=2 * rows * 512 * 2048,
        moved=9 * 2**20,
    )


def attend_back_kernel(
    rows, scale, place, order, inverse, cosine, sine, o_low, qcat, kcat, vcat, *rest
):
    dos, pieces, sent, parts = rest[:16], rest[16], rest[17:25], rest[25:29]
    docat, slab, dq, dk, dv, groups, total, sems, wsems = rest[29:]
    copies = []
    for m in range(8):
        for side in (0, 1):
            copies.append(pltpu.make_async_copy(dos[2 * m + side], docat.at[m, side], sems.at[side, m]))
    for copy in copies:
        copy.start()
    slabs = [fetch_slab(order, j, pieces, slab.at[j], wsems.at[j]) for j in range(6)]
    for copy in copies:
        copy.wait()
    dq[...] = jnp.zeros_like(dq)
    dk[...] = jnp.zeros_like(dk)
    dv[...] = jnp.zeros_like(dv)
    me = place[0]
    reach = -(-WINDOW // rows)
    down = lax.broadcasted_iota(jnp.int32, (rows, rows), 0)
    along = lax.broadcasted_iota(jnp.int32, (rows, rows), 1)

    def head_cut(h):
        return h // 2, slice((h % 2) * HEAD_DIM, (h % 2 + 1) * HEAD_DIM), slice(h * HEAD_DIM, (h + 1) * HEAD_DIM)

    def sums_of(lines, at):
        return lines[at : at + 1] + lines[4 + at : 5 + at] + lines[8 + at : 9 + at]

    def lines_of(m, side):
        return docat[m, side, pl.ds(rows, 16), :].astype(F32)

    own = []
    for side in (0, 1):
        lines = lines_of(0, side)
        whole = lines[0:4] + lines[4:8] + lines[8:12]
        own.append(jnp.concatenate([whole, jnp.zeros((124, 256), F32)], axis=0).T[:rows, :])

    def step(m, _):
        apart = me - (me ^ m)

        @pl.when((apart >= 0) & (apart <= reach))
        def _():
            ahead = apart * rows + down - along
            allowed = (ahead >= 0) & (ahead < WINDOW)
            for h in range(4):
                side, two, cut = head_cut(h)
                k, do = kcat[pl.ds(pl.multiple_of(m * rows, 64), rows), cut], docat[0, side, pl.ds(0, rows), two]
                s = lax.dot_general(qcat[0, side, :, two], k, NT, preferred_element_type=F32)
                p = jnp.where(allowed, jnp.exp(s * scale - own[side][:, h % 2 : h % 2 + 1]), 0.0)
                dp = lax.dot_general(do, vcat[pl.ds(pl.multiple_of(m * rows, 64), rows), cut], NT, preferred_element_type=F32)
                ds = (p * (dp - own[side][:, 2 + h % 2 : 3 + h % 2]) * scale).astype(BF16)
                dq[:, cut] += jnp.dot(ds, k, preferred_element_type=F32)

        @pl.when((apart <= 0) & (apart >= -reach))
        def _():
            ahead = along - down - apart * rows
            allowed = (ahead >= 0) & (ahead < WINDOW)
            for side in (0, 1):
                lines = lines_of(m, side)
                for i in (0, 1):
                    side, two, cut = head_cut(2 * side + i)
                    q, do = qcat[m, side, :, two], docat[m, side, pl.ds(0, rows), two]
                    top, delta = sums_of(lines, i)[:, :rows], sums_of(lines, 2 + i)[:, :rows]
                    s = lax.dot_general(kcat[pl.ds(0, rows), cut], q, NT, preferred_element_type=F32)
                    p = jnp.where(allowed, jnp.exp(s * scale - top), 0.0)
                    dv[:, cut] += jnp.dot(p.astype(BF16), do, preferred_element_type=F32)
                    dp = lax.dot_general(vcat[pl.ds(0, rows), cut], do, NT, preferred_element_type=F32)
                    ds = (p * (dp - delta) * scale).astype(BF16)
                    dk[:, cut] += jnp.dot(ds, q, preferred_element_type=F32)

        return 0

    lax.fori_loop(0, 8, step, 0)
    for j in range(8):
        cut = slice((j % 2) * 256, (j % 2 + 1) * 256)
        if j < 4:
            made = turn((dq, dk)[j // 2][:, cut], cosine[...], -sine[...])
            for i in (0, 1):
                groups[j, :, i * HEAD_DIM : (i + 1) * HEAD_DIM] = made[i].astype(BF16)
        elif j < 6:
            groups[j] = dv[:, cut].astype(BF16)
        else:
            groups[j] = o_low[:, cut]
    for m in range(8):
        sent[m][...] = groups[inverse[me ^ m]]
    for j in range(6):
        slabs[j].wait()
        for side in (0, 1):
            out = jnp.dot(groups[j], slab[j, side], preferred_element_type=F32)
            columns = slice(side * HALF, (side + 1) * HALF)
            total[:, columns] = out if j == 0 else total[:, columns] + out
    quarter_out(place, total, parts)


def attend_back(place, order, inverse, cosine, sine, o_low, qcat, kcat, vcat, dos, pieces, scale):
    rows = o_low.shape[0]
    return call(
        functools.partial(attend_back_kernel, rows, scale),
        [shape(rows, 256)] * 8 + quarter_shapes(rows),
        [SM] * 3 + [VM] * 6 + [HB] * 17,
        [place, order, inverse, cosine, sine, o_low, qcat, kcat, vcat, *flat(dos), pieces],
        [
            pltpu.VMEM((8, 2, rows + 16, 256), BF16),
            pltpu.VMEM((6, 2, 256, HALF), BF16),
            pltpu.VMEM((rows, QUART), F32),
            pltpu.VMEM((rows, QUART), F32),
            pltpu.VMEM((rows, QUART), F32),
            pltpu.VMEM((8, rows, 256), BF16),
            pltpu.VMEM((rows, 2 * HALF), F32),
            pltpu.SemaphoreType.DMA((2, 8)),
            pltpu.SemaphoreType.DMA((6,)),
        ],
        flops=3 * 10**9,
        moved=20 * 2**20,
    )


def back_one_kernel(place, tokens, d_in, gains, s0, s1, s2, s3, out, gain_out, full):
    quarter_in(place, (s0, s1, s2, s3), full)
    normed_grad = full[...]
    x = tokens[...].astype(F32)
    root = root_of(x)
    gain_out[...] = jnp.sum(normed_grad * x * root, axis=0, keepdims=True)
    weighted = normed_grad * gains[0:1, :]
    inner = jnp.mean(weighted * x, axis=-1, keepdims=True)
    out[...] = d_in[...] + root * weighted - x * (root * root * root) * inner


def back_one(place, tokens, d_in, gains, sums):
    rows = tokens.shape[0]
    return call(
        back_one_kernel,
        [shape(rows, 2 * HALF, F32), shape(1, 2 * HALF, F32)],
        [SM] + [VM] * 7,
        [place, tokens, d_in, gains, *sums],
        [pltpu.VMEM((rows, 2 * HALF), F32)],
        moved=5 * 2**20,
    )


TILE = 256


def update_kernel(rows, branch, slabs, basis, *rest):
    zs, gs, rest = rest[:8], rest[8:16], rest[16:]
    acts, rest = [rest[16 * i : 16 * i + 16] for i in range(4)], rest[64:]
    olds, news, low_new, rest = rest[:3], rest[3:7], rest[7], rest[8:]
    turned_g, act, old, new, asem, osem, nsem = rest
    tile, tiles = pl.program_id(0), pl.num_programs(0)
    slot = tile % 2
    a_slab, f_slab = slabs[0], slabs[1]

    def columns_of(t):
        return pl.ds(pl.multiple_of(t * TILE, TILE), TILE)

    def act_copies(t, kind, which):
        for side in (0, 1):

            @pl.when((t >= HALF // TILE) == (side == 1))
            def _():
                at = pl.ds(pl.multiple_of((t - side * (HALF // TILE)) * TILE, TILE), TILE)
                for m in range(8):
                    pltpu.make_async_copy(
                        acts[kind][2 * m + side].at[:, at],
                        act.at[t % 2, which, pl.ds(m * rows, rows)],
                        asem.at[t % 2, which],
                    ).start()

    def act_wait(which):
        for m in range(8):
            part = act.at[slot, which, pl.ds(m * rows, rows)]
            pltpu.make_async_copy(part, part, asem.at[slot, which]).wait()

    def fetch_acts(t):
        pl.when(a_slab < 6)(lambda: act_copies(t, 0, 0))
        pl.when(a_slab >= 6)(lambda: act_copies(t, 3, 0))
        pl.when(f_slab <= 5)(lambda: act_copies(t, 1, 1))
        pl.when(f_slab > 5)(lambda: act_copies(t, 2, 1))
        pl.when(f_slab == 5)(lambda: act_copies(t, 2, 2))

    def old_copy(i, t):
        return pltpu.make_async_copy(olds[i].at[:, 0, columns_of(t)], old.at[t % 2, i], osem.at[t % 2, i])

    def new_copy(i, t):
        return pltpu.make_async_copy(new.at[t % 2, i], news[i].at[:, 0, columns_of(t)], nsem.at[t % 2, i])

    def fetch(t):
        fetch_acts(t)
        for i in range(3):
            old_copy(i, t).start()

    @pl.when(tile == 0)
    def _():
        fetch(0)
        for m in range(8):
            turned_g[:, m * rows : (m + 1) * rows] = gs[m][...].T

    pl.when(tile + 1 < tiles)(lambda: fetch(tile + 1))

    @pl.when(tile >= 2)
    def _():
        for i in range(4):
            new_copy(i, tile - 2).wait()

    grad, first_new, second_new, master_new = (new.at[slot, i] for i in range(4))
    first, second, master = (old.at[slot, i] for i in range(3))

    def ffn_rows(which):
        total = jnp.dot(zs[0][...], act[slot, which, pl.ds(0, rows), :], preferred_element_type=F32)
        for m in range(1, 8):
            total += jnp.dot(zs[m][...], act[slot, which, pl.ds(m * rows, rows), :], preferred_element_type=F32)
        return total[:SLAB]

    act_wait(0)
    factor = jnp.where(a_slab < 6, 1.0, branch)
    grad[pl.ds(0, 256), :] = factor * jnp.dot(turned_g[...], act[slot, 0], preferred_element_type=F32)
    act_wait(1)
    grad[pl.ds(256, SLAB), :] = ffn_rows(1)
    first_of_down = 2 * UNITS - f_slab * SLAB

    @pl.when(f_slab == 5)
    def _():
        act_wait(2)
        row = lax.broadcasted_iota(jnp.int32, (SLAB, 1), 0)
        grad[pl.ds(256, SLAB), :] = jnp.where(row < first_of_down, grad[pl.ds(256, SLAB), :], ffn_rows(2))

    for i in range(3):
        old_copy(i, tile).wait()
    row = lax.broadcasted_iota(jnp.int32, (256 + SLAB, 1), 0)
    rate = jnp.where((row < 256) | (row - 256 < first_of_down), 0.5 * (2 * HALF) ** (-0.5), 0.5 * FF ** (-0.5))
    for b in range(TILE // HEAD_DIM):
        cut = slice(b * HEAD_DIM, (b + 1) * HEAD_DIM)
        turned = jnp.dot(grad[:, cut], basis[b], precision=lax.Precision.HIGH, preferred_element_type=F32)
        one = BETA_FIRST * first[:, cut] + (1.0 - BETA_FIRST) * turned
        two = BETA_SECOND * second[:, cut] + (1.0 - BETA_SECOND) * turned * turned
        first_new[:, cut] = one
        second_new[:, cut] = two
        adam = (one / (1.0 - BETA_FIRST**ADAM_STEP)) / (
            jnp.sqrt(two / (1.0 - BETA_SECOND**ADAM_STEP)) + ADAM_EPS
        )
        back = lax.dot_general(
            adam, basis[b], NT, precision=lax.Precision.HIGH, preferred_element_type=F32
        )
        before = master[:, cut]
        after = before - rate * (back + DECAY_RATE * before)
        master_new[:, cut] = after
        low_new[:, cut] = after.astype(BF16)
    for i in range(4):
        new_copy(i, tile).start()

    @pl.when(tile == tiles - 1)
    def _():
        for t in (tile - 1, tile):
            for i in range(4):
                new_copy(i, t).wait()


def update(slabs, zs, gs, acts, basis, olds, branch):
    rows = gs[0].shape[0]
    height, _, width = olds[0].shape

    def whole(array):
        return pl.BlockSpec(array.shape, lambda i: (0,) * array.ndim)

    tall = pl.BlockSpec((height, TILE), lambda i: (0, i))
    per = TILE // HEAD_DIM
    return call(
        functools.partial(update_kernel, rows, branch),
        [jax.ShapeDtypeStruct(olds[0].shape, F32)] * 4 + [shape(height, width)],
        [SM, pl.BlockSpec((per, HEAD_DIM, HEAD_DIM), lambda i: (i, 0, 0))]
        + [whole(z) for z in zs]
        + [whole(g) for g in gs]
        + [HB] * 67,
        [slabs, basis, *zs, *gs, *[part for pairs in acts for part in flat(pairs)], *olds],
        [
            pltpu.VMEM((256, 8 * rows), BF16),
            pltpu.VMEM((2, 3, 8 * rows, TILE), BF16),
            pltpu.VMEM((2, 3, height, TILE), F32),
            pltpu.VMEM((2, 4, height, TILE), F32),
            pltpu.SemaphoreType.DMA((2, 3)),
            pltpu.SemaphoreType.DMA((2, 3)),
            pltpu.SemaphoreType.DMA((2, 4)),
        ],
        out_specs=[HB] * 4 + [tall],
        grid=(width // TILE,),
        flops=2 * 8 * rows * height * width,
        moved=70 * 2**20,
    )


def plane_mesh(
    tokens,
    cotangent,
    owners,
    master,
    first_moment,
    second_moment,
    eigenbases,
    norm_gains,
    gain_first,
    gain_second,
):
    rows, width = tokens.shape
    me, line = lax.axis_index("seq"), lax.axis_index("head")
    scale = HEAD_DIM ** (-0.5)
    branch = (WINDOW / 3.0) ** 0.5
    place = jnp.stack([me, line]).astype(jnp.int32)
    inverse_attn, inverse_ffn = inverse_order(owners[0]), inverse_order(owners[1])
    order_attn, order_ffn = owners[0] ^ me, owners[1] ^ me
    slabs = jnp.stack([inverse_attn[me], inverse_ffn[me]]).astype(jnp.int32)
    tall = [array.reshape(array.shape[2], 1, width) for array in (first_moment, second_moment, master)]
    cosine, sine = angles((me * rows + jnp.arange(rows, dtype=jnp.int32)).astype(F32))
    cosine, sine = cosine[:, 0, :], sine[:, 0, :]
    cosine = jnp.concatenate([cosine, cosine], axis=1)
    sine = jnp.concatenate([-sine, sine], axis=1)
    a_low, gains, b_low, h, o_low, o_wide, stats, kcat, vcat, qcat, attn, sent_ffn, n_parts, b_parts = front(
        order_attn, order_ffn, inverse_ffn, tokens, cotangent, norm_gains, cosine, sine, tall[2], scale, branch
    )
    n_parts = [n_parts[0]] + [n_parts[m].astype(BF16) for m in (1, 2, 3)]
    b_parts = [b_parts[0]] + [b_parts[m].astype(BF16) for m in (1, 2, 3)]
    a_l, a_r, b_l, b_r = a_low[0], a_low[1], b_low[0], b_low[1]
    n_sums = line_sum(n_parts)
    d_one, d_l, d_r, gain_two, do_l, do_r = back_two(
        place, order_attn, cotangent, h, gains, o_wide, stats, n_sums, attn, branch
    )
    dos = gather_plane(do_l, do_r)
    *sent_attn, p0, p1, p2, p3 = attend_back(
        place, order_attn, inverse_attn, cosine, sine, o_low, qcat, kcat, vcat, dos, attn, scale
    )
    input_grad, gain_one = back_one(place, tokens, d_one, gains, line_sum([p0, p1, p2, p3]))
    dy_l, dy_r = cotangent[:, :HALF], cotangent[:, HALF:]
    a_l, a_r, dy_l, dy_r = gate([a_l, a_r, dy_l, dy_r], [do_l])
    acts = [gather_plane(a_l, a_r), gather_plane(b_l, b_r), gather_plane(dy_l, dy_r), gather_plane(d_l, d_r)]
    zs = [sent_ffn[0]] + [hop(sent_ffn[m], "seq", m) for m in range(1, 8)]
    gs = [sent_attn[0]] + [hop(sent_attn[m], "seq", m) for m in range(1, 8)]
    grad, first_new, second_new, master_new, low_new = update(
        slabs, zs, gs, acts, eigenbases[0, 0], tall, branch
    )
    whole = (1, 1, *tall[0].shape[::2])
    got = [hop(b_parts[m], "head", m) for m in (1, 2, 3)]
    kept = lax.dynamic_slice_in_dim(h, line * QUART, QUART, 1)
    block_out = kept + b_parts[0] + got[0].astype(F32) + got[1].astype(F32) + got[2].astype(F32)
    gain_parts = jnp.concatenate([gain_one, gain_two], axis=0)
    share = width // 8
    gain_grad = lax.dynamic_slice_in_dim(gain_parts, me * share, share, 1)
    for m in range(1, 8):
        gain_grad += hop(lax.dynamic_slice_in_dim(gain_parts, (me ^ m) * share, share, 1), "seq", m)
    gain_first_new = BETA_FIRST * gain_first + (1.0 - BETA_FIRST) * gain_grad
    gain_second_new = BETA_SECOND * gain_second + (1.0 - BETA_SECOND) * gain_grad * gain_grad
    gain_new = norm_gains - GAIN_RATE * (gain_first_new / (1.0 - BETA_FIRST**ADAM_STEP)) / (
        jnp.sqrt(gain_second_new / (1.0 - BETA_SECOND**ADAM_STEP)) + ADAM_EPS
    )
    return (
        block_out.astype(BF16),
        input_grad,
        grad.reshape(whole),
        first_new.reshape(whole),
        second_new.reshape(whole),
        master_new.reshape(whole),
        low_new[None, None],
        gain_grad,
        gain_first_new,
        gain_second_new,
        gain_new,
    )


def solution(mesh):
    in_specs = (
        P("seq", None),
        P("seq", None),
        P(),
        P("head", "seq", None, None),
        P("head", "seq", None, None),
        P("head", "seq", None, None),
        P("head", "seq", None, None, None),
        P(None, "seq"),
        P(None, "seq"),
        P(None, "seq"),
    )
    out_specs = (
        P("seq", "head"),
        P("seq", None),
        P("head", "seq", None, None),
        P("head", "seq", None, None),
        P("head", "seq", None, None),
        P("head", "seq", None, None),
        P("head", "seq", None, None),
        P(None, "seq"),
        P(None, "seq"),
        P(None, "seq"),
        P(None, "seq"),
    )
    plane = mesh.shape["seq"] == 8 and mesh.shape["head"] == 4
    return jax.shard_map(
        plane_mesh if plane else any_mesh, mesh=mesh, in_specs=in_specs, out_specs=out_specs, check_vma=False
    )
```

```python
import functools

import jax
import jax.numpy as jnp
from jax import lax
from jax.experimental import pallas as pl
from jax.experimental.pallas import tpu as pltpu
from jax.sharding import PartitionSpec as P

HEADS = 16
HEAD_DIM = 128
FF = 5504
WINDOW = 1024
ADAM_STEP = 5


EPS_NORM = 1e-05
BETA_FIRST = 0.5
BETA_SECOND = 0.6
ADAM_EPS = 1e-08
DECAY_RATE = 0.1
GAIN_RATE = 0.25
ROPE_BASE = 10000.0
NEGATIVE = -1e30
PRECISE = lax.Precision.HIGHEST

BF16 = jnp.bfloat16
F32 = jnp.float32


def passed_along(shard, axis, by):
    devices = lax.axis_size(axis)
    pairs = [(i, i + by) for i in range(devices) if 0 <= i + by < devices]
    return lax.ppermute(shard, axis, pairs)


def inverse_order(owner_row):
    places = jnp.arange(owner_row.shape[0], dtype=jnp.int32)
    matches = (owner_row[:, None] == places[None, :]).astype(jnp.int32)
    return jnp.sum(matches * places[:, None], axis=0)


def kind_rates(kinds, width):
    wide = width ** (-0.5)
    spreads = jnp.array([wide, wide, wide, wide, wide, wide, FF ** (-0.5)], jnp.float32)
    matches = (kinds[..., None] == jnp.arange(7, dtype=jnp.int32)).astype(jnp.float32)
    return 0.5 * jnp.sum(matches * spreads, axis=-1)


def angles(positions):
    half_dim = HEAD_DIM // 2
    frequencies = ROPE_BASE ** (-jnp.arange(half_dim, dtype=jnp.float32) / half_dim)
    turning = positions[:, None] * frequencies[None, :]
    return (jnp.cos(turning)[:, None, :], jnp.sin(turning)[:, None, :])


def rotate(vectors, cosine, sine):
    half_dim = vectors.shape[-1] // 2
    former = vectors[..., :half_dim]
    latter = vectors[..., half_dim:]
    return jnp.concatenate(
        [former * cosine - latter * sine, latter * cosine + former * sine], axis=-1
    )


def inverse_rms(vectors):
    return lax.rsqrt(jnp.mean(vectors * vectors, axis=-1, keepdims=True) + EPS_NORM)


def norm_back(grad_normed, inputs, rms_values, gain_row):
    weighted = grad_normed * gain_row
    inner = jnp.mean(weighted * inputs, axis=-1, keepdims=True)
    input_part = rms_values * weighted - inputs * rms_values**3 * inner
    return (input_part, jnp.sum(grad_normed * inputs * rms_values, axis=0))


def any_mesh(
    tokens,
    cotangent,
    owners,
    master,
    first_moment,
    second_moment,
    eigenbases,
    norm_gains,
    gain_first,
    gain_second,
):
    tok_rows, width = tokens.shape
    seq_devices = lax.axis_size("seq")
    head_devices = lax.axis_size("head")
    seq_place = lax.axis_index("seq")
    head_place = lax.axis_index("head")
    slab_rows = master.shape[2]
    attn_slab = 4 * width // (head_devices * seq_devices)
    ffn_slab = slab_rows - attn_slab
    head_width = width // head_devices
    ffn_width = FF // head_devices
    local_heads = HEADS // head_devices
    score_scale = HEAD_DIM ** (-0.5)
    branch_scale = (WINDOW / 3.0) ** 0.5
    inverse_attn = inverse_order(owners[0])
    inverse_ffn = inverse_order(owners[1])
    master_low = master[0, 0].astype(jnp.bfloat16)
    gathered, gains_all = (
        lax.all_gather(master_low, "seq", axis=0, tiled=True),
        lax.all_gather(norm_gains.astype(jnp.bfloat16), "seq", axis=1, tiled=True),
    )
    gathered = gathered.reshape(seq_devices, slab_rows, width)
    attn_rows = jnp.take(gathered[:, :attn_slab], owners[0], axis=0).reshape(4 * head_width, width)
    ffn_rows = jnp.take(gathered[:, attn_slab:], owners[1], axis=0).reshape(3 * ffn_width, width)
    w_query = attn_rows[:head_width]
    w_key = attn_rows[head_width : 2 * head_width]
    w_value = attn_rows[2 * head_width : 3 * head_width]
    w_out = attn_rows[3 * head_width :]
    w_gate = ffn_rows[:ffn_width]
    w_up = ffn_rows[ffn_width : 2 * ffn_width]
    w_down = ffn_rows[2 * ffn_width :]
    gain_one = gains_all[0].astype(jnp.float32)
    gain_two = gains_all[1].astype(jnp.float32)
    inputs = tokens.astype(jnp.float32)
    rms_one = inverse_rms(inputs)
    normed_one = (inputs * rms_one * gain_one).astype(jnp.bfloat16)
    positions = (seq_place * tok_rows + jnp.arange(tok_rows, dtype=jnp.int32)).astype(jnp.float32)
    cosine, sine = angles(positions)
    head_shape = (tok_rows, local_heads, HEAD_DIM)

    def project(weight_rows):
        return jnp.einsum("td,id->ti", normed_one, weight_rows, preferred_element_type=jnp.float32)

    queries = rotate(project(w_query).reshape(head_shape), cosine, sine).astype(jnp.bfloat16)
    keys_own = rotate(project(w_key).reshape(head_shape), cosine, sine).astype(jnp.bfloat16)
    values_own = project(w_value).reshape(head_shape).astype(jnp.bfloat16)
    hop_total = -(-WINDOW // tok_rows)
    hop_sizes = [
        min(tok_rows, WINDOW - (hop_index - 1) * tok_rows) for hop_index in range(1, hop_total + 1)
    ]
    halo_keys = []
    halo_values = []
    for hop_index in range(hop_total, 0, -1):
        hop_rows = hop_sizes[hop_index - 1]
        far_keys, far_values = passed_along(
            (keys_own[tok_rows - hop_rows :], values_own[tok_rows - hop_rows :]), "seq", hop_index
        )
        halo_keys.append(far_keys)
        halo_values.append(far_values)
    keys_all = jnp.concatenate(halo_keys + [keys_own], axis=0)
    values_all = jnp.concatenate(halo_values + [values_own], axis=0)
    row_ids = jnp.arange(tok_rows, dtype=jnp.int32)[:, None]
    col_ids = jnp.arange(WINDOW + tok_rows, dtype=jnp.int32)[None, :]
    allowed = (
        (col_ids > row_ids)
        & (col_ids <= row_ids + WINDOW)
        & (seq_place * tok_rows - WINDOW + col_ids >= 0)
    )

    def scores_of():
        raw = jnp.einsum("thd,chd->htc", queries, keys_all, preferred_element_type=jnp.float32)
        return jnp.where(allowed[None], raw * score_scale, NEGATIVE)

    scores = scores_of()
    row_top = jnp.max(scores, axis=-1, keepdims=True)
    exp_scores = jnp.exp(scores - row_top)
    exp_total = jnp.sum(exp_scores, axis=-1, keepdims=True)
    soft_low = (exp_scores / exp_total).astype(jnp.bfloat16)
    log_total = row_top + jnp.log(exp_total)
    attended = jnp.einsum("htc,chd->thd", soft_low, values_all, preferred_element_type=jnp.float32)
    attended_low = attended.reshape(tok_rows, head_width).astype(jnp.bfloat16)
    attn_part = branch_scale * jnp.dot(attended_low, w_out, preferred_element_type=jnp.float32)
    hidden_one = inputs + lax.psum(attn_part, "head")
    rms_two = inverse_rms(hidden_one)
    normed_two = (hidden_one * rms_two * gain_two).astype(jnp.bfloat16)
    gate_pre = jnp.einsum("td,fd->tf", normed_two, w_gate, preferred_element_type=jnp.float32)
    up_pre = jnp.einsum("td,fd->tf", normed_two, w_up, preferred_element_type=jnp.float32)
    sigma = jax.nn.sigmoid(gate_pre)
    hidden_low = (gate_pre * sigma * up_pre).astype(jnp.bfloat16)
    ffn_part = jnp.dot(hidden_low, w_down, preferred_element_type=jnp.float32)
    ffn_share = lax.psum_scatter(ffn_part, "head", scatter_dimension=1, tiled=True)
    share_width = width // head_devices
    residual_share = lax.dynamic_slice_in_dim(hidden_one, head_place * share_width, share_width, 1)
    block_out = (residual_share + ffn_share).astype(jnp.bfloat16)
    grad_out_f = cotangent.astype(jnp.float32)
    hidden_grad = jnp.einsum("td,fd->tf", cotangent, w_down, preferred_element_type=jnp.float32)
    silu_grad = sigma * (1.0 + gate_pre * (1.0 - sigma))
    gate_grad = (hidden_grad * up_pre * silu_grad).astype(jnp.bfloat16)
    up_grad = (hidden_grad * gate_pre * sigma).astype(jnp.bfloat16)
    down_grad = jnp.einsum("tf,td->fd", hidden_low, cotangent, preferred_element_type=jnp.float32)
    gate_w_grad = jnp.einsum("tf,td->fd", gate_grad, normed_two, preferred_element_type=jnp.float32)
    up_w_grad = jnp.einsum("tf,td->fd", up_grad, normed_two, preferred_element_type=jnp.float32)
    ffn_rows_grad = jnp.concatenate([gate_w_grad, up_w_grad, down_grad], axis=0)
    ffn_owner = jnp.take(ffn_rows_grad.reshape(seq_devices, ffn_slab, width), inverse_ffn, axis=0)
    normed_two_part = jnp.einsum(
        "tf,fd->td", gate_grad, w_gate, preferred_element_type=jnp.float32
    ) + jnp.einsum("tf,fd->td", up_grad, w_up, preferred_element_type=jnp.float32)
    normed_two_share = lax.psum_scatter(normed_two_part, "head", scatter_dimension=1, tiled=True)
    normed_two_grad = lax.all_gather(normed_two_share, "head", axis=1, tiled=True)
    back_two, gain_two_grad = norm_back(normed_two_grad, hidden_one, rms_two, gain_two)
    hidden_one_grad = grad_out_f + back_two
    hidden_grad_low = hidden_one_grad.astype(jnp.bfloat16)
    attended_grad = branch_scale * jnp.einsum(
        "td,id->ti", hidden_grad_low, w_out, preferred_element_type=jnp.float32
    )
    attended_grad = attended_grad.reshape(head_shape).astype(jnp.bfloat16)
    soft_again = jnp.exp(scores_of() - log_total)
    soft_grad = jnp.einsum(
        "thd,chd->htc", attended_grad, values_all, preferred_element_type=jnp.float32
    )
    inner_sum = jnp.sum(soft_again * soft_grad, axis=-1, keepdims=True)
    score_grad = (soft_again * (soft_grad - inner_sum) * score_scale).astype(jnp.bfloat16)
    query_grad_turned = jnp.einsum(
        "htc,chd->thd", score_grad, keys_all, preferred_element_type=jnp.float32
    )
    key_grad_all = jnp.einsum(
        "htc,thd->chd", score_grad, queries, preferred_element_type=jnp.float32
    )
    value_grad_all = jnp.einsum(
        "htc,thd->chd", soft_low, attended_grad, preferred_element_type=jnp.float32
    )
    key_grad_own = key_grad_all[WINDOW:]
    value_grad_own = value_grad_all[WINDOW:]
    start_at = 0
    for hop_index in range(hop_total, 0, -1):
        hop_rows = hop_sizes[hop_index - 1]
        back_keys, back_values = passed_along(
            (
                key_grad_all[start_at : start_at + hop_rows],
                value_grad_all[start_at : start_at + hop_rows],
            ),
            "seq",
            -hop_index,
        )
        key_grad_own = key_grad_own.at[tok_rows - hop_rows :].add(back_keys)
        value_grad_own = value_grad_own.at[tok_rows - hop_rows :].add(back_values)
        start_at = start_at + hop_rows
    query_grad = (
        rotate(query_grad_turned, cosine, -sine).reshape(tok_rows, head_width).astype(jnp.bfloat16)
    )
    key_grad = (
        rotate(key_grad_own, cosine, -sine).reshape(tok_rows, head_width).astype(jnp.bfloat16)
    )
    value_grad = value_grad_own.reshape(tok_rows, head_width).astype(jnp.bfloat16)

    def input_part(row_grad, weight_rows):
        return jnp.einsum("ti,id->td", row_grad, weight_rows, preferred_element_type=jnp.float32)

    normed_one_part = (
        input_part(query_grad, w_query)
        + input_part(key_grad, w_key)
        + input_part(value_grad, w_value)
    )
    normed_one_share = lax.psum_scatter(normed_one_part, "head", scatter_dimension=1, tiled=True)
    normed_one_grad = lax.all_gather(
        normed_one_share.astype(jnp.bfloat16), "head", axis=1, tiled=True
    ).astype(normed_one_share.dtype)
    back_one, gain_one_grad = norm_back(normed_one_grad, inputs, rms_one, gain_one)
    input_grad = hidden_one_grad + back_one
    gain_grads = jnp.stack([gain_one_grad, gain_two_grad])

    def rows_grad(row_grad):
        return jnp.einsum("ti,td->id", row_grad, normed_one, preferred_element_type=jnp.float32)

    out_w_grad = branch_scale * jnp.einsum(
        "ti,td->id", attended_low, hidden_grad_low, preferred_element_type=jnp.float32
    )
    attn_rows_grad = jnp.concatenate(
        [rows_grad(query_grad), rows_grad(key_grad), rows_grad(value_grad), out_w_grad], axis=0
    )
    attn_owner = jnp.take(
        attn_rows_grad.reshape(seq_devices, attn_slab, width), inverse_attn, axis=0
    )
    owner_rows = jnp.concatenate([attn_owner, ffn_owner], axis=1).reshape(
        seq_devices * slab_rows, width
    )
    reduced, gain_reduced = (
        lax.psum_scatter(owner_rows, "seq", scatter_dimension=0, tiled=True),
        lax.psum_scatter(gain_grads, "seq", scatter_dimension=1, tiled=True),
    )
    attn_kinds = (
        inverse_attn[seq_place] * attn_slab + jnp.arange(attn_slab, dtype=jnp.int32)
    ) // head_width
    ffn_kinds = (
        4 + (inverse_ffn[seq_place] * ffn_slab + jnp.arange(ffn_slab, dtype=jnp.int32)) // ffn_width
    )
    row_rates = kind_rates(jnp.concatenate([attn_kinds, ffn_kinds]), width)[:, None]
    basis = eigenbases[0, 0]
    block_size = basis.shape[-1]
    split_shape = (slab_rows, width // block_size, block_size)
    turned = jnp.einsum(
        "rbk,bkl->rbl", reduced.reshape(split_shape), basis, precision=PRECISE
    ).reshape(slab_rows, width)
    first_new = BETA_FIRST * first_moment[0, 0] + (1.0 - BETA_FIRST) * turned
    second_new = BETA_SECOND * second_moment[0, 0] + (1.0 - BETA_SECOND) * turned * turned
    adam_dir = (
        first_new
        / (1.0 - BETA_FIRST**ADAM_STEP)
        / (jnp.sqrt(second_new / (1.0 - BETA_SECOND**ADAM_STEP)) + ADAM_EPS)
    )
    backward_dir = jnp.einsum(
        "rbl,bkl->rbk", adam_dir.reshape(split_shape), basis, precision=PRECISE
    ).reshape(slab_rows, width)
    master_old = master[0, 0]
    master_new = master_old - row_rates * (backward_dir + DECAY_RATE * master_old)
    gain_first_new = BETA_FIRST * gain_first + (1.0 - BETA_FIRST) * gain_reduced
    gain_second_new = BETA_SECOND * gain_second + (1.0 - BETA_SECOND) * gain_reduced * gain_reduced
    gain_new = norm_gains - GAIN_RATE * (gain_first_new / (1.0 - BETA_FIRST**ADAM_STEP)) / (
        jnp.sqrt(gain_second_new / (1.0 - BETA_SECOND**ADAM_STEP)) + ADAM_EPS
    )
    return (
        block_out,
        input_grad,
        reduced[None, None],
        first_new[None, None],
        second_new[None, None],
        master_new[None, None],
        master_new.astype(jnp.bfloat16)[None, None],
        gain_reduced,
        gain_first_new,
        gain_second_new,
        gain_new,
    )


SLAB = 516
PAD = 528
HALF = 1024
QUART = 512
UNITS = 1376
NT = (((1,), (1,)), ((), ()))
TN = (((0,), (0,)), ((), ()))


VM = pl.BlockSpec(memory_space=pltpu.VMEM)
SM = pl.BlockSpec(memory_space=pltpu.SMEM)
HB = pl.BlockSpec(memory_space=pl.ANY)


def shape(rows, columns, dtype=BF16):
    return jax.ShapeDtypeStruct((rows, columns), dtype)


def call(kernel, outs, specs, args, scratch=(), flops=0, moved=0, out_specs=None, grid=None):
    extra = {} if grid is None else {"grid": grid}
    return pl.pallas_call(
        kernel,
        out_shape=outs,
        in_specs=specs,
        out_specs=[VM] * len(outs) if out_specs is None else out_specs,
        scratch_shapes=list(scratch),
        compiler_params=pltpu.CompilerParams(vmem_limit_bytes=56 * 2**20),
        cost_estimate=pl.CostEstimate(flops=flops, bytes_accessed=moved, transcendentals=0),
        name=getattr(kernel, "func", kernel).__name__,
        **extra,
    )(*args)


def root_of(values):
    return lax.rsqrt(jnp.mean(values * values, axis=-1, keepdims=True) + EPS_NORM)


def turn(values, cosine, sine):
    parts = []
    for h in range(values.shape[1] // HEAD_DIM):
        v = values[:, h * HEAD_DIM : (h + 1) * HEAD_DIM]
        parts.append(v * cosine + pltpu.roll(v, HEAD_DIM // 2, 1) * sine)
    return parts


MESH = pl.DeviceIdType.MESH


def flip(index, mask):
    for bit in (1, 2, 4):
        if mask & bit:
            index = index + bit - 2 * bit * lax.rem(lax.div(index, bit), 2)
    return index


class Plane:
    def __init__(self, at, sent, got, me, line):
        self.at, self.sent, self.got, self.me, self.line = at, sent, got, me, line

    def copy(self, src, dst, side, hop_mask):
        return pltpu.make_async_remote_copy(
            src_ref=self.at(src, side),
            dst_ref=self.at(dst, side),
            send_sem=self.sent.at[dst, side],
            recv_sem=self.got.at[dst, side],
            device_id=(flip(self.me, hop_mask), self.line),
            device_id_type=MESH,
        )

    def start(self):
        for mask, side in ((2, 0), (4, 1), (2, 1), (4, 0)):
            self.copy(0, mask, side, mask).start()
        for side in (0, 1):
            self.copy(0, 1, side, 1).start()

    def arrive(self, mask, side):
        self.copy(mask, mask, side, 1).wait_recv()

    def twin(self, mask, side):
        self.copy(mask, mask + 1, side, 1).start()

    def relay_first(self):
        for mask, side in ((2, 0), (4, 1)):
            self.arrive(mask, side)
            self.copy(mask, 6, side, 6 - mask).start()
            self.twin(mask, side)

    def relay_second(self):
        for mask, side in ((2, 1), (4, 0)):
            self.arrive(mask, side)
            self.twin(mask, side)

    def relay_last(self):
        for side in (0, 1):
            self.arrive(6, side)
            self.twin(6, side)

    def finish(self):
        for mask in (1, 3, 5, 7):
            for side in (0, 1):
                self.arrive(mask, side)

    def drain(self):
        for mask in range(1, 8):
            for side in (0, 1):
                self.copy(0, mask, side, 1).wait_send()


def line_copy(src, dst, sent, got, m, me, line):
    return pltpu.make_async_remote_copy(
        src_ref=src,
        dst_ref=dst,
        send_sem=sent.at[m],
        recv_sem=got.at[m],
        device_id=(me, flip(line, m)),
        device_id_type=MESH,
    )


def greet(me, line, plane_masks, line_masks):
    barrier = pltpu.get_barrier_semaphore()
    for mask in plane_masks:
        pl.semaphore_signal(barrier, inc=1, device_id=(flip(me, mask), line), device_id_type=MESH)
    for mask in line_masks:
        pl.semaphore_signal(barrier, inc=1, device_id=(me, flip(line, mask)), device_id_type=MESH)
    return lambda: pl.semaphore_wait(barrier, len(plane_masks) + len(line_masks))


def front_kernel(
    rows, scale, branch,
    order_a, order_f, inverse_f, tokens, dy, own_gains, cosine, sine, master,
    a_low, gains, b_low, h_out, o_low, o_wide, stats, kcat, vcat, qcat, w_out, sent, n_own, n_parts, b_own, b_parts,
    wide, w_a, w_f, made, cut, total, z_out, z_in, z_sum, work,
    sem_w, sem_o, a_sent, a_got, f_sent, f_got, k_sent, k_got, q_sent, q_got, z_sems,
):
    me, line = lax.axis_index("seq"), lax.axis_index("head")
    ready = greet(me, line, (1, 2, 4), (1, 2, 3))
    w_a_plane = Plane(lambda m, s: w_a.at[m, s], a_sent, a_got, me, line)
    w_f_plane = Plane(lambda m, s: w_f.at[m, s], f_sent, f_got, me, line)
    kv_plane = Plane(lambda m, s: (kcat, vcat)[s].at[pl.ds(m * rows, rows)], k_sent, k_got, me, line)
    q_plane = Plane(lambda m, s: qcat.at[m, s], q_sent, q_got, me, line)

    load = pltpu.make_async_copy(master.at[pl.ds(0, 256), 0, :], wide.at[pl.ds(0, 256)], sem_w.at[0])
    load.start()
    w_a[0, 0, pl.ds(256, 16), :] = jnp.zeros((16, HALF), BF16)
    w_a[0, 1, pl.ds(256, 16), :] = jnp.zeros((16, HALF), BF16)
    w_a[0, 1, 256:258, 0:256] = own_gains[...].astype(BF16)
    load.wait()
    for side in (0, 1):
        w_a[0, side, pl.ds(0, 256), :] = wide[pl.ds(0, 256), side * HALF : (side + 1) * HALF].astype(BF16)
    load = pltpu.make_async_copy(master.at[pl.ds(256, SLAB), 0, :], wide, sem_w.at[1])
    load.start()
    ready()
    w_a_plane.start()
    load.wait()
    for side in (0, 1):
        columns = slice(side * HALF, (side + 1) * HALF)
        w_f[0, side, pl.ds(0, 512), :] = wide[pl.ds(0, 512), columns].astype(BF16)
        last = jnp.concatenate([wide[512:SLAB, columns], jnp.zeros((PAD - SLAB, HALF), F32)], axis=0)
        w_f[0, side, pl.ds(512, 16), :] = last.astype(BF16)
    w_a_plane.relay_first()
    w_a_plane.relay_second()
    w_a_plane.relay_last()
    w_f_plane.start()
    w_a_plane.finish()
    keep = pltpu.make_async_copy(w_a, w_out, sem_o.at[0])
    keep.start()

    for m in range(8):
        at = pl.multiple_of(flip(me, m) * 256, 256)
        gains[:, pl.ds(at, 256)] = w_a[m, 1, 256:258, 0:256].astype(F32)
    x = tokens[...].astype(F32)
    normed = (x * root_of(x) * gains[0:1, :]).astype(BF16)
    for side in (0, 1):
        a_low[side] = normed[:, side * HALF : (side + 1) * HALF]
    for j in (2, 3, 4, 5, 0, 1):
        out = lax.dot_general(a_low[0], w_a[order_a[j], 0, pl.ds(0, 256), :], NT, preferred_element_type=F32)
        out += lax.dot_general(a_low[1], w_a[order_a[j], 1, pl.ds(0, 256), :], NT, preferred_element_type=F32)
        if j < 4:
            parts = turn(out, cosine[...], sine[...])
        else:
            parts = [out[:, :HEAD_DIM], out[:, HEAD_DIM:]]
        for i, part in enumerate(parts):
            if j < 2:
                qcat[0, j, :, i * HEAD_DIM : (i + 1) * HEAD_DIM] = part.astype(BF16)
            else:
                at = (2 * (j % 2) + i) * HEAD_DIM
                (kcat, vcat)[j // 2 - 1][pl.ds(0, rows), at : at + HEAD_DIM] = part.astype(BF16)
        if j == 5:
            kv_plane.start()
    kv_plane.relay_first()
    kv_plane.relay_second()
    kv_plane.relay_last()
    q_plane.start()
    kv_plane.finish()

    at_q = me * rows + lax.broadcasted_iota(jnp.int32, (rows, 1), 0)
    along = lax.broadcasted_iota(jnp.int32, (1, rows), 1)
    lane = lax.broadcasted_iota(jnp.int32, (rows, HEAD_DIM), 1)
    stat = jnp.zeros((rows, HEAD_DIM), F32)
    for h in range(4):
        columns = slice(h * HEAD_DIM, (h + 1) * HEAD_DIM)
        q = qcat[0, h // 2, :, (h % 2) * HEAD_DIM : (h % 2 + 1) * HEAD_DIM]
        top = jnp.full((rows, 1), NEGATIVE, F32)
        for m in range(8):
            ahead = at_q - (flip(me, m) * rows + along)
            s = lax.dot_general(q, kcat[pl.ds(m * rows, rows), columns], NT, preferred_element_type=F32)
            s = jnp.where((ahead >= 0) & (ahead < WINDOW), s * scale, NEGATIVE)
            work[m] = s
            top = jnp.maximum(top, jnp.max(s, axis=-1, keepdims=True))
        sums = jnp.zeros((rows, 1), F32)
        for m in range(8):
            e = jnp.exp(work[m] - top)
            work[m] = e
            sums += jnp.sum(e, axis=-1, keepdims=True)
        share = 1.0 / sums
        o = jnp.zeros((rows, HEAD_DIM), F32)
        for m in range(8):
            soft = (work[m] * share).astype(BF16)
            o += jnp.dot(soft, vcat[pl.ds(m * rows, rows), columns], preferred_element_type=F32)
        o_wide[:, columns] = o
        o_low[:, columns] = o.astype(BF16)
        stat = jnp.where(lane == h, top + jnp.log(sums), stat)
    stats[...] = stat
    for side in (0, 1):
        out = jnp.dot(o_low[:, :256], w_a[order_a[6], side, pl.ds(0, 256), :], preferred_element_type=F32)
        out += jnp.dot(o_low[:, 256:], w_a[order_a[7], side, pl.ds(0, 256), :], preferred_element_type=F32)
        total[:, side * HALF : (side + 1) * HALF] = branch * out

    def quarter(m):
        return pl.ds(pl.multiple_of(flip(line, m) * QUART, QUART), QUART)

    def piece(m):
        return line_copy(z_out.at[m], z_in.at[m], z_sems.at[0], z_sems.at[1], m, me, line)

    def whole(m):
        return line_copy(z_sum.at[0], z_sum.at[m], z_sems.at[2], z_sems.at[3], m, me, line)

    for m in (3, 2, 1):
        z_out[m] = total[:, quarter(m)].astype(BF16)
        piece(m).start()
    w_f_plane.relay_first()
    for m in (1, 2, 3):
        piece(m).wait_recv()
    summed = total[:, quarter(0)]
    for m in (1, 2, 3):
        summed += z_in[m].astype(F32)
    z_sum[0] = summed.astype(BF16)
    for m in (3, 2, 1):
        whole(m).start()
    w_f_plane.relay_second()
    q_plane.relay_first()
    q_plane.relay_second()
    q_plane.relay_last()
    for m in (1, 2, 3):
        whole(m).wait_recv()

    for m in range(4):
        h_out[:, quarter(m)] = z_sum[m].astype(F32)
    h = h_out[...] + tokens[...].astype(F32)
    h_out[...] = h
    normed = (h * root_of(h) * gains[1:2, :]).astype(BF16)
    for side in (0, 1):
        b_low[side] = normed[:, side * HALF : (side + 1) * HALF]
    w_f_plane.relay_last()
    w_f_plane.finish()

    def through(j, left, right):
        out = lax.dot_general(w_f[order_f[j], 0], left, NT, preferred_element_type=F32)
        return out + lax.dot_general(w_f[order_f[j], 1], right, NT, preferred_element_type=F32)

    made[pl.ds(8 * SLAB, 16), :] = jnp.zeros((16, rows), F32)
    row = lax.broadcasted_iota(jnp.int32, (PAD, 1), 0)
    gate_rows = row < 2 * UNITS - 5 * SLAB
    for j in range(8):
        if j < 5:
            out = through(j, b_low[0], b_low[1])
        elif j > 5:
            out = through(j, dy[:, :HALF], dy[:, HALF:])
        else:
            out = jnp.where(gate_rows, through(j, b_low[0], b_low[1]), through(j, dy[:, :HALF], dy[:, HALF:]))
        made[pl.ds(j * SLAB, PAD), :] = out

    def mix(i, _):
        at = pl.multiple_of(i * 32, 8)
        gate = made[pl.ds(at, 32), :]
        up = made[pl.ds(UNITS + at, 32), :]
        back = made[pl.ds(2 * UNITS + at, 32), :]
        sigma = 1.0 / (1.0 + jnp.exp(-gate))
        silu = gate * sigma
        made[pl.ds(at, 32), :] = back * up * (sigma * (1.0 + gate * (1.0 - sigma)))
        made[pl.ds(UNITS + at, 32), :] = back * silu
        made[pl.ds(2 * UNITS + at, 32), :] = silu * up
        return 0

    lax.fori_loop(0, UNITS // 32, mix, 0)
    for j in range(8):
        cut[j] = made[pl.ds(j * SLAB, PAD), :].astype(BF16)
    for m in range(8):
        sent[m] = cut[inverse_f[flip(me, m)]]
    for own, parts, kinds in ((n_own, n_parts, range(0, 6)), (b_own, b_parts, range(5, 8))):
        for side in (0, 1):
            columns = slice(side * HALF, (side + 1) * HALF)
            for j in kinds:
                z = cut[j]
                if j == 5:
                    z = jnp.where(gate_rows if parts is n_parts else ~gate_rows, z, jnp.zeros_like(z))
                out = lax.dot_general(z, w_f[order_f[j], side], TN, preferred_element_type=F32)
                total[:, columns] = out if j == kinds[0] else total[:, columns] + out
        own[...] = total[:, quarter(0)]
        for m in (1, 2, 3):
            parts[m - 1] = total[:, quarter(m)].astype(BF16)

    q_plane.finish()
    for plane in (w_a_plane, w_f_plane, kv_plane, q_plane):
        plane.drain()
    for m in (1, 2, 3):
        piece(m).wait_send()
        whole(m).wait_send()
    keep.wait()


def front(order_a, order_f, inverse_f, tokens, dy, own_gains, cosine, sine, master, scale, branch):
    rows = tokens.shape[0]
    array = jax.ShapeDtypeStruct
    outs = [
        array((2, rows, HALF), BF16),
        array((2, 2 * HALF), F32),
        array((2, rows, HALF), BF16),
        array((rows, 2 * HALF), F32),
        array((rows, QUART), BF16),
        array((rows, QUART), F32),
        array((rows, HEAD_DIM), F32),
        array((8 * rows, QUART), BF16),
        array((8 * rows, QUART), BF16),
        array((8, 2, rows, 256), BF16),
        array((8, 2, 272, HALF), BF16),
        array((8, PAD, rows), BF16),
        array((rows, QUART), F32),
        array((3, rows, QUART), BF16),
        array((rows, QUART), F32),
        array((3, rows, QUART), BF16),
    ]
    out_specs = [VM] * len(outs)
    out_specs[10] = HB
    dma = pltpu.SemaphoreType.DMA
    return pl.pallas_call(
        functools.partial(front_kernel, rows, scale, branch),
        out_shape=outs,
        in_specs=[SM] * 3 + [VM] * 5 + [HB],
        out_specs=out_specs,
        scratch_shapes=[
            pltpu.VMEM((SLAB, 2 * HALF), F32),
            pltpu.VMEM((8, 2, 272, HALF), BF16),
            pltpu.VMEM((8, 2, PAD, HALF), BF16),
            pltpu.VMEM((8 * SLAB + 16, rows), F32),
            pltpu.VMEM((8, PAD, rows), BF16),
            pltpu.VMEM((rows, 2 * HALF), F32),
            pltpu.VMEM((4, rows, QUART), BF16),
            pltpu.VMEM((4, rows, QUART), BF16),
            pltpu.VMEM((4, rows, QUART), BF16),
            pltpu.VMEM((8, rows, rows), F32),
            dma((2,)),
            dma((1,)),
        ]
        + [dma((8, 2))] * 8
        + [dma((4, 4))],
        compiler_params=pltpu.CompilerParams(
            collective_id=0, has_side_effects=True, vmem_limit_bytes=62 * 2**20
        ),
        cost_estimate=pl.CostEstimate(flops=10**10, bytes_accessed=30 * 2**20, transcendentals=0),
        name="front",
    )(order_a, order_f, inverse_f, tokens, dy, own_gains, cosine, sine, master)


def back_kernel(
    rows, scale, branch,
    order_a, inverse_a, tokens, dy, gains, cosine, sine, h_in, o_low, o_wide, stats, n_own, n_parts, b_own, b_parts,
    norm_gains, gain_first, gain_second, q_in, k_in, v_in, w_in, a_low, b_low, z_own,
    block_out, input_grad, gain_grad, gain_first_new, gain_second_new, gain_new, acts, z_all, g_all,
    w_a, qcat, kcat, vcat, docat, d_one, d_low, dq, dk, dv, groups, sent, total, stat_l, stat_r,
    z_in, z_sum, b_in, gain_out, gain_in,
    load_sems, keep_sems, n_sems, p_sems, b_sems, act_sent, act_got, do_sent, do_got, a2a_sems,
):
    me, line = lax.axis_index("seq"), lax.axis_index("head")
    ready = greet(me, line, range(1, 8), (1, 2, 3))
    loads = [
        pltpu.make_async_copy(src, dst, load_sems.at[i])
        for i, (src, dst) in enumerate(((w_in, w_a), (q_in, qcat), (k_in, kcat), (v_in, vcat)))
    ]
    for load in loads:
        load.start()
    own = {0: a_low, 1: b_low}
    keeps = [pltpu.make_async_copy(own[kind], acts.at[kind, 0], keep_sems.at[kind]) for kind in (0, 1)]
    keeps.append(pltpu.make_async_copy(d_low, acts.at[3, 0], keep_sems.at[3]))
    keeps.append(pltpu.make_async_copy(z_own.at[0], z_all.at[0], keep_sems.at[4]))
    keeps.append(pltpu.make_async_copy(sent.at[0], g_all.at[0], keep_sems.at[5]))
    for s in (0, 1):
        half = dy.at[:, pl.ds(s * HALF, HALF)]
        keeps.append(pltpu.make_async_copy(half, acts.at[2, 0, s], keep_sems.at[(2, 6)[s]]))

    def act_plane(kind):
        def at(m, s):
            if m == 0:
                if kind == 2:
                    return dy.at[:, pl.ds(s * HALF, HALF)]
                return (a_low, b_low, None, d_low)[kind].at[s]
            return acts.at[kind, m, s]

        return Plane(at, act_sent.at[kind], act_got.at[kind], me, line)

    a_plane, b_plane, dy_plane, d_plane = (act_plane(kind) for kind in range(4))
    do_plane = Plane(lambda m, s: docat.at[m, s], do_sent, do_got, me, line)

    def straight(src, dst, which, m):
        return pltpu.make_async_remote_copy(
            src_ref=src.at[m],
            dst_ref=dst.at[m],
            send_sem=a2a_sems.at[which, 0, m],
            recv_sem=a2a_sems.at[which, 1, m],
            device_id=(flip(me, m), line),
            device_id_type=MESH,
        )

    def quarter(m):
        return pl.ds(pl.multiple_of(flip(line, m) * QUART, QUART), QUART)

    def n_piece(m):
        return line_copy(n_parts.at[m - 1], z_in.at[0, m], n_sems.at[0], n_sems.at[1], m, me, line)

    def p_piece(m):
        return line_copy(z_sum.at[1, m], z_in.at[1, m], p_sems.at[0], p_sems.at[1], m, me, line)

    def b_piece(m):
        return line_copy(b_parts.at[m - 1], b_in.at[m], b_sems.at[0], b_sems.at[1], m, me, line)

    def n_whole(m):
        return line_copy(z_sum.at[0, 0], z_sum.at[0, m], n_sems.at[2], n_sems.at[3], m, me, line)

    def p_whole(m):
        return line_copy(z_sum.at[2, 0], z_sum.at[2, m], p_sems.at[2], p_sems.at[3], m, me, line)

    ready()
    for m in (3, 2, 1):
        n_piece(m).start()
    b_plane.start()
    for m in range(1, 8):
        straight(z_own, z_all, 0, m).start()
    keeps[0].start()
    keeps[1].start()
    for i in (3, 5, 6):
        keeps[i].start()
    for m in (1, 2, 3):
        n_piece(m).wait_recv()
    summed = n_own[...]
    for m in (1, 2, 3):
        summed += z_in[0, m].astype(F32)
    z_sum[0, 0] = summed.astype(BF16)
    for m in (3, 2, 1):
        n_whole(m).start()
    b_plane.relay_first()
    for m in (1, 2, 3):
        n_whole(m).wait_recv()
    for m in (3, 2, 1):
        b_piece(m).start()

    for m in range(4):
        total[:, quarter(m)] = z_sum[0, m].astype(F32)
    normed_grad = total[...]
    h = h_in[...]
    root = root_of(h)
    gain_two = jnp.sum(normed_grad * h * root, axis=0, keepdims=True)
    weighted = normed_grad * gains[1:2, :]
    inner = jnp.mean(weighted * h, axis=-1, keepdims=True)
    grad = dy[...].astype(F32) + root * weighted - h * (root * root * root) * inner
    d_one[...] = grad
    low = grad.astype(BF16)
    for side in (0, 1):
        d_low[side] = low[:, side * HALF : (side + 1) * HALF]
    keeps[2].start()
    total[0:1, :] = gain_two
    for m in range(8):
        at = pl.multiple_of(flip(me, m) * 256, 256)
        gain_out[m, 1:2, :] = total[0:1, pl.ds(at, 256)]
    loads[0].wait()
    lane = lax.broadcasted_iota(jnp.int32, (rows, HEAD_DIM), 1)
    own_lines = []
    for j, stat in enumerate((stat_l, stat_r)):
        out = lax.dot_general(d_low[0], w_a[order_a[6 + j], 0, pl.ds(0, 256), :], NT, preferred_element_type=F32)
        out += lax.dot_general(d_low[1], w_a[order_a[6 + j], 1, pl.ds(0, 256), :], NT, preferred_element_type=F32)
        out = (branch * out).astype(BF16)
        docat[0, j, pl.ds(0, rows), :] = out
        lines = jnp.zeros((rows, HEAD_DIM), F32)
        columns = []
        for i in (0, 1):
            h_at = 2 * j + i
            cut = slice(h_at * HEAD_DIM, (h_at + 1) * HEAD_DIM)
            delta = jnp.sum(
                out[:, i * HEAD_DIM : (i + 1) * HEAD_DIM].astype(F32) * o_wide[:, cut], axis=-1, keepdims=True
            )
            top = stats[:, h_at : h_at + 1]
            columns.append((top, delta))
            for at, value in ((i, top), (2 + i, delta)):
                for step in range(3):
                    part = value.astype(BF16).astype(F32)
                    value = value - part
                    lines = jnp.where(lane == 4 * step + at, part, lines)
        own_lines.append(columns)
        stat[pl.ds(0, rows), :] = lines
        stat[pl.ds(rows, 256 - rows), :] = jnp.zeros((256 - rows, HEAD_DIM), F32)
        docat[0, j, pl.ds(rows, 16), :] = stat[...].T[:16, :].astype(BF16)
    do_plane.start()
    b_plane.relay_second()
    b_plane.relay_last()

    for load in loads[1:]:
        load.wait()
    dq[...] = jnp.zeros_like(dq)
    dk[...] = jnp.zeros_like(dk)
    dv[...] = jnp.zeros_like(dv)
    reach = -(-WINDOW // rows)
    down = lax.broadcasted_iota(jnp.int32, (rows, rows), 0)
    along = lax.broadcasted_iota(jnp.int32, (rows, rows), 1)

    def head_cut(h):
        return h // 2, slice((h % 2) * HEAD_DIM, (h % 2 + 1) * HEAD_DIM), slice(h * HEAD_DIM, (h + 1) * HEAD_DIM)

    def rows_of(m):
        return pl.ds(m * rows, rows)

    def query_side(m):
        apart = me - flip(me, m)

        @pl.when((apart >= 0) & (apart <= reach))
        def _():
            ahead = apart * rows + down - along
            allowed = (ahead >= 0) & (ahead < WINDOW)
            for h in range(4):
                side, two, cut = head_cut(h)
                top, delta = own_lines[side][h % 2]
                k, do = kcat[rows_of(m), cut], docat[0, side, pl.ds(0, rows), two]
                s = lax.dot_general(qcat[0, side, :, two], k, NT, preferred_element_type=F32)
                p = jnp.where(allowed, jnp.exp(s * scale - top), 0.0)
                dp = lax.dot_general(do, vcat[rows_of(m), cut], NT, preferred_element_type=F32)
                ds = (p * (dp - delta) * scale).astype(BF16)
                dq[:, cut] += jnp.dot(ds, k, preferred_element_type=F32)

    def key_side(m):
        apart = me - flip(me, m)

        @pl.when((apart <= 0) & (apart >= -reach))
        def _():
            ahead = along - down - apart * rows
            allowed = (ahead >= 0) & (ahead < WINDOW)
            for h in range(4):
                side, two, cut = head_cut(h)
                lines = docat[m, side, pl.ds(rows, 16), :].astype(F32)
                lines = (lines[0:4] + lines[4:8] + lines[8:12])[:, :rows]
                top, delta = lines[h % 2 : h % 2 + 1], lines[2 + h % 2 : 3 + h % 2]
                q, do = qcat[m, side, :, two], docat[m, side, pl.ds(0, rows), two]
                s = lax.dot_general(kcat[pl.ds(0, rows), cut], q, NT, preferred_element_type=F32)
                p = jnp.where(allowed, jnp.exp(s * scale - top), 0.0)
                dv[:, cut] += jnp.dot(p.astype(BF16), do, preferred_element_type=F32)
                dp = lax.dot_general(vcat[pl.ds(0, rows), cut], do, NT, preferred_element_type=F32)
                ds = (p * (dp - delta) * scale).astype(BF16)
                dk[:, cut] += jnp.dot(ds, q, preferred_element_type=F32)

    for m in range(4):
        query_side(m)
    do_plane.relay_first()
    for m in range(4, 8):
        query_side(m)
    do_plane.relay_second()
    do_plane.relay_last()
    d_plane.start()
    a_plane.start()
    dy_plane.start()
    do_plane.finish()
    for m in range(8):
        key_side(m)
    for j in range(8):
        cut = slice((j % 2) * 256, (j % 2 + 1) * 256)
        if j < 4:
            made = turn((dq, dk)[j // 2][:, cut], cosine[...], -sine[...])
            for i in (0, 1):
                groups[j, :, i * HEAD_DIM : (i + 1) * HEAD_DIM] = made[i].astype(BF16)
        elif j < 6:
            groups[j] = dv[:, cut].astype(BF16)
        else:
            groups[j] = o_low[:, cut]
    for j in range(6):
        for side in (0, 1):
            out = jnp.dot(groups[j], w_a[order_a[j], side, pl.ds(0, 256), :], preferred_element_type=F32)
            columns = slice(side * HALF, (side + 1) * HALF)
            total[:, columns] = out if j == 0 else total[:, columns] + out
    for m in (3, 2, 1):
        z_sum[1, m] = total[:, quarter(m)].astype(BF16)
        p_piece(m).start()
    for m in range(8):
        sent[m] = groups[inverse_a[flip(me, m)]]
    keeps[4].start()
    for m in range(1, 8):
        straight(sent, g_all, 1, m).start()
    for m in (1, 2, 3):
        p_piece(m).wait_recv()
    summed = total[:, quarter(0)]
    for m in (1, 2, 3):
        summed += z_in[1, m].astype(F32)
    z_sum[2, 0] = summed.astype(BF16)
    for m in (3, 2, 1):
        p_whole(m).start()
    d_plane.relay_first()
    a_plane.relay_first()
    dy_plane.relay_first()
    for m in (1, 2, 3):
        b_piece(m).wait_recv()
    out = h_in[:, quarter(0)] + b_own[...]
    for m in (1, 2, 3):
        out += b_in[m].astype(F32)
    block_out[...] = out.astype(BF16)

    for m in (1, 2, 3):
        p_whole(m).wait_recv()
    for m in range(4):
        total[:, quarter(m)] = z_sum[2, m].astype(F32)
    normed_grad = total[...]
    x = tokens[...].astype(F32)
    root = root_of(x)
    gain_one = jnp.sum(normed_grad * x * root, axis=0, keepdims=True)
    weighted = normed_grad * gains[0:1, :]
    inner = jnp.mean(weighted * x, axis=-1, keepdims=True)
    input_grad[...] = d_one[...] + root * weighted - x * (root * root * root) * inner
    total[0:1, :] = gain_one
    for m in range(8):
        at = pl.multiple_of(flip(me, m) * 256, 256)
        gain_out[m, 0:1, :] = total[0:1, pl.ds(at, 256)]
    for m in range(1, 8):
        straight(gain_out, gain_in, 2, m).start()
    for plane in (d_plane, a_plane, dy_plane):
        plane.relay_second()
        plane.relay_last()
    for m in range(1, 8):
        straight(gain_out, gain_in, 2, m).wait_recv()
    made = gain_out[0, 0:2, :]
    for m in range(1, 8):
        made += gain_in[m, 0:2, :]
    gain_grad[...] = made
    first = BETA_FIRST * gain_first[...] + (1.0 - BETA_FIRST) * made
    second = BETA_SECOND * gain_second[...] + (1.0 - BETA_SECOND) * made * made
    gain_first_new[...] = first
    gain_second_new[...] = second
    gain_new[...] = norm_gains[...] - GAIN_RATE * (first / (1.0 - BETA_FIRST**ADAM_STEP)) / (
        jnp.sqrt(second / (1.0 - BETA_SECOND**ADAM_STEP)) + ADAM_EPS
    )
    for plane in (b_plane, d_plane, a_plane, dy_plane):
        plane.finish()
    for m in range(1, 8):
        straight(z_own, z_all, 0, m).wait_recv()
        straight(sent, g_all, 1, m).wait_recv()
    for plane in (b_plane, d_plane, a_plane, dy_plane, do_plane):
        plane.drain()
    for m in range(1, 8):
        straight(z_own, z_all, 0, m).wait_send()
        straight(sent, g_all, 1, m).wait_send()
        straight(gain_out, gain_in, 2, m).wait_send()
    for m in (1, 2, 3):
        for copy in (n_piece(m), n_whole(m), p_piece(m), p_whole(m), b_piece(m)):
            copy.wait_send()
    for keep in keeps:
        keep.wait()


def back(small, arrays, big, rows, scale, branch):
    array = jax.ShapeDtypeStruct
    dma = pltpu.SemaphoreType.DMA
    gains = array((2, 256), F32)
    return pl.pallas_call(
        functools.partial(back_kernel, rows, scale, branch),
        out_shape=[
            shape(rows, QUART), shape(rows, 2 * HALF, F32), gains, gains, gains, gains,
            array((4, 8, 2, rows, HALF), BF16), array((8, PAD, rows), BF16), array((8, rows, 256), BF16),
        ],
        in_specs=[SM] * len(small) + [VM] * len(arrays) + [HB] * len(big),
        out_specs=[VM] * 6 + [HB] * 3,
        scratch_shapes=[
            pltpu.VMEM((8, 2, 272, HALF), BF16),
            pltpu.VMEM((8, 2, rows, 256), BF16),
            pltpu.VMEM((8 * rows, QUART), BF16),
            pltpu.VMEM((8 * rows, QUART), BF16),
            pltpu.VMEM((8, 2, rows + 16, 256), BF16),
            pltpu.VMEM((rows, 2 * HALF), F32),
            pltpu.VMEM((2, rows, HALF), BF16),
            pltpu.VMEM((rows, QUART), F32),
            pltpu.VMEM((rows, QUART), F32),
            pltpu.VMEM((rows, QUART), F32),
            pltpu.VMEM((8, rows, 256), BF16),
            pltpu.VMEM((8, rows, 256), BF16),
            pltpu.VMEM((rows, 2 * HALF), F32),
            pltpu.VMEM((256, HEAD_DIM), F32),
            pltpu.VMEM((256, HEAD_DIM), F32),
            pltpu.VMEM((2, 4, rows, QUART), BF16),
            pltpu.VMEM((3, 4, rows, QUART), BF16),
            pltpu.VMEM((4, rows, QUART), BF16),
            pltpu.VMEM((8, 8, 256), F32),
            pltpu.VMEM((8, 8, 256), F32),
            dma((4,)),
            dma((7,)),
            dma((4, 4)),
            dma((4, 4)),
            dma((2, 4)),
            dma((4, 8, 2)),
            dma((4, 8, 2)),
            dma((8, 2)),
            dma((8, 2)),
            dma((3, 2, 8)),
        ],
        compiler_params=pltpu.CompilerParams(
            collective_id=1, has_side_effects=True, vmem_limit_bytes=62 * 2**20
        ),
        cost_estimate=pl.CostEstimate(flops=10**10, bytes_accessed=30 * 2**20, transcendentals=0),
        name="back",
    )(*small, *arrays, *big)


TILE = 256


def update_kernel(rows, branch, slabs, basis, *rest):
    zs, gs, acts, rest = rest[0], rest[1], rest[2], rest[3:]
    olds, news, low_new, rest = rest[:3], rest[3:7], rest[7], rest[8:]
    turned_g, act, old, new, asem, osem, nsem = rest
    tile, tiles = pl.program_id(0), pl.num_programs(0)
    slot = tile % 2
    a_slab, f_slab = slabs[0], slabs[1]

    def columns_of(t):
        return pl.ds(pl.multiple_of(t * TILE, TILE), TILE)

    def act_copies(t, kind, which):
        for side in (0, 1):

            @pl.when((t >= HALF // TILE) == (side == 1))
            def _():
                at = pl.ds(pl.multiple_of((t - side * (HALF // TILE)) * TILE, TILE), TILE)
                for m in range(8):
                    pltpu.make_async_copy(
                        acts.at[kind, m, side, :, at],
                        act.at[t % 2, which, pl.ds(m * rows, rows)],
                        asem.at[t % 2, which],
                    ).start()

    def act_wait(which):
        for m in range(8):
            part = act.at[slot, which, pl.ds(m * rows, rows)]
            pltpu.make_async_copy(part, part, asem.at[slot, which]).wait()

    def fetch_acts(t):
        pl.when(a_slab < 6)(lambda: act_copies(t, 0, 0))
        pl.when(a_slab >= 6)(lambda: act_copies(t, 3, 0))
        pl.when(f_slab <= 5)(lambda: act_copies(t, 1, 1))
        pl.when(f_slab > 5)(lambda: act_copies(t, 2, 1))
        pl.when(f_slab == 5)(lambda: act_copies(t, 2, 2))

    def old_copy(i, t):
        return pltpu.make_async_copy(olds[i].at[:, 0, columns_of(t)], old.at[t % 2, i], osem.at[t % 2, i])

    def new_copy(i, t):
        return pltpu.make_async_copy(new.at[t % 2, i], news[i].at[:, 0, columns_of(t)], nsem.at[t % 2, i])

    def fetch(t):
        fetch_acts(t)
        for i in range(3):
            old_copy(i, t).start()

    @pl.when(tile == 0)
    def _():
        fetch(0)
        for m in range(8):
            turned_g[:, m * rows : (m + 1) * rows] = gs[m].T

    pl.when(tile + 1 < tiles)(lambda: fetch(tile + 1))

    @pl.when(tile >= 2)
    def _():
        for i in range(4):
            new_copy(i, tile - 2).wait()

    grad, first_new, second_new, master_new = (new.at[slot, i] for i in range(4))
    first, second, master = (old.at[slot, i] for i in range(3))

    def ffn_rows(which):
        total = jnp.dot(zs[0], act[slot, which, pl.ds(0, rows), :], preferred_element_type=F32)
        for m in range(1, 8):
            total += jnp.dot(zs[m], act[slot, which, pl.ds(m * rows, rows), :], preferred_element_type=F32)
        return total[:SLAB]

    act_wait(0)
    factor = jnp.where(a_slab < 6, 1.0, branch)
    grad[pl.ds(0, 256), :] = factor * jnp.dot(turned_g[...], act[slot, 0], preferred_element_type=F32)
    act_wait(1)
    grad[pl.ds(256, SLAB), :] = ffn_rows(1)
    first_of_down = 2 * UNITS - f_slab * SLAB

    @pl.when(f_slab == 5)
    def _():
        act_wait(2)
        row = lax.broadcasted_iota(jnp.int32, (SLAB, 1), 0)
        grad[pl.ds(256, SLAB), :] = jnp.where(row < first_of_down, grad[pl.ds(256, SLAB), :], ffn_rows(2))

    for i in range(3):
        old_copy(i, tile).wait()
    row = lax.broadcasted_iota(jnp.int32, (256 + SLAB, 1), 0)
    rate = jnp.where((row < 256) | (row - 256 < first_of_down), 0.5 * (2 * HALF) ** (-0.5), 0.5 * FF ** (-0.5))
    for b in range(TILE // HEAD_DIM):
        cut = slice(b * HEAD_DIM, (b + 1) * HEAD_DIM)
        turned = jnp.dot(grad[:, cut], basis[b], precision=lax.Precision.HIGH, preferred_element_type=F32)
        one = BETA_FIRST * first[:, cut] + (1.0 - BETA_FIRST) * turned
        two = BETA_SECOND * second[:, cut] + (1.0 - BETA_SECOND) * turned * turned
        first_new[:, cut] = one
        second_new[:, cut] = two
        adam = (one / (1.0 - BETA_FIRST**ADAM_STEP)) / (
            jnp.sqrt(two / (1.0 - BETA_SECOND**ADAM_STEP)) + ADAM_EPS
        )
        back = lax.dot_general(
            adam, basis[b], NT, precision=lax.Precision.HIGH, preferred_element_type=F32
        )
        before = master[:, cut]
        after = before - rate * (back + DECAY_RATE * before)
        master_new[:, cut] = after
        low_new[:, cut] = after.astype(BF16)
    for i in range(4):
        new_copy(i, tile).start()

    @pl.when(tile == tiles - 1)
    def _():
        for t in (tile - 1, tile):
            for i in range(4):
                new_copy(i, t).wait()


def update(slabs, zs, gs, acts, basis, olds, branch):
    rows = gs.shape[1]
    height, _, width = olds[0].shape

    def whole(array):
        return pl.BlockSpec(array.shape, lambda i: (0,) * array.ndim)

    tall = pl.BlockSpec((height, TILE), lambda i: (0, i))
    per = TILE // HEAD_DIM
    return call(
        functools.partial(update_kernel, rows, branch),
        [jax.ShapeDtypeStruct(olds[0].shape, F32)] * 4 + [shape(height, width)],
        [SM, pl.BlockSpec((per, HEAD_DIM, HEAD_DIM), lambda i: (i, 0, 0))]
        + [whole(zs), whole(gs)]
        + [HB] * 4,
        [slabs, basis, zs, gs, acts, *olds],
        [
            pltpu.VMEM((256, 8 * rows), BF16),
            pltpu.VMEM((2, 3, 8 * rows, TILE), BF16),
            pltpu.VMEM((2, 3, height, TILE), F32),
            pltpu.VMEM((2, 4, height, TILE), F32),
            pltpu.SemaphoreType.DMA((2, 3)),
            pltpu.SemaphoreType.DMA((2, 3)),
            pltpu.SemaphoreType.DMA((2, 4)),
        ],
        out_specs=[HB] * 4 + [tall],
        grid=(width // TILE,),
        flops=2 * 8 * rows * height * width,
        moved=70 * 2**20,
    )


def plane_mesh(
    tokens,
    cotangent,
    owners,
    master,
    first_moment,
    second_moment,
    eigenbases,
    norm_gains,
    gain_first,
    gain_second,
):
    rows, width = tokens.shape
    me = lax.axis_index("seq")
    scale = HEAD_DIM ** (-0.5)
    branch = (WINDOW / 3.0) ** 0.5
    inverse_attn, inverse_ffn = inverse_order(owners[0]), inverse_order(owners[1])
    order_attn, order_ffn = owners[0] ^ me, owners[1] ^ me
    slabs = jnp.stack([inverse_attn[me], inverse_ffn[me]]).astype(jnp.int32)
    tall = [array.reshape(array.shape[2], 1, width) for array in (first_moment, second_moment, master)]
    cosine, sine = angles((me * rows + jnp.arange(rows, dtype=jnp.int32)).astype(F32))
    cosine, sine = cosine[:, 0, :], sine[:, 0, :]
    cosine = jnp.concatenate([cosine, cosine], axis=1)
    sine = jnp.concatenate([-sine, sine], axis=1)
    (
        a_low, gains, b_low, h, o_low, o_wide, stats, kcat, vcat, qcat, attn, z_own, n_own, n_parts, b_own, b_parts
    ) = front(
        order_attn, order_ffn, inverse_ffn, tokens, cotangent, norm_gains, cosine, sine, tall[2], scale, branch
    )
    block_out, input_grad, gain_grad, gain_first_new, gain_second_new, gain_new, acts, zs, gs = back(
        [order_attn, inverse_attn],
        [tokens, cotangent, gains, cosine, sine, h, o_low, o_wide, stats, n_own, n_parts, b_own, b_parts]
        + [norm_gains, gain_first, gain_second],
        [qcat, kcat, vcat, attn, a_low, b_low, z_own],
        rows,
        scale,
        branch,
    )
    grad, first_new, second_new, master_new, low_new = update(
        slabs, zs, gs, acts, eigenbases[0, 0], tall, branch
    )
    whole = (1, 1, *tall[0].shape[::2])
    return (
        block_out,
        input_grad,
        grad.reshape(whole),
        first_new.reshape(whole),
        second_new.reshape(whole),
        master_new.reshape(whole),
        low_new[None, None],
        gain_grad,
        gain_first_new,
        gain_second_new,
        gain_new,
    )


def solution(mesh):
    in_specs = (
        P("seq", None),
        P("seq", None),
        P(),
        P("head", "seq", None, None),
        P("head", "seq", None, None),
        P("head", "seq", None, None),
        P("head", "seq", None, None, None),
        P(None, "seq"),
        P(None, "seq"),
        P(None, "seq"),
    )
    out_specs = (
        P("seq", "head"),
        P("seq", None),
        P("head", "seq", None, None),
        P("head", "seq", None, None),
        P("head", "seq", None, None),
        P("head", "seq", None, None),
        P("head", "seq", None, None),
        P(None, "seq"),
        P(None, "seq"),
        P(None, "seq"),
        P(None, "seq"),
    )
    plane = mesh.shape["seq"] == 8 and mesh.shape["head"] == 4
    return jax.shard_map(
        plane_mesh if plane else any_mesh, mesh=mesh, in_specs=in_specs, out_specs=out_specs, check_vma=False
    )
```

```python
import functools

import jax
import jax.numpy as jnp
from jax import lax
from jax.experimental import pallas as pl
from jax.experimental.pallas import tpu as pltpu
from jax.sharding import PartitionSpec as P

HEADS = 16
HEAD_DIM = 128
FF = 5504
WINDOW = 1024
ADAM_STEP = 5


EPS_NORM = 1e-05
BETA_FIRST = 0.5
BETA_SECOND = 0.6
ADAM_EPS = 1e-08
DECAY_RATE = 0.1
GAIN_RATE = 0.25
ROPE_BASE = 10000.0
NEGATIVE = -1e30
PRECISE = lax.Precision.HIGHEST

BF16 = jnp.bfloat16
F32 = jnp.float32


def passed_along(shard, axis, by):
    devices = lax.axis_size(axis)
    pairs = [(i, i + by) for i in range(devices) if 0 <= i + by < devices]
    return lax.ppermute(shard, axis, pairs)


def inverse_order(owner_row):
    places = jnp.arange(owner_row.shape[0], dtype=jnp.int32)
    matches = (owner_row[:, None] == places[None, :]).astype(jnp.int32)
    return jnp.sum(matches * places[:, None], axis=0)


def kind_rates(kinds, width):
    wide = width ** (-0.5)
    spreads = jnp.array([wide, wide, wide, wide, wide, wide, FF ** (-0.5)], jnp.float32)
    matches = (kinds[..., None] == jnp.arange(7, dtype=jnp.int32)).astype(jnp.float32)
    return 0.5 * jnp.sum(matches * spreads, axis=-1)


def angles(positions):
    half_dim = HEAD_DIM // 2
    frequencies = ROPE_BASE ** (-jnp.arange(half_dim, dtype=jnp.float32) / half_dim)
    turning = positions[:, None] * frequencies[None, :]
    return (jnp.cos(turning)[:, None, :], jnp.sin(turning)[:, None, :])


def rotate(vectors, cosine, sine):
    half_dim = vectors.shape[-1] // 2
    former = vectors[..., :half_dim]
    latter = vectors[..., half_dim:]
    return jnp.concatenate(
        [former * cosine - latter * sine, latter * cosine + former * sine], axis=-1
    )


def inverse_rms(vectors):
    return lax.rsqrt(jnp.mean(vectors * vectors, axis=-1, keepdims=True) + EPS_NORM)


def norm_back(grad_normed, inputs, rms_values, gain_row):
    weighted = grad_normed * gain_row
    inner = jnp.mean(weighted * inputs, axis=-1, keepdims=True)
    input_part = rms_values * weighted - inputs * rms_values**3 * inner
    return (input_part, jnp.sum(grad_normed * inputs * rms_values, axis=0))


def any_mesh(
    tokens,
    cotangent,
    owners,
    master,
    first_moment,
    second_moment,
    eigenbases,
    norm_gains,
    gain_first,
    gain_second,
):
    tok_rows, width = tokens.shape
    seq_devices = lax.axis_size("seq")
    head_devices = lax.axis_size("head")
    seq_place = lax.axis_index("seq")
    head_place = lax.axis_index("head")
    slab_rows = master.shape[2]
    attn_slab = 4 * width // (head_devices * seq_devices)
    ffn_slab = slab_rows - attn_slab
    head_width = width // head_devices
    ffn_width = FF // head_devices
    local_heads = HEADS // head_devices
    score_scale = HEAD_DIM ** (-0.5)
    branch_scale = (WINDOW / 3.0) ** 0.5
    inverse_attn = inverse_order(owners[0])
    inverse_ffn = inverse_order(owners[1])
    master_low = master[0, 0].astype(jnp.bfloat16)
    gathered, gains_all = (
        lax.all_gather(master_low, "seq", axis=0, tiled=True),
        lax.all_gather(norm_gains.astype(jnp.bfloat16), "seq", axis=1, tiled=True),
    )
    gathered = gathered.reshape(seq_devices, slab_rows, width)
    attn_rows = jnp.take(gathered[:, :attn_slab], owners[0], axis=0).reshape(4 * head_width, width)
    ffn_rows = jnp.take(gathered[:, attn_slab:], owners[1], axis=0).reshape(3 * ffn_width, width)
    w_query = attn_rows[:head_width]
    w_key = attn_rows[head_width : 2 * head_width]
    w_value = attn_rows[2 * head_width : 3 * head_width]
    w_out = attn_rows[3 * head_width :]
    w_gate = ffn_rows[:ffn_width]
    w_up = ffn_rows[ffn_width : 2 * ffn_width]
    w_down = ffn_rows[2 * ffn_width :]
    gain_one = gains_all[0].astype(jnp.float32)
    gain_two = gains_all[1].astype(jnp.float32)
    inputs = tokens.astype(jnp.float32)
    rms_one = inverse_rms(inputs)
    normed_one = (inputs * rms_one * gain_one).astype(jnp.bfloat16)
    positions = (seq_place * tok_rows + jnp.arange(tok_rows, dtype=jnp.int32)).astype(jnp.float32)
    cosine, sine = angles(positions)
    head_shape = (tok_rows, local_heads, HEAD_DIM)

    def project(weight_rows):
        return jnp.einsum("td,id->ti", normed_one, weight_rows, preferred_element_type=jnp.float32)

    queries = rotate(project(w_query).reshape(head_shape), cosine, sine).astype(jnp.bfloat16)
    keys_own = rotate(project(w_key).reshape(head_shape), cosine, sine).astype(jnp.bfloat16)
    values_own = project(w_value).reshape(head_shape).astype(jnp.bfloat16)
    hop_total = -(-WINDOW // tok_rows)
    hop_sizes = [
        min(tok_rows, WINDOW - (hop_index - 1) * tok_rows) for hop_index in range(1, hop_total + 1)
    ]
    halo_keys = []
    halo_values = []
    for hop_index in range(hop_total, 0, -1):
        hop_rows = hop_sizes[hop_index - 1]
        far_keys, far_values = passed_along(
            (keys_own[tok_rows - hop_rows :], values_own[tok_rows - hop_rows :]), "seq", hop_index
        )
        halo_keys.append(far_keys)
        halo_values.append(far_values)
    keys_all = jnp.concatenate(halo_keys + [keys_own], axis=0)
    values_all = jnp.concatenate(halo_values + [values_own], axis=0)
    row_ids = jnp.arange(tok_rows, dtype=jnp.int32)[:, None]
    col_ids = jnp.arange(WINDOW + tok_rows, dtype=jnp.int32)[None, :]
    allowed = (
        (col_ids > row_ids)
        & (col_ids <= row_ids + WINDOW)
        & (seq_place * tok_rows - WINDOW + col_ids >= 0)
    )

    def scores_of():
        raw = jnp.einsum("thd,chd->htc", queries, keys_all, preferred_element_type=jnp.float32)
        return jnp.where(allowed[None], raw * score_scale, NEGATIVE)

    scores = scores_of()
    row_top = jnp.max(scores, axis=-1, keepdims=True)
    exp_scores = jnp.exp(scores - row_top)
    exp_total = jnp.sum(exp_scores, axis=-1, keepdims=True)
    soft_low = (exp_scores / exp_total).astype(jnp.bfloat16)
    log_total = row_top + jnp.log(exp_total)
    attended = jnp.einsum("htc,chd->thd", soft_low, values_all, preferred_element_type=jnp.float32)
    attended_low = attended.reshape(tok_rows, head_width).astype(jnp.bfloat16)
    attn_part = branch_scale * jnp.dot(attended_low, w_out, preferred_element_type=jnp.float32)
    hidden_one = inputs + lax.psum(attn_part, "head")
    rms_two = inverse_rms(hidden_one)
    normed_two = (hidden_one * rms_two * gain_two).astype(jnp.bfloat16)
    gate_pre = jnp.einsum("td,fd->tf", normed_two, w_gate, preferred_element_type=jnp.float32)
    up_pre = jnp.einsum("td,fd->tf", normed_two, w_up, preferred_element_type=jnp.float32)
    sigma = jax.nn.sigmoid(gate_pre)
    hidden_low = (gate_pre * sigma * up_pre).astype(jnp.bfloat16)
    ffn_part = jnp.dot(hidden_low, w_down, preferred_element_type=jnp.float32)
    ffn_share = lax.psum_scatter(ffn_part, "head", scatter_dimension=1, tiled=True)
    share_width = width // head_devices
    residual_share = lax.dynamic_slice_in_dim(hidden_one, head_place * share_width, share_width, 1)
    block_out = (residual_share + ffn_share).astype(jnp.bfloat16)
    grad_out_f = cotangent.astype(jnp.float32)
    hidden_grad = jnp.einsum("td,fd->tf", cotangent, w_down, preferred_element_type=jnp.float32)
    silu_grad = sigma * (1.0 + gate_pre * (1.0 - sigma))
    gate_grad = (hidden_grad * up_pre * silu_grad).astype(jnp.bfloat16)
    up_grad = (hidden_grad * gate_pre * sigma).astype(jnp.bfloat16)
    down_grad = jnp.einsum("tf,td->fd", hidden_low, cotangent, preferred_element_type=jnp.float32)
    gate_w_grad = jnp.einsum("tf,td->fd", gate_grad, normed_two, preferred_element_type=jnp.float32)
    up_w_grad = jnp.einsum("tf,td->fd", up_grad, normed_two, preferred_element_type=jnp.float32)
    ffn_rows_grad = jnp.concatenate([gate_w_grad, up_w_grad, down_grad], axis=0)
    ffn_owner = jnp.take(ffn_rows_grad.reshape(seq_devices, ffn_slab, width), inverse_ffn, axis=0)
    normed_two_part = jnp.einsum(
        "tf,fd->td", gate_grad, w_gate, preferred_element_type=jnp.float32
    ) + jnp.einsum("tf,fd->td", up_grad, w_up, preferred_element_type=jnp.float32)
    normed_two_share = lax.psum_scatter(normed_two_part, "head", scatter_dimension=1, tiled=True)
    normed_two_grad = lax.all_gather(normed_two_share, "head", axis=1, tiled=True)
    back_two, gain_two_grad = norm_back(normed_two_grad, hidden_one, rms_two, gain_two)
    hidden_one_grad = grad_out_f + back_two
    hidden_grad_low = hidden_one_grad.astype(jnp.bfloat16)
    attended_grad = branch_scale * jnp.einsum(
        "td,id->ti", hidden_grad_low, w_out, preferred_element_type=jnp.float32
    )
    attended_grad = attended_grad.reshape(head_shape).astype(jnp.bfloat16)
    soft_again = jnp.exp(scores_of() - log_total)
    soft_grad = jnp.einsum(
        "thd,chd->htc", attended_grad, values_all, preferred_element_type=jnp.float32
    )
    inner_sum = jnp.sum(soft_again * soft_grad, axis=-1, keepdims=True)
    score_grad = (soft_again * (soft_grad - inner_sum) * score_scale).astype(jnp.bfloat16)
    query_grad_turned = jnp.einsum(
        "htc,chd->thd", score_grad, keys_all, preferred_element_type=jnp.float32
    )
    key_grad_all = jnp.einsum(
        "htc,thd->chd", score_grad, queries, preferred_element_type=jnp.float32
    )
    value_grad_all = jnp.einsum(
        "htc,thd->chd", soft_low, attended_grad, preferred_element_type=jnp.float32
    )
    key_grad_own = key_grad_all[WINDOW:]
    value_grad_own = value_grad_all[WINDOW:]
    start_at = 0
    for hop_index in range(hop_total, 0, -1):
        hop_rows = hop_sizes[hop_index - 1]
        back_keys, back_values = passed_along(
            (
                key_grad_all[start_at : start_at + hop_rows],
                value_grad_all[start_at : start_at + hop_rows],
            ),
            "seq",
            -hop_index,
        )
        key_grad_own = key_grad_own.at[tok_rows - hop_rows :].add(back_keys)
        value_grad_own = value_grad_own.at[tok_rows - hop_rows :].add(back_values)
        start_at = start_at + hop_rows
    query_grad = (
        rotate(query_grad_turned, cosine, -sine).reshape(tok_rows, head_width).astype(jnp.bfloat16)
    )
    key_grad = (
        rotate(key_grad_own, cosine, -sine).reshape(tok_rows, head_width).astype(jnp.bfloat16)
    )
    value_grad = value_grad_own.reshape(tok_rows, head_width).astype(jnp.bfloat16)

    def input_part(row_grad, weight_rows):
        return jnp.einsum("ti,id->td", row_grad, weight_rows, preferred_element_type=jnp.float32)

    normed_one_part = (
        input_part(query_grad, w_query)
        + input_part(key_grad, w_key)
        + input_part(value_grad, w_value)
    )
    normed_one_share = lax.psum_scatter(normed_one_part, "head", scatter_dimension=1, tiled=True)
    normed_one_grad = lax.all_gather(
        normed_one_share.astype(jnp.bfloat16), "head", axis=1, tiled=True
    ).astype(normed_one_share.dtype)
    back_one, gain_one_grad = norm_back(normed_one_grad, inputs, rms_one, gain_one)
    input_grad = hidden_one_grad + back_one
    gain_grads = jnp.stack([gain_one_grad, gain_two_grad])

    def rows_grad(row_grad):
        return jnp.einsum("ti,td->id", row_grad, normed_one, preferred_element_type=jnp.float32)

    out_w_grad = branch_scale * jnp.einsum(
        "ti,td->id", attended_low, hidden_grad_low, preferred_element_type=jnp.float32
    )
    attn_rows_grad = jnp.concatenate(
        [rows_grad(query_grad), rows_grad(key_grad), rows_grad(value_grad), out_w_grad], axis=0
    )
    attn_owner = jnp.take(
        attn_rows_grad.reshape(seq_devices, attn_slab, width), inverse_attn, axis=0
    )
    owner_rows = jnp.concatenate([attn_owner, ffn_owner], axis=1).reshape(
        seq_devices * slab_rows, width
    )
    reduced, gain_reduced = (
        lax.psum_scatter(owner_rows, "seq", scatter_dimension=0, tiled=True),
        lax.psum_scatter(gain_grads, "seq", scatter_dimension=1, tiled=True),
    )
    attn_kinds = (
        inverse_attn[seq_place] * attn_slab + jnp.arange(attn_slab, dtype=jnp.int32)
    ) // head_width
    ffn_kinds = (
        4 + (inverse_ffn[seq_place] * ffn_slab + jnp.arange(ffn_slab, dtype=jnp.int32)) // ffn_width
    )
    row_rates = kind_rates(jnp.concatenate([attn_kinds, ffn_kinds]), width)[:, None]
    basis = eigenbases[0, 0]
    block_size = basis.shape[-1]
    split_shape = (slab_rows, width // block_size, block_size)
    turned = jnp.einsum(
        "rbk,bkl->rbl", reduced.reshape(split_shape), basis, precision=PRECISE
    ).reshape(slab_rows, width)
    first_new = BETA_FIRST * first_moment[0, 0] + (1.0 - BETA_FIRST) * turned
    second_new = BETA_SECOND * second_moment[0, 0] + (1.0 - BETA_SECOND) * turned * turned
    adam_dir = (
        first_new
        / (1.0 - BETA_FIRST**ADAM_STEP)
        / (jnp.sqrt(second_new / (1.0 - BETA_SECOND**ADAM_STEP)) + ADAM_EPS)
    )
    backward_dir = jnp.einsum(
        "rbl,bkl->rbk", adam_dir.reshape(split_shape), basis, precision=PRECISE
    ).reshape(slab_rows, width)
    master_old = master[0, 0]
    master_new = master_old - row_rates * (backward_dir + DECAY_RATE * master_old)
    gain_first_new = BETA_FIRST * gain_first + (1.0 - BETA_FIRST) * gain_reduced
    gain_second_new = BETA_SECOND * gain_second + (1.0 - BETA_SECOND) * gain_reduced * gain_reduced
    gain_new = norm_gains - GAIN_RATE * (gain_first_new / (1.0 - BETA_FIRST**ADAM_STEP)) / (
        jnp.sqrt(gain_second_new / (1.0 - BETA_SECOND**ADAM_STEP)) + ADAM_EPS
    )
    return (
        block_out,
        input_grad,
        reduced[None, None],
        first_new[None, None],
        second_new[None, None],
        master_new[None, None],
        master_new.astype(jnp.bfloat16)[None, None],
        gain_reduced,
        gain_first_new,
        gain_second_new,
        gain_new,
    )


SLAB = 516
PAD = 528
HALF = 1024
QUART = 512
UNITS = 1376
NT = (((1,), (1,)), ((), ()))
TN = (((0,), (0,)), ((), ()))


VM = pl.BlockSpec(memory_space=pltpu.VMEM)
SM = pl.BlockSpec(memory_space=pltpu.SMEM)
HB = pl.BlockSpec(memory_space=pl.ANY)


def shape(rows, columns, dtype=BF16):
    return jax.ShapeDtypeStruct((rows, columns), dtype)


def call(kernel, outs, specs, args, scratch=(), flops=0, moved=0, out_specs=None, grid=None):
    extra = {} if grid is None else {"grid": grid}
    return pl.pallas_call(
        kernel,
        out_shape=outs,
        in_specs=specs,
        out_specs=[VM] * len(outs) if out_specs is None else out_specs,
        scratch_shapes=list(scratch),
        compiler_params=pltpu.CompilerParams(vmem_limit_bytes=56 * 2**20),
        cost_estimate=pl.CostEstimate(flops=flops, bytes_accessed=moved, transcendentals=0),
        name=getattr(kernel, "func", kernel).__name__,
        **extra,
    )(*args)


def root_of(values):
    return lax.rsqrt(jnp.mean(values * values, axis=-1, keepdims=True) + EPS_NORM)


def turn(values, cosine, sine):
    parts = []
    for h in range(values.shape[1] // HEAD_DIM):
        v = values[:, h * HEAD_DIM : (h + 1) * HEAD_DIM]
        parts.append(v * cosine + pltpu.roll(v, HEAD_DIM // 2, 1) * sine)
    return parts


MESH = pl.DeviceIdType.MESH


def flip(index, mask):
    for bit in (1, 2, 4):
        if mask & bit:
            index = index + bit - 2 * bit * lax.rem(lax.div(index, bit), 2)
    return index


def twist(left, right):
    out = 0
    for bit in (1, 2, 4):
        out = out + bit * lax.rem(lax.rem(lax.div(left, bit), 2) + lax.rem(lax.div(right, bit), 2), 2)
    return out


def slab_of(owners, kind, device):
    found = 0
    for j in range(8):
        found = jnp.where(owners[kind, j] == device, j, found)
    return found


class Plane:
    def __init__(self, at, sent, got, me, line):
        self.at, self.sent, self.got, self.me, self.line = at, sent, got, me, line

    def copy(self, src, dst, side, hop_mask):
        return pltpu.make_async_remote_copy(
            src_ref=self.at(src, side),
            dst_ref=self.at(dst, side),
            send_sem=self.sent.at[dst, side],
            recv_sem=self.got.at[dst, side],
            device_id=(flip(self.me, hop_mask), self.line),
            device_id_type=MESH,
        )

    def start_first(self):
        for mask, side in ((2, 0), (4, 1)):
            self.copy(0, mask, side, mask).start()
        for side in (0, 1):
            self.copy(0, 1, side, 1).start()

    def start_second(self):
        for mask, side in ((2, 1), (4, 0)):
            self.copy(0, mask, side, mask).start()

    def start(self):
        self.start_first()
        self.start_second()

    def arrive(self, mask, side):
        self.copy(mask, mask, side, 1).wait_recv()

    def twin(self, mask, side):
        self.copy(mask, mask + 1, side, 1).start()

    def relay_first(self):
        for mask, side in ((2, 0), (4, 1)):
            self.arrive(mask, side)
            self.copy(mask, 6, side, 6 - mask).start()
            self.twin(mask, side)

    def relay_second(self):
        for mask, side in ((2, 1), (4, 0)):
            self.arrive(mask, side)
            self.twin(mask, side)

    def relay_last(self):
        for side in (0, 1):
            self.arrive(6, side)
            self.twin(6, side)

    def finish(self):
        for mask in (1, 3, 5, 7):
            for side in (0, 1):
                self.arrive(mask, side)

    def drain(self, masks=range(1, 8)):
        for mask in masks:
            for side in (0, 1):
                self.copy(0, mask, side, 1).wait_send()


def line_copy(src, dst, sent, got, m, me, line):
    return pltpu.make_async_remote_copy(
        src_ref=src,
        dst_ref=dst,
        send_sem=sent.at[m],
        recv_sem=got.at[m],
        device_id=(me, flip(line, m)),
        device_id_type=MESH,
    )


def greet(me, line, plane_masks, line_masks):
    barrier = pltpu.get_barrier_semaphore()
    for mask in plane_masks:
        pl.semaphore_signal(barrier, inc=1, device_id=(flip(me, mask), line), device_id_type=MESH)
    for mask in line_masks:
        pl.semaphore_signal(barrier, inc=1, device_id=(me, flip(line, mask)), device_id_type=MESH)
    return lambda: pl.semaphore_wait(barrier, len(plane_masks) + len(line_masks))


def front_kernel(
    rows, scale, branch,
    owners, tokens, dy, own_gains, speeds, master,
    gains, o_low, o_wide, stats, n_own, n_parts, b_own, b_parts,
    a_out, h_keep, k_out, v_out, q_out, w_out, z_keep, dy_all, b_all,
    a_low, h_out, kcat, vcat, q_low, sent, b_low, wide, w_a, w_f, made, cut, total, z_out, z_in, z_sum, work, dy_own,
    sem_w, sem_o, a_sent, a_got, f_sent, f_got, k_sent, k_got, b_sent, b_got, y_sent, y_got, z_sems, r_up, r_down, r_got,
    t_sent, t_got,
):
    me, line = lax.axis_index("seq"), lax.axis_index("head")
    ready = greet(me, line, (1, 2, 4), (1, 2, 3))
    order_a, order_f = ([twist(owners[kind, j], me) for j in range(8)] for kind in (0, 1))
    keeps = [
        pltpu.make_async_copy(src, dst, sem_o.at[i])
        for i, (src, dst) in enumerate(
            (
                (w_a, w_out), (a_low, a_out), (kcat, k_out), (vcat, v_out), (q_low, q_out),
                (h_out, h_keep), (b_low, b_all.at[0]), (sent, z_keep), (dy_own, dy_all.at[line, 0]),
            )
        )
    ]
    y_plane = Plane(
        lambda m, s: dy_own.at[s] if m == 0 else dy_all.at[line, m, s], y_sent, y_got, me, line
    )

    def along_line(quarter_index, m, up):
        return pltpu.make_async_remote_copy(
            src_ref=dy_all.at[quarter_index, m],
            dst_ref=dy_all.at[quarter_index, m],
            send_sem=(r_up if up else r_down).at[quarter_index, m],
            recv_sem=r_got.at[quarter_index, m],
            device_id=(me, line + 1 if up else line - 1),
            device_id_type=MESH,
        )

    def twin_quarter(quarter_index, m):
        return pltpu.make_async_remote_copy(
            src_ref=dy_all.at[quarter_index, m],
            dst_ref=dy_all.at[quarter_index, m + 1],
            send_sem=t_sent.at[quarter_index, m],
            recv_sem=t_got.at[quarter_index, m],
            device_id=(flip(me, 1), line),
            device_id_type=MESH,
        )

    def line_round(step):
        if step == 0:
            for up, last in ((True, 3), (False, 0)):

                @pl.when(line != last)
                def _():
                    for m in (0, 2, 4, 6):
                        along_line(line, m, up).start()

            return
        for up, first, last in ((True, step, 3), (False, 3 - step, 0)):
            index = line - step if up else line + step

            @pl.when(line >= first if up else line <= first)
            def _():
                for m in (0, 2, 4, 6):
                    along_line(index, m, up).wait_recv()

                @pl.when(line != last)
                def _():
                    for m in (0, 2, 4, 6):
                        along_line(index, m, up).start()

                for m in (0, 2, 4, 6):
                    twin_quarter(index, m).start()

    def line_end():
        for apart in (1, 2, 3):
            for up in (True, False):
                index = line - apart if up else line + apart

                @pl.when(line >= apart if up else line <= 3 - apart)
                def _():
                    for m in (0, 2, 4, 6):
                        twin_quarter(index, m).wait_recv()
                        twin_quarter(index, m).wait_send()

        for step in range(3):
            for up in (True, False):
                index = line - step if up else line + step

                @pl.when((line >= step) & (line != 3) if up else (line <= 3 - step) & (line != 0))
                def _():
                    for m in (0, 2, 4, 6):
                        along_line(index, m, up).wait_send()

    w_a_plane = Plane(lambda m, s: w_a.at[m, s], a_sent, a_got, me, line)
    w_f_plane = Plane(lambda m, s: w_f.at[m, s], f_sent, f_got, me, line)
    kv_plane = Plane(lambda m, s: (kcat, vcat)[s].at[pl.ds(m * rows, rows)], k_sent, k_got, me, line)
    b_plane = Plane(lambda m, s: b_low.at[s] if m == 0 else b_all.at[m, s], b_sent, b_got, me, line)

    load = pltpu.make_async_copy(master.at[pl.ds(0, 256), 0, :], wide.at[pl.ds(0, 256)], sem_w.at[0])
    load.start()
    for side in (0, 1):
        at = pl.multiple_of(line * QUART + side * 256, 256)
        dy_own[side] = dy[:, pl.ds(at, 256)]
    keeps[8].start()
    w_a[0, 0, pl.ds(256, 16), :] = jnp.zeros((16, HALF), BF16)
    w_a[0, 1, pl.ds(256, 16), :] = jnp.zeros((16, HALF), BF16)
    w_a[0, 1, 256:258, 0:256] = own_gains[...].astype(BF16)
    load.wait()
    for side in (0, 1):
        w_a[0, side, pl.ds(0, 256), :] = wide[pl.ds(0, 256), side * HALF : (side + 1) * HALF].astype(BF16)
    load = pltpu.make_async_copy(master.at[pl.ds(256, SLAB), 0, :], wide, sem_w.at[1])
    load.start()
    ready()
    w_a_plane.start()
    y_plane.start()
    load.wait()
    for side in (0, 1):
        columns = slice(side * HALF, (side + 1) * HALF)
        w_f[0, side, pl.ds(0, 512), :] = wide[pl.ds(0, 512), columns].astype(BF16)
        last = jnp.concatenate([wide[512:SLAB, columns], jnp.zeros((PAD - SLAB, HALF), F32)], axis=0)
        w_f[0, side, pl.ds(512, 16), :] = last.astype(BF16)
    angle = (me * rows + lax.broadcasted_iota(jnp.int32, (rows, 1), 0)).astype(F32) * speeds[...]
    cosine, sine = jnp.cos(angle), jnp.sin(angle)
    sine = jnp.where(lax.broadcasted_iota(jnp.int32, (1, HEAD_DIM), 1) < HEAD_DIM // 2, -sine, sine)
    w_a_plane.relay_first()
    w_a_plane.relay_second()
    y_plane.relay_first()
    y_plane.relay_second()
    keeps[8].wait()
    w_a_plane.relay_last()
    w_f_plane.start_first()
    y_plane.relay_last()
    line_round(0)
    w_a_plane.finish()
    keeps[0].start()

    for m in range(8):
        at = pl.multiple_of(flip(me, m) * 256, 256)
        gains[:, pl.ds(at, 256)] = w_a[m, 1, 256:258, 0:256].astype(F32)
    x = tokens[...].astype(F32)
    normed = (x * root_of(x) * gains[0:1, :]).astype(BF16)
    for side in (0, 1):
        a_low[side] = normed[:, side * HALF : (side + 1) * HALF]
    for j in (2, 3, 4, 5, 0, 1):
        out = lax.dot_general(a_low[0], w_a[order_a[j], 0, pl.ds(0, 256), :], NT, preferred_element_type=F32)
        out += lax.dot_general(a_low[1], w_a[order_a[j], 1, pl.ds(0, 256), :], NT, preferred_element_type=F32)
        if j < 4:
            parts = turn(out, cosine, sine)
        else:
            parts = [out[:, :HEAD_DIM], out[:, HEAD_DIM:]]
        for i, part in enumerate(parts):
            if j < 2:
                q_low[j, :, i * HEAD_DIM : (i + 1) * HEAD_DIM] = part.astype(BF16)
            else:
                at = (2 * (j % 2) + i) * HEAD_DIM
                (kcat, vcat)[j // 2 - 1][pl.ds(0, rows), at : at + HEAD_DIM] = part.astype(BF16)
        if j == 5:
            kv_plane.start()
    keeps[1].start()
    keeps[4].start()
    line_round(1)
    kv_plane.relay_first()
    kv_plane.relay_second()
    w_f_plane.relay_first()
    w_f_plane.start_second()
    kv_plane.relay_last()
    kv_plane.finish()
    keeps[2].start()
    keeps[3].start()

    at_q = me * rows + lax.broadcasted_iota(jnp.int32, (rows, 1), 0)
    along = lax.broadcasted_iota(jnp.int32, (1, rows), 1)
    lane = lax.broadcasted_iota(jnp.int32, (rows, HEAD_DIM), 1)
    stat = jnp.zeros((rows, HEAD_DIM), F32)
    for h in range(4):
        if h == 2:
            line_round(2)
        columns = slice(h * HEAD_DIM, (h + 1) * HEAD_DIM)
        q = q_low[h // 2, :, (h % 2) * HEAD_DIM : (h % 2 + 1) * HEAD_DIM]
        top = jnp.full((rows, 1), NEGATIVE, F32)
        for m in range(8):
            ahead = at_q - (flip(me, m) * rows + along)
            s = lax.dot_general(q, kcat[pl.ds(m * rows, rows), columns], NT, preferred_element_type=F32)
            s = jnp.where((ahead >= 0) & (ahead < WINDOW), s * scale, NEGATIVE)
            work[m] = s
            top = jnp.maximum(top, jnp.max(s, axis=-1, keepdims=True))
        sums = jnp.zeros((rows, 1), F32)
        for m in range(8):
            e = jnp.exp(work[m] - top)
            work[m] = e
            sums += jnp.sum(e, axis=-1, keepdims=True)
        share = 1.0 / sums
        o = jnp.zeros((rows, HEAD_DIM), F32)
        for m in range(8):
            soft = (work[m] * share).astype(BF16)
            o += jnp.dot(soft, vcat[pl.ds(m * rows, rows), columns], preferred_element_type=F32)
        o_wide[:, columns] = o
        o_low[:, columns] = o.astype(BF16)
        stat = jnp.where(lane == h, top + jnp.log(sums), stat)
    stats[...] = stat
    for side in (0, 1):
        out = jnp.dot(o_low[:, :256], w_a[order_a[6], side, pl.ds(0, 256), :], preferred_element_type=F32)
        out += jnp.dot(o_low[:, 256:], w_a[order_a[7], side, pl.ds(0, 256), :], preferred_element_type=F32)
        total[:, side * HALF : (side + 1) * HALF] = branch * out

    def quarter(m):
        return pl.ds(pl.multiple_of(flip(line, m) * QUART, QUART), QUART)

    def piece(m):
        return line_copy(z_out.at[m], z_in.at[m], z_sems.at[0], z_sems.at[1], m, me, line)

    def whole(m):
        return line_copy(z_sum.at[0], z_sum.at[m], z_sems.at[2], z_sems.at[3], m, me, line)

    for m in (3, 2, 1):
        z_out[m] = total[:, quarter(m)].astype(BF16)
        piece(m).start()
    for m in (1, 2, 3):
        piece(m).wait_recv()
    summed = total[:, quarter(0)]
    for m in (1, 2, 3):
        summed += z_in[m].astype(F32)
    z_sum[0] = summed.astype(BF16)
    for m in (3, 2, 1):
        whole(m).start()
    w_f_plane.relay_last()
    for m in (1, 2, 3):
        whole(m).wait_recv()

    for m in range(4):
        h_out[:, quarter(m)] = z_sum[m].astype(F32)
    h = h_out[...] + tokens[...].astype(F32)
    h_out[...] = h
    normed = (h * root_of(h) * gains[1:2, :]).astype(BF16)
    for side in (0, 1):
        b_low[side] = normed[:, side * HALF : (side + 1) * HALF]
    keeps[5].start()
    keeps[6].start()
    b_plane.start()
    w_f_plane.relay_second()
    w_f_plane.finish()

    def through(j, left, right):
        out = lax.dot_general(w_f[order_f[j], 0], left, NT, preferred_element_type=F32)
        return out + lax.dot_general(w_f[order_f[j], 1], right, NT, preferred_element_type=F32)

    made[pl.ds(8 * SLAB, 16), :] = jnp.zeros((16, rows), F32)
    row = lax.broadcasted_iota(jnp.int32, (PAD, 1), 0)
    gate_rows = row < 2 * UNITS - 5 * SLAB
    for j in range(8):
        if j < 5:
            out = through(j, b_low[0], b_low[1])
        elif j > 5:
            out = through(j, dy[:, :HALF], dy[:, HALF:])
        else:
            out = jnp.where(gate_rows, through(j, b_low[0], b_low[1]), through(j, dy[:, :HALF], dy[:, HALF:]))
        made[pl.ds(j * SLAB, PAD), :] = out

    def mix(i, _):
        at = pl.multiple_of(i * 32, 8)
        gate = made[pl.ds(at, 32), :]
        up = made[pl.ds(UNITS + at, 32), :]
        back = made[pl.ds(2 * UNITS + at, 32), :]
        sigma = 1.0 / (1.0 + jnp.exp(-gate))
        silu = gate * sigma
        made[pl.ds(at, 32), :] = back * up * (sigma * (1.0 + gate * (1.0 - sigma)))
        made[pl.ds(UNITS + at, 32), :] = back * silu
        made[pl.ds(2 * UNITS + at, 32), :] = silu * up
        return 0

    lax.fori_loop(0, UNITS // 32, mix, 0)
    for j in range(8):
        cut[j] = made[pl.ds(j * SLAB, PAD), :].astype(BF16)
    for m in range(8):
        sent[m] = cut[slab_of(owners, 1, flip(me, m))]
    keeps[7].start()
    for own, parts, kinds in ((n_own, n_parts, range(0, 6)), (b_own, b_parts, range(5, 8))):
        for side in (0, 1):
            columns = slice(side * HALF, (side + 1) * HALF)
            for j in kinds:
                z = cut[j]
                if j == 5:
                    z = jnp.where(gate_rows if parts is n_parts else ~gate_rows, z, jnp.zeros_like(z))
                out = lax.dot_general(z, w_f[order_f[j], side], TN, preferred_element_type=F32)
                total[:, columns] = out if j == kinds[0] else total[:, columns] + out
        own[...] = total[:, quarter(0)]
        for m in (1, 2, 3):
            parts[m - 1] = total[:, quarter(m)].astype(BF16)

    line_round(3)
    y_plane.finish()
    line_end()
    for mask in (2, 4, 1):
        for side in (0, 1):
            b_plane.arrive(mask, side)
    b_plane.drain((1, 2, 4))
    for plane in (y_plane, w_a_plane, w_f_plane, kv_plane):
        plane.drain()
    for m in (1, 2, 3):
        piece(m).wait_send()
        whole(m).wait_send()
    for keep in keeps[:8]:
        keep.wait()


def front(owners, tokens, dy, own_gains, speeds, master, scale, branch):
    rows = tokens.shape[0]
    array = jax.ShapeDtypeStruct
    kept = [
        array((2, rows, HALF), BF16),
        array((rows, 2 * HALF), F32),
        array((8 * rows, QUART), BF16),
        array((8 * rows, QUART), BF16),
        array((2, rows, 256), BF16),
        array((8, PAD, rows), BF16),
    ]
    outs = [
        array((2, 2 * HALF), F32),
        array((rows, QUART), BF16),
        array((rows, QUART), F32),
        array((rows, HEAD_DIM), F32),
        array((rows, QUART), F32),
        array((3, rows, QUART), BF16),
        array((rows, QUART), F32),
        array((3, rows, QUART), BF16),
        *kept[:5],
        array((8, 2, 272, HALF), BF16),
        kept[5],
        array((4, 8, 2, rows, 256), BF16),
        array((8, 2, rows, HALF), BF16),
    ]
    dma = pltpu.SemaphoreType.DMA
    return pl.pallas_call(
        functools.partial(front_kernel, rows, scale, branch),
        out_shape=outs,
        in_specs=[SM] + [VM] * 4 + [HB],
        out_specs=[VM] * 8 + [HB] * 9,
        scratch_shapes=[pltpu.VMEM(k.shape, k.dtype) for k in kept]
        + [
            pltpu.VMEM((2, rows, HALF), BF16),
            pltpu.VMEM((SLAB, 2 * HALF), F32),
            pltpu.VMEM((8, 2, 272, HALF), BF16),
            pltpu.VMEM((8, 2, PAD, HALF), BF16),
            pltpu.VMEM((8 * SLAB + 16, rows), F32),
            pltpu.VMEM((8, PAD, rows), BF16),
            pltpu.VMEM((rows, 2 * HALF), F32),
            pltpu.VMEM((4, rows, QUART), BF16),
            pltpu.VMEM((4, rows, QUART), BF16),
            pltpu.VMEM((4, rows, QUART), BF16),
            pltpu.VMEM((8, rows, rows), F32),
            pltpu.VMEM((2, rows, 256), BF16),
            dma((2,)),
            dma((9,)),
        ]
        + [dma((8, 2))] * 10
        + [dma((4, 4))]
        + [dma((4, 8))] * 5,
        compiler_params=pltpu.CompilerParams(
            collective_id=0, has_side_effects=True, vmem_limit_bytes=62 * 2**20
        ),
        cost_estimate=pl.CostEstimate(flops=10**10, bytes_accessed=30 * 2**20, transcendentals=0),
        name="front",
    )(owners, tokens, dy, own_gains, speeds, master)


def back_kernel(
    rows, scale, branch,
    owners, tokens, dy, gains, speeds, o_low, o_wide, stats, n_own, n_parts, b_own, b_parts,
    h_in, q_in, k_in, v_in, w_in, a_low, z_own, b_in_place,
    block_out, input_grad, gain_grad, acts, z_all, g_all, b_all,
    h_got, w_a, qcat, kcat, vcat, docat, d_one, d_low, dq, dk, dv, groups, sent, total, stat_l, stat_r,
    z_in, z_sum, b_in, gain_out, gain_in,
    load_sems, keep_sems, n_sems, p_sems, b_sems, act_sent, act_got, do_sent, do_got, q_sent, q_got, a2a_sems,
):
    me, line = lax.axis_index("seq"), lax.axis_index("head")
    ready = greet(me, line, range(1, 8), (1, 2, 3))
    loads = [
        pltpu.make_async_copy(src, dst, load_sems.at[i])
        for i, (src, dst) in enumerate(((w_in, w_a), (q_in, qcat.at[0]), (k_in, kcat), (v_in, vcat), (h_in, h_got)))
    ]
    order_a = [twist(owners[0, j], me) for j in range(8)]
    for load in loads:
        load.start()
    keeps = [
        pltpu.make_async_copy(src, dst, keep_sems.at[i])
        for i, (src, dst) in enumerate(
            (
                (a_low, acts.at[0, 0]), (d_low, acts.at[1, 0]),
                (z_own.at[0], z_all.at[0]), (sent.at[0], g_all.at[0]),
            )
        )
    ]
    def act_plane(kind):
        def at(m, s):
            if kind == 2:
                return b_all.at[m, s]
            return (a_low, d_low)[kind].at[s] if m == 0 else acts.at[kind, m, s]

        return Plane(at, act_sent.at[kind], act_got.at[kind], me, line)

    a_plane, d_plane, b_plane = (act_plane(kind) for kind in range(3))
    q_plane = Plane(lambda m, s: qcat.at[m, s], q_sent, q_got, me, line)
    do_plane = Plane(lambda m, s: docat.at[m, s], do_sent, do_got, me, line)

    def straight(src, dst, which, m):
        return pltpu.make_async_remote_copy(
            src_ref=src.at[m],
            dst_ref=dst.at[m],
            send_sem=a2a_sems.at[which, 0, m],
            recv_sem=a2a_sems.at[which, 1, m],
            device_id=(flip(me, m), line),
            device_id_type=MESH,
        )

    def quarter(m):
        return pl.ds(pl.multiple_of(flip(line, m) * QUART, QUART), QUART)

    def n_piece(m):
        return line_copy(n_parts.at[m - 1], z_in.at[0, m], n_sems.at[0], n_sems.at[1], m, me, line)

    def p_piece(m):
        return line_copy(z_sum.at[1, m], z_in.at[1, m], p_sems.at[0], p_sems.at[1], m, me, line)

    def b_piece(m):
        return line_copy(b_parts.at[m - 1], b_in.at[m], b_sems.at[0], b_sems.at[1], m, me, line)

    def n_whole(m):
        return line_copy(z_sum.at[0, 0], z_sum.at[0, m], n_sems.at[2], n_sems.at[3], m, me, line)

    def p_whole(m):
        return line_copy(z_sum.at[2, 0], z_sum.at[2, m], p_sems.at[2], p_sems.at[3], m, me, line)

    ready()
    for m in (3, 2, 1):
        n_piece(m).start()
    for mask, side in ((2, 0), (4, 1)):
        b_plane.copy(mask, 6, side, 6 - mask).start()
    loads[1].wait()
    q_plane.start()
    for m in range(1, 8):
        straight(z_own, z_all, 0, m).start()
    for mask in (2, 4):
        for side in (0, 1):
            b_plane.twin(mask, side)
    keeps[0].start()
    keeps[2].start()
    q_plane.relay_first()
    q_plane.relay_second()
    for m in (1, 2, 3):
        n_piece(m).wait_recv()
    summed = n_own[...]
    for m in (1, 2, 3):
        summed += z_in[0, m].astype(F32)
    z_sum[0, 0] = summed.astype(BF16)
    for m in (3, 2, 1):
        n_whole(m).start()
    b_plane.relay_last()
    q_plane.relay_last()
    for m in (1, 2, 3):
        n_whole(m).wait_recv()
    for m in (3, 2, 1):
        b_piece(m).start()

    for m in range(4):
        total[:, quarter(m)] = z_sum[0, m].astype(F32)
    normed_grad = total[...]
    loads[4].wait()
    h = h_got[...]
    root = root_of(h)
    gain_two = jnp.sum(normed_grad * h * root, axis=0, keepdims=True)
    weighted = normed_grad * gains[1:2, :]
    inner = jnp.mean(weighted * h, axis=-1, keepdims=True)
    grad = dy[...].astype(F32) + root * weighted - h * (root * root * root) * inner
    d_one[...] = grad
    low = grad.astype(BF16)
    for side in (0, 1):
        d_low[side] = low[:, side * HALF : (side + 1) * HALF]
    keeps[1].start()
    total[0:1, :] = gain_two
    for m in range(8):
        at = pl.multiple_of(flip(me, m) * 256, 256)
        gain_out[m, 1:2, :] = total[0:1, pl.ds(at, 256)]
    loads[0].wait()
    lane = lax.broadcasted_iota(jnp.int32, (rows, HEAD_DIM), 1)
    own_lines = []
    for j, stat in enumerate((stat_l, stat_r)):
        out = lax.dot_general(d_low[0], w_a[order_a[6 + j], 0, pl.ds(0, 256), :], NT, preferred_element_type=F32)
        out += lax.dot_general(d_low[1], w_a[order_a[6 + j], 1, pl.ds(0, 256), :], NT, preferred_element_type=F32)
        out = (branch * out).astype(BF16)
        docat[0, j, pl.ds(0, rows), :] = out
        lines = jnp.zeros((rows, HEAD_DIM), F32)
        columns = []
        for i in (0, 1):
            h_at = 2 * j + i
            cut = slice(h_at * HEAD_DIM, (h_at + 1) * HEAD_DIM)
            delta = jnp.sum(
                out[:, i * HEAD_DIM : (i + 1) * HEAD_DIM].astype(F32) * o_wide[:, cut], axis=-1, keepdims=True
            )
            top = stats[:, h_at : h_at + 1]
            columns.append((top, delta))
            for at, value in ((i, top), (2 + i, delta)):
                for step in range(3):
                    part = value.astype(BF16).astype(F32)
                    value = value - part
                    lines = jnp.where(lane == 4 * step + at, part, lines)
        own_lines.append(columns)
        stat[pl.ds(0, rows), :] = lines
        stat[pl.ds(rows, 256 - rows), :] = jnp.zeros((256 - rows, HEAD_DIM), F32)
        docat[0, j, pl.ds(rows, 16), :] = stat[...].T[:16, :].astype(BF16)
    do_plane.start()

    for load in loads[2:4]:
        load.wait()
    angle = (me * rows + lax.broadcasted_iota(jnp.int32, (rows, 1), 0)).astype(F32) * speeds[...]
    cosine, sine = jnp.cos(angle), jnp.sin(angle)
    sine = jnp.where(lax.broadcasted_iota(jnp.int32, (1, HEAD_DIM), 1) < HEAD_DIM // 2, sine, -sine)
    dq[...] = jnp.zeros_like(dq)
    dk[...] = jnp.zeros_like(dk)
    dv[...] = jnp.zeros_like(dv)
    reach = -(-WINDOW // rows)
    down = lax.broadcasted_iota(jnp.int32, (rows, rows), 0)
    along = lax.broadcasted_iota(jnp.int32, (rows, rows), 1)

    def head_cut(h):
        return h // 2, slice((h % 2) * HEAD_DIM, (h % 2 + 1) * HEAD_DIM), slice(h * HEAD_DIM, (h + 1) * HEAD_DIM)

    def rows_of(m):
        return pl.ds(m * rows, rows)

    def query_side(m):
        apart = me - flip(me, m)

        @pl.when((apart >= 0) & (apart <= reach))
        def _():
            ahead = apart * rows + down - along
            allowed = (ahead >= 0) & (ahead < WINDOW)
            for h in range(4):
                side, two, cut = head_cut(h)
                top, delta = own_lines[side][h % 2]
                k, do = kcat[rows_of(m), cut], docat[0, side, pl.ds(0, rows), two]
                s = lax.dot_general(qcat[0, side, :, two], k, NT, preferred_element_type=F32)
                p = jnp.where(allowed, jnp.exp(s * scale - top), 0.0)
                dp = lax.dot_general(do, vcat[rows_of(m), cut], NT, preferred_element_type=F32)
                ds = (p * (dp - delta) * scale).astype(BF16)
                dq[:, cut] += jnp.dot(ds, k, preferred_element_type=F32)

    def key_side(m):
        apart = me - flip(me, m)

        @pl.when((apart <= 0) & (apart >= -reach))
        def _():
            ahead = along - down - apart * rows
            allowed = (ahead >= 0) & (ahead < WINDOW)
            for h in range(4):
                side, two, cut = head_cut(h)
                lines = docat[m, side, pl.ds(rows, 16), :].astype(F32)
                lines = (lines[0:4] + lines[4:8] + lines[8:12])[:, :rows]
                top, delta = lines[h % 2 : h % 2 + 1], lines[2 + h % 2 : 3 + h % 2]
                q, do = qcat[m, side, :, two], docat[m, side, pl.ds(0, rows), two]
                s = lax.dot_general(kcat[pl.ds(0, rows), cut], q, NT, preferred_element_type=F32)
                p = jnp.where(allowed, jnp.exp(s * scale - top), 0.0)
                dv[:, cut] += jnp.dot(p.astype(BF16), do, preferred_element_type=F32)
                dp = lax.dot_general(vcat[pl.ds(0, rows), cut], do, NT, preferred_element_type=F32)
                ds = (p * (dp - delta) * scale).astype(BF16)
                dk[:, cut] += jnp.dot(ds, q, preferred_element_type=F32)

    for m in range(4):
        query_side(m)
    do_plane.relay_first()
    for m in range(4, 8):
        query_side(m)
    do_plane.relay_second()
    do_plane.relay_last()
    d_plane.start()
    a_plane.start()
    do_plane.finish()
    q_plane.finish()
    for m in range(8):
        key_side(m)
    for j in range(8):
        cut = slice((j % 2) * 256, (j % 2 + 1) * 256)
        if j < 4:
            made = turn((dq, dk)[j // 2][:, cut], cosine, sine)
            for i in (0, 1):
                groups[j, :, i * HEAD_DIM : (i + 1) * HEAD_DIM] = made[i].astype(BF16)
        elif j < 6:
            groups[j] = dv[:, cut].astype(BF16)
        else:
            groups[j] = o_low[:, cut]
    for j in range(6):
        for side in (0, 1):
            out = jnp.dot(groups[j], w_a[order_a[j], side, pl.ds(0, 256), :], preferred_element_type=F32)
            columns = slice(side * HALF, (side + 1) * HALF)
            total[:, columns] = out if j == 0 else total[:, columns] + out
    for m in (3, 2, 1):
        z_sum[1, m] = total[:, quarter(m)].astype(BF16)
        p_piece(m).start()
    for m in range(8):
        sent[m] = groups[slab_of(owners, 0, flip(me, m))]
    keeps[3].start()
    for m in range(1, 8):
        straight(sent, g_all, 1, m).start()
    for m in (1, 2, 3):
        p_piece(m).wait_recv()
    summed = total[:, quarter(0)]
    for m in (1, 2, 3):
        summed += z_in[1, m].astype(F32)
    z_sum[2, 0] = summed.astype(BF16)
    for m in (3, 2, 1):
        p_whole(m).start()
    d_plane.relay_first()
    a_plane.relay_first()
    for m in (1, 2, 3):
        b_piece(m).wait_recv()
    out = h_got[:, quarter(0)] + b_own[...]
    for m in (1, 2, 3):
        out += b_in[m].astype(F32)
    block_out[...] = out.astype(BF16)

    for m in (1, 2, 3):
        p_whole(m).wait_recv()
    for m in range(4):
        total[:, quarter(m)] = z_sum[2, m].astype(F32)
    normed_grad = total[...]
    x = tokens[...].astype(F32)
    root = root_of(x)
    gain_one = jnp.sum(normed_grad * x * root, axis=0, keepdims=True)
    weighted = normed_grad * gains[0:1, :]
    inner = jnp.mean(weighted * x, axis=-1, keepdims=True)
    input_grad[...] = d_one[...] + root * weighted - x * (root * root * root) * inner
    total[0:1, :] = gain_one
    for m in range(8):
        at = pl.multiple_of(flip(me, m) * 256, 256)
        gain_out[m, 0:1, :] = total[0:1, pl.ds(at, 256)]
    for m in range(1, 8):
        straight(gain_out, gain_in, 2, m).start()
    for plane in (d_plane, a_plane):
        plane.relay_second()
        plane.relay_last()
    for m in range(1, 8):
        straight(gain_out, gain_in, 2, m).wait_recv()
    made = gain_out[0, 0:2, :]
    for m in range(1, 8):
        made += gain_in[m, 0:2, :]
    gain_grad[...] = made
    for plane in (d_plane, a_plane):
        plane.finish()
    for mask in (3, 5, 7):
        for side in (0, 1):
            b_plane.arrive(mask, side)
    for m in range(1, 8):
        straight(z_own, z_all, 0, m).wait_recv()
        straight(sent, g_all, 1, m).wait_recv()
    b_plane.drain((3, 5, 6, 7))
    for plane in (d_plane, a_plane, do_plane, q_plane):
        plane.drain()
    for m in range(1, 8):
        straight(z_own, z_all, 0, m).wait_send()
        straight(sent, g_all, 1, m).wait_send()
        straight(gain_out, gain_in, 2, m).wait_send()
    for m in (1, 2, 3):
        for copy in (n_piece(m), n_whole(m), p_piece(m), p_whole(m), b_piece(m)):
            copy.wait_send()
    for keep in keeps:
        keep.wait()


def back(small, arrays, big, rows, scale, branch):
    array = jax.ShapeDtypeStruct
    dma = pltpu.SemaphoreType.DMA
    return pl.pallas_call(
        functools.partial(back_kernel, rows, scale, branch),
        out_shape=[
            shape(rows, QUART), shape(rows, 2 * HALF, F32), array((2, 256), F32),
            array((2, 8, 2, rows, HALF), BF16), array((8, PAD, rows), BF16), array((8, rows, 256), BF16),
            array((8, 2, rows, HALF), BF16),
        ],
        in_specs=[SM] * len(small) + [VM] * len(arrays) + [HB] * len(big),
        out_specs=[VM] * 3 + [HB] * 4,
        input_output_aliases={len(small) + len(arrays) + len(big) - 1: 6},
        scratch_shapes=[
            pltpu.VMEM((rows, 2 * HALF), F32),
            pltpu.VMEM((8, 2, 272, HALF), BF16),
            pltpu.VMEM((8, 2, rows, 256), BF16),
            pltpu.VMEM((8 * rows, QUART), BF16),
            pltpu.VMEM((8 * rows, QUART), BF16),
            pltpu.VMEM((8, 2, rows + 16, 256), BF16),
            pltpu.VMEM((rows, 2 * HALF), F32),
            pltpu.VMEM((2, rows, HALF), BF16),
            pltpu.VMEM((rows, QUART), F32),
            pltpu.VMEM((rows, QUART), F32),
            pltpu.VMEM((rows, QUART), F32),
            pltpu.VMEM((8, rows, 256), BF16),
            pltpu.VMEM((8, rows, 256), BF16),
            pltpu.VMEM((rows, 2 * HALF), F32),
            pltpu.VMEM((256, HEAD_DIM), F32),
            pltpu.VMEM((256, HEAD_DIM), F32),
            pltpu.VMEM((2, 4, rows, QUART), BF16),
            pltpu.VMEM((3, 4, rows, QUART), BF16),
            pltpu.VMEM((4, rows, QUART), BF16),
            pltpu.VMEM((8, 8, 256), F32),
            pltpu.VMEM((8, 8, 256), F32),
            dma((5,)),
            dma((4,)),
            dma((4, 4)),
            dma((4, 4)),
            dma((2, 4)),
            dma((3, 8, 2)),
            dma((3, 8, 2)),
            dma((8, 2)),
            dma((8, 2)),
            dma((8, 2)),
            dma((8, 2)),
            dma((3, 2, 8)),
        ],
        compiler_params=pltpu.CompilerParams(
            collective_id=1, has_side_effects=True, vmem_limit_bytes=62 * 2**20
        ),
        cost_estimate=pl.CostEstimate(flops=10**10, bytes_accessed=30 * 2**20, transcendentals=0),
        name="back",
    )(*small, *arrays, *big)


TILE = 256


def update_kernel(rows, branch, owners, basis, gain_grad, norm_gains, gain_first, gain_second, *rest):
    (zs, gs, acts, bs, dys), olds, through, rest = rest[:5], rest[5:8], rest[8:10], rest[10:]
    news, low_new, passed, gain_news, rest = rest[:4], rest[4], rest[5:7], rest[7:11], rest[11:]
    turned_g, act, old, new, asem, osem, nsem = rest
    me, line = lax.axis_index("seq"), lax.axis_index("head")
    tile, tiles = pl.program_id(0), pl.num_programs(0)
    slot = tile % 2
    a_slab, f_slab = slab_of(owners, 0, me), slab_of(owners, 1, me)

    def columns_of(t):
        return pl.ds(pl.multiple_of(t * TILE, TILE), TILE)

    def act_copies(t, kind, which):
        at = pl.ds(pl.multiple_of(lax.rem(t, HALF // TILE) * TILE, TILE), TILE)
        for m in range(8):
            if kind == 3:
                part = dys.at[lax.div(t, 2), m, lax.rem(t, 2)]
            elif kind == 2:
                part = bs.at[m, lax.div(t, HALF // TILE), :, at]
            else:
                part = acts.at[kind, m, lax.div(t, HALF // TILE), :, at]
            pltpu.make_async_copy(part, act.at[t % 2, which, pl.ds(m * rows, rows)], asem.at[t % 2, which]).start()

    def act_wait(which):
        for m in range(8):
            part = act.at[slot, which, pl.ds(m * rows, rows)]
            pltpu.make_async_copy(part, part, asem.at[slot, which]).wait()

    def fetch_acts(t):
        pl.when(a_slab < 6)(lambda: act_copies(t, 0, 0))
        pl.when(a_slab >= 6)(lambda: act_copies(t, 1, 0))
        pl.when(f_slab <= 5)(lambda: act_copies(t, 2, 1))
        pl.when(f_slab > 5)(lambda: act_copies(t, 3, 1))
        pl.when(f_slab == 5)(lambda: act_copies(t, 3, 2))

    def old_copy(i, t):
        return pltpu.make_async_copy(olds[i].at[:, 0, columns_of(t)], old.at[t % 2, i], osem.at[t % 2, i])

    def new_copy(i, t):
        return pltpu.make_async_copy(new.at[t % 2, i], news[i].at[:, 0, columns_of(t)], nsem.at[t % 2, i])

    def fetch(t):
        fetch_acts(t)
        for i in range(3):
            old_copy(i, t).start()

    @pl.when(tile == 0)
    def _():
        fetch(0)
        for i in (0, 1):
            passed[i][...] = through[i][...]
        made = gain_grad[...]
        one = BETA_FIRST * gain_first[...] + (1.0 - BETA_FIRST) * made
        two = BETA_SECOND * gain_second[...] + (1.0 - BETA_SECOND) * made * made
        gain_news[0][...] = made
        gain_news[1][...] = one
        gain_news[2][...] = two
        gain_news[3][...] = norm_gains[...] - GAIN_RATE * (one / (1.0 - BETA_FIRST**ADAM_STEP)) / (
            jnp.sqrt(two / (1.0 - BETA_SECOND**ADAM_STEP)) + ADAM_EPS
        )
        for m in range(8):
            turned_g[:, m * rows : (m + 1) * rows] = gs[m].T

    pl.when(tile + 1 < tiles)(lambda: fetch(tile + 1))

    @pl.when(tile >= 2)
    def _():
        for i in range(4):
            new_copy(i, tile - 2).wait()

    grad, first_new, second_new, master_new = (new.at[slot, i] for i in range(4))
    first, second, master = (old.at[slot, i] for i in range(3))

    def ffn_rows(which):
        total = jnp.dot(zs[0], act[slot, which, pl.ds(0, rows), :], preferred_element_type=F32)
        for m in range(1, 8):
            total += jnp.dot(zs[m], act[slot, which, pl.ds(m * rows, rows), :], preferred_element_type=F32)
        return total[:SLAB]

    act_wait(0)
    factor = jnp.where(a_slab < 6, 1.0, branch)
    grad[pl.ds(0, 256), :] = factor * jnp.dot(turned_g[...], act[slot, 0], preferred_element_type=F32)
    act_wait(1)
    grad[pl.ds(256, SLAB), :] = ffn_rows(1)
    first_of_down = 2 * UNITS - f_slab * SLAB

    @pl.when(f_slab == 5)
    def _():
        act_wait(2)
        row = lax.broadcasted_iota(jnp.int32, (SLAB, 1), 0)
        grad[pl.ds(256, SLAB), :] = jnp.where(row < first_of_down, grad[pl.ds(256, SLAB), :], ffn_rows(2))

    for i in range(3):
        old_copy(i, tile).wait()
    row = lax.broadcasted_iota(jnp.int32, (256 + SLAB, 1), 0)
    rate = jnp.where((row < 256) | (row - 256 < first_of_down), 0.5 * (2 * HALF) ** (-0.5), 0.5 * FF ** (-0.5))
    basis_low = basis[...].astype(BF16)
    for b in range(TILE // HEAD_DIM):
        cut = slice(b * HEAD_DIM, (b + 1) * HEAD_DIM)
        turned = jnp.dot(grad[:, cut].astype(BF16), basis_low[b], preferred_element_type=F32)
        one = BETA_FIRST * first[:, cut] + (1.0 - BETA_FIRST) * turned
        two = BETA_SECOND * second[:, cut] + (1.0 - BETA_SECOND) * turned * turned
        first_new[:, cut] = one
        second_new[:, cut] = two
        adam = (one / (1.0 - BETA_FIRST**ADAM_STEP)) / (
            jnp.sqrt(two / (1.0 - BETA_SECOND**ADAM_STEP)) + ADAM_EPS
        )
        back = lax.dot_general(adam.astype(BF16), basis_low[b], NT, preferred_element_type=F32)
        before = master[:, cut]
        after = before - rate * (back + DECAY_RATE * before)
        master_new[:, cut] = after
        low_new[:, cut] = after.astype(BF16)
    for i in range(4):
        new_copy(i, tile).start()

    @pl.when(tile == tiles - 1)
    def _():
        for t in (tile - 1, tile):
            for i in range(4):
                new_copy(i, t).wait()


def update(owners, basis, small, zs, gs, acts, bs, dys, olds, through, branch):
    rows = gs.shape[1]
    height, _, width = olds[0].shape

    def whole(array):
        return pl.BlockSpec(array.shape, lambda i: (0,) * array.ndim)

    tall = pl.BlockSpec((height, TILE), lambda i: (0, i))
    per = TILE // HEAD_DIM
    gains = [shape(*array.shape, F32) for array in small]
    return call(
        functools.partial(update_kernel, rows, branch),
        [jax.ShapeDtypeStruct(olds[0].shape, F32)] * 4
        + [shape(height, width)]
        + [jax.ShapeDtypeStruct(array.shape, array.dtype) for array in through]
        + gains,
        [SM, pl.BlockSpec((per, HEAD_DIM, HEAD_DIM), lambda i: (i, 0, 0))]
        + [whole(array) for array in small]
        + [whole(zs), whole(gs)]
        + [HB] * 6
        + [whole(array) for array in through],
        [owners, basis, *small, zs, gs, acts, bs, dys, *olds, *through],
        [
            pltpu.VMEM((256, 8 * rows), BF16),
            pltpu.VMEM((2, 3, 8 * rows, TILE), BF16),
            pltpu.VMEM((2, 3, height, TILE), F32),
            pltpu.VMEM((2, 4, height, TILE), F32),
            pltpu.SemaphoreType.DMA((2, 3)),
            pltpu.SemaphoreType.DMA((2, 3)),
            pltpu.SemaphoreType.DMA((2, 4)),
        ],
        out_specs=[HB] * 4 + [tall] + [whole(array) for array in through] + [whole(array) for array in small],
        grid=(width // TILE,),
        flops=2 * 8 * rows * height * width,
        moved=70 * 2**20,
    )


def plane_mesh(
    tokens,
    cotangent,
    owners,
    master,
    first_moment,
    second_moment,
    eigenbases,
    norm_gains,
    gain_first,
    gain_second,
):
    rows, width = tokens.shape
    scale = HEAD_DIM ** (-0.5)
    branch = (WINDOW / 3.0) ** 0.5
    half = HEAD_DIM // 2
    speeds = ROPE_BASE ** (-jnp.arange(half, dtype=F32) / half)
    speeds = jnp.concatenate([speeds, speeds])[None, :]
    tall = [array.reshape(array.shape[2], 1, width) for array in (first_moment, second_moment, master)]
    (
        gains, o_low, o_wide, stats, n_own, n_parts, b_own, b_parts, a_low, h, kcat, vcat, q_low, attn, z_own, dys, bs
    ) = front(owners, tokens, cotangent, norm_gains, speeds, tall[2], scale, branch)
    block_out, input_grad, gain_grad, acts, zs, gs, bs = back(
        [owners],
        [tokens, cotangent, gains, speeds, o_low, o_wide, stats, n_own, n_parts, b_own, b_parts],
        [h, q_low, kcat, vcat, attn, a_low, z_own, bs],
        rows,
        scale,
        branch,
    )
    (
        grad, first_new, second_new, master_new, low_new, block_out, input_grad, gain_grad, gain_first_new,
        gain_second_new, gain_new,
    ) = update(
        owners, eigenbases[0, 0], [gain_grad, norm_gains, gain_first, gain_second], zs, gs, acts, bs, dys, tall,
        [block_out, input_grad], branch,
    )
    whole = (1, 1, *tall[0].shape[::2])
    return (
        block_out,
        input_grad,
        grad.reshape(whole),
        first_new.reshape(whole),
        second_new.reshape(whole),
        master_new.reshape(whole),
        low_new[None, None],
        gain_grad,
        gain_first_new,
        gain_second_new,
        gain_new,
    )


def solution(mesh):
    in_specs = (
        P("seq", None),
        P("seq", None),
        P(),
        P("head", "seq", None, None),
        P("head", "seq", None, None),
        P("head", "seq", None, None),
        P("head", "seq", None, None, None),
        P(None, "seq"),
        P(None, "seq"),
        P(None, "seq"),
    )
    out_specs = (
        P("seq", "head"),
        P("seq", None),
        P("head", "seq", None, None),
        P("head", "seq", None, None),
        P("head", "seq", None, None),
        P("head", "seq", None, None),
        P("head", "seq", None, None),
        P(None, "seq"),
        P(None, "seq"),
        P(None, "seq"),
        P(None, "seq"),
    )
    plane = mesh.shape["seq"] == 8 and mesh.shape["head"] == 4
    return jax.shard_map(
        plane_mesh if plane else any_mesh, mesh=mesh, in_specs=in_specs, out_specs=out_specs, check_vma=False
    )
```

```python
import functools

import jax
import jax.numpy as jnp
from jax import lax
from jax.experimental import pallas as pl
from jax.experimental.pallas import tpu as pltpu
from jax.sharding import PartitionSpec as P

HEADS = 16
HEAD_DIM = 128
FF = 5504
WINDOW = 1024
ADAM_STEP = 5


EPS_NORM = 1e-05
BETA_FIRST = 0.5
BETA_SECOND = 0.6
ADAM_EPS = 1e-08
DECAY_RATE = 0.1
GAIN_RATE = 0.25
ROPE_BASE = 10000.0
NEGATIVE = -1e30
PRECISE = lax.Precision.HIGHEST

BF16 = jnp.bfloat16
F32 = jnp.float32


def passed_along(shard, axis, by):
    devices = lax.axis_size(axis)
    pairs = [(i, i + by) for i in range(devices) if 0 <= i + by < devices]
    return lax.ppermute(shard, axis, pairs)


def inverse_order(owner_row):
    places = jnp.arange(owner_row.shape[0], dtype=jnp.int32)
    matches = (owner_row[:, None] == places[None, :]).astype(jnp.int32)
    return jnp.sum(matches * places[:, None], axis=0)


def kind_rates(kinds, width):
    wide = width ** (-0.5)
    spreads = jnp.array([wide, wide, wide, wide, wide, wide, FF ** (-0.5)], jnp.float32)
    matches = (kinds[..., None] == jnp.arange(7, dtype=jnp.int32)).astype(jnp.float32)
    return 0.5 * jnp.sum(matches * spreads, axis=-1)


def angles(positions):
    half_dim = HEAD_DIM // 2
    frequencies = ROPE_BASE ** (-jnp.arange(half_dim, dtype=jnp.float32) / half_dim)
    turning = positions[:, None] * frequencies[None, :]
    return (jnp.cos(turning)[:, None, :], jnp.sin(turning)[:, None, :])


def rotate(vectors, cosine, sine):
    half_dim = vectors.shape[-1] // 2
    former = vectors[..., :half_dim]
    latter = vectors[..., half_dim:]
    return jnp.concatenate(
        [former * cosine - latter * sine, latter * cosine + former * sine], axis=-1
    )


def inverse_rms(vectors):
    return lax.rsqrt(jnp.mean(vectors * vectors, axis=-1, keepdims=True) + EPS_NORM)


def norm_back(grad_normed, inputs, rms_values, gain_row):
    weighted = grad_normed * gain_row
    inner = jnp.mean(weighted * inputs, axis=-1, keepdims=True)
    input_part = rms_values * weighted - inputs * rms_values**3 * inner
    return (input_part, jnp.sum(grad_normed * inputs * rms_values, axis=0))


def any_mesh(
    tokens,
    cotangent,
    owners,
    master,
    first_moment,
    second_moment,
    eigenbases,
    norm_gains,
    gain_first,
    gain_second,
):
    tok_rows, width = tokens.shape
    seq_devices = lax.axis_size("seq")
    head_devices = lax.axis_size("head")
    seq_place = lax.axis_index("seq")
    head_place = lax.axis_index("head")
    slab_rows = master.shape[2]
    attn_slab = 4 * width // (head_devices * seq_devices)
    ffn_slab = slab_rows - attn_slab
    head_width = width // head_devices
    ffn_width = FF // head_devices
    local_heads = HEADS // head_devices
    score_scale = HEAD_DIM ** (-0.5)
    branch_scale = (WINDOW / 3.0) ** 0.5
    inverse_attn = inverse_order(owners[0])
    inverse_ffn = inverse_order(owners[1])
    master_low = master[0, 0].astype(jnp.bfloat16)
    gathered, gains_all = (
        lax.all_gather(master_low, "seq", axis=0, tiled=True),
        lax.all_gather(norm_gains.astype(jnp.bfloat16), "seq", axis=1, tiled=True),
    )
    gathered = gathered.reshape(seq_devices, slab_rows, width)
    attn_rows = jnp.take(gathered[:, :attn_slab], owners[0], axis=0).reshape(4 * head_width, width)
    ffn_rows = jnp.take(gathered[:, attn_slab:], owners[1], axis=0).reshape(3 * ffn_width, width)
    w_query = attn_rows[:head_width]
    w_key = attn_rows[head_width : 2 * head_width]
    w_value = attn_rows[2 * head_width : 3 * head_width]
    w_out = attn_rows[3 * head_width :]
    w_gate = ffn_rows[:ffn_width]
    w_up = ffn_rows[ffn_width : 2 * ffn_width]
    w_down = ffn_rows[2 * ffn_width :]
    gain_one = gains_all[0].astype(jnp.float32)
    gain_two = gains_all[1].astype(jnp.float32)
    inputs = tokens.astype(jnp.float32)
    rms_one = inverse_rms(inputs)
    normed_one = (inputs * rms_one * gain_one).astype(jnp.bfloat16)
    positions = (seq_place * tok_rows + jnp.arange(tok_rows, dtype=jnp.int32)).astype(jnp.float32)
    cosine, sine = angles(positions)
    head_shape = (tok_rows, local_heads, HEAD_DIM)

    def project(weight_rows):
        return jnp.einsum("td,id->ti", normed_one, weight_rows, preferred_element_type=jnp.float32)

    queries = rotate(project(w_query).reshape(head_shape), cosine, sine).astype(jnp.bfloat16)
    keys_own = rotate(project(w_key).reshape(head_shape), cosine, sine).astype(jnp.bfloat16)
    values_own = project(w_value).reshape(head_shape).astype(jnp.bfloat16)
    hop_total = -(-WINDOW // tok_rows)
    hop_sizes = [
        min(tok_rows, WINDOW - (hop_index - 1) * tok_rows) for hop_index in range(1, hop_total + 1)
    ]
    halo_keys = []
    halo_values = []
    for hop_index in range(hop_total, 0, -1):
        hop_rows = hop_sizes[hop_index - 1]
        far_keys, far_values = passed_along(
            (keys_own[tok_rows - hop_rows :], values_own[tok_rows - hop_rows :]), "seq", hop_index
        )
        halo_keys.append(far_keys)
        halo_values.append(far_values)
    keys_all = jnp.concatenate(halo_keys + [keys_own], axis=0)
    values_all = jnp.concatenate(halo_values + [values_own], axis=0)
    row_ids = jnp.arange(tok_rows, dtype=jnp.int32)[:, None]
    col_ids = jnp.arange(WINDOW + tok_rows, dtype=jnp.int32)[None, :]
    allowed = (
        (col_ids > row_ids)
        & (col_ids <= row_ids + WINDOW)
        & (seq_place * tok_rows - WINDOW + col_ids >= 0)
    )

    def scores_of():
        raw = jnp.einsum("thd,chd->htc", queries, keys_all, preferred_element_type=jnp.float32)
        return jnp.where(allowed[None], raw * score_scale, NEGATIVE)

    scores = scores_of()
    row_top = jnp.max(scores, axis=-1, keepdims=True)
    exp_scores = jnp.exp(scores - row_top)
    exp_total = jnp.sum(exp_scores, axis=-1, keepdims=True)
    soft_low = (exp_scores / exp_total).astype(jnp.bfloat16)
    log_total = row_top + jnp.log(exp_total)
    attended = jnp.einsum("htc,chd->thd", soft_low, values_all, preferred_element_type=jnp.float32)
    attended_low = attended.reshape(tok_rows, head_width).astype(jnp.bfloat16)
    attn_part = branch_scale * jnp.dot(attended_low, w_out, preferred_element_type=jnp.float32)
    hidden_one = inputs + lax.psum(attn_part, "head")
    rms_two = inverse_rms(hidden_one)
    normed_two = (hidden_one * rms_two * gain_two).astype(jnp.bfloat16)
    gate_pre = jnp.einsum("td,fd->tf", normed_two, w_gate, preferred_element_type=jnp.float32)
    up_pre = jnp.einsum("td,fd->tf", normed_two, w_up, preferred_element_type=jnp.float32)
    sigma = jax.nn.sigmoid(gate_pre)
    hidden_low = (gate_pre * sigma * up_pre).astype(jnp.bfloat16)
    ffn_part = jnp.dot(hidden_low, w_down, preferred_element_type=jnp.float32)
    ffn_share = lax.psum_scatter(ffn_part, "head", scatter_dimension=1, tiled=True)
    share_width = width // head_devices
    residual_share = lax.dynamic_slice_in_dim(hidden_one, head_place * share_width, share_width, 1)
    block_out = (residual_share + ffn_share).astype(jnp.bfloat16)
    grad_out_f = cotangent.astype(jnp.float32)
    hidden_grad = jnp.einsum("td,fd->tf", cotangent, w_down, preferred_element_type=jnp.float32)
    silu_grad = sigma * (1.0 + gate_pre * (1.0 - sigma))
    gate_grad = (hidden_grad * up_pre * silu_grad).astype(jnp.bfloat16)
    up_grad = (hidden_grad * gate_pre * sigma).astype(jnp.bfloat16)
    down_grad = jnp.einsum("tf,td->fd", hidden_low, cotangent, preferred_element_type=jnp.float32)
    gate_w_grad = jnp.einsum("tf,td->fd", gate_grad, normed_two, preferred_element_type=jnp.float32)
    up_w_grad = jnp.einsum("tf,td->fd", up_grad, normed_two, preferred_element_type=jnp.float32)
    ffn_rows_grad = jnp.concatenate([gate_w_grad, up_w_grad, down_grad], axis=0)
    ffn_owner = jnp.take(ffn_rows_grad.reshape(seq_devices, ffn_slab, width), inverse_ffn, axis=0)
    normed_two_part = jnp.einsum(
        "tf,fd->td", gate_grad, w_gate, preferred_element_type=jnp.float32
    ) + jnp.einsum("tf,fd->td", up_grad, w_up, preferred_element_type=jnp.float32)
    normed_two_share = lax.psum_scatter(normed_two_part, "head", scatter_dimension=1, tiled=True)
    normed_two_grad = lax.all_gather(normed_two_share, "head", axis=1, tiled=True)
    back_two, gain_two_grad = norm_back(normed_two_grad, hidden_one, rms_two, gain_two)
    hidden_one_grad = grad_out_f + back_two
    hidden_grad_low = hidden_one_grad.astype(jnp.bfloat16)
    attended_grad = branch_scale * jnp.einsum(
        "td,id->ti", hidden_grad_low, w_out, preferred_element_type=jnp.float32
    )
    attended_grad = attended_grad.reshape(head_shape).astype(jnp.bfloat16)
    soft_again = jnp.exp(scores_of() - log_total)
    soft_grad = jnp.einsum(
        "thd,chd->htc", attended_grad, values_all, preferred_element_type=jnp.float32
    )
    inner_sum = jnp.sum(soft_again * soft_grad, axis=-1, keepdims=True)
    score_grad = (soft_again * (soft_grad - inner_sum) * score_scale).astype(jnp.bfloat16)
    query_grad_turned = jnp.einsum(
        "htc,chd->thd", score_grad, keys_all, preferred_element_type=jnp.float32
    )
    key_grad_all = jnp.einsum(
        "htc,thd->chd", score_grad, queries, preferred_element_type=jnp.float32
    )
    value_grad_all = jnp.einsum(
        "htc,thd->chd", soft_low, attended_grad, preferred_element_type=jnp.float32
    )
    key_grad_own = key_grad_all[WINDOW:]
    value_grad_own = value_grad_all[WINDOW:]
    start_at = 0
    for hop_index in range(hop_total, 0, -1):
        hop_rows = hop_sizes[hop_index - 1]
        back_keys, back_values = passed_along(
            (
                key_grad_all[start_at : start_at + hop_rows],
                value_grad_all[start_at : start_at + hop_rows],
            ),
            "seq",
            -hop_index,
        )
        key_grad_own = key_grad_own.at[tok_rows - hop_rows :].add(back_keys)
        value_grad_own = value_grad_own.at[tok_rows - hop_rows :].add(back_values)
        start_at = start_at + hop_rows
    query_grad = (
        rotate(query_grad_turned, cosine, -sine).reshape(tok_rows, head_width).astype(jnp.bfloat16)
    )
    key_grad = (
        rotate(key_grad_own, cosine, -sine).reshape(tok_rows, head_width).astype(jnp.bfloat16)
    )
    value_grad = value_grad_own.reshape(tok_rows, head_width).astype(jnp.bfloat16)

    def input_part(row_grad, weight_rows):
        return jnp.einsum("ti,id->td", row_grad, weight_rows, preferred_element_type=jnp.float32)

    normed_one_part = (
        input_part(query_grad, w_query)
        + input_part(key_grad, w_key)
        + input_part(value_grad, w_value)
    )
    normed_one_share = lax.psum_scatter(normed_one_part, "head", scatter_dimension=1, tiled=True)
    normed_one_grad = lax.all_gather(
        normed_one_share.astype(jnp.bfloat16), "head", axis=1, tiled=True
    ).astype(normed_one_share.dtype)
    back_one, gain_one_grad = norm_back(normed_one_grad, inputs, rms_one, gain_one)
    input_grad = hidden_one_grad + back_one
    gain_grads = jnp.stack([gain_one_grad, gain_two_grad])

    def rows_grad(row_grad):
        return jnp.einsum("ti,td->id", row_grad, normed_one, preferred_element_type=jnp.float32)

    out_w_grad = branch_scale * jnp.einsum(
        "ti,td->id", attended_low, hidden_grad_low, preferred_element_type=jnp.float32
    )
    attn_rows_grad = jnp.concatenate(
        [rows_grad(query_grad), rows_grad(key_grad), rows_grad(value_grad), out_w_grad], axis=0
    )
    attn_owner = jnp.take(
        attn_rows_grad.reshape(seq_devices, attn_slab, width), inverse_attn, axis=0
    )
    owner_rows = jnp.concatenate([attn_owner, ffn_owner], axis=1).reshape(
        seq_devices * slab_rows, width
    )
    reduced, gain_reduced = (
        lax.psum_scatter(owner_rows, "seq", scatter_dimension=0, tiled=True),
        lax.psum_scatter(gain_grads, "seq", scatter_dimension=1, tiled=True),
    )
    attn_kinds = (
        inverse_attn[seq_place] * attn_slab + jnp.arange(attn_slab, dtype=jnp.int32)
    ) // head_width
    ffn_kinds = (
        4 + (inverse_ffn[seq_place] * ffn_slab + jnp.arange(ffn_slab, dtype=jnp.int32)) // ffn_width
    )
    row_rates = kind_rates(jnp.concatenate([attn_kinds, ffn_kinds]), width)[:, None]
    basis = eigenbases[0, 0]
    block_size = basis.shape[-1]
    split_shape = (slab_rows, width // block_size, block_size)
    turned = jnp.einsum(
        "rbk,bkl->rbl", reduced.reshape(split_shape), basis, precision=PRECISE
    ).reshape(slab_rows, width)
    first_new = BETA_FIRST * first_moment[0, 0] + (1.0 - BETA_FIRST) * turned
    second_new = BETA_SECOND * second_moment[0, 0] + (1.0 - BETA_SECOND) * turned * turned
    adam_dir = (
        first_new
        / (1.0 - BETA_FIRST**ADAM_STEP)
        / (jnp.sqrt(second_new / (1.0 - BETA_SECOND**ADAM_STEP)) + ADAM_EPS)
    )
    backward_dir = jnp.einsum(
        "rbl,bkl->rbk", adam_dir.reshape(split_shape), basis, precision=PRECISE
    ).reshape(slab_rows, width)
    master_old = master[0, 0]
    master_new = master_old - row_rates * (backward_dir + DECAY_RATE * master_old)
    gain_first_new = BETA_FIRST * gain_first + (1.0 - BETA_FIRST) * gain_reduced
    gain_second_new = BETA_SECOND * gain_second + (1.0 - BETA_SECOND) * gain_reduced * gain_reduced
    gain_new = norm_gains - GAIN_RATE * (gain_first_new / (1.0 - BETA_FIRST**ADAM_STEP)) / (
        jnp.sqrt(gain_second_new / (1.0 - BETA_SECOND**ADAM_STEP)) + ADAM_EPS
    )
    return (
        block_out,
        input_grad,
        reduced[None, None],
        first_new[None, None],
        second_new[None, None],
        master_new[None, None],
        master_new.astype(jnp.bfloat16)[None, None],
        gain_reduced,
        gain_first_new,
        gain_second_new,
        gain_new,
    )


SLAB = 516
PAD = 528
HALF = 1024
QUART = 512
PACKED = 800
UNITS = 1376
NT = (((1,), (1,)), ((), ()))
TN = (((0,), (0,)), ((), ()))


VM = pl.BlockSpec(memory_space=pltpu.VMEM)
SM = pl.BlockSpec(memory_space=pltpu.SMEM)
HB = pl.BlockSpec(memory_space=pl.ANY)


def shape(rows, columns, dtype=BF16):
    return jax.ShapeDtypeStruct((rows, columns), dtype)


def call(kernel, outs, specs, args, scratch=(), flops=0, moved=0, out_specs=None, grid=None):
    extra = {} if grid is None else {"grid": grid}
    return pl.pallas_call(
        kernel,
        out_shape=outs,
        in_specs=specs,
        out_specs=[VM] * len(outs) if out_specs is None else out_specs,
        scratch_shapes=list(scratch),
        compiler_params=pltpu.CompilerParams(vmem_limit_bytes=56 * 2**20),
        cost_estimate=pl.CostEstimate(flops=flops, bytes_accessed=moved, transcendentals=0),
        name=getattr(kernel, "func", kernel).__name__,
        **extra,
    )(*args)


def root_of(values):
    return lax.rsqrt(jnp.mean(values * values, axis=-1, keepdims=True) + EPS_NORM)


def turn(values, cosine, sine):
    parts = []
    for h in range(values.shape[1] // HEAD_DIM):
        v = values[:, h * HEAD_DIM : (h + 1) * HEAD_DIM]
        parts.append(v * cosine + pltpu.roll(v, HEAD_DIM // 2, 1) * sine)
    return parts


MESH = pl.DeviceIdType.MESH


def flip(index, mask):
    for bit in (1, 2, 4):
        if mask & bit:
            index = index + bit - 2 * bit * lax.rem(lax.div(index, bit), 2)
    return index


def twist(left, right):
    out = 0
    for bit in (1, 2, 4):
        out = out + bit * lax.rem(lax.rem(lax.div(left, bit), 2) + lax.rem(lax.div(right, bit), 2), 2)
    return out


def slab_of(owners, kind, device):
    found = 0
    for j in range(8):
        found = jnp.where(owners[kind, j] == device, j, found)
    return found


class Plane:
    def __init__(self, at, sent, got, me, line):
        self.at, self.sent, self.got, self.me, self.line = at, sent, got, me, line

    def copy(self, src, dst, side, hop_mask):
        return pltpu.make_async_remote_copy(
            src_ref=self.at(src, side),
            dst_ref=self.at(dst, side),
            send_sem=self.sent.at[dst, side],
            recv_sem=self.got.at[dst, side],
            device_id=(flip(self.me, hop_mask), self.line),
            device_id_type=MESH,
        )

    def start_first(self):
        for mask, side in ((2, 0), (4, 1)):
            self.copy(0, mask, side, mask).start()
        for side in (0, 1):
            self.copy(0, 1, side, 1).start()

    def start_second(self):
        for mask, side in ((2, 1), (4, 0)):
            self.copy(0, mask, side, mask).start()

    def start(self):
        self.start_first()
        self.start_second()

    def arrive(self, mask, side):
        self.copy(mask, mask, side, 1).wait_recv()

    def twin(self, mask, side):
        self.copy(mask, mask + 1, side, 1).start()

    def relay_first(self):
        for mask, side in ((2, 0), (4, 1)):
            self.arrive(mask, side)
            self.copy(mask, 6, side, 6 - mask).start()
            self.twin(mask, side)

    def relay_second(self):
        for mask, side in ((2, 1), (4, 0)):
            self.arrive(mask, side)
            self.twin(mask, side)

    def relay_last(self):
        for side in (0, 1):
            self.arrive(6, side)
            self.twin(6, side)

    def finish(self):
        for mask in (1, 3, 5, 7):
            for side in (0, 1):
                self.arrive(mask, side)

    def drain(self, masks=range(1, 8)):
        for mask in masks:
            for side in (0, 1):
                self.copy(0, mask, side, 1).wait_send()


def line_copy(src, dst, sent, got, m, me, line):
    return pltpu.make_async_remote_copy(
        src_ref=src,
        dst_ref=dst,
        send_sem=sent.at[m],
        recv_sem=got.at[m],
        device_id=(me, flip(line, m)),
        device_id_type=MESH,
    )


def greet(me, line, plane_masks, line_masks):
    barrier = pltpu.get_barrier_semaphore()
    for mask in plane_masks:
        pl.semaphore_signal(barrier, inc=1, device_id=(flip(me, mask), line), device_id_type=MESH)
    for mask in line_masks:
        pl.semaphore_signal(barrier, inc=1, device_id=(me, flip(line, mask)), device_id_type=MESH)
    return lambda: pl.semaphore_wait(barrier, len(plane_masks) + len(line_masks))


def layer_kernel(
    rows, scale, branch,
    owners, tokens, dy, own_gains, speeds, master,
    block_out, gain_grad, input_grad, acts, z_all, g_all, b_all, dy_all,
    gains, o_low, o_wide, stats, a_low, b_low, kcat, vcat, qcat, docat, sent, g_sent, wide, w_a, w_f, made, cut,
    total, z_out, z_in, z_sum, n_own, b_own, work, dy_own, stat_l, stat_r, gain_out, gain_in,
    sem_w, sem_k, plane_sent, plane_got, z_sems, r_up, r_down, r_got, t_sent, t_got, a2a_sems,
):
    me, line = lax.axis_index("seq"), lax.axis_index("head")
    ready = greet(me, line, range(1, 8), (1, 2, 3))
    order_a, order_f = ([twist(owners[kind, j], me) for j in range(8)] for kind in (0, 1))
    d_low = a_low
    h_out = wide.at[pl.ds(0, rows)]
    kept = {}

    def keep(i, src, dst):
        kept[i] = pltpu.make_async_copy(src, dst, sem_k.at[i])
        kept[i].start()

    def plane(i, at):
        return Plane(at, plane_sent.at[i], plane_got.at[i], me, line)

    w_a_plane = plane(0, lambda m, s: w_a.at[m, s] if s else w_a.at[m, s, pl.ds(0, 256)])
    w_f_plane = plane(1, lambda m, s: w_f.at[m, s])
    kv_plane = plane(2, lambda m, s: (kcat, vcat)[s].at[pl.ds(m * rows, rows)])
    q_plane = plane(3, lambda m, s: qcat.at[m, s])
    y_plane = plane(4, lambda m, s: dy_own.at[s] if m == 0 else dy_all.at[line, m, s])
    b_plane = plane(5, lambda m, s: b_low.at[s] if m == 0 else b_all.at[m, s])
    a_plane = plane(6, lambda m, s: acts.at[0, m, s])
    d_plane = plane(7, lambda m, s: d_low.at[s] if m == 0 else acts.at[1, m, s])
    do_plane = plane(8, lambda m, s: docat.at[m, s])

    def straight(src, dst, which, m):
        return pltpu.make_async_remote_copy(
            src_ref=src.at[m],
            dst_ref=dst.at[m],
            send_sem=a2a_sems.at[which, 0, m],
            recv_sem=a2a_sems.at[which, 1, m],
            device_id=(flip(me, m), line),
            device_id_type=MESH,
        )

    def quarter(m):
        return pl.ds(pl.multiple_of(flip(line, m) * QUART, QUART), QUART)

    def piece(which, m):
        buffer = 0 if which == 2 else which
        return line_copy(
            z_out.at[buffer, m - 1], z_in.at[which, m - 1], z_sems.at[which, 0], z_sems.at[which, 1], m, me, line
        )

    def whole(which, m):
        return line_copy(
            z_sum.at[which, 0], z_sum.at[which, m], z_sems.at[which, 2], z_sems.at[which, 3], m, me, line
        )

    def scatter(which):
        buffer = 0 if which == 2 else which
        for m in (3, 2, 1):
            z_out[buffer, m - 1] = total[:, quarter(m)].astype(BF16)
            piece(which, m).start()

    def gathered(which, own):
        for m in (1, 2, 3):
            piece(which, m).wait_recv()
        for m in (1, 2, 3):
            own += z_in[which, m - 1].astype(F32)
        return own

    def spread(which, own):
        z_sum[which, 0] = gathered(which, own).astype(BF16)
        for m in (3, 2, 1):
            whole(which, m).start()

    def along_line(quarter_index, m, up):
        return pltpu.make_async_remote_copy(
            src_ref=dy_all.at[quarter_index, m],
            dst_ref=dy_all.at[quarter_index, m],
            send_sem=(r_up if up else r_down).at[quarter_index, m],
            recv_sem=r_got.at[quarter_index, m],
            device_id=(me, line + 1 if up else line - 1),
            device_id_type=MESH,
        )

    def twin_quarter(quarter_index, m):
        return pltpu.make_async_remote_copy(
            src_ref=dy_all.at[quarter_index, m],
            dst_ref=dy_all.at[quarter_index, m + 1],
            send_sem=t_sent.at[quarter_index, m],
            recv_sem=t_got.at[quarter_index, m],
            device_id=(flip(me, 1), line),
            device_id_type=MESH,
        )

    def line_round(step):
        if step == 0:
            for up, last in ((True, 3), (False, 0)):

                @pl.when(line != last)
                def _():
                    for m in (0, 2, 4, 6):
                        along_line(line, m, up).start()

            return
        for up, first, last in ((True, step, 3), (False, 3 - step, 0)):
            index = line - step if up else line + step

            @pl.when(line >= first if up else line <= first)
            def _():
                for m in (0, 2, 4, 6):
                    along_line(index, m, up).wait_recv()

                @pl.when(line != last)
                def _():
                    for m in (0, 2, 4, 6):
                        along_line(index, m, up).start()

                for m in (0, 2, 4, 6):
                    twin_quarter(index, m).start()

    def line_end():
        for apart in (1, 2, 3):
            for up in (True, False):
                index = line - apart if up else line + apart

                @pl.when(line >= apart if up else line <= 3 - apart)
                def _():
                    for m in (0, 2, 4, 6):
                        twin_quarter(index, m).wait_recv()
                        twin_quarter(index, m).wait_send()

        for step in range(3):
            for up in (True, False):
                index = line - step if up else line + step

                @pl.when((line >= step) & (line != 3) if up else (line <= 3 - step) & (line != 0))
                def _():
                    for m in (0, 2, 4, 6):
                        along_line(index, m, up).wait_send()

    load = pltpu.make_async_copy(master.at[pl.ds(0, 256), 0, :], wide.at[pl.ds(0, 256)], sem_w.at[0])
    load.start()
    for side in (0, 1):
        at = pl.multiple_of(line * QUART + side * 256, 256)
        dy_own[side] = dy[:, pl.ds(at, 256)]
    keep(8, dy_own, dy_all.at[line, 0])
    ready()
    y_plane.start()
    w_a[0, 0, pl.ds(256, 16), :] = jnp.zeros((16, HALF), BF16)
    w_a[0, 1, pl.ds(256, 16), :] = jnp.zeros((16, HALF), BF16)
    w_a[0, 1, 256:258, 0:256] = own_gains[...].astype(BF16)
    load.wait()
    for side in (0, 1):
        w_a[0, side, pl.ds(0, 256), :] = wide[pl.ds(0, 256), side * HALF : (side + 1) * HALF].astype(BF16)
    load = pltpu.make_async_copy(master.at[pl.ds(256, 256), 0, :], wide.at[pl.ds(0, 256)], sem_w.at[1])
    load.start()
    w_a_plane.start()
    load.wait()
    for side in (0, 1):
        columns = slice(side * HALF, (side + 1) * HALF)
        w_f[0, side, pl.ds(0, 256), :] = wide[pl.ds(0, 256), columns].astype(BF16)
    load = pltpu.make_async_copy(master.at[pl.ds(512, SLAB - 256), 0, :], wide, sem_w.at[2])
    load.start()
    load.wait()
    for side in (0, 1):
        columns = slice(side * HALF, (side + 1) * HALF)
        w_f[0, side, pl.ds(256, 256), :] = wide[pl.ds(0, 256), columns].astype(BF16)
        last = jnp.concatenate([wide[256 : SLAB - 256, columns], jnp.zeros((PAD - SLAB, HALF), F32)], axis=0)
        w_f[0, side, pl.ds(512, 16), :] = last.astype(BF16)
    angle = (me * rows + lax.broadcasted_iota(jnp.int32, (rows, 1), 0)).astype(F32) * speeds[...]
    cosine, sine = jnp.cos(angle), jnp.sin(angle)
    sine = jnp.where(lax.broadcasted_iota(jnp.int32, (1, HEAD_DIM), 1) < HEAD_DIM // 2, -sine, sine)
    y_plane.relay_first()
    y_plane.relay_second()
    y_plane.relay_last()
    kept[8].wait()
    line_round(0)
    w_a_plane.relay_first()
    w_a_plane.relay_second()
    w_a_plane.relay_last()
    w_f_plane.start_first()
    w_a_plane.finish()

    for m in range(8):
        at = pl.multiple_of(flip(me, m) * 256, 256)
        gains[:, pl.ds(at, 256)] = w_a[m, 1, 256:258, 0:256].astype(F32)
    x = tokens[...].astype(F32)
    normed = (x * root_of(x) * gains[0:1, :]).astype(BF16)
    for side in (0, 1):
        a_low[side] = normed[:, side * HALF : (side + 1) * HALF]
    for j in (2, 3, 4, 5, 0, 1):
        out = lax.dot_general(a_low[0], w_a[order_a[j], 0, pl.ds(0, 256), :], NT, preferred_element_type=F32)
        out += lax.dot_general(a_low[1], w_a[order_a[j], 1, pl.ds(0, 256), :], NT, preferred_element_type=F32)
        if j < 4:
            parts = turn(out, cosine, sine)
        else:
            parts = [out[:, :HEAD_DIM], out[:, HEAD_DIM:]]
        for i, part in enumerate(parts):
            if j < 2:
                qcat[0, j, :, i * HEAD_DIM : (i + 1) * HEAD_DIM] = part.astype(BF16)
            else:
                at = (2 * (j % 2) + i) * HEAD_DIM
                (kcat, vcat)[j // 2 - 1][pl.ds(0, rows), at : at + HEAD_DIM] = part.astype(BF16)
        if j == 5:
            kv_plane.start()
    keep(0, a_low, acts.at[0, 0])
    line_round(1)
    kv_plane.relay_first()
    kv_plane.relay_second()
    w_f_plane.relay_first()
    w_f_plane.start_second()
    kv_plane.relay_last()
    kv_plane.finish()

    at_q = me * rows + lax.broadcasted_iota(jnp.int32, (rows, 1), 0)
    along = lax.broadcasted_iota(jnp.int32, (1, rows), 1)
    lane = lax.broadcasted_iota(jnp.int32, (rows, HEAD_DIM), 1)
    stat = jnp.zeros((rows, HEAD_DIM), F32)
    for h in range(4):
        if h == 2:
            line_round(2)
        columns = slice(h * HEAD_DIM, (h + 1) * HEAD_DIM)
        q = qcat[0, h // 2, :, (h % 2) * HEAD_DIM : (h % 2 + 1) * HEAD_DIM]
        top = jnp.full((rows, 1), NEGATIVE, F32)
        for m in range(8):
            ahead = at_q - (flip(me, m) * rows + along)
            s = lax.dot_general(q, kcat[pl.ds(m * rows, rows), columns], NT, preferred_element_type=F32)
            s = jnp.where((ahead >= 0) & (ahead < WINDOW), s * scale, NEGATIVE)
            work[m, :, pl.ds(0, rows)] = s
            top = jnp.maximum(top, jnp.max(s, axis=-1, keepdims=True))
        sums = jnp.zeros((rows, 1), F32)
        for m in range(8):
            e = jnp.exp(work[m, :, pl.ds(0, rows)] - top)
            work[m, :, pl.ds(0, rows)] = e
            sums += jnp.sum(e, axis=-1, keepdims=True)
        share = 1.0 / sums
        o = jnp.zeros((rows, HEAD_DIM), F32)
        for m in range(8):
            soft = (work[m, :, pl.ds(0, rows)] * share).astype(BF16)
            o += jnp.dot(soft, vcat[pl.ds(m * rows, rows), columns], preferred_element_type=F32)
        o_wide[:, columns] = o
        o_low[:, columns] = o.astype(BF16)
        stat = jnp.where(lane == h, top + jnp.log(sums), stat)
    stats[...] = stat
    for side in (0, 1):
        out = jnp.dot(o_low[:, :256], w_a[order_a[6], side, pl.ds(0, 256), :], preferred_element_type=F32)
        out += jnp.dot(o_low[:, 256:], w_a[order_a[7], side, pl.ds(0, 256), :], preferred_element_type=F32)
        total[:, side * HALF : (side + 1) * HALF] = branch * out

    scatter(0)
    spread(0, total[:, quarter(0)])
    w_f_plane.relay_last()
    for m in (1, 2, 3):
        whole(0, m).wait_recv()

    for m in range(4):
        h_out[:, quarter(m)] = z_sum[0, m].astype(F32)
    h = h_out[...] + tokens[...].astype(F32)
    h_out[...] = h
    normed = (h * root_of(h) * gains[1:2, :]).astype(BF16)
    for side in (0, 1):
        b_low[side] = normed[:, side * HALF : (side + 1) * HALF]
    keep(1, b_low, b_all.at[0])
    b_plane.start()
    w_f_plane.relay_second()
    w_f_plane.finish()

    def through(j, left, right):
        out = lax.dot_general(w_f[order_f[j], 0], left, NT, preferred_element_type=F32)
        return out + lax.dot_general(w_f[order_f[j], 1], right, NT, preferred_element_type=F32)

    some = pl.ds(0, rows)
    made[pl.ds(8 * SLAB, 16), some] = jnp.zeros((16, rows), F32)
    row = lax.broadcasted_iota(jnp.int32, (PAD, 1), 0)
    gate_rows = row < 2 * UNITS - 5 * SLAB
    for j in range(8):
        if j < 5:
            out = through(j, b_low[0], b_low[1])
        elif j > 5:
            out = through(j, dy[:, :HALF], dy[:, HALF:])
        else:
            out = jnp.where(gate_rows, through(j, b_low[0], b_low[1]), through(j, dy[:, :HALF], dy[:, HALF:]))
        made[pl.ds(j * SLAB, PAD), some] = out

    def mix(i, _):
        at = pl.multiple_of(i * 32, 8)
        gate = made[pl.ds(at, 32), some]
        up = made[pl.ds(UNITS + at, 32), some]
        back = made[pl.ds(2 * UNITS + at, 32), some]
        sigma = 1.0 / (1.0 + jnp.exp(-gate))
        silu = gate * sigma
        made[pl.ds(at, 32), some] = back * up * (sigma * (1.0 + gate * (1.0 - sigma)))
        made[pl.ds(UNITS + at, 32), some] = back * silu
        made[pl.ds(2 * UNITS + at, 32), some] = silu * up
        return 0

    lax.fori_loop(0, UNITS // 32, mix, 0)
    for j in range(8):
        cut[j, :, pl.ds(0, rows)] = made[pl.ds(j * SLAB, PAD), some].astype(BF16)
    def down(first):
        kinds = range(0, 6) if first else range(5, 8)
        for side in (0, 1):
            columns = slice(side * HALF, (side + 1) * HALF)
            for j in kinds:
                z = cut[j, :, pl.ds(0, rows)]
                if j == 5:
                    z = jnp.where(gate_rows if first else ~gate_rows, z, jnp.zeros_like(z))
                out = lax.dot_general(z, w_f[order_f[j], side], TN, preferred_element_type=F32)
                total[:, columns] = out if j == kinds[0] else total[:, columns] + out

    down(True)
    n_own[...] = total[:, quarter(0)]
    scatter(1)
    q_plane.start()
    for m in range(8):
        z = cut[slab_of(owners, 1, flip(me, m)), :, pl.ds(0, rows)]
        sent[m, pl.ds(0, PAD), :] = z[:, :128]
        late = z[:, 128:].astype(F32)
        late = jnp.concatenate([late[: PAD // 2], late[PAD // 2 :]], axis=1)
        late = jnp.concatenate([late, jnp.zeros((PACKED - PAD - PAD // 2, 128), F32)], axis=0)
        sent[m, pl.ds(PAD, PACKED - PAD), :] = late.astype(BF16)
    keep(2, sent.at[0], z_all.at[0])
    for m in range(1, 8):
        straight(sent, z_all, 0, m).start()
    down(False)
    b_own[...] = total[:, quarter(0)]
    for m in (3, 2, 1):
        z_out[3, m - 1] = total[:, quarter(m)].astype(BF16)
    line_round(3)
    spread(1, n_own[...])
    b_plane.relay_first()
    b_plane.relay_second()
    q_plane.relay_first()
    q_plane.relay_second()
    for m in (1, 2, 3):
        whole(1, m).wait_recv()
    for m in (3, 2, 1):
        piece(3, m).start()

    for m in range(4):
        total[:, quarter(m)] = z_sum[1, m].astype(F32)
    normed_grad = total[...]
    h = h_out[...]
    root = root_of(h)
    gain_two = jnp.sum(normed_grad * h * root, axis=0, keepdims=True)
    weighted = normed_grad * gains[1:2, :]
    inner = jnp.mean(weighted * h, axis=-1, keepdims=True)
    grad = dy[...].astype(F32) + root * weighted - h * (root * root * root) * inner
    for c in range(8):
        made[pl.ds(c * rows, rows), :] = grad[:, c * 256 : (c + 1) * 256]
    low = grad.astype(BF16)
    kept[0].wait()
    for side in (0, 1):
        d_low[side] = low[:, side * HALF : (side + 1) * HALF]
    keep(3, d_low, acts.at[1, 0])
    total[0:1, :] = gain_two
    for m in range(8):
        at = pl.multiple_of(flip(me, m) * 256, 256)
        gain_out[m, 1:2, :] = total[0:1, pl.ds(at, 256)]
    lane = lax.broadcasted_iota(jnp.int32, (rows, HEAD_DIM), 1)
    own_lines = []
    for j, stat in enumerate((stat_l, stat_r)):
        out = lax.dot_general(d_low[0], w_a[order_a[6 + j], 0, pl.ds(0, 256), :], NT, preferred_element_type=F32)
        out += lax.dot_general(d_low[1], w_a[order_a[6 + j], 1, pl.ds(0, 256), :], NT, preferred_element_type=F32)
        out = (branch * out).astype(BF16)
        docat[0, j, pl.ds(0, rows), :] = out
        lines = jnp.zeros((rows, HEAD_DIM), F32)
        columns = []
        for i in (0, 1):
            h_at = 2 * j + i
            span = slice(h_at * HEAD_DIM, (h_at + 1) * HEAD_DIM)
            delta = jnp.sum(
                out[:, i * HEAD_DIM : (i + 1) * HEAD_DIM].astype(F32) * o_wide[:, span], axis=-1, keepdims=True
            )
            top = stats[:, h_at : h_at + 1]
            columns.append((top, delta))
            for at, value in ((i, top), (2 + i, delta)):
                for step in range(3):
                    part = value.astype(BF16).astype(F32)
                    value = value - part
                    lines = jnp.where(lane == 4 * step + at, part, lines)
        own_lines.append(columns)
        stat[pl.ds(0, rows), :] = lines
        stat[pl.ds(rows, 256 - rows), :] = jnp.zeros((256 - rows, HEAD_DIM), F32)
        docat[0, j, pl.ds(rows, 16), :] = stat[...].T[:16, :].astype(BF16)
    do_plane.start()
    b_plane.relay_last()
    q_plane.relay_last()

    for i in range(6):
        work[i] = jnp.zeros((rows, 256), F32)
    reach = -(-WINDOW // rows)
    below = lax.broadcasted_iota(jnp.int32, (rows, rows), 0)
    along = lax.broadcasted_iota(jnp.int32, (rows, rows), 1)

    def head_cut(h):
        return h // 2, slice((h % 2) * HEAD_DIM, (h % 2 + 1) * HEAD_DIM), slice(h * HEAD_DIM, (h + 1) * HEAD_DIM)

    def rows_of(m):
        return pl.ds(m * rows, rows)

    def query_side(m):
        apart = me - flip(me, m)

        @pl.when((apart >= 0) & (apart <= reach))
        def _():
            ahead = apart * rows + below - along
            allowed = (ahead >= 0) & (ahead < WINDOW)
            for h in range(4):
                side, two, span = head_cut(h)
                top, delta = own_lines[side][h % 2]
                k, do = kcat[rows_of(m), span], docat[0, side, pl.ds(0, rows), two]
                s = lax.dot_general(qcat[0, side, :, two], k, NT, preferred_element_type=F32)
                p = jnp.where(allowed, jnp.exp(s * scale - top), 0.0)
                dp = lax.dot_general(do, vcat[rows_of(m), span], NT, preferred_element_type=F32)
                ds = (p * (dp - delta) * scale).astype(BF16)
                work[side, :, two] += jnp.dot(ds, k, preferred_element_type=F32)

    def key_side(m):
        apart = me - flip(me, m)

        @pl.when((apart <= 0) & (apart >= -reach))
        def _():
            ahead = along - below - apart * rows
            allowed = (ahead >= 0) & (ahead < WINDOW)
            for h in range(4):
                side, two, span = head_cut(h)
                lines = docat[m, side, pl.ds(rows, 16), :].astype(F32)
                lines = (lines[0:4] + lines[4:8] + lines[8:12])[:, :rows]
                top, delta = lines[h % 2 : h % 2 + 1], lines[2 + h % 2 : 3 + h % 2]
                q, do = qcat[m, side, :, two], docat[m, side, pl.ds(0, rows), two]
                s = lax.dot_general(kcat[pl.ds(0, rows), span], q, NT, preferred_element_type=F32)
                p = jnp.where(allowed, jnp.exp(s * scale - top), 0.0)
                work[4 + side, :, two] += jnp.dot(p.astype(BF16), do, preferred_element_type=F32)
                dp = lax.dot_general(vcat[pl.ds(0, rows), span], do, NT, preferred_element_type=F32)
                ds = (p * (dp - delta) * scale).astype(BF16)
                work[2 + side, :, two] += jnp.dot(ds, q, preferred_element_type=F32)

    for m in range(4):
        query_side(m)
    do_plane.relay_first()
    for m in range(4, 8):
        query_side(m)
    do_plane.relay_second()
    do_plane.relay_last()
    d_plane.start()
    a_plane.start()
    do_plane.finish()
    q_plane.finish()
    for m in range(8):
        key_side(m)
    for j in range(8):
        two = slice((j % 2) * 256, (j % 2 + 1) * 256)
        if j < 4:
            made_j = turn(work[j], cosine, -sine)
            for i in (0, 1):
                cut[j, pl.ds(0, rows), i * HEAD_DIM : (i + 1) * HEAD_DIM] = made_j[i].astype(BF16)
        elif j < 6:
            cut[j, pl.ds(0, rows), :] = work[j].astype(BF16)
        else:
            cut[j, pl.ds(0, rows), :] = o_low[:, two]
    for j in range(6):
        for side in (0, 1):
            out = jnp.dot(cut[j, pl.ds(0, rows), :], w_a[order_a[j], side, pl.ds(0, 256), :], preferred_element_type=F32)
            columns = slice(side * HALF, (side + 1) * HALF)
            total[:, columns] = out if j == 0 else total[:, columns] + out
    for m in (1, 2, 3):
        piece(0, m).wait_send()
    scatter(2)
    for m in range(8):
        g_sent[m] = cut[slab_of(owners, 0, flip(me, m)), pl.ds(0, rows), :]
    keep(4, g_sent.at[0], g_all.at[0])
    for m in range(1, 8):
        straight(g_sent, g_all, 1, m).start()
    spread(2, total[:, quarter(0)])
    d_plane.relay_first()
    a_plane.relay_first()
    block_out[...] = gathered(3, h_out[:, quarter(0)] + b_own[...]).astype(BF16)

    for m in (1, 2, 3):
        whole(2, m).wait_recv()
    for m in range(4):
        total[:, quarter(m)] = z_sum[2, m].astype(F32)
    normed_grad = total[...]
    x = tokens[...].astype(F32)
    root = root_of(x)
    gain_one = jnp.sum(normed_grad * x * root, axis=0, keepdims=True)
    weighted = normed_grad * gains[0:1, :]
    inner = jnp.mean(weighted * x, axis=-1, keepdims=True)
    grad = root * weighted - x * (root * root * root) * inner
    for c in range(8):
        made[pl.ds(c * rows, rows), :] += grad[:, c * 256 : (c + 1) * 256]
    total[0:1, :] = gain_one
    for m in range(8):
        at = pl.multiple_of(flip(me, m) * 256, 256)
        gain_out[m, 0:1, :] = total[0:1, pl.ds(at, 256)]
    for c in range(8):
        keep(9 + c, made.at[pl.ds(c * rows, rows)], input_grad.at[:, pl.ds(c * 256, 256)])
    for m in range(1, 8):
        straight(gain_out, gain_in, 2, m).start()
    for one in (d_plane, a_plane):
        one.relay_second()
        one.relay_last()
    for m in range(1, 8):
        straight(gain_out, gain_in, 2, m).wait_recv()
    made = gain_out[0, 0:2, :]
    for m in range(1, 8):
        made += gain_in[m, 0:2, :]
    gain_grad[...] = made
    for one in (y_plane, b_plane, d_plane, a_plane):
        one.finish()
    line_end()
    for m in range(1, 8):
        straight(sent, z_all, 0, m).wait_recv()
        straight(g_sent, g_all, 1, m).wait_recv()
    for one in (
        w_a_plane, w_f_plane, kv_plane, q_plane, y_plane, b_plane, a_plane, d_plane, do_plane
    ):
        one.drain()
    for m in range(1, 8):
        straight(sent, z_all, 0, m).wait_send()
        straight(g_sent, g_all, 1, m).wait_send()
        straight(gain_out, gain_in, 2, m).wait_send()
    for m in (1, 2, 3):
        for which in (0, 1, 2):
            whole(which, m).wait_send()
        for which in (1, 2, 3):
            piece(which, m).wait_send()
    for i in kept:
        if i not in (0, 8):
            kept[i].wait()


def layer(owners, tokens, dy, own_gains, speeds, master, scale, branch):
    rows, width = tokens.shape
    array = jax.ShapeDtypeStruct
    dma = pltpu.SemaphoreType.DMA

    def low(*sizes):
        return pltpu.VMEM(sizes, BF16)

    def wide(*sizes):
        return pltpu.VMEM(sizes, F32)

    return pl.pallas_call(
        functools.partial(layer_kernel, rows, scale, branch),
        out_shape=[
            shape(rows, QUART),
            array((2, 256), F32),
            shape(rows, width, F32),
            array((2, 8, 2, rows, HALF), BF16),
            array((8, PACKED, 128), BF16),
            array((8, rows, 256), BF16),
            array((8, 2, rows, HALF), BF16),
            array((4, 8, 2, rows, 256), BF16),
        ],
        in_specs=[SM] + [VM] * 4 + [HB],
        out_specs=[VM] * 2 + [HB] * 6,
        scratch_shapes=[
            wide(2, width),
            low(rows, QUART),
            wide(rows, QUART),
            wide(rows, HEAD_DIM),
            low(2, rows, HALF),
            low(2, rows, HALF),
            low(8 * rows, QUART),
            low(8 * rows, QUART),
            low(8, 2, rows, 256),
            low(8, 2, rows + 16, 256),
            low(8, PACKED, 128),
            low(8, rows, 256),
            wide(SLAB - 256, width),
            low(8, 2, 272, HALF),
            low(8, 2, PAD, HALF),
            wide(8 * SLAB + 16, 256),
            low(8, PAD, 256),
            wide(rows, width),
            low(4, 3, rows, QUART),
            low(4, 3, rows, QUART),
            low(3, 4, rows, QUART),
            wide(rows, QUART),
            wide(rows, QUART),
            wide(8, rows, 256),
            low(2, rows, 256),
            wide(256, HEAD_DIM),
            wide(256, HEAD_DIM),
            wide(8, 8, 256),
            wide(8, 8, 256),
            dma((3,)),
            dma((17,)),
            dma((9, 8, 2)),
            dma((9, 8, 2)),
            dma((4, 4, 4)),
        ]
        + [dma((4, 8))] * 5
        + [dma((3, 2, 8))],
        compiler_params=pltpu.CompilerParams(
            collective_id=0, has_side_effects=True, vmem_limit_bytes=63 * 2**20
        ),
        cost_estimate=pl.CostEstimate(flops=2 * 10**10, bytes_accessed=60 * 2**20, transcendentals=0),
        name="layer",
    )(owners, tokens, dy, own_gains, speeds, master)


TILE = 256


def update_kernel(rows, branch, owners, basis, gain_grad, norm_gains, gain_first, gain_second, *rest):
    (zs, gs, acts, bs, dys), olds, through, rest = rest[:5], rest[5:8], rest[8:10], rest[10:]
    news, low_new, passed, gain_news, rest = rest[:4], rest[4], rest[5:7], rest[7:11], rest[11:]
    turned_g, turned_z, wide_basis, act, old, new, asem, osem, nsem = rest
    me, line = lax.axis_index("seq"), lax.axis_index("head")
    tile, tiles = pl.program_id(0), pl.num_programs(0)
    slot = tile % 2
    a_slab, f_slab = slab_of(owners, 0, me), slab_of(owners, 1, me)

    def columns_of(t):
        return pl.ds(pl.multiple_of(t * TILE, TILE), TILE)

    def spans(m):
        late = rows - 128
        return ((pl.ds(0, 128), pl.ds(m * 128, 128)), (pl.ds(128, late), pl.ds(8 * 128 + m * late, late)))

    def act_copies(t, kind, which):
        at = pl.ds(pl.multiple_of(lax.rem(t, HALF // TILE) * TILE, TILE), TILE)
        for m in range(8):
            if kind == 3:
                part = dys.at[lax.div(t, 2), m, lax.rem(t, 2)]
            elif kind == 2:
                part = bs.at[m, lax.div(t, HALF // TILE), :, at]
            else:
                part = acts.at[kind, m, lax.div(t, HALF // TILE), :, at]
            for source, target in spans(m):
                pltpu.make_async_copy(part.at[source], act.at[t % 2, which, target], asem.at[t % 2, which]).start()

    def act_wait(which):
        for m in range(8):
            for _, target in spans(m):
                part = act.at[slot, which, target]
                pltpu.make_async_copy(part, part, asem.at[slot, which]).wait()

    def fetch_acts(t):
        pl.when(a_slab < 6)(lambda: act_copies(t, 0, 0))
        pl.when(a_slab >= 6)(lambda: act_copies(t, 1, 0))
        pl.when(f_slab <= 5)(lambda: act_copies(t, 2, 1))
        pl.when(f_slab > 5)(lambda: act_copies(t, 3, 1))
        pl.when(f_slab == 5)(lambda: act_copies(t, 3, 2))

    def old_copy(i, t):
        return pltpu.make_async_copy(olds[i].at[:, 0, columns_of(t)], old.at[t % 2, i], osem.at[t % 2, i])

    def new_copy(i, t):
        return pltpu.make_async_copy(new.at[t % 2, i], news[i].at[:, 0, columns_of(t)], nsem.at[t % 2, i])

    def fetch(t):
        fetch_acts(t)
        for i in range(3):
            old_copy(i, t).start()

    @pl.when(tile == 0)
    def _():
        fetch(0)
        for i in (0, 1):
            passed[i][...] = through[i][...]
        made = gain_grad[...]
        one = BETA_FIRST * gain_first[...] + (1.0 - BETA_FIRST) * made
        two = BETA_SECOND * gain_second[...] + (1.0 - BETA_SECOND) * made * made
        gain_news[0][...] = made
        gain_news[1][...] = one
        gain_news[2][...] = two
        gain_news[3][...] = norm_gains[...] - GAIN_RATE * (one / (1.0 - BETA_FIRST**ADAM_STEP)) / (
            jnp.sqrt(two / (1.0 - BETA_SECOND**ADAM_STEP)) + ADAM_EPS
        )
        wide_basis[...] = jnp.zeros_like(wide_basis)
        lane = lax.broadcasted_iota(jnp.int32, (PAD // 2, 128), 1)
        for m in range(8):
            turned_g[:, m * 128 : (m + 1) * 128] = gs[m, pl.ds(0, 128), :].T
            turned_z[:, m * 128 : (m + 1) * 128] = zs[m, pl.ds(0, PAD), :]
            if m % 2 == 0:
                at = 8 * 128 + m * 64
                late = jnp.concatenate([gs[m, pl.ds(128, 64), :], gs[m + 1, pl.ds(128, 64), :]], axis=0)
                turned_g[:, at : at + 128] = late.T
                even, odd = (zs[m + i, pl.ds(PAD, PAD // 2), :].astype(F32) for i in (0, 1))
                upper = jnp.where(lane < 64, even, pltpu.roll(odd, 64, 1))
                lower = jnp.where(lane < 64, pltpu.roll(even, 64, 1), odd)
                turned_z[:, at : at + 128] = jnp.concatenate([upper, lower], axis=0).astype(BF16)

    pl.when(tile + 1 < tiles)(lambda: fetch(tile + 1))

    @pl.when(tile >= 2)
    def _():
        for i in range(4):
            new_copy(i, tile - 2).wait()

    grad, first_new, second_new, master_new = (new.at[slot, i] for i in range(4))
    first, second, master = (old.at[slot, i] for i in range(3))

    def ffn_rows(which):
        return jnp.dot(turned_z[...], act[slot, which], preferred_element_type=F32)[:SLAB]

    act_wait(0)
    factor = jnp.where(a_slab < 6, 1.0, branch)
    grad[pl.ds(0, 256), :] = factor * jnp.dot(turned_g[...], act[slot, 0], preferred_element_type=F32)
    act_wait(1)
    grad[pl.ds(256, SLAB), :] = ffn_rows(1)
    first_of_down = 2 * UNITS - f_slab * SLAB

    @pl.when(f_slab == 5)
    def _():
        act_wait(2)
        row = lax.broadcasted_iota(jnp.int32, (SLAB, 1), 0)
        grad[pl.ds(256, SLAB), :] = jnp.where(row < first_of_down, grad[pl.ds(256, SLAB), :], ffn_rows(2))

    for i in range(3):
        old_copy(i, tile).wait()
    row = lax.broadcasted_iota(jnp.int32, (256 + SLAB, 1), 0)
    rate = jnp.where((row < 256) | (row - 256 < first_of_down), 0.5 * (2 * HALF) ** (-0.5), 0.5 * FF ** (-0.5))
    for b in range(TILE // HEAD_DIM):
        cut = slice(b * HEAD_DIM, (b + 1) * HEAD_DIM)
        wide_basis[cut, cut] = basis[b].astype(BF16)
    turned = jnp.dot(grad[...].astype(BF16), wide_basis[...], preferred_element_type=F32)
    one = BETA_FIRST * first[...] + (1.0 - BETA_FIRST) * turned
    two = BETA_SECOND * second[...] + (1.0 - BETA_SECOND) * turned * turned
    first_new[...] = one
    second_new[...] = two
    adam = (one / (1.0 - BETA_FIRST**ADAM_STEP)) / (jnp.sqrt(two / (1.0 - BETA_SECOND**ADAM_STEP)) + ADAM_EPS)
    back = lax.dot_general(adam.astype(BF16), wide_basis[...], NT, preferred_element_type=F32)
    before = master[...]
    after = before - rate * (back + DECAY_RATE * before)
    master_new[...] = after
    low_new[...] = after.astype(BF16)
    for i in range(4):
        new_copy(i, tile).start()

    @pl.when(tile == tiles - 1)
    def _():
        for t in (tile - 1, tile):
            for i in range(4):
                new_copy(i, t).wait()


def update(owners, basis, small, zs, gs, acts, bs, dys, olds, through, branch):
    rows = gs.shape[1]
    height, _, width = olds[0].shape

    def whole(array):
        return pl.BlockSpec(array.shape, lambda i: (0,) * array.ndim)

    tall = pl.BlockSpec((height, TILE), lambda i: (0, i))
    per = TILE // HEAD_DIM
    gains = [shape(*array.shape, F32) for array in small]
    return call(
        functools.partial(update_kernel, rows, branch),
        [jax.ShapeDtypeStruct(olds[0].shape, F32)] * 4
        + [shape(height, width)]
        + [jax.ShapeDtypeStruct(array.shape, array.dtype) for array in through]
        + gains,
        [SM, pl.BlockSpec((per, HEAD_DIM, HEAD_DIM), lambda i: (i, 0, 0))]
        + [whole(array) for array in small]
        + [whole(zs), whole(gs)]
        + [HB] * 6
        + [whole(array) for array in through],
        [owners, basis, *small, zs, gs, acts, bs, dys, *olds, *through],
        [
            pltpu.VMEM((256, 8 * rows), BF16),
            pltpu.VMEM((PAD, 8 * rows), BF16),
            pltpu.VMEM((TILE, TILE), BF16),
            pltpu.VMEM((2, 3, 8 * rows, TILE), BF16),
            pltpu.VMEM((2, 3, height, TILE), F32),
            pltpu.VMEM((2, 4, height, TILE), F32),
            pltpu.SemaphoreType.DMA((2, 3)),
            pltpu.SemaphoreType.DMA((2, 3)),
            pltpu.SemaphoreType.DMA((2, 4)),
        ],
        out_specs=[HB] * 4 + [tall] + [whole(array) for array in through] + [whole(array) for array in small],
        grid=(width // TILE,),
        flops=2 * 8 * rows * height * width,
        moved=70 * 2**20,
    )


def plane_mesh(
    tokens,
    cotangent,
    owners,
    master,
    first_moment,
    second_moment,
    eigenbases,
    norm_gains,
    gain_first,
    gain_second,
):
    rows, width = tokens.shape
    scale = HEAD_DIM ** (-0.5)
    branch = (WINDOW / 3.0) ** 0.5
    half = HEAD_DIM // 2
    speeds = ROPE_BASE ** (-jnp.arange(half, dtype=F32) / half)
    speeds = jnp.concatenate([speeds, speeds])[None, :]
    tall = [array.reshape(array.shape[2], 1, width) for array in (first_moment, second_moment, master)]
    block_out, gain_grad, input_grad, acts, zs, gs, bs, dys = layer(
        owners, tokens, cotangent, norm_gains, speeds, tall[2], scale, branch
    )
    (
        grad, first_new, second_new, master_new, low_new, block_out, input_grad, gain_grad, gain_first_new,
        gain_second_new, gain_new,
    ) = update(
        owners, eigenbases[0, 0], [gain_grad, norm_gains, gain_first, gain_second], zs, gs, acts, bs, dys, tall,
        [block_out, input_grad], branch,
    )
    whole = (1, 1, *tall[0].shape[::2])
    return (
        block_out,
        input_grad,
        grad.reshape(whole),
        first_new.reshape(whole),
        second_new.reshape(whole),
        master_new.reshape(whole),
        low_new[None, None],
        gain_grad,
        gain_first_new,
        gain_second_new,
        gain_new,
    )


def solution(mesh):
    in_specs = (
        P("seq", None),
        P("seq", None),
        P(),
        P("head", "seq", None, None),
        P("head", "seq", None, None),
        P("head", "seq", None, None),
        P("head", "seq", None, None, None),
        P(None, "seq"),
        P(None, "seq"),
        P(None, "seq"),
    )
    out_specs = (
        P("seq", "head"),
        P("seq", None),
        P("head", "seq", None, None),
        P("head", "seq", None, None),
        P("head", "seq", None, None),
        P("head", "seq", None, None),
        P("head", "seq", None, None),
        P(None, "seq"),
        P(None, "seq"),
        P(None, "seq"),
        P(None, "seq"),
    )
    plane = mesh.shape["seq"] == 8 and mesh.shape["head"] == 4
    return jax.shard_map(
        plane_mesh if plane else any_mesh, mesh=mesh, in_specs=in_specs, out_specs=out_specs, check_vma=False
    )
```

```python
import functools

import jax
import jax.numpy as jnp
from jax import lax
from jax.experimental import pallas as pl
from jax.experimental.pallas import tpu as pltpu
from jax.sharding import PartitionSpec as P

HEADS = 16
HEAD_DIM = 128
FF = 5504
WINDOW = 1024
ADAM_STEP = 5


EPS_NORM = 1e-05
BETA_FIRST = 0.5
BETA_SECOND = 0.6
ADAM_EPS = 1e-08
DECAY_RATE = 0.1
GAIN_RATE = 0.25
ROPE_BASE = 10000.0
NEGATIVE = -1e30
PRECISE = lax.Precision.HIGHEST

BF16 = jnp.bfloat16
F32 = jnp.float32


def passed_along(shard, axis, by):
    devices = lax.axis_size(axis)
    pairs = [(i, i + by) for i in range(devices) if 0 <= i + by < devices]
    return lax.ppermute(shard, axis, pairs)


def inverse_order(owner_row):
    places = jnp.arange(owner_row.shape[0], dtype=jnp.int32)
    matches = (owner_row[:, None] == places[None, :]).astype(jnp.int32)
    return jnp.sum(matches * places[:, None], axis=0)


def kind_rates(kinds, width):
    wide = width ** (-0.5)
    spreads = jnp.array([wide, wide, wide, wide, wide, wide, FF ** (-0.5)], jnp.float32)
    matches = (kinds[..., None] == jnp.arange(7, dtype=jnp.int32)).astype(jnp.float32)
    return 0.5 * jnp.sum(matches * spreads, axis=-1)


def angles(positions):
    half_dim = HEAD_DIM // 2
    frequencies = ROPE_BASE ** (-jnp.arange(half_dim, dtype=jnp.float32) / half_dim)
    turning = positions[:, None] * frequencies[None, :]
    return (jnp.cos(turning)[:, None, :], jnp.sin(turning)[:, None, :])


def rotate(vectors, cosine, sine):
    half_dim = vectors.shape[-1] // 2
    former = vectors[..., :half_dim]
    latter = vectors[..., half_dim:]
    return jnp.concatenate(
        [former * cosine - latter * sine, latter * cosine + former * sine], axis=-1
    )


def inverse_rms(vectors):
    return lax.rsqrt(jnp.mean(vectors * vectors, axis=-1, keepdims=True) + EPS_NORM)


def norm_back(grad_normed, inputs, rms_values, gain_row):
    weighted = grad_normed * gain_row
    inner = jnp.mean(weighted * inputs, axis=-1, keepdims=True)
    input_part = rms_values * weighted - inputs * rms_values**3 * inner
    return (input_part, jnp.sum(grad_normed * inputs * rms_values, axis=0))


def any_mesh(
    tokens,
    cotangent,
    owners,
    master,
    first_moment,
    second_moment,
    eigenbases,
    norm_gains,
    gain_first,
    gain_second,
):
    tok_rows, width = tokens.shape
    seq_devices = lax.axis_size("seq")
    head_devices = lax.axis_size("head")
    seq_place = lax.axis_index("seq")
    head_place = lax.axis_index("head")
    slab_rows = master.shape[2]
    attn_slab = 4 * width // (head_devices * seq_devices)
    ffn_slab = slab_rows - attn_slab
    head_width = width // head_devices
    ffn_width = FF // head_devices
    local_heads = HEADS // head_devices
    score_scale = HEAD_DIM ** (-0.5)
    branch_scale = (WINDOW / 3.0) ** 0.5
    inverse_attn = inverse_order(owners[0])
    inverse_ffn = inverse_order(owners[1])
    master_low = master[0, 0].astype(jnp.bfloat16)
    gathered, gains_all = (
        lax.all_gather(master_low, "seq", axis=0, tiled=True),
        lax.all_gather(norm_gains.astype(jnp.bfloat16), "seq", axis=1, tiled=True),
    )
    gathered = gathered.reshape(seq_devices, slab_rows, width)
    attn_rows = jnp.take(gathered[:, :attn_slab], owners[0], axis=0).reshape(4 * head_width, width)
    ffn_rows = jnp.take(gathered[:, attn_slab:], owners[1], axis=0).reshape(3 * ffn_width, width)
    w_query = attn_rows[:head_width]
    w_key = attn_rows[head_width : 2 * head_width]
    w_value = attn_rows[2 * head_width : 3 * head_width]
    w_out = attn_rows[3 * head_width :]
    w_gate = ffn_rows[:ffn_width]
    w_up = ffn_rows[ffn_width : 2 * ffn_width]
    w_down = ffn_rows[2 * ffn_width :]
    gain_one = gains_all[0].astype(jnp.float32)
    gain_two = gains_all[1].astype(jnp.float32)
    inputs = tokens.astype(jnp.float32)
    rms_one = inverse_rms(inputs)
    normed_one = (inputs * rms_one * gain_one).astype(jnp.bfloat16)
    positions = (seq_place * tok_rows + jnp.arange(tok_rows, dtype=jnp.int32)).astype(jnp.float32)
    cosine, sine = angles(positions)
    head_shape = (tok_rows, local_heads, HEAD_DIM)

    def project(weight_rows):
        return jnp.einsum("td,id->ti", normed_one, weight_rows, preferred_element_type=jnp.float32)

    queries = rotate(project(w_query).reshape(head_shape), cosine, sine).astype(jnp.bfloat16)
    keys_own = rotate(project(w_key).reshape(head_shape), cosine, sine).astype(jnp.bfloat16)
    values_own = project(w_value).reshape(head_shape).astype(jnp.bfloat16)
    hop_total = -(-WINDOW // tok_rows)
    hop_sizes = [
        min(tok_rows, WINDOW - (hop_index - 1) * tok_rows) for hop_index in range(1, hop_total + 1)
    ]
    halo_keys = []
    halo_values = []
    for hop_index in range(hop_total, 0, -1):
        hop_rows = hop_sizes[hop_index - 1]
        far_keys, far_values = passed_along(
            (keys_own[tok_rows - hop_rows :], values_own[tok_rows - hop_rows :]), "seq", hop_index
        )
        halo_keys.append(far_keys)
        halo_values.append(far_values)
    keys_all = jnp.concatenate(halo_keys + [keys_own], axis=0)
    values_all = jnp.concatenate(halo_values + [values_own], axis=0)
    row_ids = jnp.arange(tok_rows, dtype=jnp.int32)[:, None]
    col_ids = jnp.arange(WINDOW + tok_rows, dtype=jnp.int32)[None, :]
    allowed = (
        (col_ids > row_ids)
        & (col_ids <= row_ids + WINDOW)
        & (seq_place * tok_rows - WINDOW + col_ids >= 0)
    )

    def scores_of():
        raw = jnp.einsum("thd,chd->htc", queries, keys_all, preferred_element_type=jnp.float32)
        return jnp.where(allowed[None], raw * score_scale, NEGATIVE)

    scores = scores_of()
    row_top = jnp.max(scores, axis=-1, keepdims=True)
    exp_scores = jnp.exp(scores - row_top)
    exp_total = jnp.sum(exp_scores, axis=-1, keepdims=True)
    soft_low = (exp_scores / exp_total).astype(jnp.bfloat16)
    log_total = row_top + jnp.log(exp_total)
    attended = jnp.einsum("htc,chd->thd", soft_low, values_all, preferred_element_type=jnp.float32)
    attended_low = attended.reshape(tok_rows, head_width).astype(jnp.bfloat16)
    attn_part = branch_scale * jnp.dot(attended_low, w_out, preferred_element_type=jnp.float32)
    hidden_one = inputs + lax.psum(attn_part, "head")
    rms_two = inverse_rms(hidden_one)
    normed_two = (hidden_one * rms_two * gain_two).astype(jnp.bfloat16)
    gate_pre = jnp.einsum("td,fd->tf", normed_two, w_gate, preferred_element_type=jnp.float32)
    up_pre = jnp.einsum("td,fd->tf", normed_two, w_up, preferred_element_type=jnp.float32)
    sigma = jax.nn.sigmoid(gate_pre)
    hidden_low = (gate_pre * sigma * up_pre).astype(jnp.bfloat16)
    ffn_part = jnp.dot(hidden_low, w_down, preferred_element_type=jnp.float32)
    ffn_share = lax.psum_scatter(ffn_part, "head", scatter_dimension=1, tiled=True)
    share_width = width // head_devices
    residual_share = lax.dynamic_slice_in_dim(hidden_one, head_place * share_width, share_width, 1)
    block_out = (residual_share + ffn_share).astype(jnp.bfloat16)
    grad_out_f = cotangent.astype(jnp.float32)
    hidden_grad = jnp.einsum("td,fd->tf", cotangent, w_down, preferred_element_type=jnp.float32)
    silu_grad = sigma * (1.0 + gate_pre * (1.0 - sigma))
    gate_grad = (hidden_grad * up_pre * silu_grad).astype(jnp.bfloat16)
    up_grad = (hidden_grad * gate_pre * sigma).astype(jnp.bfloat16)
    down_grad = jnp.einsum("tf,td->fd", hidden_low, cotangent, preferred_element_type=jnp.float32)
    gate_w_grad = jnp.einsum("tf,td->fd", gate_grad, normed_two, preferred_element_type=jnp.float32)
    up_w_grad = jnp.einsum("tf,td->fd", up_grad, normed_two, preferred_element_type=jnp.float32)
    ffn_rows_grad = jnp.concatenate([gate_w_grad, up_w_grad, down_grad], axis=0)
    ffn_owner = jnp.take(ffn_rows_grad.reshape(seq_devices, ffn_slab, width), inverse_ffn, axis=0)
    normed_two_part = jnp.einsum(
        "tf,fd->td", gate_grad, w_gate, preferred_element_type=jnp.float32
    ) + jnp.einsum("tf,fd->td", up_grad, w_up, preferred_element_type=jnp.float32)
    normed_two_share = lax.psum_scatter(normed_two_part, "head", scatter_dimension=1, tiled=True)
    normed_two_grad = lax.all_gather(normed_two_share, "head", axis=1, tiled=True)
    back_two, gain_two_grad = norm_back(normed_two_grad, hidden_one, rms_two, gain_two)
    hidden_one_grad = grad_out_f + back_two
    hidden_grad_low = hidden_one_grad.astype(jnp.bfloat16)
    attended_grad = branch_scale * jnp.einsum(
        "td,id->ti", hidden_grad_low, w_out, preferred_element_type=jnp.float32
    )
    attended_grad = attended_grad.reshape(head_shape).astype(jnp.bfloat16)
    soft_again = jnp.exp(scores_of() - log_total)
    soft_grad = jnp.einsum(
        "thd,chd->htc", attended_grad, values_all, preferred_element_type=jnp.float32
    )
    inner_sum = jnp.sum(soft_again * soft_grad, axis=-1, keepdims=True)
    score_grad = (soft_again * (soft_grad - inner_sum) * score_scale).astype(jnp.bfloat16)
    query_grad_turned = jnp.einsum(
        "htc,chd->thd", score_grad, keys_all, preferred_element_type=jnp.float32
    )
    key_grad_all = jnp.einsum(
        "htc,thd->chd", score_grad, queries, preferred_element_type=jnp.float32
    )
    value_grad_all = jnp.einsum(
        "htc,thd->chd", soft_low, attended_grad, preferred_element_type=jnp.float32
    )
    key_grad_own = key_grad_all[WINDOW:]
    value_grad_own = value_grad_all[WINDOW:]
    start_at = 0
    for hop_index in range(hop_total, 0, -1):
        hop_rows = hop_sizes[hop_index - 1]
        back_keys, back_values = passed_along(
            (
                key_grad_all[start_at : start_at + hop_rows],
                value_grad_all[start_at : start_at + hop_rows],
            ),
            "seq",
            -hop_index,
        )
        key_grad_own = key_grad_own.at[tok_rows - hop_rows :].add(back_keys)
        value_grad_own = value_grad_own.at[tok_rows - hop_rows :].add(back_values)
        start_at = start_at + hop_rows
    query_grad = (
        rotate(query_grad_turned, cosine, -sine).reshape(tok_rows, head_width).astype(jnp.bfloat16)
    )
    key_grad = (
        rotate(key_grad_own, cosine, -sine).reshape(tok_rows, head_width).astype(jnp.bfloat16)
    )
    value_grad = value_grad_own.reshape(tok_rows, head_width).astype(jnp.bfloat16)

    def input_part(row_grad, weight_rows):
        return jnp.einsum("ti,id->td", row_grad, weight_rows, preferred_element_type=jnp.float32)

    normed_one_part = (
        input_part(query_grad, w_query)
        + input_part(key_grad, w_key)
        + input_part(value_grad, w_value)
    )
    normed_one_share = lax.psum_scatter(normed_one_part, "head", scatter_dimension=1, tiled=True)
    normed_one_grad = lax.all_gather(
        normed_one_share.astype(jnp.bfloat16), "head", axis=1, tiled=True
    ).astype(normed_one_share.dtype)
    back_one, gain_one_grad = norm_back(normed_one_grad, inputs, rms_one, gain_one)
    input_grad = hidden_one_grad + back_one
    gain_grads = jnp.stack([gain_one_grad, gain_two_grad])

    def rows_grad(row_grad):
        return jnp.einsum("ti,td->id", row_grad, normed_one, preferred_element_type=jnp.float32)

    out_w_grad = branch_scale * jnp.einsum(
        "ti,td->id", attended_low, hidden_grad_low, preferred_element_type=jnp.float32
    )
    attn_rows_grad = jnp.concatenate(
        [rows_grad(query_grad), rows_grad(key_grad), rows_grad(value_grad), out_w_grad], axis=0
    )
    attn_owner = jnp.take(
        attn_rows_grad.reshape(seq_devices, attn_slab, width), inverse_attn, axis=0
    )
    owner_rows = jnp.concatenate([attn_owner, ffn_owner], axis=1).reshape(
        seq_devices * slab_rows, width
    )
    reduced, gain_reduced = (
        lax.psum_scatter(owner_rows, "seq", scatter_dimension=0, tiled=True),
        lax.psum_scatter(gain_grads, "seq", scatter_dimension=1, tiled=True),
    )
    attn_kinds = (
        inverse_attn[seq_place] * attn_slab + jnp.arange(attn_slab, dtype=jnp.int32)
    ) // head_width
    ffn_kinds = (
        4 + (inverse_ffn[seq_place] * ffn_slab + jnp.arange(ffn_slab, dtype=jnp.int32)) // ffn_width
    )
    row_rates = kind_rates(jnp.concatenate([attn_kinds, ffn_kinds]), width)[:, None]
    basis = eigenbases[0, 0]
    block_size = basis.shape[-1]
    split_shape = (slab_rows, width // block_size, block_size)
    turned = jnp.einsum(
        "rbk,bkl->rbl", reduced.reshape(split_shape), basis, precision=PRECISE
    ).reshape(slab_rows, width)
    first_new = BETA_FIRST * first_moment[0, 0] + (1.0 - BETA_FIRST) * turned
    second_new = BETA_SECOND * second_moment[0, 0] + (1.0 - BETA_SECOND) * turned * turned
    adam_dir = (
        first_new
        / (1.0 - BETA_FIRST**ADAM_STEP)
        / (jnp.sqrt(second_new / (1.0 - BETA_SECOND**ADAM_STEP)) + ADAM_EPS)
    )
    backward_dir = jnp.einsum(
        "rbl,bkl->rbk", adam_dir.reshape(split_shape), basis, precision=PRECISE
    ).reshape(slab_rows, width)
    master_old = master[0, 0]
    master_new = master_old - row_rates * (backward_dir + DECAY_RATE * master_old)
    gain_first_new = BETA_FIRST * gain_first + (1.0 - BETA_FIRST) * gain_reduced
    gain_second_new = BETA_SECOND * gain_second + (1.0 - BETA_SECOND) * gain_reduced * gain_reduced
    gain_new = norm_gains - GAIN_RATE * (gain_first_new / (1.0 - BETA_FIRST**ADAM_STEP)) / (
        jnp.sqrt(gain_second_new / (1.0 - BETA_SECOND**ADAM_STEP)) + ADAM_EPS
    )
    return (
        block_out,
        input_grad,
        reduced[None, None],
        first_new[None, None],
        second_new[None, None],
        master_new[None, None],
        master_new.astype(jnp.bfloat16)[None, None],
        gain_reduced,
        gain_first_new,
        gain_second_new,
        gain_new,
    )


SLAB = 516
PAD = 528
HALF = 1024
QUART = 512
PACKED = 800
UNITS = 1376
NT = (((1,), (1,)), ((), ()))
TN = (((0,), (0,)), ((), ()))


VM = pl.BlockSpec(memory_space=pltpu.VMEM)
SM = pl.BlockSpec(memory_space=pltpu.SMEM)
HB = pl.BlockSpec(memory_space=pl.ANY)


def shape(rows, columns, dtype=BF16):
    return jax.ShapeDtypeStruct((rows, columns), dtype)


def call(kernel, outs, specs, args, scratch=(), flops=0, moved=0, out_specs=None, grid=None):
    extra = {} if grid is None else {"grid": grid}
    return pl.pallas_call(
        kernel,
        out_shape=outs,
        in_specs=specs,
        out_specs=[VM] * len(outs) if out_specs is None else out_specs,
        scratch_shapes=list(scratch),
        compiler_params=pltpu.CompilerParams(vmem_limit_bytes=56 * 2**20),
        cost_estimate=pl.CostEstimate(flops=flops, bytes_accessed=moved, transcendentals=0),
        name=getattr(kernel, "func", kernel).__name__,
        **extra,
    )(*args)


def root_of(values):
    return lax.rsqrt(jnp.mean(values * values, axis=-1, keepdims=True) + EPS_NORM)


def turn(values, cosine, sine):
    parts = []
    for h in range(values.shape[1] // HEAD_DIM):
        v = values[:, h * HEAD_DIM : (h + 1) * HEAD_DIM]
        parts.append(v * cosine + pltpu.roll(v, HEAD_DIM // 2, 1) * sine)
    return parts


MESH = pl.DeviceIdType.MESH


def flip(index, mask):
    for bit in (1, 2, 4):
        if mask & bit:
            index = index + bit - 2 * bit * lax.rem(lax.div(index, bit), 2)
    return index


def twist(left, right):
    out = 0
    for bit in (1, 2, 4):
        out = out + bit * lax.rem(lax.rem(lax.div(left, bit), 2) + lax.rem(lax.div(right, bit), 2), 2)
    return out


def slab_of(owners, kind, device):
    found = 0
    for j in range(8):
        found = jnp.where(owners[kind, j] == device, j, found)
    return found


class Plane:
    def __init__(self, at, sent, got, me, line):
        self.at, self.sent, self.got, self.me, self.line = at, sent, got, me, line

    def copy(self, src, dst, side, hop_mask):
        return pltpu.make_async_remote_copy(
            src_ref=self.at(src, side),
            dst_ref=self.at(dst, side),
            send_sem=self.sent.at[dst, side],
            recv_sem=self.got.at[dst, side],
            device_id=(flip(self.me, hop_mask), self.line),
            device_id_type=MESH,
        )

    def start_first(self):
        for mask, side in ((2, 0), (4, 1)):
            self.copy(0, mask, side, mask).start()
        for side in (0, 1):
            self.copy(0, 1, side, 1).start()

    def start_second(self):
        for mask, side in ((2, 1), (4, 0)):
            self.copy(0, mask, side, mask).start()

    def start(self):
        self.start_first()
        self.start_second()

    def arrive(self, mask, side):
        self.copy(mask, mask, side, 1).wait_recv()

    def twin(self, mask, side):
        self.copy(mask, mask + 1, side, 1).start()

    def relay_first(self):
        for mask, side in ((2, 0), (4, 1)):
            self.arrive(mask, side)
            self.copy(mask, 6, side, 6 - mask).start()
            self.twin(mask, side)

    def relay_second(self):
        for mask, side in ((2, 1), (4, 0)):
            self.arrive(mask, side)
            self.twin(mask, side)

    def relay_last(self):
        for side in (0, 1):
            self.arrive(6, side)
            self.twin(6, side)

    def finish(self):
        for mask in (1, 3, 5, 7):
            for side in (0, 1):
                self.arrive(mask, side)

    def drain(self, masks=range(1, 8)):
        for mask in masks:
            for side in (0, 1):
                self.copy(0, mask, side, 1).wait_send()


def line_copy(src, dst, sent, got, m, me, line):
    return pltpu.make_async_remote_copy(
        src_ref=src,
        dst_ref=dst,
        send_sem=sent.at[m],
        recv_sem=got.at[m],
        device_id=(me, flip(line, m)),
        device_id_type=MESH,
    )


def greet(me, line, plane_masks, line_masks):
    barrier = pltpu.get_barrier_semaphore()
    for mask in plane_masks:
        pl.semaphore_signal(barrier, inc=1, device_id=(flip(me, mask), line), device_id_type=MESH)
    for mask in line_masks:
        pl.semaphore_signal(barrier, inc=1, device_id=(me, flip(line, mask)), device_id_type=MESH)
    return lambda: pl.semaphore_wait(barrier, len(plane_masks) + len(line_masks))


def layer_kernel(
    rows, scale, branch,
    owners, tokens, dy, own_gains, speeds, master,
    block_out, gain_grad, input_grad, acts, z_all, g_all, b_all, dy_all,
    gains, o_low, o_wide, stats, a_low, b_low, kcat, vcat, qcat, docat, sent, g_sent, wide, w_a, w_f, made, cut,
    total, z_out, z_in, z_sum, line_out, line_in, b_own, work, dy_own, stat_l, stat_r, gain_out, gain_in,
    sem_w, sem_k, plane_sent, plane_got, z_sems, line_sems, sum_sems, r_up, r_down, r_got, t_sent, t_got, a2a_sems,
):
    me, line = lax.axis_index("seq"), lax.axis_index("head")
    ready = greet(me, line, range(1, 8), (1, 2, 3))
    order_a, order_f = ([twist(owners[kind, j], me) for j in range(8)] for kind in (0, 1))
    d_low = a_low
    h_out = wide.at[pl.ds(0, rows)]
    kept = {}

    def keep(i, src, dst):
        kept[i] = pltpu.make_async_copy(src, dst, sem_k.at[i])
        kept[i].start()

    def plane(i, at):
        return Plane(at, plane_sent.at[i], plane_got.at[i], me, line)

    w_a_plane = plane(0, lambda m, s: w_a.at[m, s] if s else w_a.at[m, s, pl.ds(0, 256)])
    w_f_plane = plane(1, lambda m, s: w_f.at[m, s])
    kv_plane = plane(2, lambda m, s: (kcat, vcat)[s].at[pl.ds(m * rows, rows)])
    q_plane = plane(3, lambda m, s: qcat.at[m, s])
    y_plane = plane(4, lambda m, s: dy_own.at[s] if m == 0 else dy_all.at[line, m, s])
    b_plane = plane(5, lambda m, s: b_low.at[s] if m == 0 else b_all.at[m, s])
    a_plane = plane(6, lambda m, s: acts.at[0, m, s])
    d_plane = plane(7, lambda m, s: d_low.at[s] if m == 0 else acts.at[1, m, s])
    do_plane = plane(8, lambda m, s: docat.at[m, s])

    def straight(src, dst, which, m):
        return pltpu.make_async_remote_copy(
            src_ref=src.at[m],
            dst_ref=dst.at[m],
            send_sem=a2a_sems.at[which, 0, m],
            recv_sem=a2a_sems.at[which, 1, m],
            device_id=(flip(me, m), line),
            device_id_type=MESH,
        )

    def quarter(m):
        return pl.ds(pl.multiple_of(flip(line, m) * QUART, QUART), QUART)

    def columns_of(q, c):
        return pl.ds(q * QUART + c * 256, 256)

    def partial(which, right, q, c):
        way, at = (0, q - 1) if right else (1, q)
        return pltpu.make_async_remote_copy(
            src_ref=line_out.at[way, at, c],
            dst_ref=line_in.at[which % 2, way, at, c],
            send_sem=line_sems.at[which, 0, way, at, c],
            recv_sem=line_sems.at[which, 1, way, at, c],
            device_id=(me, line + 1 if right else line - 1),
            device_id_type=MESH,
        )

    def summed(which, right, q, c):
        way = 0 if right else 1
        return pltpu.make_async_remote_copy(
            src_ref=z_sum.at[which, q, c],
            dst_ref=z_sum.at[which, q, c],
            send_sem=sum_sems.at[which, way, q, c],
            recv_sem=sum_sems.at[which, 2, q, c],
            device_id=(me, line + 1 if right else line - 1),
            device_id_type=MESH,
        )

    def pass_on(which, right, q, c, first):
        way, at = (0, q - 1) if right else (1, q)
        value = total[:, columns_of(q, c)]
        if not first:
            partial(which, right, q, c).wait_recv()
            value += line_in[which % 2, way, at, c].astype(F32)
        line_out[way, at, c] = value.astype(BF16)
        partial(which, right, q, c).start()

    ways = ((True, (3, 2, 1)), (False, (0, 1, 2)))

    def line_post(which):
        for c in (0, 1):
            for right, order in ways:

                @pl.when(line == (0 if right else 3))
                def _():
                    for q in order:
                        pass_on(which, right, q, c, True)

    merges = {1: ((True, 3), (True, 2), (False, 0)), 2: ((False, 0), (False, 1), (True, 3))}
    shares = {
        0: ((False, 1), (False, 2), (False, 3)),
        1: ((False, 2), (True, 0), (False, 3)),
        2: ((True, 1), (False, 3), (True, 0)),
        3: ((True, 2), (True, 1), (True, 0)),
    }

    def line_merge(which, chores=()):
        chores = list(chores)
        for c in (0, 1):
            for step in range(3):
                for here, order in merges.items():

                    @pl.when(line == here)
                    def _():
                        pass_on(which, *order[step], c, False)

                if chores:
                    chores.pop(0)()
            for q in range(4):

                @pl.when(line == q)
                def _():
                    value = total[:, columns_of(q, c)]
                    for right, _ in ways:
                        if q != (0 if right else 3):
                            way, at = (0, q - 1) if right else (1, q)
                            partial(which, right, q, c).wait_recv()
                            value += line_in[which % 2, way, at, c].astype(F32)
                    z_sum[which, q, c] = value.astype(BF16)
                    for right, _ in ways:
                        if q != (3 if right else 0):
                            summed(which, right, q, c).start()

            if chores:
                chores.pop(0)()
        for chore in chores:
            chore()

    def line_share(which, chores=()):
        chores = list(chores)
        for c in (0, 1):
            for step in range(3):
                for here, order in shares.items():
                    right, q = order[step]

                    @pl.when(line == here)
                    def _():
                        summed(which, right, q, c).wait_recv()
                        if here != (3 if right else 0):
                            summed(which, right, q, c).start()

                if chores:
                    chores.pop(0)()
        for chore in chores:
            chore()

    def line_sent(which):
        for c in (0, 1):
            for right, order in ways:
                for q in order:

                    @pl.when(line < q if right else line > q)
                    def _():
                        partial(which, right, q, c).wait_send()

    def line_all_sent(which):
        for c in (0, 1):
            for q in range(4):
                for right, _ in ways:

                    @pl.when((line >= q) & (line < 3) if right else (line <= q) & (line > 0))
                    def _():
                        summed(which, right, q, c).wait_send()

    def gather_sum(which, out):
        for q in range(4):
            for c in (0, 1):
                out[:, columns_of(q, c)] = z_sum[which, q, c].astype(F32)

    def b_piece(m):
        return line_copy(z_out.at[m - 1], z_in.at[m - 1], z_sems.at[0], z_sems.at[1], m, me, line)

    def along_line(quarter_index, m, up):
        return pltpu.make_async_remote_copy(
            src_ref=dy_all.at[quarter_index, m],
            dst_ref=dy_all.at[quarter_index, m],
            send_sem=(r_up if up else r_down).at[quarter_index, m],
            recv_sem=r_got.at[quarter_index, m],
            device_id=(me, line + 1 if up else line - 1),
            device_id_type=MESH,
        )

    def twin_quarter(quarter_index, m):
        return pltpu.make_async_remote_copy(
            src_ref=dy_all.at[quarter_index, m],
            dst_ref=dy_all.at[quarter_index, m + 1],
            send_sem=t_sent.at[quarter_index, m],
            recv_sem=t_got.at[quarter_index, m],
            device_id=(flip(me, 1), line),
            device_id_type=MESH,
        )

    def line_round(step):
        if step == 0:
            for up, last in ((True, 3), (False, 0)):

                @pl.when(line != last)
                def _():
                    for m in (0, 2, 4, 6):
                        along_line(line, m, up).start()

            return
        for up, first, last in ((True, step, 3), (False, 3 - step, 0)):
            index = line - step if up else line + step

            @pl.when(line >= first if up else line <= first)
            def _():
                for m in (0, 2, 4, 6):
                    along_line(index, m, up).wait_recv()

                @pl.when(line != last)
                def _():
                    for m in (0, 2, 4, 6):
                        along_line(index, m, up).start()

                for m in (0, 2, 4, 6):
                    twin_quarter(index, m).start()

    def line_end():
        for apart in (1, 2, 3):
            for up in (True, False):
                index = line - apart if up else line + apart

                @pl.when(line >= apart if up else line <= 3 - apart)
                def _():
                    for m in (0, 2, 4, 6):
                        twin_quarter(index, m).wait_recv()
                        twin_quarter(index, m).wait_send()

        for step in range(3):
            for up in (True, False):
                index = line - step if up else line + step

                @pl.when((line >= step) & (line != 3) if up else (line <= 3 - step) & (line != 0))
                def _():
                    for m in (0, 2, 4, 6):
                        along_line(index, m, up).wait_send()

    load = pltpu.make_async_copy(master.at[pl.ds(0, 256), 0, :], wide.at[pl.ds(0, 256)], sem_w.at[0])
    load.start()
    for side in (0, 1):
        at = pl.multiple_of(line * QUART + side * 256, 256)
        dy_own[side] = dy[:, pl.ds(at, 256)]
    keep(8, dy_own, dy_all.at[line, 0])
    ready()
    y_plane.start()
    w_a[0, 0, pl.ds(256, 16), :] = jnp.zeros((16, HALF), BF16)
    w_a[0, 1, pl.ds(256, 16), :] = jnp.zeros((16, HALF), BF16)
    w_a[0, 1, 256:258, 0:256] = own_gains[...].astype(BF16)
    load.wait()
    for side in (0, 1):
        w_a[0, side, pl.ds(0, 256), :] = wide[pl.ds(0, 256), side * HALF : (side + 1) * HALF].astype(BF16)
    load = pltpu.make_async_copy(master.at[pl.ds(256, 256), 0, :], wide.at[pl.ds(0, 256)], sem_w.at[1])
    load.start()
    w_a_plane.start()
    load.wait()
    for side in (0, 1):
        columns = slice(side * HALF, (side + 1) * HALF)
        w_f[0, side, pl.ds(0, 256), :] = wide[pl.ds(0, 256), columns].astype(BF16)
    load = pltpu.make_async_copy(master.at[pl.ds(512, SLAB - 256), 0, :], wide, sem_w.at[2])
    load.start()
    load.wait()
    for side in (0, 1):
        columns = slice(side * HALF, (side + 1) * HALF)
        w_f[0, side, pl.ds(256, 256), :] = wide[pl.ds(0, 256), columns].astype(BF16)
        last = jnp.concatenate([wide[256 : SLAB - 256, columns], jnp.zeros((PAD - SLAB, HALF), F32)], axis=0)
        w_f[0, side, pl.ds(512, 16), :] = last.astype(BF16)
    angle = (me * rows + lax.broadcasted_iota(jnp.int32, (rows, 1), 0)).astype(F32) * speeds[...]
    cosine, sine = jnp.cos(angle), jnp.sin(angle)
    sine = jnp.where(lax.broadcasted_iota(jnp.int32, (1, HEAD_DIM), 1) < HEAD_DIM // 2, -sine, sine)
    y_plane.relay_first()
    y_plane.relay_second()
    y_plane.relay_last()
    kept[8].wait()
    line_round(0)
    w_a_plane.relay_first()
    w_a_plane.relay_second()
    w_a_plane.relay_last()
    w_f_plane.start_first()
    w_a_plane.finish()

    for m in range(8):
        at = pl.multiple_of(flip(me, m) * 256, 256)
        gains[:, pl.ds(at, 256)] = w_a[m, 1, 256:258, 0:256].astype(F32)
    x = tokens[...].astype(F32)
    normed = (x * root_of(x) * gains[0:1, :]).astype(BF16)
    for side in (0, 1):
        a_low[side] = normed[:, side * HALF : (side + 1) * HALF]
    for j in (2, 3, 4, 5, 0, 1):
        out = lax.dot_general(a_low[0], w_a[order_a[j], 0, pl.ds(0, 256), :], NT, preferred_element_type=F32)
        out += lax.dot_general(a_low[1], w_a[order_a[j], 1, pl.ds(0, 256), :], NT, preferred_element_type=F32)
        if j < 4:
            parts = turn(out, cosine, sine)
        else:
            parts = [out[:, :HEAD_DIM], out[:, HEAD_DIM:]]
        for i, part in enumerate(parts):
            if j < 2:
                qcat[0, j, :, i * HEAD_DIM : (i + 1) * HEAD_DIM] = part.astype(BF16)
            else:
                at = (2 * (j % 2) + i) * HEAD_DIM
                (kcat, vcat)[j // 2 - 1][pl.ds(0, rows), at : at + HEAD_DIM] = part.astype(BF16)
        if j == 5:
            kv_plane.start()
    keep(0, a_low, acts.at[0, 0])
    line_round(1)
    kv_plane.relay_first()
    kv_plane.relay_second()
    w_f_plane.relay_first()
    w_f_plane.start_second()
    kv_plane.relay_last()
    kv_plane.finish()

    at_q = me * rows + lax.broadcasted_iota(jnp.int32, (rows, 1), 0)
    along = lax.broadcasted_iota(jnp.int32, (1, rows), 1)
    lane = lax.broadcasted_iota(jnp.int32, (rows, HEAD_DIM), 1)
    stat = jnp.zeros((rows, HEAD_DIM), F32)
    for h in range(4):
        if h == 2:
            line_round(2)
        columns = slice(h * HEAD_DIM, (h + 1) * HEAD_DIM)
        q = qcat[0, h // 2, :, (h % 2) * HEAD_DIM : (h % 2 + 1) * HEAD_DIM]
        top = jnp.full((rows, 1), NEGATIVE, F32)
        for m in range(8):
            ahead = at_q - (flip(me, m) * rows + along)
            s = lax.dot_general(q, kcat[pl.ds(m * rows, rows), columns], NT, preferred_element_type=F32)
            s = jnp.where((ahead >= 0) & (ahead < WINDOW), s * scale, NEGATIVE)
            work[m, :, pl.ds(0, rows)] = s
            top = jnp.maximum(top, jnp.max(s, axis=-1, keepdims=True))
        sums = jnp.zeros((rows, 1), F32)
        for m in range(8):
            e = jnp.exp(work[m, :, pl.ds(0, rows)] - top)
            work[m, :, pl.ds(0, rows)] = e
            sums += jnp.sum(e, axis=-1, keepdims=True)
        share = 1.0 / sums
        o = jnp.zeros((rows, HEAD_DIM), F32)
        for m in range(8):
            soft = (work[m, :, pl.ds(0, rows)] * share).astype(BF16)
            o += jnp.dot(soft, vcat[pl.ds(m * rows, rows), columns], preferred_element_type=F32)
        o_wide[:, columns] = o
        o_low[:, columns] = o.astype(BF16)
        stat = jnp.where(lane == h, top + jnp.log(sums), stat)
    stats[...] = stat
    for side in (0, 1):
        out = jnp.dot(o_low[:, :256], w_a[order_a[6], side, pl.ds(0, 256), :], preferred_element_type=F32)
        out += jnp.dot(o_low[:, 256:], w_a[order_a[7], side, pl.ds(0, 256), :], preferred_element_type=F32)
        total[:, side * HALF : (side + 1) * HALF] = branch * out

    line_post(0)
    line_merge(0)
    line_share(0, [lambda: None, w_f_plane.relay_last])

    gather_sum(0, h_out)
    h = h_out[...] + tokens[...].astype(F32)
    h_out[...] = h
    normed = (h * root_of(h) * gains[1:2, :]).astype(BF16)
    for side in (0, 1):
        b_low[side] = normed[:, side * HALF : (side + 1) * HALF]
    keep(1, b_low, b_all.at[0])
    b_plane.start()
    w_f_plane.relay_second()
    w_f_plane.finish()

    def through(j, left, right):
        out = lax.dot_general(w_f[order_f[j], 0], left, NT, preferred_element_type=F32)
        return out + lax.dot_general(w_f[order_f[j], 1], right, NT, preferred_element_type=F32)

    some = pl.ds(0, rows)
    made[pl.ds(8 * SLAB, 16), some] = jnp.zeros((16, rows), F32)
    row = lax.broadcasted_iota(jnp.int32, (PAD, 1), 0)
    gate_rows = row < 2 * UNITS - 5 * SLAB
    for j in range(8):
        if j < 5:
            out = through(j, b_low[0], b_low[1])
        elif j > 5:
            out = through(j, dy[:, :HALF], dy[:, HALF:])
        else:
            out = jnp.where(gate_rows, through(j, b_low[0], b_low[1]), through(j, dy[:, :HALF], dy[:, HALF:]))
        made[pl.ds(j * SLAB, PAD), some] = out

    def mix(i, _):
        at = pl.multiple_of(i * 32, 8)
        gate = made[pl.ds(at, 32), some]
        up = made[pl.ds(UNITS + at, 32), some]
        back = made[pl.ds(2 * UNITS + at, 32), some]
        sigma = 1.0 / (1.0 + jnp.exp(-gate))
        silu = gate * sigma
        made[pl.ds(at, 32), some] = back * up * (sigma * (1.0 + gate * (1.0 - sigma)))
        made[pl.ds(UNITS + at, 32), some] = back * silu
        made[pl.ds(2 * UNITS + at, 32), some] = silu * up
        return 0

    lax.fori_loop(0, UNITS // 32, mix, 0)
    for j in range(8):
        cut[j, :, pl.ds(0, rows)] = made[pl.ds(j * SLAB, PAD), some].astype(BF16)
    def down(first, side):
        out = None
        for j in range(0, 6) if first else range(5, 8):
            z = cut[j, :, pl.ds(0, rows)]
            if j == 5:
                z = jnp.where(gate_rows if first else ~gate_rows, z, jnp.zeros_like(z))
            made_j = lax.dot_general(z, w_f[order_f[j], side], TN, preferred_element_type=F32)
            out = made_j if out is None else out + made_j
        return out

    line_sent(0)
    for side in (0, 1):
        total[:, side * HALF : (side + 1) * HALF] = down(True, side)
    line_post(1)
    q_plane.start()
    def pack(m):
        z = cut[slab_of(owners, 1, flip(me, m)), :, pl.ds(0, rows)]
        sent[m, pl.ds(0, PAD), :] = z[:, :128]
        late = z[:, 128:].astype(F32)
        late = jnp.concatenate([late[: PAD // 2], late[PAD // 2 :]], axis=1)
        late = jnp.concatenate([late, jnp.zeros((PACKED - PAD - PAD // 2, 128), F32)], axis=0)
        sent[m, pl.ds(PAD, PACKED - PAD), :] = late.astype(BF16)
        if m:
            straight(sent, z_all, 0, m).start()
        else:
            keep(2, sent.at[0], z_all.at[0])

    def down_out(side):
        out = down(False, side)
        for c in range(4):
            made[pl.ds((4 * side + c) * rows, rows), :] = out[:, c * 256 : (c + 1) * 256]

    def down_parts():
        for m in range(4):
            for c in (0, 1):
                at = pl.multiple_of((2 * flip(line, m) + c) * rows, 64)
                block = made[pl.ds(at, rows), :]
                if m == 0:
                    b_own[:, c * 256 : (c + 1) * 256] = block
                else:
                    z_out[m - 1, :, c * 256 : (c + 1) * 256] = block.astype(BF16)

    line_merge(1, [functools.partial(pack, m) for m in (2, 4, 6, 3, 5, 7, 1, 0)])
    line_share(
        1,
        [
            b_plane.relay_first, q_plane.relay_first, functools.partial(down_out, 0), functools.partial(down_out, 1),
            b_plane.relay_second, q_plane.relay_second, down_parts, lambda: line_round(3),
        ],
    )
    for m in (3, 2, 1):
        b_piece(m).start()

    gather_sum(1, total)
    normed_grad = total[...]
    h = h_out[...]
    root = root_of(h)
    gain_two = jnp.sum(normed_grad * h * root, axis=0, keepdims=True)
    weighted = normed_grad * gains[1:2, :]
    inner = jnp.mean(weighted * h, axis=-1, keepdims=True)
    grad = dy[...].astype(F32) + root * weighted - h * (root * root * root) * inner
    for c in range(8):
        made[pl.ds(c * rows, rows), :] = grad[:, c * 256 : (c + 1) * 256]
    low = grad.astype(BF16)
    kept[0].wait()
    for side in (0, 1):
        d_low[side] = low[:, side * HALF : (side + 1) * HALF]
    keep(3, d_low, acts.at[1, 0])
    total[0:1, :] = gain_two
    for m in range(8):
        at = pl.multiple_of(flip(me, m) * 256, 256)
        gain_out[m, 1:2, :] = total[0:1, pl.ds(at, 256)]
    lane = lax.broadcasted_iota(jnp.int32, (rows, HEAD_DIM), 1)
    own_lines = []
    for j, stat in enumerate((stat_l, stat_r)):
        out = lax.dot_general(d_low[0], w_a[order_a[6 + j], 0, pl.ds(0, 256), :], NT, preferred_element_type=F32)
        out += lax.dot_general(d_low[1], w_a[order_a[6 + j], 1, pl.ds(0, 256), :], NT, preferred_element_type=F32)
        out = (branch * out).astype(BF16)
        docat[0, j, pl.ds(0, rows), :] = out
        lines = jnp.zeros((rows, HEAD_DIM), F32)
        columns = []
        for i in (0, 1):
            h_at = 2 * j + i
            span = slice(h_at * HEAD_DIM, (h_at + 1) * HEAD_DIM)
            delta = jnp.sum(
                out[:, i * HEAD_DIM : (i + 1) * HEAD_DIM].astype(F32) * o_wide[:, span], axis=-1, keepdims=True
            )
            top = stats[:, h_at : h_at + 1]
            columns.append((top, delta))
            for at, value in ((i, top), (2 + i, delta)):
                for step in range(3):
                    part = value.astype(BF16).astype(F32)
                    value = value - part
                    lines = jnp.where(lane == 4 * step + at, part, lines)
        own_lines.append(columns)
        stat[pl.ds(0, rows), :] = lines
        stat[pl.ds(rows, 256 - rows), :] = jnp.zeros((256 - rows, HEAD_DIM), F32)
        docat[0, j, pl.ds(rows, 16), :] = stat[...].T[:16, :].astype(BF16)
    do_plane.start()
    b_plane.relay_last()
    q_plane.relay_last()

    for i in range(6):
        work[i] = jnp.zeros((rows, 256), F32)
    reach = -(-WINDOW // rows)
    below = lax.broadcasted_iota(jnp.int32, (rows, rows), 0)
    along = lax.broadcasted_iota(jnp.int32, (rows, rows), 1)

    def head_cut(h):
        return h // 2, slice((h % 2) * HEAD_DIM, (h % 2 + 1) * HEAD_DIM), slice(h * HEAD_DIM, (h + 1) * HEAD_DIM)

    def rows_of(m):
        return pl.ds(m * rows, rows)

    def query_side(m):
        apart = me - flip(me, m)

        @pl.when((apart >= 0) & (apart <= reach))
        def _():
            ahead = apart * rows + below - along
            allowed = (ahead >= 0) & (ahead < WINDOW)
            for h in range(4):
                side, two, span = head_cut(h)
                top, delta = own_lines[side][h % 2]
                k, do = kcat[rows_of(m), span], docat[0, side, pl.ds(0, rows), two]
                s = lax.dot_general(qcat[0, side, :, two], k, NT, preferred_element_type=F32)
                p = jnp.where(allowed, jnp.exp(s * scale - top), 0.0)
                dp = lax.dot_general(do, vcat[rows_of(m), span], NT, preferred_element_type=F32)
                ds = (p * (dp - delta) * scale).astype(BF16)
                work[side, :, two] += jnp.dot(ds, k, preferred_element_type=F32)

    def key_side(m):
        apart = me - flip(me, m)

        @pl.when((apart <= 0) & (apart >= -reach))
        def _():
            ahead = along - below - apart * rows
            allowed = (ahead >= 0) & (ahead < WINDOW)
            for h in range(4):
                side, two, span = head_cut(h)
                lines = docat[m, side, pl.ds(rows, 16), :].astype(F32)
                lines = (lines[0:4] + lines[4:8] + lines[8:12])[:, :rows]
                top, delta = lines[h % 2 : h % 2 + 1], lines[2 + h % 2 : 3 + h % 2]
                q, do = qcat[m, side, :, two], docat[m, side, pl.ds(0, rows), two]
                s = lax.dot_general(kcat[pl.ds(0, rows), span], q, NT, preferred_element_type=F32)
                p = jnp.where(allowed, jnp.exp(s * scale - top), 0.0)
                work[4 + side, :, two] += jnp.dot(p.astype(BF16), do, preferred_element_type=F32)
                dp = lax.dot_general(vcat[pl.ds(0, rows), span], do, NT, preferred_element_type=F32)
                ds = (p * (dp - delta) * scale).astype(BF16)
                work[2 + side, :, two] += jnp.dot(ds, q, preferred_element_type=F32)

    for m in range(4):
        query_side(m)
    do_plane.relay_first()
    for m in range(4, 8):
        query_side(m)
    do_plane.relay_second()
    do_plane.relay_last()
    d_plane.start()
    a_plane.start()
    do_plane.finish()
    q_plane.finish()
    for m in range(8):
        key_side(m)
    for j in range(8):
        two = slice((j % 2) * 256, (j % 2 + 1) * 256)
        if j < 4:
            made_j = turn(work[j], cosine, -sine)
            for i in (0, 1):
                cut[j, pl.ds(0, rows), i * HEAD_DIM : (i + 1) * HEAD_DIM] = made_j[i].astype(BF16)
        elif j < 6:
            cut[j, pl.ds(0, rows), :] = work[j].astype(BF16)
        else:
            cut[j, pl.ds(0, rows), :] = o_low[:, two]
    line_sent(1)
    for j in range(6):
        for side in (0, 1):
            out = jnp.dot(cut[j, pl.ds(0, rows), :], w_a[order_a[j], side, pl.ds(0, 256), :], preferred_element_type=F32)
            columns = slice(side * HALF, (side + 1) * HALF)
            total[:, columns] = out if j == 0 else total[:, columns] + out
    line_post(2)

    def send_group(m):
        g_sent[m] = cut[slab_of(owners, 0, flip(me, m)), pl.ds(0, rows), :]
        if m:
            straight(g_sent, g_all, 1, m).start()
        else:
            keep(4, g_sent.at[0], g_all.at[0])

    line_merge(2, [functools.partial(send_group, m) for m in (2, 4, 6, 3, 5, 7, 1, 0)])
    line_share(2, [d_plane.relay_first, a_plane.relay_first, d_plane.relay_second, a_plane.relay_second])
    out = h_out[:, quarter(0)] + b_own[...]
    for m in (1, 2, 3):
        b_piece(m).wait_recv()
        out += z_in[m - 1].astype(F32)
    block_out[...] = out.astype(BF16)

    gather_sum(2, total)
    normed_grad = total[...]
    x = tokens[...].astype(F32)
    root = root_of(x)
    gain_one = jnp.sum(normed_grad * x * root, axis=0, keepdims=True)
    weighted = normed_grad * gains[0:1, :]
    inner = jnp.mean(weighted * x, axis=-1, keepdims=True)
    grad = root * weighted - x * (root * root * root) * inner
    for c in range(8):
        made[pl.ds(c * rows, rows), :] += grad[:, c * 256 : (c + 1) * 256]
    total[0:1, :] = gain_one
    for m in range(8):
        at = pl.multiple_of(flip(me, m) * 256, 256)
        gain_out[m, 0:1, :] = total[0:1, pl.ds(at, 256)]
    for c in range(8):
        keep(9 + c, made.at[pl.ds(c * rows, rows)], input_grad.at[:, pl.ds(c * 256, 256)])
    for m in range(1, 8):
        straight(gain_out, gain_in, 2, m).start()
    for one in (d_plane, a_plane):
        one.relay_last()
    for m in range(1, 8):
        straight(gain_out, gain_in, 2, m).wait_recv()
    made = gain_out[0, 0:2, :]
    for m in range(1, 8):
        made += gain_in[m, 0:2, :]
    gain_grad[...] = made
    for one in (y_plane, b_plane, d_plane, a_plane):
        one.finish()
    line_end()
    for m in range(1, 8):
        straight(sent, z_all, 0, m).wait_recv()
        straight(g_sent, g_all, 1, m).wait_recv()
    for one in (
        w_a_plane, w_f_plane, kv_plane, q_plane, y_plane, b_plane, a_plane, d_plane, do_plane
    ):
        one.drain()
    for m in range(1, 8):
        straight(sent, z_all, 0, m).wait_send()
        straight(g_sent, g_all, 1, m).wait_send()
        straight(gain_out, gain_in, 2, m).wait_send()
    line_sent(2)
    for which in range(3):
        line_all_sent(which)
    for m in (1, 2, 3):
        b_piece(m).wait_send()
    for i in kept:
        if i not in (0, 8):
            kept[i].wait()


def layer(owners, tokens, dy, own_gains, speeds, master, scale, branch):
    rows, width = tokens.shape
    array = jax.ShapeDtypeStruct
    dma = pltpu.SemaphoreType.DMA

    def low(*sizes):
        return pltpu.VMEM(sizes, BF16)

    def wide(*sizes):
        return pltpu.VMEM(sizes, F32)

    return pl.pallas_call(
        functools.partial(layer_kernel, rows, scale, branch),
        out_shape=[
            shape(rows, QUART),
            array((2, 256), F32),
            shape(rows, width, F32),
            array((2, 8, 2, rows, HALF), BF16),
            array((8, PACKED, 128), BF16),
            array((8, rows, 256), BF16),
            array((8, 2, rows, HALF), BF16),
            array((4, 8, 2, rows, 256), BF16),
        ],
        in_specs=[SM] + [VM] * 4 + [HB],
        out_specs=[VM] * 2 + [HB] * 6,
        scratch_shapes=[
            wide(2, width),
            low(rows, QUART),
            wide(rows, QUART),
            wide(rows, HEAD_DIM),
            low(2, rows, HALF),
            low(2, rows, HALF),
            low(8 * rows, QUART),
            low(8 * rows, QUART),
            low(8, 2, rows, 256),
            low(8, 2, rows + 16, 256),
            low(8, PACKED, 128),
            low(8, rows, 256),
            wide(SLAB - 256, width),
            low(8, 2, 272, HALF),
            low(8, 2, PAD, HALF),
            wide(8 * SLAB + 16, 256),
            low(8, PAD, 256),
            wide(rows, width),
            low(3, rows, QUART),
            low(3, rows, QUART),
            low(3, 4, 2, rows, 256),
            low(2, 3, 2, rows, 256),
            low(2, 2, 3, 2, rows, 256),
            wide(rows, QUART),
            wide(8, rows, 256),
            low(2, rows, 256),
            wide(256, HEAD_DIM),
            wide(256, HEAD_DIM),
            wide(8, 8, 256),
            wide(8, 8, 256),
            dma((3,)),
            dma((17,)),
            dma((9, 8, 2)),
            dma((9, 8, 2)),
            dma((2, 4)),
            dma((3, 2, 2, 3, 2)),
            dma((3, 3, 4, 2)),
        ]
        + [dma((4, 8))] * 5
        + [dma((3, 2, 8))],
        compiler_params=pltpu.CompilerParams(
            collective_id=0, has_side_effects=True, vmem_limit_bytes=63 * 2**20
        ),
        cost_estimate=pl.CostEstimate(flops=2 * 10**10, bytes_accessed=60 * 2**20, transcendentals=0),
        name="layer",
    )(owners, tokens, dy, own_gains, speeds, master)


TILE = 256


def update_kernel(rows, branch, owners, basis, gain_grad, norm_gains, gain_first, gain_second, *rest):
    (zs, gs, acts, bs, dys), olds, through, rest = rest[:5], rest[5:8], rest[8:10], rest[10:]
    news, low_new, passed, gain_news, rest = rest[:4], rest[4], rest[5:7], rest[7:11], rest[11:]
    turned_g, turned_z, wide_basis, act, old, new, asem, osem, nsem = rest
    me, line = lax.axis_index("seq"), lax.axis_index("head")
    tile, tiles = pl.program_id(0), pl.num_programs(0)
    slot = tile % 2
    a_slab, f_slab = slab_of(owners, 0, me), slab_of(owners, 1, me)

    def columns_of(t):
        return pl.ds(pl.multiple_of(t * TILE, TILE), TILE)

    def spans(m):
        late = rows - 128
        return ((pl.ds(0, 128), pl.ds(m * 128, 128)), (pl.ds(128, late), pl.ds(8 * 128 + m * late, late)))

    def act_copies(t, kind, which):
        at = pl.ds(pl.multiple_of(lax.rem(t, HALF // TILE) * TILE, TILE), TILE)
        for m in range(8):
            if kind == 3:
                part = dys.at[lax.div(t, 2), m, lax.rem(t, 2)]
            elif kind == 2:
                part = bs.at[m, lax.div(t, HALF // TILE), :, at]
            else:
                part = acts.at[kind, m, lax.div(t, HALF // TILE), :, at]
            for source, target in spans(m):
                pltpu.make_async_copy(part.at[source], act.at[t % 2, which, target], asem.at[t % 2, which]).start()

    def act_wait(which):
        for m in range(8):
            for _, target in spans(m):
                part = act.at[slot, which, target]
                pltpu.make_async_copy(part, part, asem.at[slot, which]).wait()

    def fetch_acts(t):
        pl.when(a_slab < 6)(lambda: act_copies(t, 0, 0))
        pl.when(a_slab >= 6)(lambda: act_copies(t, 1, 0))
        pl.when(f_slab <= 5)(lambda: act_copies(t, 2, 1))
        pl.when(f_slab > 5)(lambda: act_copies(t, 3, 1))
        pl.when(f_slab == 5)(lambda: act_copies(t, 3, 2))

    def old_copy(i, t):
        return pltpu.make_async_copy(olds[i].at[:, 0, columns_of(t)], old.at[t % 2, i], osem.at[t % 2, i])

    def new_copy(i, t):
        return pltpu.make_async_copy(new.at[t % 2, i], news[i].at[:, 0, columns_of(t)], nsem.at[t % 2, i])

    def fetch(t):
        fetch_acts(t)
        for i in range(3):
            old_copy(i, t).start()

    @pl.when(tile == 0)
    def _():
        fetch(0)
        for i in (0, 1):
            passed[i][...] = through[i][...]
        made = gain_grad[...]
        one = BETA_FIRST * gain_first[...] + (1.0 - BETA_FIRST) * made
        two = BETA_SECOND * gain_second[...] + (1.0 - BETA_SECOND) * made * made
        gain_news[0][...] = made
        gain_news[1][...] = one
        gain_news[2][...] = two
        gain_news[3][...] = norm_gains[...] - GAIN_RATE * (one / (1.0 - BETA_FIRST**ADAM_STEP)) / (
            jnp.sqrt(two / (1.0 - BETA_SECOND**ADAM_STEP)) + ADAM_EPS
        )
        wide_basis[...] = jnp.zeros_like(wide_basis)
        lane = lax.broadcasted_iota(jnp.int32, (PAD // 2, 128), 1)
        for m in range(8):
            turned_g[:, m * 128 : (m + 1) * 128] = gs[m, pl.ds(0, 128), :].T
            turned_z[:, m * 128 : (m + 1) * 128] = zs[m, pl.ds(0, PAD), :]
            if m % 2 == 0:
                at = 8 * 128 + m * 64
                late = jnp.concatenate([gs[m, pl.ds(128, 64), :], gs[m + 1, pl.ds(128, 64), :]], axis=0)
                turned_g[:, at : at + 128] = late.T
                even, odd = (zs[m + i, pl.ds(PAD, PAD // 2), :].astype(F32) for i in (0, 1))
                upper = jnp.where(lane < 64, even, pltpu.roll(odd, 64, 1))
                lower = jnp.where(lane < 64, pltpu.roll(even, 64, 1), odd)
                turned_z[:, at : at + 128] = jnp.concatenate([upper, lower], axis=0).astype(BF16)

    pl.when(tile + 1 < tiles)(lambda: fetch(tile + 1))

    @pl.when(tile >= 2)
    def _():
        for i in range(4):
            new_copy(i, tile - 2).wait()

    grad, first_new, second_new, master_new = (new.at[slot, i] for i in range(4))
    first, second, master = (old.at[slot, i] for i in range(3))

    def ffn_rows(which):
        return jnp.dot(turned_z[...], act[slot, which], preferred_element_type=F32)[:SLAB]

    act_wait(0)
    factor = jnp.where(a_slab < 6, 1.0, branch)
    grad[pl.ds(0, 256), :] = factor * jnp.dot(turned_g[...], act[slot, 0], preferred_element_type=F32)
    act_wait(1)
    grad[pl.ds(256, SLAB), :] = ffn_rows(1)
    first_of_down = 2 * UNITS - f_slab * SLAB

    @pl.when(f_slab == 5)
    def _():
        act_wait(2)
        row = lax.broadcasted_iota(jnp.int32, (SLAB, 1), 0)
        grad[pl.ds(256, SLAB), :] = jnp.where(row < first_of_down, grad[pl.ds(256, SLAB), :], ffn_rows(2))

    for i in range(3):
        old_copy(i, tile).wait()
    row = lax.broadcasted_iota(jnp.int32, (256 + SLAB, 1), 0)
    rate = jnp.where((row < 256) | (row - 256 < first_of_down), 0.5 * (2 * HALF) ** (-0.5), 0.5 * FF ** (-0.5))
    for b in range(TILE // HEAD_DIM):
        cut = slice(b * HEAD_DIM, (b + 1) * HEAD_DIM)
        wide_basis[cut, cut] = basis[b].astype(BF16)
    turned = jnp.dot(grad[...].astype(BF16), wide_basis[...], preferred_element_type=F32)
    one = BETA_FIRST * first[...] + (1.0 - BETA_FIRST) * turned
    two = BETA_SECOND * second[...] + (1.0 - BETA_SECOND) * turned * turned
    first_new[...] = one
    second_new[...] = two
    adam = (one / (1.0 - BETA_FIRST**ADAM_STEP)) / (jnp.sqrt(two / (1.0 - BETA_SECOND**ADAM_STEP)) + ADAM_EPS)
    back = lax.dot_general(adam.astype(BF16), wide_basis[...], NT, preferred_element_type=F32)
    before = master[...]
    after = before - rate * (back + DECAY_RATE * before)
    master_new[...] = after
    low_new[...] = after.astype(BF16)
    for i in range(4):
        new_copy(i, tile).start()

    @pl.when(tile == tiles - 1)
    def _():
        for t in (tile - 1, tile):
            for i in range(4):
                new_copy(i, t).wait()


def update(owners, basis, small, zs, gs, acts, bs, dys, olds, through, branch):
    rows = gs.shape[1]
    height, _, width = olds[0].shape

    def whole(array):
        return pl.BlockSpec(array.shape, lambda i: (0,) * array.ndim)

    tall = pl.BlockSpec((height, TILE), lambda i: (0, i))
    per = TILE // HEAD_DIM
    gains = [shape(*array.shape, F32) for array in small]
    return call(
        functools.partial(update_kernel, rows, branch),
        [jax.ShapeDtypeStruct(olds[0].shape, F32)] * 4
        + [shape(height, width)]
        + [jax.ShapeDtypeStruct(array.shape, array.dtype) for array in through]
        + gains,
        [SM, pl.BlockSpec((per, HEAD_DIM, HEAD_DIM), lambda i: (i, 0, 0))]
        + [whole(array) for array in small]
        + [whole(zs), whole(gs)]
        + [HB] * 6
        + [whole(array) for array in through],
        [owners, basis, *small, zs, gs, acts, bs, dys, *olds, *through],
        [
            pltpu.VMEM((256, 8 * rows), BF16),
            pltpu.VMEM((PAD, 8 * rows), BF16),
            pltpu.VMEM((TILE, TILE), BF16),
            pltpu.VMEM((2, 3, 8 * rows, TILE), BF16),
            pltpu.VMEM((2, 3, height, TILE), F32),
            pltpu.VMEM((2, 4, height, TILE), F32),
            pltpu.SemaphoreType.DMA((2, 3)),
            pltpu.SemaphoreType.DMA((2, 3)),
            pltpu.SemaphoreType.DMA((2, 4)),
        ],
        out_specs=[HB] * 4 + [tall] + [whole(array) for array in through] + [whole(array) for array in small],
        grid=(width // TILE,),
        flops=2 * 8 * rows * height * width,
        moved=70 * 2**20,
    )


def plane_mesh(
    tokens,
    cotangent,
    owners,
    master,
    first_moment,
    second_moment,
    eigenbases,
    norm_gains,
    gain_first,
    gain_second,
):
    rows, width = tokens.shape
    scale = HEAD_DIM ** (-0.5)
    branch = (WINDOW / 3.0) ** 0.5
    half = HEAD_DIM // 2
    speeds = ROPE_BASE ** (-jnp.arange(half, dtype=F32) / half)
    speeds = jnp.concatenate([speeds, speeds])[None, :]
    tall = [array.reshape(array.shape[2], 1, width) for array in (first_moment, second_moment, master)]
    block_out, gain_grad, input_grad, acts, zs, gs, bs, dys = layer(
        owners, tokens, cotangent, norm_gains, speeds, tall[2], scale, branch
    )
    (
        grad, first_new, second_new, master_new, low_new, block_out, input_grad, gain_grad, gain_first_new,
        gain_second_new, gain_new,
    ) = update(
        owners, eigenbases[0, 0], [gain_grad, norm_gains, gain_first, gain_second], zs, gs, acts, bs, dys, tall,
        [block_out, input_grad], branch,
    )
    whole = (1, 1, *tall[0].shape[::2])
    return (
        block_out,
        input_grad,
        grad.reshape(whole),
        first_new.reshape(whole),
        second_new.reshape(whole),
        master_new.reshape(whole),
        low_new[None, None],
        gain_grad,
        gain_first_new,
        gain_second_new,
        gain_new,
    )


def solution(mesh):
    in_specs = (
        P("seq", None),
        P("seq", None),
        P(),
        P("head", "seq", None, None),
        P("head", "seq", None, None),
        P("head", "seq", None, None),
        P("head", "seq", None, None, None),
        P(None, "seq"),
        P(None, "seq"),
        P(None, "seq"),
    )
    out_specs = (
        P("seq", "head"),
        P("seq", None),
        P("head", "seq", None, None),
        P("head", "seq", None, None),
        P("head", "seq", None, None),
        P("head", "seq", None, None),
        P("head", "seq", None, None),
        P(None, "seq"),
        P(None, "seq"),
        P(None, "seq"),
        P(None, "seq"),
    )
    plane = mesh.shape["seq"] == 8 and mesh.shape["head"] == 4
    return jax.shard_map(
        plane_mesh if plane else any_mesh, mesh=mesh, in_specs=in_specs, out_specs=out_specs, check_vma=False
    )
```

```python
import functools

import jax
import jax.numpy as jnp
from jax import lax
from jax.experimental import pallas as pl
from jax.experimental.pallas import tpu as pltpu
from jax.sharding import PartitionSpec as P

HEADS = 16
HEAD_DIM = 128
FF = 5504
WINDOW = 1024
ADAM_STEP = 5


EPS_NORM = 1e-05
BETA_FIRST = 0.5
BETA_SECOND = 0.6
ADAM_EPS = 1e-08
DECAY_RATE = 0.1
GAIN_RATE = 0.25
ROPE_BASE = 10000.0
NEGATIVE = -1e30
PRECISE = lax.Precision.HIGHEST

BF16 = jnp.bfloat16
F32 = jnp.float32


def passed_along(shard, axis, by):
    devices = lax.axis_size(axis)
    pairs = [(i, i + by) for i in range(devices) if 0 <= i + by < devices]
    return lax.ppermute(shard, axis, pairs)


def inverse_order(owner_row):
    places = jnp.arange(owner_row.shape[0], dtype=jnp.int32)
    matches = (owner_row[:, None] == places[None, :]).astype(jnp.int32)
    return jnp.sum(matches * places[:, None], axis=0)


def kind_rates(kinds, width):
    wide = width ** (-0.5)
    spreads = jnp.array([wide, wide, wide, wide, wide, wide, FF ** (-0.5)], jnp.float32)
    matches = (kinds[..., None] == jnp.arange(7, dtype=jnp.int32)).astype(jnp.float32)
    return 0.5 * jnp.sum(matches * spreads, axis=-1)


def angles(positions):
    half_dim = HEAD_DIM // 2
    frequencies = ROPE_BASE ** (-jnp.arange(half_dim, dtype=jnp.float32) / half_dim)
    turning = positions[:, None] * frequencies[None, :]
    return (jnp.cos(turning)[:, None, :], jnp.sin(turning)[:, None, :])


def rotate(vectors, cosine, sine):
    half_dim = vectors.shape[-1] // 2
    former = vectors[..., :half_dim]
    latter = vectors[..., half_dim:]
    return jnp.concatenate(
        [former * cosine - latter * sine, latter * cosine + former * sine], axis=-1
    )


def inverse_rms(vectors):
    return lax.rsqrt(jnp.mean(vectors * vectors, axis=-1, keepdims=True) + EPS_NORM)


def norm_back(grad_normed, inputs, rms_values, gain_row):
    weighted = grad_normed * gain_row
    inner = jnp.mean(weighted * inputs, axis=-1, keepdims=True)
    input_part = rms_values * weighted - inputs * rms_values**3 * inner
    return (input_part, jnp.sum(grad_normed * inputs * rms_values, axis=0))


def any_mesh(
    tokens,
    cotangent,
    owners,
    master,
    first_moment,
    second_moment,
    eigenbases,
    norm_gains,
    gain_first,
    gain_second,
):
    tok_rows, width = tokens.shape
    seq_devices = lax.axis_size("seq")
    head_devices = lax.axis_size("head")
    seq_place = lax.axis_index("seq")
    head_place = lax.axis_index("head")
    slab_rows = master.shape[2]
    attn_slab = 4 * width // (head_devices * seq_devices)
    ffn_slab = slab_rows - attn_slab
    head_width = width // head_devices
    ffn_width = FF // head_devices
    local_heads = HEADS // head_devices
    score_scale = HEAD_DIM ** (-0.5)
    branch_scale = (WINDOW / 3.0) ** 0.5
    inverse_attn = inverse_order(owners[0])
    inverse_ffn = inverse_order(owners[1])
    master_low = master[0, 0].astype(jnp.bfloat16)
    gathered, gains_all = (
        lax.all_gather(master_low, "seq", axis=0, tiled=True),
        lax.all_gather(norm_gains.astype(jnp.bfloat16), "seq", axis=1, tiled=True),
    )
    gathered = gathered.reshape(seq_devices, slab_rows, width)
    attn_rows = jnp.take(gathered[:, :attn_slab], owners[0], axis=0).reshape(4 * head_width, width)
    ffn_rows = jnp.take(gathered[:, attn_slab:], owners[1], axis=0).reshape(3 * ffn_width, width)
    w_query = attn_rows[:head_width]
    w_key = attn_rows[head_width : 2 * head_width]
    w_value = attn_rows[2 * head_width : 3 * head_width]
    w_out = attn_rows[3 * head_width :]
    w_gate = ffn_rows[:ffn_width]
    w_up = ffn_rows[ffn_width : 2 * ffn_width]
    w_down = ffn_rows[2 * ffn_width :]
    gain_one = gains_all[0].astype(jnp.float32)
    gain_two = gains_all[1].astype(jnp.float32)
    inputs = tokens.astype(jnp.float32)
    rms_one = inverse_rms(inputs)
    normed_one = (inputs * rms_one * gain_one).astype(jnp.bfloat16)
    positions = (seq_place * tok_rows + jnp.arange(tok_rows, dtype=jnp.int32)).astype(jnp.float32)
    cosine, sine = angles(positions)
    head_shape = (tok_rows, local_heads, HEAD_DIM)

    def project(weight_rows):
        return jnp.einsum("td,id->ti", normed_one, weight_rows, preferred_element_type=jnp.float32)

    queries = rotate(project(w_query).reshape(head_shape), cosine, sine).astype(jnp.bfloat16)
    keys_own = rotate(project(w_key).reshape(head_shape), cosine, sine).astype(jnp.bfloat16)
    values_own = project(w_value).reshape(head_shape).astype(jnp.bfloat16)
    hop_total = -(-WINDOW // tok_rows)
    hop_sizes = [
        min(tok_rows, WINDOW - (hop_index - 1) * tok_rows) for hop_index in range(1, hop_total + 1)
    ]
    halo_keys = []
    halo_values = []
    for hop_index in range(hop_total, 0, -1):
        hop_rows = hop_sizes[hop_index - 1]
        far_keys, far_values = passed_along(
            (keys_own[tok_rows - hop_rows :], values_own[tok_rows - hop_rows :]), "seq", hop_index
        )
        halo_keys.append(far_keys)
        halo_values.append(far_values)
    keys_all = jnp.concatenate(halo_keys + [keys_own], axis=0)
    values_all = jnp.concatenate(halo_values + [values_own], axis=0)
    row_ids = jnp.arange(tok_rows, dtype=jnp.int32)[:, None]
    col_ids = jnp.arange(WINDOW + tok_rows, dtype=jnp.int32)[None, :]
    allowed = (
        (col_ids > row_ids)
        & (col_ids <= row_ids + WINDOW)
        & (seq_place * tok_rows - WINDOW + col_ids >= 0)
    )

    def scores_of():
        raw = jnp.einsum("thd,chd->htc", queries, keys_all, preferred_element_type=jnp.float32)
        return jnp.where(allowed[None], raw * score_scale, NEGATIVE)

    scores = scores_of()
    row_top = jnp.max(scores, axis=-1, keepdims=True)
    exp_scores = jnp.exp(scores - row_top)
    exp_total = jnp.sum(exp_scores, axis=-1, keepdims=True)
    soft_low = (exp_scores / exp_total).astype(jnp.bfloat16)
    log_total = row_top + jnp.log(exp_total)
    attended = jnp.einsum("htc,chd->thd", soft_low, values_all, preferred_element_type=jnp.float32)
    attended_low = attended.reshape(tok_rows, head_width).astype(jnp.bfloat16)
    attn_part = branch_scale * jnp.dot(attended_low, w_out, preferred_element_type=jnp.float32)
    hidden_one = inputs + lax.psum(attn_part, "head")
    rms_two = inverse_rms(hidden_one)
    normed_two = (hidden_one * rms_two * gain_two).astype(jnp.bfloat16)
    gate_pre = jnp.einsum("td,fd->tf", normed_two, w_gate, preferred_element_type=jnp.float32)
    up_pre = jnp.einsum("td,fd->tf", normed_two, w_up, preferred_element_type=jnp.float32)
    sigma = jax.nn.sigmoid(gate_pre)
    hidden_low = (gate_pre * sigma * up_pre).astype(jnp.bfloat16)
    ffn_part = jnp.dot(hidden_low, w_down, preferred_element_type=jnp.float32)
    ffn_share = lax.psum_scatter(ffn_part, "head", scatter_dimension=1, tiled=True)
    share_width = width // head_devices
    residual_share = lax.dynamic_slice_in_dim(hidden_one, head_place * share_width, share_width, 1)
    block_out = (residual_share + ffn_share).astype(jnp.bfloat16)
    grad_out_f = cotangent.astype(jnp.float32)
    hidden_grad = jnp.einsum("td,fd->tf", cotangent, w_down, preferred_element_type=jnp.float32)
    silu_grad = sigma * (1.0 + gate_pre * (1.0 - sigma))
    gate_grad = (hidden_grad * up_pre * silu_grad).astype(jnp.bfloat16)
    up_grad = (hidden_grad * gate_pre * sigma).astype(jnp.bfloat16)
    down_grad = jnp.einsum("tf,td->fd", hidden_low, cotangent, preferred_element_type=jnp.float32)
    gate_w_grad = jnp.einsum("tf,td->fd", gate_grad, normed_two, preferred_element_type=jnp.float32)
    up_w_grad = jnp.einsum("tf,td->fd", up_grad, normed_two, preferred_element_type=jnp.float32)
    ffn_rows_grad = jnp.concatenate([gate_w_grad, up_w_grad, down_grad], axis=0)
    ffn_owner = jnp.take(ffn_rows_grad.reshape(seq_devices, ffn_slab, width), inverse_ffn, axis=0)
    normed_two_part = jnp.einsum(
        "tf,fd->td", gate_grad, w_gate, preferred_element_type=jnp.float32
    ) + jnp.einsum("tf,fd->td", up_grad, w_up, preferred_element_type=jnp.float32)
    normed_two_share = lax.psum_scatter(normed_two_part, "head", scatter_dimension=1, tiled=True)
    normed_two_grad = lax.all_gather(normed_two_share, "head", axis=1, tiled=True)
    back_two, gain_two_grad = norm_back(normed_two_grad, hidden_one, rms_two, gain_two)
    hidden_one_grad = grad_out_f + back_two
    hidden_grad_low = hidden_one_grad.astype(jnp.bfloat16)
    attended_grad = branch_scale * jnp.einsum(
        "td,id->ti", hidden_grad_low, w_out, preferred_element_type=jnp.float32
    )
    attended_grad = attended_grad.reshape(head_shape).astype(jnp.bfloat16)
    soft_again = jnp.exp(scores_of() - log_total)
    soft_grad = jnp.einsum(
        "thd,chd->htc", attended_grad, values_all, preferred_element_type=jnp.float32
    )
    inner_sum = jnp.sum(soft_again * soft_grad, axis=-1, keepdims=True)
    score_grad = (soft_again * (soft_grad - inner_sum) * score_scale).astype(jnp.bfloat16)
    query_grad_turned = jnp.einsum(
        "htc,chd->thd", score_grad, keys_all, preferred_element_type=jnp.float32
    )
    key_grad_all = jnp.einsum(
        "htc,thd->chd", score_grad, queries, preferred_element_type=jnp.float32
    )
    value_grad_all = jnp.einsum(
        "htc,thd->chd", soft_low, attended_grad, preferred_element_type=jnp.float32
    )
    key_grad_own = key_grad_all[WINDOW:]
    value_grad_own = value_grad_all[WINDOW:]
    start_at = 0
    for hop_index in range(hop_total, 0, -1):
        hop_rows = hop_sizes[hop_index - 1]
        back_keys, back_values = passed_along(
            (
                key_grad_all[start_at : start_at + hop_rows],
                value_grad_all[start_at : start_at + hop_rows],
            ),
            "seq",
            -hop_index,
        )
        key_grad_own = key_grad_own.at[tok_rows - hop_rows :].add(back_keys)
        value_grad_own = value_grad_own.at[tok_rows - hop_rows :].add(back_values)
        start_at = start_at + hop_rows
    query_grad = (
        rotate(query_grad_turned, cosine, -sine).reshape(tok_rows, head_width).astype(jnp.bfloat16)
    )
    key_grad = (
        rotate(key_grad_own, cosine, -sine).reshape(tok_rows, head_width).astype(jnp.bfloat16)
    )
    value_grad = value_grad_own.reshape(tok_rows, head_width).astype(jnp.bfloat16)

    def input_part(row_grad, weight_rows):
        return jnp.einsum("ti,id->td", row_grad, weight_rows, preferred_element_type=jnp.float32)

    normed_one_part = (
        input_part(query_grad, w_query)
        + input_part(key_grad, w_key)
        + input_part(value_grad, w_value)
    )
    normed_one_share = lax.psum_scatter(normed_one_part, "head", scatter_dimension=1, tiled=True)
    normed_one_grad = lax.all_gather(
        normed_one_share.astype(jnp.bfloat16), "head", axis=1, tiled=True
    ).astype(normed_one_share.dtype)
    back_one, gain_one_grad = norm_back(normed_one_grad, inputs, rms_one, gain_one)
    input_grad = hidden_one_grad + back_one
    gain_grads = jnp.stack([gain_one_grad, gain_two_grad])

    def rows_grad(row_grad):
        return jnp.einsum("ti,td->id", row_grad, normed_one, preferred_element_type=jnp.float32)

    out_w_grad = branch_scale * jnp.einsum(
        "ti,td->id", attended_low, hidden_grad_low, preferred_element_type=jnp.float32
    )
    attn_rows_grad = jnp.concatenate(
        [rows_grad(query_grad), rows_grad(key_grad), rows_grad(value_grad), out_w_grad], axis=0
    )
    attn_owner = jnp.take(
        attn_rows_grad.reshape(seq_devices, attn_slab, width), inverse_attn, axis=0
    )
    owner_rows = jnp.concatenate([attn_owner, ffn_owner], axis=1).reshape(
        seq_devices * slab_rows, width
    )
    reduced, gain_reduced = (
        lax.psum_scatter(owner_rows, "seq", scatter_dimension=0, tiled=True),
        lax.psum_scatter(gain_grads, "seq", scatter_dimension=1, tiled=True),
    )
    attn_kinds = (
        inverse_attn[seq_place] * attn_slab + jnp.arange(attn_slab, dtype=jnp.int32)
    ) // head_width
    ffn_kinds = (
        4 + (inverse_ffn[seq_place] * ffn_slab + jnp.arange(ffn_slab, dtype=jnp.int32)) // ffn_width
    )
    row_rates = kind_rates(jnp.concatenate([attn_kinds, ffn_kinds]), width)[:, None]
    basis = eigenbases[0, 0]
    block_size = basis.shape[-1]
    split_shape = (slab_rows, width // block_size, block_size)
    turned = jnp.einsum(
        "rbk,bkl->rbl", reduced.reshape(split_shape), basis, precision=PRECISE
    ).reshape(slab_rows, width)
    first_new = BETA_FIRST * first_moment[0, 0] + (1.0 - BETA_FIRST) * turned
    second_new = BETA_SECOND * second_moment[0, 0] + (1.0 - BETA_SECOND) * turned * turned
    adam_dir = (
        first_new
        / (1.0 - BETA_FIRST**ADAM_STEP)
        / (jnp.sqrt(second_new / (1.0 - BETA_SECOND**ADAM_STEP)) + ADAM_EPS)
    )
    backward_dir = jnp.einsum(
        "rbl,bkl->rbk", adam_dir.reshape(split_shape), basis, precision=PRECISE
    ).reshape(slab_rows, width)
    master_old = master[0, 0]
    master_new = master_old - row_rates * (backward_dir + DECAY_RATE * master_old)
    gain_first_new = BETA_FIRST * gain_first + (1.0 - BETA_FIRST) * gain_reduced
    gain_second_new = BETA_SECOND * gain_second + (1.0 - BETA_SECOND) * gain_reduced * gain_reduced
    gain_new = norm_gains - GAIN_RATE * (gain_first_new / (1.0 - BETA_FIRST**ADAM_STEP)) / (
        jnp.sqrt(gain_second_new / (1.0 - BETA_SECOND**ADAM_STEP)) + ADAM_EPS
    )
    return (
        block_out,
        input_grad,
        reduced[None, None],
        first_new[None, None],
        second_new[None, None],
        master_new[None, None],
        master_new.astype(jnp.bfloat16)[None, None],
        gain_reduced,
        gain_first_new,
        gain_second_new,
        gain_new,
    )


SLAB = 516
PAD = 528
HALF = 1024
QUART = 512
PACKED = 800
UNITS = 1376
NT = (((1,), (1,)), ((), ()))
TN = (((0,), (0,)), ((), ()))


VM = pl.BlockSpec(memory_space=pltpu.VMEM)
SM = pl.BlockSpec(memory_space=pltpu.SMEM)
HB = pl.BlockSpec(memory_space=pl.ANY)


def shape(rows, columns, dtype=BF16):
    return jax.ShapeDtypeStruct((rows, columns), dtype)


def call(kernel, outs, specs, args, scratch=(), flops=0, moved=0, out_specs=None, grid=None):
    extra = {} if grid is None else {"grid": grid}
    return pl.pallas_call(
        kernel,
        out_shape=outs,
        in_specs=specs,
        out_specs=[VM] * len(outs) if out_specs is None else out_specs,
        scratch_shapes=list(scratch),
        compiler_params=pltpu.CompilerParams(vmem_limit_bytes=56 * 2**20),
        cost_estimate=pl.CostEstimate(flops=flops, bytes_accessed=moved, transcendentals=0),
        name=getattr(kernel, "func", kernel).__name__,
        **extra,
    )(*args)


def root_of(values):
    return lax.rsqrt(jnp.mean(values * values, axis=-1, keepdims=True) + EPS_NORM)


def turn(values, cosine, sine):
    parts = []
    for h in range(values.shape[1] // HEAD_DIM):
        v = values[:, h * HEAD_DIM : (h + 1) * HEAD_DIM]
        parts.append(v * cosine + pltpu.roll(v, HEAD_DIM // 2, 1) * sine)
    return parts


MESH = pl.DeviceIdType.MESH


def flip(index, mask):
    for bit in (1, 2, 4):
        if mask & bit:
            index = index + bit - 2 * bit * lax.rem(lax.div(index, bit), 2)
    return index


def twist(left, right):
    out = 0
    for bit in (1, 2, 4):
        out = out + bit * lax.rem(lax.rem(lax.div(left, bit), 2) + lax.rem(lax.div(right, bit), 2), 2)
    return out


def slab_of(owners, kind, device):
    found = 0
    for j in range(8):
        found = jnp.where(owners[kind, j] == device, j, found)
    return found


class Plane:
    def __init__(self, at, sent, got, me, line):
        self.at, self.sent, self.got, self.me, self.line = at, sent, got, me, line

    def copy(self, src, dst, side, hop_mask):
        return pltpu.make_async_remote_copy(
            src_ref=self.at(src, side),
            dst_ref=self.at(dst, side),
            send_sem=self.sent.at[dst, side],
            recv_sem=self.got.at[dst, side],
            device_id=(flip(self.me, hop_mask), self.line),
            device_id_type=MESH,
        )

    def post(self, src, dst, side, hop_mask):
        self.copy(src, dst, side, hop_mask).start()

    def start_first(self):
        for mask, side in ((2, 0), (4, 1)):
            self.post(0, mask, side, mask)
        for side in (0, 1):
            self.post(0, 1, side, 1)

    def start_second(self):
        for mask, side in ((2, 1), (4, 0)):
            self.post(0, mask, side, mask)

    def start(self):
        self.start_first()
        self.start_second()

    def arrive(self, mask, side):
        self.copy(mask, mask, side, 1).wait_recv()

    def twin(self, mask, side):
        self.post(mask, mask + 1, side, 1)

    def relay_first(self):
        for mask, side in ((2, 0), (4, 1)):
            self.arrive(mask, side)
            self.post(mask, 6, side, 6 - mask)
            self.twin(mask, side)

    def relay_second(self):
        for mask, side in ((2, 1), (4, 0)):
            self.arrive(mask, side)
            self.twin(mask, side)

    def relay_last(self):
        for side in (0, 1):
            self.arrive(6, side)
            self.twin(6, side)

    def finish(self):
        for mask in (1, 3, 5, 7):
            for side in (0, 1):
                self.arrive(mask, side)

    def drain(self, masks=range(1, 8)):
        for mask in masks:
            for side in (0, 1):
                self.copy(0, mask, side, 1).wait_send()


class OneWay(Plane):
    def __init__(self, want, *rest):
        super().__init__(*rest)
        self.core, self.x, self.y = (lax.rem(lax.div(self.me, bit), 2) == want for bit in (1, 2, 4))
        self.sends = {
            (1, 0): self.core, (1, 1): self.core, (2, 0): self.x | self.y, (2, 1): self.x, (4, 0): self.y,
            (4, 1): self.y, (6, 0): self.y, (6, 1): ~self.y,
        }
        self.sends |= {(m, side): ~self.x if m == 3 else ~self.y for m in (3, 5, 7) for side in (0, 1)}
        self.gets = {
            (m, side): ~(self.core if m == 1 else self.x if m < 4 else self.y) for m in range(1, 8) for side in (0, 1)
        }
        self.gets[2, 0] = ~self.x | self.y

    def post(self, src, dst, side, hop_mask):
        pl.when(self.sends[dst, side])(lambda: self.copy(src, dst, side, hop_mask).start())

    def arrive(self, mask, side):
        pl.when(self.gets[mask, side])(lambda: self.copy(mask, mask, side, 1).wait_recv())

    def drain(self):
        for mask in range(1, 8):
            for side in (0, 1):
                pl.when(self.sends[mask, side])(lambda m=mask, s=side: self.copy(0, m, s, 1).wait_send())


def line_copy(src, dst, sent, got, m, me, line):
    return pltpu.make_async_remote_copy(
        src_ref=src,
        dst_ref=dst,
        send_sem=sent.at[m],
        recv_sem=got.at[m],
        device_id=(me, flip(line, m)),
        device_id_type=MESH,
    )


def greet(me, line, plane_masks, line_masks):
    barrier = pltpu.get_barrier_semaphore()
    for mask in plane_masks:
        pl.semaphore_signal(barrier, inc=1, device_id=(flip(me, mask), line), device_id_type=MESH)
    for mask in line_masks:
        pl.semaphore_signal(barrier, inc=1, device_id=(me, flip(line, mask)), device_id_type=MESH)
    return lambda: pl.semaphore_wait(barrier, len(plane_masks) + len(line_masks))


def layer_kernel(
    rows, scale, branch,
    owners, tokens, dy, own_gains, speeds, master,
    block_out, gain_grad, input_grad, acts, z_all, g_all, b_all, dy_all,
    gains, o_low, o_wide, stats, a_low, b_low, kcat, vcat, qcat, docat, sent, g_sent, wide, w_a, w_f, made, cut,
    total, z_out, z_in, z_sum, line_out, line_in, b_own, work, dy_own, stat_l, stat_r, gain_out, gain_in,
    sem_w, sem_k, plane_sent, plane_got, z_sems, line_sems, sum_sems, r_up, r_down, r_got, t_sent, t_got, a2a_sems, pair_sems,
):
    me, line = lax.axis_index("seq"), lax.axis_index("head")
    ready = greet(me, line, range(1, 8), (1, 2, 3))
    order_a, order_f = ([twist(owners[kind, j], me) for j in range(8)] for kind in (0, 1))
    d_low = a_low
    h_out = wide.at[pl.ds(0, rows)]
    kept = {}

    def keep(i, src, dst):
        kept[i] = pltpu.make_async_copy(src, dst, sem_k.at[i])
        kept[i].start()

    def plane(i, at):
        return Plane(at, plane_sent.at[i], plane_got.at[i], me, line)

    w_a_plane = plane(0, lambda m, s: w_a.at[m, s] if s else w_a.at[m, s, pl.ds(0, 256)])
    w_f_plane = plane(1, lambda m, s: w_f.at[m, s])
    kv_plane = OneWay(
        0, lambda m, s: (kcat, vcat)[s].at[pl.ds(m * rows, rows)], plane_sent.at[2], plane_got.at[2], me, line
    )
    q_plane = OneWay(1, lambda m, s: qcat.at[m, s], plane_sent.at[3], plane_got.at[3], me, line)
    y_plane = plane(4, lambda m, s: dy_own.at[s] if m == 0 else dy_all.at[line, m, s])
    b_plane = plane(5, lambda m, s: b_low.at[s] if m == 0 else b_all.at[m, s])
    mine = lax.rem(line, 2)
    other = 1 - mine
    a_plane = plane(
        6, lambda m, s: (acts.at[0, m, mine] if m else a_low.at[mine]).at[:, pl.ds(s * QUART, QUART)]
    )

    def a_beside():
        return pltpu.make_async_remote_copy(
            src_ref=a_low.at[other],
            dst_ref=acts.at[0, 1, other],
            send_sem=pair_sems.at[0, 0],
            recv_sem=pair_sems.at[1, 0],
            device_id=(flip(me, 1), line),
            device_id_type=MESH,
        )

    def a_exchange(m):
        return pltpu.make_async_remote_copy(
            src_ref=acts.at[0, m, mine],
            dst_ref=acts.at[0, m, mine],
            send_sem=pair_sems.at[0, m],
            recv_sem=pair_sems.at[1, m],
            device_id=(me, flip(line, 1)),
            device_id_type=MESH,
        )

    def a_twin(m):
        return pltpu.make_async_remote_copy(
            src_ref=acts.at[0, m, other],
            dst_ref=acts.at[0, m + 1, other],
            send_sem=pair_sems.at[0, m + 1],
            recv_sem=pair_sems.at[1, m + 1],
            device_id=(flip(me, 1), line),
            device_id_type=MESH,
        )

    def a_pair_on():
        for m in (2, 4, 6):
            a_exchange(m).wait_recv()
            a_twin(m).start()

    d_plane = plane(7, lambda m, s: d_low.at[s] if m == 0 else acts.at[1, m, s])
    do_plane = plane(8, lambda m, s: docat.at[m, s])

    def straight(src, dst, which, m):
        return pltpu.make_async_remote_copy(
            src_ref=src.at[m],
            dst_ref=dst.at[m],
            send_sem=a2a_sems.at[which, 0, m],
            recv_sem=a2a_sems.at[which, 1, m],
            device_id=(flip(me, m), line),
            device_id_type=MESH,
        )

    def quarter(m):
        return pl.ds(pl.multiple_of(flip(line, m) * QUART, QUART), QUART)

    def columns_of(q, c):
        return pl.ds(q * QUART + c * 256, 256)

    def partial(which, right, q, c):
        way, at = (0, q - 1) if right else (1, q)
        return pltpu.make_async_remote_copy(
            src_ref=line_out.at[way, at, c],
            dst_ref=line_in.at[which % 2, way, at, c],
            send_sem=line_sems.at[which, 0, way, at, c],
            recv_sem=line_sems.at[which, 1, way, at, c],
            device_id=(me, line + 1 if right else line - 1),
            device_id_type=MESH,
        )

    def summed(which, right, q, c):
        way = 0 if right else 1
        return pltpu.make_async_remote_copy(
            src_ref=z_sum.at[which, q, c],
            dst_ref=z_sum.at[which, q, c],
            send_sem=sum_sems.at[which, way, q, c],
            recv_sem=sum_sems.at[which, 2, q, c],
            device_id=(me, line + 1 if right else line - 1),
            device_id_type=MESH,
        )

    def pass_on(which, right, q, c, first):
        way, at = (0, q - 1) if right else (1, q)
        value = total[:, columns_of(q, c)]
        if not first:
            partial(which, right, q, c).wait_recv()
            value += line_in[which % 2, way, at, c].astype(F32)
        line_out[way, at, c] = value.astype(BF16)
        partial(which, right, q, c).start()

    ways = ((True, (3, 2, 1)), (False, (0, 1, 2)))

    def line_post(which):
        for c in (0, 1):
            for right, order in ways:

                @pl.when(line == (0 if right else 3))
                def _():
                    for q in order:
                        pass_on(which, right, q, c, True)

    merges = {1: ((True, 3), (True, 2), (False, 0)), 2: ((False, 0), (False, 1), (True, 3))}
    shares = {
        0: ((False, 1), (False, 2), (False, 3)),
        1: ((False, 2), (True, 0), (False, 3)),
        2: ((True, 1), (False, 3), (True, 0)),
        3: ((True, 2), (True, 1), (True, 0)),
    }

    def line_merge(which, chores=()):
        chores = list(chores)
        for c in (0, 1):
            for step in range(3):
                for here, order in merges.items():

                    @pl.when(line == here)
                    def _():
                        pass_on(which, *order[step], c, False)

                if chores:
                    chores.pop(0)()
            for q in range(4):

                @pl.when(line == q)
                def _():
                    value = total[:, columns_of(q, c)]
                    for right, _ in ways:
                        if q != (0 if right else 3):
                            way, at = (0, q - 1) if right else (1, q)
                            partial(which, right, q, c).wait_recv()
                            value += line_in[which % 2, way, at, c].astype(F32)
                    z_sum[which, q, c] = value.astype(BF16)
                    for right, _ in ways:
                        if q != (3 if right else 0):
                            summed(which, right, q, c).start()

            if chores:
                chores.pop(0)()
        for chore in chores:
            chore()

    def line_share(which, chores=()):
        chores = list(chores)
        for c in (0, 1):
            for step in range(3):
                for here, order in shares.items():
                    right, q = order[step]

                    @pl.when(line == here)
                    def _():
                        summed(which, right, q, c).wait_recv()
                        if here != (3 if right else 0):
                            summed(which, right, q, c).start()

                if chores:
                    chores.pop(0)()
        for chore in chores:
            chore()

    def line_sent(which):
        for c in (0, 1):
            for right, order in ways:
                for q in order:

                    @pl.when(line < q if right else line > q)
                    def _():
                        partial(which, right, q, c).wait_send()

    def line_all_sent(which):
        for c in (0, 1):
            for q in range(4):
                for right, _ in ways:

                    @pl.when((line >= q) & (line < 3) if right else (line <= q) & (line > 0))
                    def _():
                        summed(which, right, q, c).wait_send()

    def gather_sum(which, out):
        for q in range(4):
            for c in (0, 1):
                out[:, columns_of(q, c)] = z_sum[which, q, c].astype(F32)

    def b_piece(m):
        return line_copy(z_out.at[m - 1], z_in.at[m - 1], z_sems.at[0], z_sems.at[1], m, me, line)

    def along_line(quarter_index, m, up):
        return pltpu.make_async_remote_copy(
            src_ref=dy_all.at[quarter_index, m],
            dst_ref=dy_all.at[quarter_index, m],
            send_sem=(r_up if up else r_down).at[quarter_index, m],
            recv_sem=r_got.at[quarter_index, m],
            device_id=(me, line + 1 if up else line - 1),
            device_id_type=MESH,
        )

    def twin_quarter(quarter_index, m):
        return pltpu.make_async_remote_copy(
            src_ref=dy_all.at[quarter_index, m],
            dst_ref=dy_all.at[quarter_index, m + 1],
            send_sem=t_sent.at[quarter_index, m],
            recv_sem=t_got.at[quarter_index, m],
            device_id=(flip(me, 1), line),
            device_id_type=MESH,
        )

    def line_round(step):
        if step == 0:
            for up, last in ((True, 3), (False, 0)):

                @pl.when(line != last)
                def _():
                    for m in (0, 2, 4, 6):
                        along_line(line, m, up).start()

            return
        for up, first, last in ((True, step, 3), (False, 3 - step, 0)):
            index = line - step if up else line + step

            @pl.when(line >= first if up else line <= first)
            def _():
                for m in (0, 2, 4, 6):
                    along_line(index, m, up).wait_recv()

                @pl.when(line != last)
                def _():
                    for m in (0, 2, 4, 6):
                        along_line(index, m, up).start()

                for m in (0, 2, 4, 6):
                    twin_quarter(index, m).start()

    def line_end():
        for apart in (1, 2, 3):
            for up in (True, False):
                index = line - apart if up else line + apart

                @pl.when(line >= apart if up else line <= 3 - apart)
                def _():
                    for m in (0, 2, 4, 6):
                        twin_quarter(index, m).wait_recv()
                        twin_quarter(index, m).wait_send()

        for step in range(3):
            for up in (True, False):
                index = line - step if up else line + step

                @pl.when((line >= step) & (line != 3) if up else (line <= 3 - step) & (line != 0))
                def _():
                    for m in (0, 2, 4, 6):
                        along_line(index, m, up).wait_send()

    load = pltpu.make_async_copy(master.at[pl.ds(0, 256), 0, :], wide.at[pl.ds(0, 256)], sem_w.at[0])
    load.start()
    for side in (0, 1):
        at = pl.multiple_of(line * QUART + side * 256, 256)
        dy_own[side] = dy[:, pl.ds(at, 256)]
    keep(8, dy_own, dy_all.at[line, 0])
    ready()
    y_plane.start()
    w_a[0, 0, pl.ds(256, 16), :] = jnp.zeros((16, HALF), BF16)
    w_a[0, 1, pl.ds(256, 16), :] = jnp.zeros((16, HALF), BF16)
    w_a[0, 1, 256:258, 0:256] = own_gains[...].astype(BF16)
    load.wait()
    for side in (0, 1):
        w_a[0, side, pl.ds(0, 256), :] = wide[pl.ds(0, 256), side * HALF : (side + 1) * HALF].astype(BF16)
    load = pltpu.make_async_copy(master.at[pl.ds(256, 256), 0, :], wide.at[pl.ds(0, 256)], sem_w.at[1])
    load.start()
    w_a_plane.start()
    load.wait()
    for side in (0, 1):
        columns = slice(side * HALF, (side + 1) * HALF)
        w_f[0, side, pl.ds(0, 256), :] = wide[pl.ds(0, 256), columns].astype(BF16)
    load = pltpu.make_async_copy(master.at[pl.ds(512, SLAB - 256), 0, :], wide, sem_w.at[2])
    load.start()
    load.wait()
    for side in (0, 1):
        columns = slice(side * HALF, (side + 1) * HALF)
        w_f[0, side, pl.ds(256, 256), :] = wide[pl.ds(0, 256), columns].astype(BF16)
        last = jnp.concatenate([wide[256 : SLAB - 256, columns], jnp.zeros((PAD - SLAB, HALF), F32)], axis=0)
        w_f[0, side, pl.ds(512, 16), :] = last.astype(BF16)
    for m in range(1, 8):

        @pl.when(flip(me, m) > me)
        def _():
            vcat[pl.ds(m * rows, rows), :] = jnp.zeros((rows, QUART), BF16)

    angle = (me * rows + lax.broadcasted_iota(jnp.int32, (rows, 1), 0)).astype(F32) * speeds[...]
    cosine, sine = jnp.cos(angle), jnp.sin(angle)
    sine = jnp.where(lax.broadcasted_iota(jnp.int32, (1, HEAD_DIM), 1) < HEAD_DIM // 2, -sine, sine)
    y_plane.relay_first()
    y_plane.relay_second()
    y_plane.relay_last()
    kept[8].wait()
    line_round(0)
    w_a_plane.relay_first()
    w_a_plane.relay_second()
    w_f_plane.start_first()
    w_a_plane.relay_last()
    w_a_plane.finish()

    for m in range(8):
        at = pl.multiple_of(flip(me, m) * 256, 256)
        gains[:, pl.ds(at, 256)] = w_a[m, 1, 256:258, 0:256].astype(F32)
    x = tokens[...].astype(F32)
    normed = (x * root_of(x) * gains[0:1, :]).astype(BF16)
    for side in (0, 1):
        a_low[side] = normed[:, side * HALF : (side + 1) * HALF]
    for j in (2, 3, 4, 5, 0, 1):
        out = lax.dot_general(a_low[0], w_a[order_a[j], 0, pl.ds(0, 256), :], NT, preferred_element_type=F32)
        out += lax.dot_general(a_low[1], w_a[order_a[j], 1, pl.ds(0, 256), :], NT, preferred_element_type=F32)
        if j < 4:
            parts = turn(out, cosine, sine)
        else:
            parts = [out[:, :HEAD_DIM], out[:, HEAD_DIM:]]
        for i, part in enumerate(parts):
            if j < 2:
                qcat[0, j, :, i * HEAD_DIM : (i + 1) * HEAD_DIM] = part.astype(BF16)
            else:
                at = (2 * (j % 2) + i) * HEAD_DIM
                (kcat, vcat)[j // 2 - 1][pl.ds(0, rows), at : at + HEAD_DIM] = part.astype(BF16)
        if j == 5:
            kv_plane.start()
    keep(0, a_low, acts.at[0, 0])
    q_plane.start()
    a_plane.start()
    a_beside().start()
    line_round(1)
    kv_plane.relay_first()
    kv_plane.relay_second()
    q_plane.relay_first()
    q_plane.relay_second()
    w_f_plane.relay_first()
    a_plane.relay_first()
    a_plane.relay_second()
    w_f_plane.start_second()
    kv_plane.relay_last()
    kv_plane.finish()
    q_plane.relay_last()

    at_q = me * rows + lax.broadcasted_iota(jnp.int32, (rows, 1), 0)
    along = lax.broadcasted_iota(jnp.int32, (1, rows), 1)
    lane = lax.broadcasted_iota(jnp.int32, (rows, HEAD_DIM), 1)
    stat = jnp.zeros((rows, HEAD_DIM), F32)
    for h in range(4):
        if h == 2:
            line_round(2)
        columns = slice(h * HEAD_DIM, (h + 1) * HEAD_DIM)
        q = qcat[0, h // 2, :, (h % 2) * HEAD_DIM : (h % 2 + 1) * HEAD_DIM]
        top = jnp.full((rows, 1), NEGATIVE, F32)
        for m in range(8):
            ahead = at_q - (flip(me, m) * rows + along)
            s = lax.dot_general(q, kcat[pl.ds(m * rows, rows), columns], NT, preferred_element_type=F32)
            s = jnp.where((ahead >= 0) & (ahead < WINDOW), s * scale, NEGATIVE)
            work[m, :, pl.ds(0, rows)] = s
            top = jnp.maximum(top, jnp.max(s, axis=-1, keepdims=True))
        sums = jnp.zeros((rows, 1), F32)
        for m in range(8):
            e = jnp.exp(work[m, :, pl.ds(0, rows)] - top)
            work[m, :, pl.ds(0, rows)] = e
            sums += jnp.sum(e, axis=-1, keepdims=True)
        share = 1.0 / sums
        o = jnp.zeros((rows, HEAD_DIM), F32)
        for m in range(8):
            soft = (work[m, :, pl.ds(0, rows)] * share).astype(BF16)
            o += jnp.dot(soft, vcat[pl.ds(m * rows, rows), columns], preferred_element_type=F32)
        o_wide[:, columns] = o
        o_low[:, columns] = o.astype(BF16)
        stat = jnp.where(lane == h, top + jnp.log(sums), stat)
    stats[...] = stat
    for side in (0, 1):
        out = jnp.dot(o_low[:, :256], w_a[order_a[6], side, pl.ds(0, 256), :], preferred_element_type=F32)
        out += jnp.dot(o_low[:, 256:], w_a[order_a[7], side, pl.ds(0, 256), :], preferred_element_type=F32)
        total[:, side * HALF : (side + 1) * HALF] = branch * out

    line_post(0)
    line_merge(0)
    line_share(0, [lambda: None, w_f_plane.relay_last])
    a_plane.relay_last()
    for m in (2, 4, 6):
        a_exchange(m).start()

    gather_sum(0, h_out)
    h = h_out[...] + tokens[...].astype(F32)
    h_out[...] = h
    normed = (h * root_of(h) * gains[1:2, :]).astype(BF16)
    for side in (0, 1):
        b_low[side] = normed[:, side * HALF : (side + 1) * HALF]
    keep(1, b_low, b_all.at[0])
    b_plane.start()
    w_f_plane.relay_second()
    w_f_plane.finish()

    def through(j, left, right):
        out = lax.dot_general(w_f[order_f[j], 0], left, NT, preferred_element_type=F32)
        return out + lax.dot_general(w_f[order_f[j], 1], right, NT, preferred_element_type=F32)

    some = pl.ds(0, rows)
    made[pl.ds(8 * SLAB, 16), some] = jnp.zeros((16, rows), F32)
    row = lax.broadcasted_iota(jnp.int32, (PAD, 1), 0)
    gate_rows = row < 2 * UNITS - 5 * SLAB
    for j in range(8):
        if j < 5:
            out = through(j, b_low[0], b_low[1])
        elif j > 5:
            out = through(j, dy[:, :HALF], dy[:, HALF:])
        else:
            out = jnp.where(gate_rows, through(j, b_low[0], b_low[1]), through(j, dy[:, :HALF], dy[:, HALF:]))
        made[pl.ds(j * SLAB, PAD), some] = out

    def mix(i, _):
        at = pl.multiple_of(i * 32, 8)
        gate = made[pl.ds(at, 32), some]
        up = made[pl.ds(UNITS + at, 32), some]
        back = made[pl.ds(2 * UNITS + at, 32), some]
        sigma = 1.0 / (1.0 + jnp.exp(-gate))
        silu = gate * sigma
        made[pl.ds(at, 32), some] = back * up * (sigma * (1.0 + gate * (1.0 - sigma)))
        made[pl.ds(UNITS + at, 32), some] = back * silu
        made[pl.ds(2 * UNITS + at, 32), some] = silu * up
        return 0

    lax.fori_loop(0, UNITS // 32, mix, 0)
    for j in range(8):
        cut[j, :, pl.ds(0, rows)] = made[pl.ds(j * SLAB, PAD), some].astype(BF16)
    def down(first, side):
        out = None
        for j in range(0, 6) if first else range(5, 8):
            z = cut[j, :, pl.ds(0, rows)]
            if j == 5:
                z = jnp.where(gate_rows if first else ~gate_rows, z, jnp.zeros_like(z))
            made_j = lax.dot_general(z, w_f[order_f[j], side], TN, preferred_element_type=F32)
            out = made_j if out is None else out + made_j
        return out

    line_sent(0)
    for side in (0, 1):
        total[:, side * HALF : (side + 1) * HALF] = down(True, side)
    line_post(1)
    def pack(m):
        z = cut[slab_of(owners, 1, flip(me, m)), :, pl.ds(0, rows)]
        sent[m, pl.ds(0, PAD), :] = z[:, :128]
        late = z[:, 128:].astype(F32)
        late = jnp.concatenate([late[: PAD // 2], late[PAD // 2 :]], axis=1)
        late = jnp.concatenate([late, jnp.zeros((PACKED - PAD - PAD // 2, 128), F32)], axis=0)
        sent[m, pl.ds(PAD, PACKED - PAD), :] = late.astype(BF16)
        if m:
            straight(sent, z_all, 0, m).start()
        else:
            keep(2, sent.at[0], z_all.at[0])

    def down_out(side):
        out = down(False, side)
        for c in range(4):
            made[pl.ds((4 * side + c) * rows, rows), :] = out[:, c * 256 : (c + 1) * 256]

    def down_parts():
        for m in range(4):
            for c in (0, 1):
                at = pl.multiple_of((2 * flip(line, m) + c) * rows, 64)
                block = made[pl.ds(at, rows), :]
                if m == 0:
                    b_own[:, c * 256 : (c + 1) * 256] = block
                else:
                    z_out[m - 1, :, c * 256 : (c + 1) * 256] = block.astype(BF16)

    line_merge(1, [functools.partial(pack, m) for m in (2, 4, 6, 3, 5, 7, 1, 0)] + [a_pair_on])
    line_share(
        1,
        [
            b_plane.relay_first, functools.partial(down_out, 0), functools.partial(down_out, 1),
            b_plane.relay_second, down_parts, lambda: line_round(3),
        ],
    )
    for m in (3, 2, 1):
        b_piece(m).start()

    gather_sum(1, total)
    normed_grad = total[...]
    h = h_out[...]
    root = root_of(h)
    gain_two = jnp.sum(normed_grad * h * root, axis=0, keepdims=True)
    weighted = normed_grad * gains[1:2, :]
    inner = jnp.mean(weighted * h, axis=-1, keepdims=True)
    grad = dy[...].astype(F32) + root * weighted - h * (root * root * root) * inner
    for c in range(8):
        made[pl.ds(c * rows, rows), :] = grad[:, c * 256 : (c + 1) * 256]
    low = grad.astype(BF16)
    kept[0].wait()
    a_plane.drain((1, 2, 4))
    a_beside().wait_send()
    for side in (0, 1):
        d_low[side] = low[:, side * HALF : (side + 1) * HALF]
    keep(3, d_low, acts.at[1, 0])
    total[0:1, :] = gain_two
    for m in range(8):
        at = pl.multiple_of(flip(me, m) * 256, 256)
        gain_out[m, 1:2, :] = total[0:1, pl.ds(at, 256)]
    lane = lax.broadcasted_iota(jnp.int32, (rows, HEAD_DIM), 1)
    own_lines = []
    for j, stat in enumerate((stat_l, stat_r)):
        out = lax.dot_general(d_low[0], w_a[order_a[6 + j], 0, pl.ds(0, 256), :], NT, preferred_element_type=F32)
        out += lax.dot_general(d_low[1], w_a[order_a[6 + j], 1, pl.ds(0, 256), :], NT, preferred_element_type=F32)
        out = (branch * out).astype(BF16)
        docat[0, j, pl.ds(0, rows), :] = out
        lines = jnp.zeros((rows, HEAD_DIM), F32)
        columns = []
        for i in (0, 1):
            h_at = 2 * j + i
            span = slice(h_at * HEAD_DIM, (h_at + 1) * HEAD_DIM)
            delta = jnp.sum(
                out[:, i * HEAD_DIM : (i + 1) * HEAD_DIM].astype(F32) * o_wide[:, span], axis=-1, keepdims=True
            )
            top = stats[:, h_at : h_at + 1]
            columns.append((top, delta))
            for at, value in ((i, top), (2 + i, delta)):
                for step in range(3):
                    part = value.astype(BF16).astype(F32)
                    value = value - part
                    lines = jnp.where(lane == 4 * step + at, part, lines)
        own_lines.append(columns)
        stat[pl.ds(0, rows), :] = lines
        stat[pl.ds(rows, 256 - rows), :] = jnp.zeros((256 - rows, HEAD_DIM), F32)
        docat[0, j, pl.ds(rows, 16), :] = stat[...].T[:16, :].astype(BF16)
    do_plane.start()
    b_plane.relay_last()

    for i in range(6):
        work[i] = jnp.zeros((rows, 256), F32)
    reach = -(-WINDOW // rows)
    below = lax.broadcasted_iota(jnp.int32, (rows, rows), 0)
    along = lax.broadcasted_iota(jnp.int32, (rows, rows), 1)

    def head_cut(h):
        return h // 2, slice((h % 2) * HEAD_DIM, (h % 2 + 1) * HEAD_DIM), slice(h * HEAD_DIM, (h + 1) * HEAD_DIM)

    def rows_of(m):
        return pl.ds(m * rows, rows)

    def query_side(m):
        apart = me - flip(me, m)

        @pl.when((apart >= 0) & (apart <= reach))
        def _():
            ahead = apart * rows + below - along
            allowed = (ahead >= 0) & (ahead < WINDOW)
            for h in range(4):
                side, two, span = head_cut(h)
                top, delta = own_lines[side][h % 2]
                k, do = kcat[rows_of(m), span], docat[0, side, pl.ds(0, rows), two]
                s = lax.dot_general(qcat[0, side, :, two], k, NT, preferred_element_type=F32)
                p = jnp.where(allowed, jnp.exp(s * scale - top), 0.0)
                dp = lax.dot_general(do, vcat[rows_of(m), span], NT, preferred_element_type=F32)
                ds = (p * (dp - delta) * scale).astype(BF16)
                work[side, :, two] += jnp.dot(ds, k, preferred_element_type=F32)

    def key_side(m):
        apart = me - flip(me, m)

        @pl.when((apart <= 0) & (apart >= -reach))
        def _():
            ahead = along - below - apart * rows
            allowed = (ahead >= 0) & (ahead < WINDOW)
            for h in range(4):
                side, two, span = head_cut(h)
                lines = docat[m, side, pl.ds(rows, 16), :].astype(F32)
                lines = (lines[0:4] + lines[4:8] + lines[8:12])[:, :rows]
                top, delta = lines[h % 2 : h % 2 + 1], lines[2 + h % 2 : 3 + h % 2]
                q, do = qcat[m, side, :, two], docat[m, side, pl.ds(0, rows), two]
                s = lax.dot_general(kcat[pl.ds(0, rows), span], q, NT, preferred_element_type=F32)
                p = jnp.where(allowed, jnp.exp(s * scale - top), 0.0)
                work[4 + side, :, two] += jnp.dot(p.astype(BF16), do, preferred_element_type=F32)
                dp = lax.dot_general(vcat[pl.ds(0, rows), span], do, NT, preferred_element_type=F32)
                ds = (p * (dp - delta) * scale).astype(BF16)
                work[2 + side, :, two] += jnp.dot(ds, q, preferred_element_type=F32)

    for m in range(4):
        query_side(m)
    do_plane.relay_first()
    for m in range(4, 8):
        query_side(m)
    do_plane.relay_second()
    do_plane.relay_last()
    d_plane.start()
    do_plane.finish()
    q_plane.finish()
    for m in range(8):
        key_side(m)
    for j in range(8):
        two = slice((j % 2) * 256, (j % 2 + 1) * 256)
        if j < 4:
            made_j = turn(work[j], cosine, -sine)
            for i in (0, 1):
                cut[j, pl.ds(0, rows), i * HEAD_DIM : (i + 1) * HEAD_DIM] = made_j[i].astype(BF16)
        elif j < 6:
            cut[j, pl.ds(0, rows), :] = work[j].astype(BF16)
        else:
            cut[j, pl.ds(0, rows), :] = o_low[:, two]
    line_sent(1)
    for j in range(6):
        for side in (0, 1):
            out = jnp.dot(cut[j, pl.ds(0, rows), :], w_a[order_a[j], side, pl.ds(0, 256), :], preferred_element_type=F32)
            columns = slice(side * HALF, (side + 1) * HALF)
            total[:, columns] = out if j == 0 else total[:, columns] + out
    line_post(2)

    def send_group(m):
        g_sent[m] = cut[slab_of(owners, 0, flip(me, m)), pl.ds(0, rows), :]
        if m:
            straight(g_sent, g_all, 1, m).start()
        else:
            keep(4, g_sent.at[0], g_all.at[0])

    line_merge(2, [functools.partial(send_group, m) for m in (2, 4, 6, 3, 5, 7, 1)] + [d_plane.relay_first])
    send_group(0)
    line_share(2, [lambda: None, d_plane.relay_second])
    out = h_out[:, quarter(0)] + b_own[...]
    for m in (1, 2, 3):
        b_piece(m).wait_recv()
        out += z_in[m - 1].astype(F32)
    block_out[...] = out.astype(BF16)

    gather_sum(2, total)
    normed_grad = total[...]
    x = tokens[...].astype(F32)
    root = root_of(x)
    gain_one = jnp.sum(normed_grad * x * root, axis=0, keepdims=True)
    weighted = normed_grad * gains[0:1, :]
    inner = jnp.mean(weighted * x, axis=-1, keepdims=True)
    grad = root * weighted - x * (root * root * root) * inner
    for c in range(8):
        made[pl.ds(c * rows, rows), :] += grad[:, c * 256 : (c + 1) * 256]
    total[0:1, :] = gain_one
    for m in range(8):
        at = pl.multiple_of(flip(me, m) * 256, 256)
        gain_out[m, 0:1, :] = total[0:1, pl.ds(at, 256)]
    for c in range(8):
        keep(9 + c, made.at[pl.ds(c * rows, rows)], input_grad.at[:, pl.ds(c * 256, 256)])
    for m in range(1, 8):
        straight(gain_out, gain_in, 2, m).start()
    d_plane.relay_last()
    for m in range(1, 8):
        straight(gain_out, gain_in, 2, m).wait_recv()
    made = gain_out[0, 0:2, :]
    for m in range(1, 8):
        made += gain_in[m, 0:2, :]
    gain_grad[...] = made
    for one in (y_plane, b_plane, d_plane, a_plane):
        one.finish()
    line_end()
    a_beside().wait_recv()
    for m in (2, 4, 6):
        a_exchange(m).wait_send()
        a_twin(m).wait_recv()
        a_twin(m).wait_send()
    for m in range(1, 8):
        straight(sent, z_all, 0, m).wait_recv()
        straight(g_sent, g_all, 1, m).wait_recv()
    a_plane.drain((3, 5, 6, 7))
    for one in (w_a_plane, w_f_plane, kv_plane, q_plane, y_plane, b_plane, d_plane, do_plane):
        one.drain()
    for m in range(1, 8):
        straight(sent, z_all, 0, m).wait_send()
        straight(g_sent, g_all, 1, m).wait_send()
        straight(gain_out, gain_in, 2, m).wait_send()
    line_sent(2)
    for which in range(3):
        line_all_sent(which)
    for m in (1, 2, 3):
        b_piece(m).wait_send()
    for i in kept:
        if i not in (0, 8):
            kept[i].wait()


def layer(owners, tokens, dy, own_gains, speeds, master, scale, branch):
    rows, width = tokens.shape
    array = jax.ShapeDtypeStruct
    dma = pltpu.SemaphoreType.DMA

    def low(*sizes):
        return pltpu.VMEM(sizes, BF16)

    def wide(*sizes):
        return pltpu.VMEM(sizes, F32)

    return pl.pallas_call(
        functools.partial(layer_kernel, rows, scale, branch),
        out_shape=[
            shape(rows, QUART),
            array((2, 256), F32),
            shape(rows, width, F32),
            array((2, 8, 2, rows, HALF), BF16),
            array((8, PACKED, 128), BF16),
            array((8, rows, 256), BF16),
            array((8, 2, rows, HALF), BF16),
            array((4, 8, 2, rows, 256), BF16),
        ],
        in_specs=[SM] + [VM] * 4 + [HB],
        out_specs=[VM] * 2 + [HB] * 6,
        scratch_shapes=[
            wide(2, width),
            low(rows, QUART),
            wide(rows, QUART),
            wide(rows, HEAD_DIM),
            low(2, rows, HALF),
            low(2, rows, HALF),
            low(8 * rows, QUART),
            low(8 * rows, QUART),
            low(8, 2, rows, 256),
            low(8, 2, rows + 16, 256),
            low(8, PACKED, 128),
            low(8, rows, 256),
            wide(SLAB - 256, width),
            low(8, 2, 272, HALF),
            low(8, 2, PAD, HALF),
            wide(8 * SLAB + 16, 256),
            low(8, PAD, 256),
            wide(rows, width),
            low(3, rows, QUART),
            low(3, rows, QUART),
            low(3, 4, 2, rows, 256),
            low(2, 3, 2, rows, 256),
            low(2, 2, 3, 2, rows, 256),
            wide(rows, QUART),
            wide(8, rows, 256),
            low(2, rows, 256),
            wide(256, HEAD_DIM),
            wide(256, HEAD_DIM),
            wide(8, 8, 256),
            wide(8, 8, 256),
            dma((3,)),
            dma((17,)),
            dma((9, 8, 2)),
            dma((9, 8, 2)),
            dma((2, 4)),
            dma((3, 2, 2, 3, 2)),
            dma((3, 3, 4, 2)),
        ]
        + [dma((4, 8))] * 5
        + [dma((3, 2, 8)), dma((2, 8))],
        compiler_params=pltpu.CompilerParams(
            collective_id=0, has_side_effects=True, vmem_limit_bytes=63 * 2**20
        ),
        cost_estimate=pl.CostEstimate(flops=2 * 10**10, bytes_accessed=60 * 2**20, transcendentals=0),
        name="layer",
    )(owners, tokens, dy, own_gains, speeds, master)


TILE = 256


def update_kernel(rows, branch, owners, basis, gain_grad, norm_gains, gain_first, gain_second, *rest):
    (zs, gs, acts, bs, dys), olds, through, rest = rest[:5], rest[5:8], rest[8:10], rest[10:]
    news, low_new, passed, gain_news, rest = rest[:4], rest[4], rest[5:7], rest[7:11], rest[11:]
    turned_g, turned_z, wide_basis, act, old, new, z_got, g_got, block, carried, asem, osem, nsem, sems = rest
    me, line = lax.axis_index("seq"), lax.axis_index("head")
    tile, tiles = pl.program_id(0), pl.num_programs(0)
    slot = tile % 2
    a_slab, f_slab = slab_of(owners, 0, me), slab_of(owners, 1, me)

    def columns_of(t):
        return pl.ds(pl.multiple_of(t * TILE, TILE), TILE)

    def act_copy(t, kind, which):
        at = pl.ds(pl.multiple_of(lax.rem(t, HALF // TILE) * TILE, TILE), TILE)
        if kind == 3:
            part = dys.at[lax.div(t, 2), :, lax.rem(t, 2)]
        elif kind == 2:
            part = bs.at[:, lax.div(t, HALF // TILE), :, at]
        else:
            part = acts.at[kind, :, lax.div(t, HALF // TILE), :, at]
        return pltpu.make_async_copy(part, act.at[t % 2, which], asem.at[t % 2, which])

    def act_copies(t, kind, which):
        act_copy(t, kind, which).start()

    def act_wait(which):
        act_copy(tile, 2, which).wait()

    def factor_of(which):
        return act[slot, which].reshape(8 * rows, TILE)

    def fetch_acts(t):
        pl.when(a_slab < 6)(lambda: act_copies(t, 0, 0))
        pl.when(a_slab >= 6)(lambda: act_copies(t, 1, 0))
        pl.when(f_slab <= 5)(lambda: act_copies(t, 2, 1))
        pl.when(f_slab > 5)(lambda: act_copies(t, 3, 1))
        pl.when(f_slab == 5)(lambda: act_copies(t, 3, 2))

    def old_copy(i, t):
        return pltpu.make_async_copy(olds[i].at[:, 0, columns_of(t)], old.at[t % 2, i], osem.at[t % 2, i])

    def new_copy(i, t):
        return pltpu.make_async_copy(new.at[t % 2, i], news[i].at[:, 0, columns_of(t)], nsem.at[t % 2, i])

    def fetch(t):
        fetch_acts(t)
        for i in range(3):
            old_copy(i, t).start()

    @pl.when(tile == 0)
    def _():
        small = [pltpu.make_async_copy(*pair, sems.at[i]) for i, pair in enumerate(((gs, g_got), (zs, z_got)))]
        for copy in small:
            copy.start()
        fetch(0)
        for i in (0, 1):
            pltpu.make_async_copy(through[i], (block, carried)[i], sems.at[2 + i]).start()
        made = gain_grad[...]
        one = BETA_FIRST * gain_first[...] + (1.0 - BETA_FIRST) * made
        two = BETA_SECOND * gain_second[...] + (1.0 - BETA_SECOND) * made * made
        gain_news[0][...] = made
        gain_news[1][...] = one
        gain_news[2][...] = two
        gain_news[3][...] = norm_gains[...] - GAIN_RATE * (one / (1.0 - BETA_FIRST**ADAM_STEP)) / (
            jnp.sqrt(two / (1.0 - BETA_SECOND**ADAM_STEP)) + ADAM_EPS
        )
        wide_basis[...] = jnp.zeros_like(wide_basis)
        for copy in small:
            copy.wait()
        turned_g[...] = g_got[...].reshape(8 * rows, 256).T
        lane = lax.broadcasted_iota(jnp.int32, (PAD, 128), 1)
        for m in range(0, 8, 2):
            early, late = [], []
            for i in (0, 1):
                early.append(z_got[m + i, pl.ds(0, PAD), :].astype(F32))
                pair = z_got[m + i, pl.ds(PAD, PAD // 2), :].astype(F32)
                other = pltpu.roll(pair, 64, 1)
                late.append(jnp.concatenate([other, pair] if i else [pair, other], axis=0))
            shifted = pltpu.roll(early[1], 64, 1)
            made = (early[0], jnp.where(lane < 64, late[0], shifted), jnp.where(lane < 64, shifted, late[1]))
            for i in range(3):
                at = m * rows + i * 128
                turned_z[:, at : at + 128] = made[i].astype(BF16)

    pl.when(tile + 1 < tiles)(lambda: fetch(tile + 1))

    @pl.when(tile == 1)
    def _():
        for i in (0, 1):
            pltpu.make_async_copy(through[i], (block, carried)[i], sems.at[2 + i]).wait()
            pltpu.make_async_copy((block, carried)[i], passed[i], sems.at[4 + i]).start()


    @pl.when(tile >= 2)
    def _():
        for i in range(4):
            new_copy(i, tile - 2).wait()

    grad, first_new, second_new, master_new = (new.at[slot, i] for i in range(4))
    first, second, master = (old.at[slot, i] for i in range(3))

    def ffn_rows(which, start, stop):
        return jnp.dot(turned_z[start:stop, :], factor_of(which), preferred_element_type=F32)

    act_wait(0)
    factor = jnp.where(a_slab < 6, 1.0, branch)
    grad[pl.ds(0, 256), :] = factor * jnp.dot(turned_g[...], factor_of(0), preferred_element_type=F32)
    act_wait(1)
    first_of_down = 2 * UNITS - f_slab * SLAB
    edge = 2 * UNITS - 5 * SLAB
    low_edge, high_edge = edge // 16 * 16, -(-edge // 16) * 16

    @pl.when(f_slab != 5)
    def _():
        grad[pl.ds(256, SLAB), :] = ffn_rows(1, 0, PAD)[:SLAB]

    @pl.when(f_slab == 5)
    def _():
        upper = ffn_rows(1, 0, high_edge)
        act_wait(2)
        lower = ffn_rows(2, low_edge, PAD)
        row = low_edge + lax.broadcasted_iota(jnp.int32, (high_edge - low_edge, 1), 0)
        grad[pl.ds(256, low_edge), :] = upper[:low_edge]
        grad[pl.ds(256 + low_edge, high_edge - low_edge), :] = jnp.where(
            row < edge, upper[low_edge:], lower[: high_edge - low_edge]
        )
        grad[pl.ds(256 + high_edge, SLAB - high_edge), :] = lower[high_edge - low_edge : SLAB - low_edge]

    for i in range(3):
        old_copy(i, tile).wait()
    row = lax.broadcasted_iota(jnp.int32, (256 + SLAB, 1), 0)
    rate = jnp.where((row < 256) | (row - 256 < first_of_down), 0.5 * (2 * HALF) ** (-0.5), 0.5 * FF ** (-0.5))
    for b in range(TILE // HEAD_DIM):
        cut = slice(b * HEAD_DIM, (b + 1) * HEAD_DIM)
        wide_basis[cut, cut] = basis[b].astype(BF16)
    turned = jnp.dot(grad[...].astype(BF16), wide_basis[...], preferred_element_type=F32)
    one = BETA_FIRST * first[...] + (1.0 - BETA_FIRST) * turned
    two = BETA_SECOND * second[...] + (1.0 - BETA_SECOND) * turned * turned
    first_new[...] = one
    second_new[...] = two
    adam = (one / (1.0 - BETA_FIRST**ADAM_STEP)) / (jnp.sqrt(two / (1.0 - BETA_SECOND**ADAM_STEP)) + ADAM_EPS)
    back = lax.dot_general(adam.astype(BF16), wide_basis[...], NT, preferred_element_type=F32)
    before = master[...]
    after = before - rate * (back + DECAY_RATE * before)
    master_new[...] = after
    low_new[...] = after.astype(BF16)
    for i in range(4):
        new_copy(i, tile).start()

    @pl.when(tile == tiles - 1)
    def _():
        for t in (tile - 1, tile):
            for i in range(4):
                new_copy(i, t).wait()
        for i in (0, 1):
            pltpu.make_async_copy((block, carried)[i], passed[i], sems.at[4 + i]).wait()


def update(owners, basis, small, zs, gs, acts, bs, dys, olds, through, branch):
    rows = gs.shape[1]
    height, _, width = olds[0].shape

    def whole(array):
        return pl.BlockSpec(array.shape, lambda i: (0,) * array.ndim)

    tall = pl.BlockSpec((height, TILE), lambda i: (0, i))
    per = TILE // HEAD_DIM
    gains = [shape(*array.shape, F32) for array in small]
    return call(
        functools.partial(update_kernel, rows, branch),
        [jax.ShapeDtypeStruct(olds[0].shape, F32)] * 4
        + [shape(height, width)]
        + [jax.ShapeDtypeStruct(array.shape, array.dtype) for array in through]
        + gains,
        [SM, pl.BlockSpec((per, HEAD_DIM, HEAD_DIM), lambda i: (i, 0, 0))]
        + [whole(array) for array in small]
        + [HB] * 10,
        [owners, basis, *small, zs, gs, acts, bs, dys, *olds, *through],
        [
            pltpu.VMEM((256, 8 * rows), BF16),
            pltpu.VMEM((PAD, 8 * rows), BF16),
            pltpu.VMEM((TILE, TILE), BF16),
            pltpu.VMEM((2, 3, 8, rows, TILE), BF16),
            pltpu.VMEM((2, 3, height, TILE), F32),
            pltpu.VMEM((2, 4, height, TILE), F32),
            pltpu.VMEM(zs.shape, BF16),
            pltpu.VMEM(gs.shape, BF16),
            *[pltpu.VMEM(array.shape, array.dtype) for array in through],
            pltpu.SemaphoreType.DMA((2, 3)),
            pltpu.SemaphoreType.DMA((2, 3)),
            pltpu.SemaphoreType.DMA((2, 4)),
            pltpu.SemaphoreType.DMA((6,)),
        ],
        out_specs=[HB] * 4 + [tall] + [HB] * 2 + [whole(array) for array in small],
        grid=(width // TILE,),
        flops=2 * 8 * rows * height * width,
        moved=70 * 2**20,
    )


def plane_mesh(
    tokens,
    cotangent,
    owners,
    master,
    first_moment,
    second_moment,
    eigenbases,
    norm_gains,
    gain_first,
    gain_second,
):
    rows, width = tokens.shape
    scale = HEAD_DIM ** (-0.5)
    branch = (WINDOW / 3.0) ** 0.5
    half = HEAD_DIM // 2
    speeds = ROPE_BASE ** (-jnp.arange(half, dtype=F32) / half)
    speeds = jnp.concatenate([speeds, speeds])[None, :]
    tall = [array.reshape(array.shape[2], 1, width) for array in (first_moment, second_moment, master)]
    block_out, gain_grad, input_grad, acts, zs, gs, bs, dys = layer(
        owners, tokens, cotangent, norm_gains, speeds, tall[2], scale, branch
    )
    (
        grad, first_new, second_new, master_new, low_new, block_out, input_grad, gain_grad, gain_first_new,
        gain_second_new, gain_new,
    ) = update(
        owners, eigenbases[0, 0], [gain_grad, norm_gains, gain_first, gain_second], zs, gs, acts, bs, dys, tall,
        [block_out, input_grad], branch,
    )
    whole = (1, 1, *tall[0].shape[::2])
    return (
        block_out,
        input_grad,
        grad.reshape(whole),
        first_new.reshape(whole),
        second_new.reshape(whole),
        master_new.reshape(whole),
        low_new[None, None],
        gain_grad,
        gain_first_new,
        gain_second_new,
        gain_new,
    )


def solution(mesh):
    in_specs = (
        P("seq", None),
        P("seq", None),
        P(),
        P("head", "seq", None, None),
        P("head", "seq", None, None),
        P("head", "seq", None, None),
        P("head", "seq", None, None, None),
        P(None, "seq"),
        P(None, "seq"),
        P(None, "seq"),
    )
    out_specs = (
        P("seq", "head"),
        P("seq", None),
        P("head", "seq", None, None),
        P("head", "seq", None, None),
        P("head", "seq", None, None),
        P("head", "seq", None, None),
        P("head", "seq", None, None),
        P(None, "seq"),
        P(None, "seq"),
        P(None, "seq"),
        P(None, "seq"),
    )
    plane = mesh.shape["seq"] == 8 and mesh.shape["head"] == 4
    return jax.shard_map(
        plane_mesh if plane else any_mesh, mesh=mesh, in_specs=in_specs, out_specs=out_specs, check_vma=False
    )
```

```python
import functools

import jax
import jax.numpy as jnp
from jax import lax
from jax.experimental import pallas as pl
from jax.experimental.pallas import tpu as pltpu
from jax.sharding import PartitionSpec as P

HEADS = 16
HEAD_DIM = 128
FF = 5504
WINDOW = 1024
ADAM_STEP = 5


EPS_NORM = 1e-05
BETA_FIRST = 0.5
BETA_SECOND = 0.6
ADAM_EPS = 1e-08
DECAY_RATE = 0.1
GAIN_RATE = 0.25
ROPE_BASE = 10000.0
NEGATIVE = -1e30
PRECISE = lax.Precision.HIGHEST

BF16 = jnp.bfloat16
F32 = jnp.float32


def passed_along(shard, axis, by):
    devices = lax.axis_size(axis)
    pairs = [(i, i + by) for i in range(devices) if 0 <= i + by < devices]
    return lax.ppermute(shard, axis, pairs)


def inverse_order(owner_row):
    places = jnp.arange(owner_row.shape[0], dtype=jnp.int32)
    matches = (owner_row[:, None] == places[None, :]).astype(jnp.int32)
    return jnp.sum(matches * places[:, None], axis=0)


def kind_rates(kinds, width):
    wide = width ** (-0.5)
    spreads = jnp.array([wide, wide, wide, wide, wide, wide, FF ** (-0.5)], jnp.float32)
    matches = (kinds[..., None] == jnp.arange(7, dtype=jnp.int32)).astype(jnp.float32)
    return 0.5 * jnp.sum(matches * spreads, axis=-1)


def angles(positions):
    half_dim = HEAD_DIM // 2
    frequencies = ROPE_BASE ** (-jnp.arange(half_dim, dtype=jnp.float32) / half_dim)
    turning = positions[:, None] * frequencies[None, :]
    return (jnp.cos(turning)[:, None, :], jnp.sin(turning)[:, None, :])


def rotate(vectors, cosine, sine):
    half_dim = vectors.shape[-1] // 2
    former = vectors[..., :half_dim]
    latter = vectors[..., half_dim:]
    return jnp.concatenate(
        [former * cosine - latter * sine, latter * cosine + former * sine], axis=-1
    )


def inverse_rms(vectors):
    return lax.rsqrt(jnp.mean(vectors * vectors, axis=-1, keepdims=True) + EPS_NORM)


def norm_back(grad_normed, inputs, rms_values, gain_row):
    weighted = grad_normed * gain_row
    inner = jnp.mean(weighted * inputs, axis=-1, keepdims=True)
    input_part = rms_values * weighted - inputs * rms_values**3 * inner
    return (input_part, jnp.sum(grad_normed * inputs * rms_values, axis=0))


def any_mesh(
    tokens,
    cotangent,
    owners,
    master,
    first_moment,
    second_moment,
    eigenbases,
    norm_gains,
    gain_first,
    gain_second,
):
    tok_rows, width = tokens.shape
    seq_devices = lax.axis_size("seq")
    head_devices = lax.axis_size("head")
    seq_place = lax.axis_index("seq")
    head_place = lax.axis_index("head")
    slab_rows = master.shape[2]
    attn_slab = 4 * width // (head_devices * seq_devices)
    ffn_slab = slab_rows - attn_slab
    head_width = width // head_devices
    ffn_width = FF // head_devices
    local_heads = HEADS // head_devices
    score_scale = HEAD_DIM ** (-0.5)
    branch_scale = (WINDOW / 3.0) ** 0.5
    inverse_attn = inverse_order(owners[0])
    inverse_ffn = inverse_order(owners[1])
    master_low = master[0, 0].astype(jnp.bfloat16)
    gathered, gains_all = (
        lax.all_gather(master_low, "seq", axis=0, tiled=True),
        lax.all_gather(norm_gains.astype(jnp.bfloat16), "seq", axis=1, tiled=True),
    )
    gathered = gathered.reshape(seq_devices, slab_rows, width)
    attn_rows = jnp.take(gathered[:, :attn_slab], owners[0], axis=0).reshape(4 * head_width, width)
    ffn_rows = jnp.take(gathered[:, attn_slab:], owners[1], axis=0).reshape(3 * ffn_width, width)
    w_query = attn_rows[:head_width]
    w_key = attn_rows[head_width : 2 * head_width]
    w_value = attn_rows[2 * head_width : 3 * head_width]
    w_out = attn_rows[3 * head_width :]
    w_gate = ffn_rows[:ffn_width]
    w_up = ffn_rows[ffn_width : 2 * ffn_width]
    w_down = ffn_rows[2 * ffn_width :]
    gain_one = gains_all[0].astype(jnp.float32)
    gain_two = gains_all[1].astype(jnp.float32)
    inputs = tokens.astype(jnp.float32)
    rms_one = inverse_rms(inputs)
    normed_one = (inputs * rms_one * gain_one).astype(jnp.bfloat16)
    positions = (seq_place * tok_rows + jnp.arange(tok_rows, dtype=jnp.int32)).astype(jnp.float32)
    cosine, sine = angles(positions)
    head_shape = (tok_rows, local_heads, HEAD_DIM)

    def project(weight_rows):
        return jnp.einsum("td,id->ti", normed_one, weight_rows, preferred_element_type=jnp.float32)

    queries = rotate(project(w_query).reshape(head_shape), cosine, sine).astype(jnp.bfloat16)
    keys_own = rotate(project(w_key).reshape(head_shape), cosine, sine).astype(jnp.bfloat16)
    values_own = project(w_value).reshape(head_shape).astype(jnp.bfloat16)
    hop_total = -(-WINDOW // tok_rows)
    hop_sizes = [
        min(tok_rows, WINDOW - (hop_index - 1) * tok_rows) for hop_index in range(1, hop_total + 1)
    ]
    halo_keys = []
    halo_values = []
    for hop_index in range(hop_total, 0, -1):
        hop_rows = hop_sizes[hop_index - 1]
        far_keys, far_values = passed_along(
            (keys_own[tok_rows - hop_rows :], values_own[tok_rows - hop_rows :]), "seq", hop_index
        )
        halo_keys.append(far_keys)
        halo_values.append(far_values)
    keys_all = jnp.concatenate(halo_keys + [keys_own], axis=0)
    values_all = jnp.concatenate(halo_values + [values_own], axis=0)
    row_ids = jnp.arange(tok_rows, dtype=jnp.int32)[:, None]
    col_ids = jnp.arange(WINDOW + tok_rows, dtype=jnp.int32)[None, :]
    allowed = (
        (col_ids > row_ids)
        & (col_ids <= row_ids + WINDOW)
        & (seq_place * tok_rows - WINDOW + col_ids >= 0)
    )

    def scores_of():
        raw = jnp.einsum("thd,chd->htc", queries, keys_all, preferred_element_type=jnp.float32)
        return jnp.where(allowed[None], raw * score_scale, NEGATIVE)

    scores = scores_of()
    row_top = jnp.max(scores, axis=-1, keepdims=True)
    exp_scores = jnp.exp(scores - row_top)
    exp_total = jnp.sum(exp_scores, axis=-1, keepdims=True)
    soft_low = (exp_scores / exp_total).astype(jnp.bfloat16)
    log_total = row_top + jnp.log(exp_total)
    attended = jnp.einsum("htc,chd->thd", soft_low, values_all, preferred_element_type=jnp.float32)
    attended_low = attended.reshape(tok_rows, head_width).astype(jnp.bfloat16)
    attn_part = branch_scale * jnp.dot(attended_low, w_out, preferred_element_type=jnp.float32)
    hidden_one = inputs + lax.psum(attn_part, "head")
    rms_two = inverse_rms(hidden_one)
    normed_two = (hidden_one * rms_two * gain_two).astype(jnp.bfloat16)
    gate_pre = jnp.einsum("td,fd->tf", normed_two, w_gate, preferred_element_type=jnp.float32)
    up_pre = jnp.einsum("td,fd->tf", normed_two, w_up, preferred_element_type=jnp.float32)
    sigma = jax.nn.sigmoid(gate_pre)
    hidden_low = (gate_pre * sigma * up_pre).astype(jnp.bfloat16)
    ffn_part = jnp.dot(hidden_low, w_down, preferred_element_type=jnp.float32)
    ffn_share = lax.psum_scatter(ffn_part, "head", scatter_dimension=1, tiled=True)
    share_width = width // head_devices
    residual_share = lax.dynamic_slice_in_dim(hidden_one, head_place * share_width, share_width, 1)
    block_out = (residual_share + ffn_share).astype(jnp.bfloat16)
    grad_out_f = cotangent.astype(jnp.float32)
    hidden_grad = jnp.einsum("td,fd->tf", cotangent, w_down, preferred_element_type=jnp.float32)
    silu_grad = sigma * (1.0 + gate_pre * (1.0 - sigma))
    gate_grad = (hidden_grad * up_pre * silu_grad).astype(jnp.bfloat16)
    up_grad = (hidden_grad * gate_pre * sigma).astype(jnp.bfloat16)
    down_grad = jnp.einsum("tf,td->fd", hidden_low, cotangent, preferred_element_type=jnp.float32)
    gate_w_grad = jnp.einsum("tf,td->fd", gate_grad, normed_two, preferred_element_type=jnp.float32)
    up_w_grad = jnp.einsum("tf,td->fd", up_grad, normed_two, preferred_element_type=jnp.float32)
    ffn_rows_grad = jnp.concatenate([gate_w_grad, up_w_grad, down_grad], axis=0)
    ffn_owner = jnp.take(ffn_rows_grad.reshape(seq_devices, ffn_slab, width), inverse_ffn, axis=0)
    normed_two_part = jnp.einsum(
        "tf,fd->td", gate_grad, w_gate, preferred_element_type=jnp.float32
    ) + jnp.einsum("tf,fd->td", up_grad, w_up, preferred_element_type=jnp.float32)
    normed_two_share = lax.psum_scatter(normed_two_part, "head", scatter_dimension=1, tiled=True)
    normed_two_grad = lax.all_gather(normed_two_share, "head", axis=1, tiled=True)
    back_two, gain_two_grad = norm_back(normed_two_grad, hidden_one, rms_two, gain_two)
    hidden_one_grad = grad_out_f + back_two
    hidden_grad_low = hidden_one_grad.astype(jnp.bfloat16)
    attended_grad = branch_scale * jnp.einsum(
        "td,id->ti", hidden_grad_low, w_out, preferred_element_type=jnp.float32
    )
    attended_grad = attended_grad.reshape(head_shape).astype(jnp.bfloat16)
    soft_again = jnp.exp(scores_of() - log_total)
    soft_grad = jnp.einsum(
        "thd,chd->htc", attended_grad, values_all, preferred_element_type=jnp.float32
    )
    inner_sum = jnp.sum(soft_again * soft_grad, axis=-1, keepdims=True)
    score_grad = (soft_again * (soft_grad - inner_sum) * score_scale).astype(jnp.bfloat16)
    query_grad_turned = jnp.einsum(
        "htc,chd->thd", score_grad, keys_all, preferred_element_type=jnp.float32
    )
    key_grad_all = jnp.einsum(
        "htc,thd->chd", score_grad, queries, preferred_element_type=jnp.float32
    )
    value_grad_all = jnp.einsum(
        "htc,thd->chd", soft_low, attended_grad, preferred_element_type=jnp.float32
    )
    key_grad_own = key_grad_all[WINDOW:]
    value_grad_own = value_grad_all[WINDOW:]
    start_at = 0
    for hop_index in range(hop_total, 0, -1):
        hop_rows = hop_sizes[hop_index - 1]
        back_keys, back_values = passed_along(
            (
                key_grad_all[start_at : start_at + hop_rows],
                value_grad_all[start_at : start_at + hop_rows],
            ),
            "seq",
            -hop_index,
        )
        key_grad_own = key_grad_own.at[tok_rows - hop_rows :].add(back_keys)
        value_grad_own = value_grad_own.at[tok_rows - hop_rows :].add(back_values)
        start_at = start_at + hop_rows
    query_grad = (
        rotate(query_grad_turned, cosine, -sine).reshape(tok_rows, head_width).astype(jnp.bfloat16)
    )
    key_grad = (
        rotate(key_grad_own, cosine, -sine).reshape(tok_rows, head_width).astype(jnp.bfloat16)
    )
    value_grad = value_grad_own.reshape(tok_rows, head_width).astype(jnp.bfloat16)

    def input_part(row_grad, weight_rows):
        return jnp.einsum("ti,id->td", row_grad, weight_rows, preferred_element_type=jnp.float32)

    normed_one_part = (
        input_part(query_grad, w_query)
        + input_part(key_grad, w_key)
        + input_part(value_grad, w_value)
    )
    normed_one_share = lax.psum_scatter(normed_one_part, "head", scatter_dimension=1, tiled=True)
    normed_one_grad = lax.all_gather(
        normed_one_share.astype(jnp.bfloat16), "head", axis=1, tiled=True
    ).astype(normed_one_share.dtype)
    back_one, gain_one_grad = norm_back(normed_one_grad, inputs, rms_one, gain_one)
    input_grad = hidden_one_grad + back_one
    gain_grads = jnp.stack([gain_one_grad, gain_two_grad])

    def rows_grad(row_grad):
        return jnp.einsum("ti,td->id", row_grad, normed_one, preferred_element_type=jnp.float32)

    out_w_grad = branch_scale * jnp.einsum(
        "ti,td->id", attended_low, hidden_grad_low, preferred_element_type=jnp.float32
    )
    attn_rows_grad = jnp.concatenate(
        [rows_grad(query_grad), rows_grad(key_grad), rows_grad(value_grad), out_w_grad], axis=0
    )
    attn_owner = jnp.take(
        attn_rows_grad.reshape(seq_devices, attn_slab, width), inverse_attn, axis=0
    )
    owner_rows = jnp.concatenate([attn_owner, ffn_owner], axis=1).reshape(
        seq_devices * slab_rows, width
    )
    reduced, gain_reduced = (
        lax.psum_scatter(owner_rows, "seq", scatter_dimension=0, tiled=True),
        lax.psum_scatter(gain_grads, "seq", scatter_dimension=1, tiled=True),
    )
    attn_kinds = (
        inverse_attn[seq_place] * attn_slab + jnp.arange(attn_slab, dtype=jnp.int32)
    ) // head_width
    ffn_kinds = (
        4 + (inverse_ffn[seq_place] * ffn_slab + jnp.arange(ffn_slab, dtype=jnp.int32)) // ffn_width
    )
    row_rates = kind_rates(jnp.concatenate([attn_kinds, ffn_kinds]), width)[:, None]
    basis = eigenbases[0, 0]
    block_size = basis.shape[-1]
    split_shape = (slab_rows, width // block_size, block_size)
    turned = jnp.einsum(
        "rbk,bkl->rbl", reduced.reshape(split_shape), basis, precision=PRECISE
    ).reshape(slab_rows, width)
    first_new = BETA_FIRST * first_moment[0, 0] + (1.0 - BETA_FIRST) * turned
    second_new = BETA_SECOND * second_moment[0, 0] + (1.0 - BETA_SECOND) * turned * turned
    adam_dir = (
        first_new
        / (1.0 - BETA_FIRST**ADAM_STEP)
        / (jnp.sqrt(second_new / (1.0 - BETA_SECOND**ADAM_STEP)) + ADAM_EPS)
    )
    backward_dir = jnp.einsum(
        "rbl,bkl->rbk", adam_dir.reshape(split_shape), basis, precision=PRECISE
    ).reshape(slab_rows, width)
    master_old = master[0, 0]
    master_new = master_old - row_rates * (backward_dir + DECAY_RATE * master_old)
    gain_first_new = BETA_FIRST * gain_first + (1.0 - BETA_FIRST) * gain_reduced
    gain_second_new = BETA_SECOND * gain_second + (1.0 - BETA_SECOND) * gain_reduced * gain_reduced
    gain_new = norm_gains - GAIN_RATE * (gain_first_new / (1.0 - BETA_FIRST**ADAM_STEP)) / (
        jnp.sqrt(gain_second_new / (1.0 - BETA_SECOND**ADAM_STEP)) + ADAM_EPS
    )
    return (
        block_out,
        input_grad,
        reduced[None, None],
        first_new[None, None],
        second_new[None, None],
        master_new[None, None],
        master_new.astype(jnp.bfloat16)[None, None],
        gain_reduced,
        gain_first_new,
        gain_second_new,
        gain_new,
    )


SLAB = 516
PAD = 528
HALF = 1024
QUART = 512
PACKED = 800
UNITS = 1376
NT = (((1,), (1,)), ((), ()))
TN = (((0,), (0,)), ((), ()))


VM = pl.BlockSpec(memory_space=pltpu.VMEM)
SM = pl.BlockSpec(memory_space=pltpu.SMEM)
HB = pl.BlockSpec(memory_space=pl.ANY)


def shape(rows, columns, dtype=BF16):
    return jax.ShapeDtypeStruct((rows, columns), dtype)


def call(kernel, outs, specs, args, scratch=(), flops=0, moved=0, out_specs=None, grid=None):
    extra = {} if grid is None else {"grid": grid}
    return pl.pallas_call(
        kernel,
        out_shape=outs,
        in_specs=specs,
        out_specs=[VM] * len(outs) if out_specs is None else out_specs,
        scratch_shapes=list(scratch),
        compiler_params=pltpu.CompilerParams(vmem_limit_bytes=56 * 2**20),
        cost_estimate=pl.CostEstimate(flops=flops, bytes_accessed=moved, transcendentals=0),
        name=getattr(kernel, "func", kernel).__name__,
        **extra,
    )(*args)


def root_of(values):
    return lax.rsqrt(jnp.mean(values * values, axis=-1, keepdims=True) + EPS_NORM)


def turn(values, cosine, sine):
    parts = []
    for h in range(values.shape[1] // HEAD_DIM):
        v = values[:, h * HEAD_DIM : (h + 1) * HEAD_DIM]
        parts.append(v * cosine + pltpu.roll(v, HEAD_DIM // 2, 1) * sine)
    return parts


MESH = pl.DeviceIdType.MESH


def flip(index, mask):
    for bit in (1, 2, 4):
        if mask & bit:
            index = index + bit - 2 * bit * lax.rem(lax.div(index, bit), 2)
    return index


def twist(left, right):
    out = 0
    for bit in (1, 2, 4):
        out = out + bit * lax.rem(lax.rem(lax.div(left, bit), 2) + lax.rem(lax.div(right, bit), 2), 2)
    return out


def slab_of(owners, kind, device):
    found = 0
    for j in range(8):
        found = jnp.where(owners[kind, j] == device, j, found)
    return found


class Plane:
    def __init__(self, at, sent, got, me, line):
        self.at, self.sent, self.got, self.me, self.line = at, sent, got, me, line

    def copy(self, src, dst, side, hop_mask):
        return pltpu.make_async_remote_copy(
            src_ref=self.at(src, side),
            dst_ref=self.at(dst, side),
            send_sem=self.sent.at[dst, side],
            recv_sem=self.got.at[dst, side],
            device_id=(flip(self.me, hop_mask), self.line),
            device_id_type=MESH,
        )

    def post(self, src, dst, side, hop_mask):
        self.copy(src, dst, side, hop_mask).start()

    def start_first(self):
        for mask, side in ((2, 0), (4, 1)):
            self.post(0, mask, side, mask)
        for side in (0, 1):
            self.post(0, 1, side, 1)

    def start_second(self):
        for mask, side in ((2, 1), (4, 0)):
            self.post(0, mask, side, mask)

    def start(self):
        self.start_first()
        self.start_second()

    def arrive(self, mask, side):
        self.copy(mask, mask, side, 1).wait_recv()

    def twin(self, mask, side):
        self.post(mask, mask + 1, side, 1)

    def relay_first(self):
        for mask, side in ((2, 0), (4, 1)):
            self.arrive(mask, side)
            self.post(mask, 6, side, 6 - mask)
            self.twin(mask, side)

    def relay_second(self):
        for mask, side in ((2, 1), (4, 0)):
            self.arrive(mask, side)
            self.twin(mask, side)

    def relay_last(self):
        for side in (0, 1):
            self.arrive(6, side)
            self.twin(6, side)

    def finish(self):
        for mask in (1, 3, 5, 7):
            for side in (0, 1):
                self.arrive(mask, side)

    def drain(self, masks=range(1, 8)):
        for mask in masks:
            for side in (0, 1):
                self.copy(0, mask, side, 1).wait_send()


class OneWay(Plane):
    def __init__(self, want, *rest):
        super().__init__(*rest)
        self.core, self.x, self.y = (lax.rem(lax.div(self.me, bit), 2) == want for bit in (1, 2, 4))
        self.sends = {
            (1, 0): self.core, (1, 1): self.core, (2, 0): self.x | self.y, (2, 1): self.x, (4, 0): self.y,
            (4, 1): self.y, (6, 0): self.y, (6, 1): ~self.y,
        }
        self.sends |= {(m, side): ~self.x if m == 3 else ~self.y for m in (3, 5, 7) for side in (0, 1)}
        self.gets = {
            (m, side): ~(self.core if m == 1 else self.x if m < 4 else self.y) for m in range(1, 8) for side in (0, 1)
        }
        self.gets[2, 0] = ~self.x | self.y

    def post(self, src, dst, side, hop_mask):
        pl.when(self.sends[dst, side])(lambda: self.copy(src, dst, side, hop_mask).start())

    def arrive(self, mask, side):
        pl.when(self.gets[mask, side])(lambda: self.copy(mask, mask, side, 1).wait_recv())

    def drain(self):
        for mask in range(1, 8):
            for side in (0, 1):
                pl.when(self.sends[mask, side])(lambda m=mask, s=side: self.copy(0, m, s, 1).wait_send())


def line_copy(src, dst, sent, got, m, me, line):
    return pltpu.make_async_remote_copy(
        src_ref=src,
        dst_ref=dst,
        send_sem=sent.at[m],
        recv_sem=got.at[m],
        device_id=(me, flip(line, m)),
        device_id_type=MESH,
    )


def greet(me, line, plane_masks, line_masks):
    barrier = pltpu.get_barrier_semaphore()
    for mask in plane_masks:
        pl.semaphore_signal(barrier, inc=1, device_id=(flip(me, mask), line), device_id_type=MESH)
    for mask in line_masks:
        pl.semaphore_signal(barrier, inc=1, device_id=(me, flip(line, mask)), device_id_type=MESH)
    return lambda: pl.semaphore_wait(barrier, len(plane_masks) + len(line_masks))


def layer_kernel(
    rows, scale, branch,
    owners, tokens, dy, own_gains, speeds, master,
    block_out, gain_grad, input_grad, acts, z_all, g_all, b_all, dy_all,
    gains, o_low, o_wide, stats, a_low, b_low, kcat, vcat, qcat, docat, sent, g_sent, wide, w_a, w_f, made, cut,
    total, z_out, z_in, z_sum, line_out, line_in, b_own, work, dy_own, stat_l, stat_r, gain_out, gain_in,
    sem_w, sem_k, plane_sent, plane_got, z_sems, line_sems, sum_sems, r_up, r_down, r_got, t_sent, t_got, a2a_sems, pair_sems,
):
    me, line = lax.axis_index("seq"), lax.axis_index("head")
    ready = greet(me, line, range(1, 8), (1, 2, 3))
    order_a, order_f = ([twist(owners[kind, j], me) for j in range(8)] for kind in (0, 1))
    d_low = a_low
    h_out = wide.at[pl.ds(0, rows)]
    kept = {}

    def keep(i, src, dst):
        kept[i] = pltpu.make_async_copy(src, dst, sem_k.at[i])
        kept[i].start()

    def plane(i, at):
        return Plane(at, plane_sent.at[i], plane_got.at[i], me, line)

    w_a_plane = plane(0, lambda m, s: w_a.at[m, s] if s else w_a.at[m, s, pl.ds(0, 256)])
    w_f_plane = plane(1, lambda m, s: w_f.at[m, s])
    kv_plane = OneWay(
        0, lambda m, s: (kcat, vcat)[s].at[pl.ds(m * rows, rows)], plane_sent.at[2], plane_got.at[2], me, line
    )
    q_plane = OneWay(1, lambda m, s: qcat.at[m, s], plane_sent.at[3], plane_got.at[3], me, line)
    y_plane = plane(4, lambda m, s: dy_own.at[s] if m == 0 else dy_all.at[line, m, s])
    b_plane = plane(5, lambda m, s: b_low.at[s] if m == 0 else b_all.at[m, s])
    mine = lax.rem(line, 2)
    other = 1 - mine
    a_plane = plane(
        6, lambda m, s: (acts.at[0, m, mine] if m else a_low.at[mine]).at[:, pl.ds(s * QUART, QUART)]
    )

    def a_beside():
        return pltpu.make_async_remote_copy(
            src_ref=a_low.at[other],
            dst_ref=acts.at[0, 1, other],
            send_sem=pair_sems.at[0, 0],
            recv_sem=pair_sems.at[1, 0],
            device_id=(flip(me, 1), line),
            device_id_type=MESH,
        )

    def a_exchange(m):
        return pltpu.make_async_remote_copy(
            src_ref=acts.at[0, m, mine],
            dst_ref=acts.at[0, m, mine],
            send_sem=pair_sems.at[0, m],
            recv_sem=pair_sems.at[1, m],
            device_id=(me, flip(line, 1)),
            device_id_type=MESH,
        )

    def a_twin(m):
        return pltpu.make_async_remote_copy(
            src_ref=acts.at[0, m, other],
            dst_ref=acts.at[0, m + 1, other],
            send_sem=pair_sems.at[0, m + 1],
            recv_sem=pair_sems.at[1, m + 1],
            device_id=(flip(me, 1), line),
            device_id_type=MESH,
        )

    def a_pair_on():
        for m in (2, 4, 6):
            a_exchange(m).wait_recv()
            a_twin(m).start()

    d_plane = plane(7, lambda m, s: d_low.at[s] if m == 0 else acts.at[1, m, s])
    do_plane = plane(8, lambda m, s: docat.at[m, s])

    def straight(src, dst, which, m):
        return pltpu.make_async_remote_copy(
            src_ref=src.at[m],
            dst_ref=dst.at[m],
            send_sem=a2a_sems.at[which, 0, m],
            recv_sem=a2a_sems.at[which, 1, m],
            device_id=(flip(me, m), line),
            device_id_type=MESH,
        )

    def quarter(m):
        return pl.ds(pl.multiple_of(flip(line, m) * QUART, QUART), QUART)

    def columns_of(q, c):
        return pl.ds(q * QUART + c * 256, 256)

    def partial(which, right, q, c):
        way, at = (0, q - 1) if right else (1, q)
        return pltpu.make_async_remote_copy(
            src_ref=line_out.at[way, at, c],
            dst_ref=line_in.at[which % 2, way, at, c],
            send_sem=line_sems.at[which, 0, way, at, c],
            recv_sem=line_sems.at[which, 1, way, at, c],
            device_id=(me, line + 1 if right else line - 1),
            device_id_type=MESH,
        )

    def summed(which, right, q, c):
        way = 0 if right else 1
        return pltpu.make_async_remote_copy(
            src_ref=z_sum.at[which, q, c],
            dst_ref=z_sum.at[which, q, c],
            send_sem=sum_sems.at[which, way, q, c],
            recv_sem=sum_sems.at[which, 2, q, c],
            device_id=(me, line + 1 if right else line - 1),
            device_id_type=MESH,
        )

    def pass_on(which, right, q, c, first):
        way, at = (0, q - 1) if right else (1, q)
        value = total[:, columns_of(q, c)]
        if not first:
            partial(which, right, q, c).wait_recv()
            value += line_in[which % 2, way, at, c].astype(F32)
        line_out[way, at, c] = value.astype(BF16)
        partial(which, right, q, c).start()

    ways = ((True, (3, 2, 1)), (False, (0, 1, 2)))

    def line_post(which):
        for c in (0, 1):
            for right, order in ways:

                @pl.when(line == (0 if right else 3))
                def _():
                    for q in order:
                        pass_on(which, right, q, c, True)

    merges = {1: ((True, 3), (True, 2), (False, 0)), 2: ((False, 0), (False, 1), (True, 3))}
    shares = {
        0: ((False, 1), (False, 2), (False, 3)),
        1: ((False, 2), (True, 0), (False, 3)),
        2: ((True, 1), (False, 3), (True, 0)),
        3: ((True, 2), (True, 1), (True, 0)),
    }

    def line_merge(which, chores=()):
        chores = list(chores)
        for c in (0, 1):
            for step in range(3):
                for here, order in merges.items():

                    @pl.when(line == here)
                    def _():
                        pass_on(which, *order[step], c, False)

                if chores:
                    chores.pop(0)()
            for q in range(4):

                @pl.when(line == q)
                def _():
                    value = total[:, columns_of(q, c)]
                    for right, _ in ways:
                        if q != (0 if right else 3):
                            way, at = (0, q - 1) if right else (1, q)
                            partial(which, right, q, c).wait_recv()
                            value += line_in[which % 2, way, at, c].astype(F32)
                    z_sum[which, q, c] = value.astype(BF16)
                    for right, _ in ways:
                        if q != (3 if right else 0):
                            summed(which, right, q, c).start()

            if chores:
                chores.pop(0)()
        for chore in chores:
            chore()

    def line_share(which, chores=()):
        chores = list(chores)
        for c in (0, 1):
            for step in range(3):
                for here, order in shares.items():
                    right, q = order[step]

                    @pl.when(line == here)
                    def _():
                        summed(which, right, q, c).wait_recv()
                        if here != (3 if right else 0):
                            summed(which, right, q, c).start()

                if chores:
                    chores.pop(0)()
        for chore in chores:
            chore()

    def line_sent(which):
        for c in (0, 1):
            for right, order in ways:
                for q in order:

                    @pl.when(line < q if right else line > q)
                    def _():
                        partial(which, right, q, c).wait_send()

    def line_all_sent(which):
        for c in (0, 1):
            for q in range(4):
                for right, _ in ways:

                    @pl.when((line >= q) & (line < 3) if right else (line <= q) & (line > 0))
                    def _():
                        summed(which, right, q, c).wait_send()

    def gather_sum(which, out):
        for q in range(4):
            for c in (0, 1):
                out[:, columns_of(q, c)] = z_sum[which, q, c].astype(F32)

    def b_piece(m):
        return line_copy(z_out.at[m - 1], z_in.at[m - 1], z_sems.at[0], z_sems.at[1], m, me, line)

    def along_line(quarter_index, m, up):
        return pltpu.make_async_remote_copy(
            src_ref=dy_all.at[quarter_index, m],
            dst_ref=dy_all.at[quarter_index, m],
            send_sem=(r_up if up else r_down).at[quarter_index, m],
            recv_sem=r_got.at[quarter_index, m],
            device_id=(me, line + 1 if up else line - 1),
            device_id_type=MESH,
        )

    def twin_quarter(quarter_index, m):
        return pltpu.make_async_remote_copy(
            src_ref=dy_all.at[quarter_index, m],
            dst_ref=dy_all.at[quarter_index, m + 1],
            send_sem=t_sent.at[quarter_index, m],
            recv_sem=t_got.at[quarter_index, m],
            device_id=(flip(me, 1), line),
            device_id_type=MESH,
        )

    def line_round(step):
        if step == 0:
            for up, last in ((True, 3), (False, 0)):

                @pl.when(line != last)
                def _():
                    for m in (0, 2, 4, 6):
                        along_line(line, m, up).start()

            return
        for up, first, last in ((True, step, 3), (False, 3 - step, 0)):
            index = line - step if up else line + step

            @pl.when(line >= first if up else line <= first)
            def _():
                for m in (0, 2, 4, 6):
                    along_line(index, m, up).wait_recv()

                @pl.when(line != last)
                def _():
                    for m in (0, 2, 4, 6):
                        along_line(index, m, up).start()

                for m in (0, 2, 4, 6):
                    twin_quarter(index, m).start()

    def line_end():
        for apart in (1, 2, 3):
            for up in (True, False):
                index = line - apart if up else line + apart

                @pl.when(line >= apart if up else line <= 3 - apart)
                def _():
                    for m in (0, 2, 4, 6):
                        twin_quarter(index, m).wait_recv()
                        twin_quarter(index, m).wait_send()

        for step in range(3):
            for up in (True, False):
                index = line - step if up else line + step

                @pl.when((line >= step) & (line != 3) if up else (line <= 3 - step) & (line != 0))
                def _():
                    for m in (0, 2, 4, 6):
                        along_line(index, m, up).wait_send()

    load = pltpu.make_async_copy(master.at[pl.ds(0, 256), 0, :], wide.at[pl.ds(0, 256)], sem_w.at[0])
    load.start()
    for side in (0, 1):
        at = pl.multiple_of(line * QUART + side * 256, 256)
        dy_own[side] = dy[:, pl.ds(at, 256)]
    keep(8, dy_own, dy_all.at[line, 0])
    ready()
    y_plane.start()
    w_a[0, 0, pl.ds(256, 16), :] = jnp.zeros((16, HALF), BF16)
    w_a[0, 1, pl.ds(256, 16), :] = jnp.zeros((16, HALF), BF16)
    w_a[0, 1, 256:258, 0:256] = own_gains[...].astype(BF16)
    load.wait()
    for side in (0, 1):
        w_a[0, side, pl.ds(0, 256), :] = wide[pl.ds(0, 256), side * HALF : (side + 1) * HALF].astype(BF16)
    load = pltpu.make_async_copy(master.at[pl.ds(256, 256), 0, :], wide.at[pl.ds(0, 256)], sem_w.at[1])
    load.start()
    w_a_plane.start()
    load.wait()
    for side in (0, 1):
        columns = slice(side * HALF, (side + 1) * HALF)
        w_f[0, side, pl.ds(0, 256), :] = wide[pl.ds(0, 256), columns].astype(BF16)
    load = pltpu.make_async_copy(master.at[pl.ds(512, SLAB - 256), 0, :], wide, sem_w.at[2])
    load.start()
    load.wait()
    for side in (0, 1):
        columns = slice(side * HALF, (side + 1) * HALF)
        w_f[0, side, pl.ds(256, 256), :] = wide[pl.ds(0, 256), columns].astype(BF16)
        last = jnp.concatenate([wide[256 : SLAB - 256, columns], jnp.zeros((PAD - SLAB, HALF), F32)], axis=0)
        w_f[0, side, pl.ds(512, 16), :] = last.astype(BF16)
    for m in range(1, 8):

        @pl.when(flip(me, m) > me)
        def _():
            vcat[pl.ds(m * rows, rows), :] = jnp.zeros((rows, QUART), BF16)

    angle = (me * rows + lax.broadcasted_iota(jnp.int32, (rows, 1), 0)).astype(F32) * speeds[...]
    cosine, sine = jnp.cos(angle), jnp.sin(angle)
    sine = jnp.where(lax.broadcasted_iota(jnp.int32, (1, HEAD_DIM), 1) < HEAD_DIM // 2, -sine, sine)
    y_plane.relay_first()
    y_plane.relay_second()
    y_plane.relay_last()
    kept[8].wait()
    line_round(0)
    w_a_plane.relay_first()
    w_a_plane.relay_second()
    w_f_plane.start_first()
    w_a_plane.relay_last()
    w_a_plane.finish()

    for m in range(8):
        at = pl.multiple_of(flip(me, m) * 256, 256)
        gains[:, pl.ds(at, 256)] = w_a[m, 1, 256:258, 0:256].astype(F32)
    x = tokens[...].astype(F32)
    normed = (x * root_of(x) * gains[0:1, :]).astype(BF16)
    for side in (0, 1):
        a_low[side] = normed[:, side * HALF : (side + 1) * HALF]
    for j in (2, 3, 4, 5, 0, 1):
        out = lax.dot_general(a_low[0], w_a[order_a[j], 0, pl.ds(0, 256), :], NT, preferred_element_type=F32)
        out += lax.dot_general(a_low[1], w_a[order_a[j], 1, pl.ds(0, 256), :], NT, preferred_element_type=F32)
        if j < 4:
            parts = turn(out, cosine, sine)
        else:
            parts = [out[:, :HEAD_DIM], out[:, HEAD_DIM:]]
        for i, part in enumerate(parts):
            if j < 2:
                qcat[0, j, :, i * HEAD_DIM : (i + 1) * HEAD_DIM] = part.astype(BF16)
            else:
                at = (2 * (j % 2) + i) * HEAD_DIM
                (kcat, vcat)[j // 2 - 1][pl.ds(0, rows), at : at + HEAD_DIM] = part.astype(BF16)
        if j == 5:
            kv_plane.start()
    keep(0, a_low, acts.at[0, 0])
    q_plane.start()
    a_plane.start()
    a_beside().start()
    line_round(1)
    kv_plane.relay_first()
    kv_plane.relay_second()
    q_plane.relay_first()
    q_plane.relay_second()
    w_f_plane.relay_first()
    a_plane.relay_first()
    a_plane.relay_second()
    w_f_plane.start_second()
    kv_plane.relay_last()
    kv_plane.finish()
    q_plane.relay_last()

    at_q = me * rows + lax.broadcasted_iota(jnp.int32, (rows, 1), 0)
    along = lax.broadcasted_iota(jnp.int32, (1, rows), 1)
    lane = lax.broadcasted_iota(jnp.int32, (rows, HEAD_DIM), 1)
    stat = jnp.zeros((rows, HEAD_DIM), F32)
    for h in range(4):
        if h == 2:
            line_round(2)
        columns = slice(h * HEAD_DIM, (h + 1) * HEAD_DIM)
        q = qcat[0, h // 2, :, (h % 2) * HEAD_DIM : (h % 2 + 1) * HEAD_DIM]
        top = jnp.full((rows, 1), NEGATIVE, F32)
        for m in range(8):
            ahead = at_q - (flip(me, m) * rows + along)
            s = lax.dot_general(q, kcat[pl.ds(m * rows, rows), columns], NT, preferred_element_type=F32)
            s = jnp.where((ahead >= 0) & (ahead < WINDOW), s * scale, NEGATIVE)
            work[m, :, pl.ds(0, rows)] = s
            top = jnp.maximum(top, jnp.max(s, axis=-1, keepdims=True))
        sums = jnp.zeros((rows, 1), F32)
        for m in range(8):
            e = jnp.exp(work[m, :, pl.ds(0, rows)] - top)
            work[m, :, pl.ds(0, rows)] = e
            sums += jnp.sum(e, axis=-1, keepdims=True)
        share = 1.0 / sums
        o = jnp.zeros((rows, HEAD_DIM), F32)
        for m in range(8):
            soft = (work[m, :, pl.ds(0, rows)] * share).astype(BF16)
            o += jnp.dot(soft, vcat[pl.ds(m * rows, rows), columns], preferred_element_type=F32)
        o_wide[:, columns] = o
        o_low[:, columns] = o.astype(BF16)
        stat = jnp.where(lane == h, top + jnp.log(sums), stat)
    stats[...] = stat
    for side in (0, 1):
        out = jnp.dot(o_low[:, :256], w_a[order_a[6], side, pl.ds(0, 256), :], preferred_element_type=F32)
        out += jnp.dot(o_low[:, 256:], w_a[order_a[7], side, pl.ds(0, 256), :], preferred_element_type=F32)
        total[:, side * HALF : (side + 1) * HALF] = branch * out

    line_post(0)
    line_merge(0)
    line_share(0, [lambda: None, w_f_plane.relay_last])
    a_plane.relay_last()
    for m in (2, 4, 6):
        a_exchange(m).start()

    gather_sum(0, h_out)
    h = h_out[...] + tokens[...].astype(F32)
    h_out[...] = h
    normed = (h * root_of(h) * gains[1:2, :]).astype(BF16)
    for side in (0, 1):
        b_low[side] = normed[:, side * HALF : (side + 1) * HALF]
    keep(1, b_low, b_all.at[0])
    b_plane.start()
    w_f_plane.relay_second()
    w_f_plane.finish()

    def through(j, left, right, start=0, stop=PAD):
        span = pl.ds(start, stop - start)
        out = lax.dot_general(w_f[order_f[j], 0, span, :], left, NT, preferred_element_type=F32)
        return out + lax.dot_general(w_f[order_f[j], 1, span, :], right, NT, preferred_element_type=F32)

    edge = 2 * UNITS - 5 * SLAB
    low_edge, high_edge = edge // 16 * 16, -(-edge // 16) * 16
    some = pl.ds(0, rows)
    made[pl.ds(8 * SLAB, 16), some] = jnp.zeros((16, rows), F32)
    row = lax.broadcasted_iota(jnp.int32, (PAD, 1), 0)
    gate_rows = row < 2 * UNITS - 5 * SLAB
    for j in range(8):
        if j < 5:
            out = through(j, b_low[0], b_low[1])
        elif j > 5:
            out = through(j, dy[:, :HALF], dy[:, HALF:])
        else:
            upper = through(j, b_low[0], b_low[1], 0, high_edge)
            lower = through(j, dy[:, :HALF], dy[:, HALF:], low_edge, PAD)
            seam = jnp.where(gate_rows[low_edge:high_edge], upper[low_edge:], lower[: high_edge - low_edge])
            out = jnp.concatenate([upper[:low_edge], seam, lower[high_edge - low_edge :]], axis=0)
        made[pl.ds(j * SLAB, PAD), some] = out

    def mix(i, _):
        at = pl.multiple_of(i * 32, 8)
        gate = made[pl.ds(at, 32), some]
        up = made[pl.ds(UNITS + at, 32), some]
        back = made[pl.ds(2 * UNITS + at, 32), some]
        sigma = 1.0 / (1.0 + jnp.exp(-gate))
        silu = gate * sigma
        made[pl.ds(at, 32), some] = back * up * (sigma * (1.0 + gate * (1.0 - sigma)))
        made[pl.ds(UNITS + at, 32), some] = back * silu
        made[pl.ds(2 * UNITS + at, 32), some] = silu * up
        return 0

    lax.fori_loop(0, UNITS // 32, mix, 0)
    for j in range(8):
        cut[j, :, pl.ds(0, rows)] = made[pl.ds(j * SLAB, PAD), some].astype(BF16)
    def down(first, side):
        out, z_last, w_last = None, [], []
        for j in range(0, 6) if first else range(5, 8):
            start, stop = 0, 512
            if j == 5:
                start, stop = (0, high_edge) if first else (low_edge, 512)
            z = cut[j, pl.ds(start, stop - start), pl.ds(0, rows)]
            if j == 5:
                kind = gate_rows[start:stop] if first else ~gate_rows[start:stop]
                z = jnp.where(kind, z, jnp.zeros_like(z))
            part = lax.dot_general(
                z, w_f[order_f[j], side, pl.ds(start, stop - start), :], TN, preferred_element_type=F32
            )
            out = part if out is None else out + part
            if j != 5 or not first:
                z_last.append(cut[j, pl.ds(512, 16), pl.ds(0, rows)])
                w_last.append(w_f[order_f[j], side, pl.ds(512, 16), :])
        z_last, w_last = jnp.concatenate(z_last, axis=0), jnp.concatenate(w_last, axis=0)
        return out + lax.dot_general(z_last, w_last, TN, preferred_element_type=F32)

    line_sent(0)
    for side in (0, 1):
        total[:, side * HALF : (side + 1) * HALF] = down(True, side)
    line_post(1)
    def pack(m):
        z = cut[slab_of(owners, 1, flip(me, m)), :, pl.ds(0, rows)]
        sent[m, pl.ds(0, PAD), :] = z[:, :128]
        late = z[:, 128:].astype(F32)
        late = jnp.concatenate([late[: PAD // 2], late[PAD // 2 :]], axis=1)
        late = jnp.concatenate([late, jnp.zeros((PACKED - PAD - PAD // 2, 128), F32)], axis=0)
        sent[m, pl.ds(PAD, PACKED - PAD), :] = late.astype(BF16)
        if m:
            straight(sent, z_all, 0, m).start()
        else:
            keep(2, sent.at[0], z_all.at[0])

    def down_out(side):
        out = down(False, side)
        for c in range(4):
            made[pl.ds((4 * side + c) * rows, rows), :] = out[:, c * 256 : (c + 1) * 256]

    def down_parts():
        for m in range(4):
            for c in (0, 1):
                at = pl.multiple_of((2 * flip(line, m) + c) * rows, 64)
                block = made[pl.ds(at, rows), :]
                if m == 0:
                    b_own[:, c * 256 : (c + 1) * 256] = block
                else:
                    z_out[m - 1, :, c * 256 : (c + 1) * 256] = block.astype(BF16)

    line_merge(1, [functools.partial(pack, m) for m in (2, 4, 6, 3, 5, 7, 1, 0)] + [a_pair_on])
    line_share(
        1,
        [
            b_plane.relay_first, functools.partial(down_out, 0), functools.partial(down_out, 1),
            b_plane.relay_second, down_parts, lambda: line_round(3),
        ],
    )
    for m in (3, 2, 1):
        b_piece(m).start()

    gather_sum(1, total)
    normed_grad = total[...]
    h = h_out[...]
    root = root_of(h)
    gain_two = jnp.sum(normed_grad * h * root, axis=0, keepdims=True)
    weighted = normed_grad * gains[1:2, :]
    inner = jnp.mean(weighted * h, axis=-1, keepdims=True)
    grad = dy[...].astype(F32) + root * weighted - h * (root * root * root) * inner
    for c in range(8):
        made[pl.ds(c * rows, rows), :] = grad[:, c * 256 : (c + 1) * 256]
    low = grad.astype(BF16)
    kept[0].wait()
    a_plane.drain((1, 2, 4))
    a_beside().wait_send()
    for side in (0, 1):
        d_low[side] = low[:, side * HALF : (side + 1) * HALF]
    keep(3, d_low, acts.at[1, 0])
    total[0:1, :] = gain_two
    for m in range(8):
        at = pl.multiple_of(flip(me, m) * 256, 256)
        gain_out[m, 1:2, :] = total[0:1, pl.ds(at, 256)]
    lane = lax.broadcasted_iota(jnp.int32, (rows, HEAD_DIM), 1)
    own_lines = []
    for j, stat in enumerate((stat_l, stat_r)):
        out = lax.dot_general(d_low[0], w_a[order_a[6 + j], 0, pl.ds(0, 256), :], NT, preferred_element_type=F32)
        out += lax.dot_general(d_low[1], w_a[order_a[6 + j], 1, pl.ds(0, 256), :], NT, preferred_element_type=F32)
        out = (branch * out).astype(BF16)
        docat[0, j, pl.ds(0, rows), :] = out
        lines = jnp.zeros((rows, HEAD_DIM), F32)
        columns = []
        for i in (0, 1):
            h_at = 2 * j + i
            span = slice(h_at * HEAD_DIM, (h_at + 1) * HEAD_DIM)
            delta = jnp.sum(
                out[:, i * HEAD_DIM : (i + 1) * HEAD_DIM].astype(F32) * o_wide[:, span], axis=-1, keepdims=True
            )
            top = stats[:, h_at : h_at + 1]
            columns.append((top, delta))
            for at, value in ((i, top), (2 + i, delta)):
                for step in range(3):
                    part = value.astype(BF16).astype(F32)
                    value = value - part
                    lines = jnp.where(lane == 4 * step + at, part, lines)
        own_lines.append(columns)
        stat[pl.ds(0, rows), :] = lines
        stat[pl.ds(rows, 256 - rows), :] = jnp.zeros((256 - rows, HEAD_DIM), F32)
        docat[0, j, pl.ds(rows, 16), :] = stat[...].T[:16, :].astype(BF16)
    do_plane.start()
    b_plane.relay_last()

    for i in range(6):
        work[i] = jnp.zeros((rows, 256), F32)
    reach = -(-WINDOW // rows)
    below = lax.broadcasted_iota(jnp.int32, (rows, rows), 0)
    along = lax.broadcasted_iota(jnp.int32, (rows, rows), 1)

    def head_cut(h):
        return h // 2, slice((h % 2) * HEAD_DIM, (h % 2 + 1) * HEAD_DIM), slice(h * HEAD_DIM, (h + 1) * HEAD_DIM)

    def rows_of(m):
        return pl.ds(m * rows, rows)

    def query_side(m):
        apart = me - flip(me, m)

        @pl.when((apart >= 0) & (apart <= reach))
        def _():
            ahead = apart * rows + below - along
            allowed = (ahead >= 0) & (ahead < WINDOW)
            for h in range(4):
                side, two, span = head_cut(h)
                top, delta = own_lines[side][h % 2]
                k, do = kcat[rows_of(m), span], docat[0, side, pl.ds(0, rows), two]
                s = lax.dot_general(qcat[0, side, :, two], k, NT, preferred_element_type=F32)
                p = jnp.where(allowed, jnp.exp(s * scale - top), 0.0)
                dp = lax.dot_general(do, vcat[rows_of(m), span], NT, preferred_element_type=F32)
                ds = (p * (dp - delta) * scale).astype(BF16)
                work[side, :, two] += jnp.dot(ds, k, preferred_element_type=F32)

    def key_side(m):
        apart = me - flip(me, m)

        @pl.when((apart <= 0) & (apart >= -reach))
        def _():
            ahead = along - below - apart * rows
            allowed = (ahead >= 0) & (ahead < WINDOW)
            for h in range(4):
                side, two, span = head_cut(h)
                lines = docat[m, side, pl.ds(rows, 16), :].astype(F32)
                lines = (lines[0:4] + lines[4:8] + lines[8:12])[:, :rows]
                top, delta = lines[h % 2 : h % 2 + 1], lines[2 + h % 2 : 3 + h % 2]
                q, do = qcat[m, side, :, two], docat[m, side, pl.ds(0, rows), two]
                s = lax.dot_general(kcat[pl.ds(0, rows), span], q, NT, preferred_element_type=F32)
                p = jnp.where(allowed, jnp.exp(s * scale - top), 0.0)
                work[4 + side, :, two] += jnp.dot(p.astype(BF16), do, preferred_element_type=F32)
                dp = lax.dot_general(vcat[pl.ds(0, rows), span], do, NT, preferred_element_type=F32)
                ds = (p * (dp - delta) * scale).astype(BF16)
                work[2 + side, :, two] += jnp.dot(ds, q, preferred_element_type=F32)

    for m in range(4):
        query_side(m)
    do_plane.relay_first()
    for m in range(4, 8):
        query_side(m)
    do_plane.relay_second()
    do_plane.relay_last()
    d_plane.start()
    do_plane.finish()
    q_plane.finish()
    for m in range(8):
        key_side(m)
    for j in range(8):
        two = slice((j % 2) * 256, (j % 2 + 1) * 256)
        if j < 4:
            made_j = turn(work[j], cosine, -sine)
            for i in (0, 1):
                cut[j, pl.ds(0, rows), i * HEAD_DIM : (i + 1) * HEAD_DIM] = made_j[i].astype(BF16)
        elif j < 6:
            cut[j, pl.ds(0, rows), :] = work[j].astype(BF16)
        else:
            cut[j, pl.ds(0, rows), :] = o_low[:, two]
    line_sent(1)
    for j in range(6):
        for side in (0, 1):
            out = jnp.dot(cut[j, pl.ds(0, rows), :], w_a[order_a[j], side, pl.ds(0, 256), :], preferred_element_type=F32)
            columns = slice(side * HALF, (side + 1) * HALF)
            total[:, columns] = out if j == 0 else total[:, columns] + out
    line_post(2)

    def send_group(m):
        g_sent[m] = cut[slab_of(owners, 0, flip(me, m)), pl.ds(0, rows), :]
        if m:
            straight(g_sent, g_all, 1, m).start()
        else:
            keep(4, g_sent.at[0], g_all.at[0])

    line_merge(2, [functools.partial(send_group, m) for m in (2, 4, 6, 3, 5, 7, 1)] + [d_plane.relay_first])
    send_group(0)
    line_share(2, [lambda: None, d_plane.relay_second])
    out = h_out[:, quarter(0)] + b_own[...]
    for m in (1, 2, 3):
        b_piece(m).wait_recv()
        out += z_in[m - 1].astype(F32)
    block_out[...] = out.astype(BF16)

    gather_sum(2, total)
    normed_grad = total[...]
    x = tokens[...].astype(F32)
    root = root_of(x)
    gain_one = jnp.sum(normed_grad * x * root, axis=0, keepdims=True)
    weighted = normed_grad * gains[0:1, :]
    inner = jnp.mean(weighted * x, axis=-1, keepdims=True)
    grad = root * weighted - x * (root * root * root) * inner
    for c in range(8):
        made[pl.ds(c * rows, rows), :] += grad[:, c * 256 : (c + 1) * 256]
    total[0:1, :] = gain_one
    for m in range(8):
        at = pl.multiple_of(flip(me, m) * 256, 256)
        gain_out[m, 0:1, :] = total[0:1, pl.ds(at, 256)]
    for c in range(8):
        keep(9 + c, made.at[pl.ds(c * rows, rows)], input_grad.at[:, pl.ds(c * 256, 256)])
    for m in range(1, 8):
        straight(gain_out, gain_in, 2, m).start()
    d_plane.relay_last()
    for m in range(1, 8):
        straight(gain_out, gain_in, 2, m).wait_recv()
    made = gain_out[0, 0:2, :]
    for m in range(1, 8):
        made += gain_in[m, 0:2, :]
    gain_grad[...] = made
    for one in (y_plane, b_plane, d_plane, a_plane):
        one.finish()
    line_end()
    a_beside().wait_recv()
    for m in (2, 4, 6):
        a_exchange(m).wait_send()
        a_twin(m).wait_recv()
        a_twin(m).wait_send()
    for m in range(1, 8):
        straight(sent, z_all, 0, m).wait_recv()
        straight(g_sent, g_all, 1, m).wait_recv()
    a_plane.drain((3, 5, 6, 7))
    for one in (w_a_plane, w_f_plane, kv_plane, q_plane, y_plane, b_plane, d_plane, do_plane):
        one.drain()
    for m in range(1, 8):
        straight(sent, z_all, 0, m).wait_send()
        straight(g_sent, g_all, 1, m).wait_send()
        straight(gain_out, gain_in, 2, m).wait_send()
    line_sent(2)
    for which in range(3):
        line_all_sent(which)
    for m in (1, 2, 3):
        b_piece(m).wait_send()
    for i in kept:
        if i not in (0, 8):
            kept[i].wait()


def layer(owners, tokens, dy, own_gains, speeds, master, scale, branch):
    rows, width = tokens.shape
    array = jax.ShapeDtypeStruct
    dma = pltpu.SemaphoreType.DMA

    def low(*sizes):
        return pltpu.VMEM(sizes, BF16)

    def wide(*sizes):
        return pltpu.VMEM(sizes, F32)

    return pl.pallas_call(
        functools.partial(layer_kernel, rows, scale, branch),
        out_shape=[
            shape(rows, QUART),
            array((2, 256), F32),
            shape(rows, width, F32),
            array((2, 8, 2, rows, HALF), BF16),
            array((8, PACKED, 128), BF16),
            array((8, rows, 256), BF16),
            array((8, 2, rows, HALF), BF16),
            array((4, 8, 2, rows, 256), BF16),
        ],
        in_specs=[SM] + [VM] * 4 + [HB],
        out_specs=[VM] * 2 + [HB] * 6,
        scratch_shapes=[
            wide(2, width),
            low(rows, QUART),
            wide(rows, QUART),
            wide(rows, HEAD_DIM),
            low(2, rows, HALF),
            low(2, rows, HALF),
            low(8 * rows, QUART),
            low(8 * rows, QUART),
            low(8, 2, rows, 256),
            low(8, 2, rows + 16, 256),
            low(8, PACKED, 128),
            low(8, rows, 256),
            wide(SLAB - 256, width),
            low(8, 2, 272, HALF),
            low(8, 2, PAD, HALF),
            wide(8 * SLAB + 16, 256),
            low(8, PAD, 256),
            wide(rows, width),
            low(3, rows, QUART),
            low(3, rows, QUART),
            low(3, 4, 2, rows, 256),
            low(2, 3, 2, rows, 256),
            low(2, 2, 3, 2, rows, 256),
            wide(rows, QUART),
            wide(8, rows, 256),
            low(2, rows, 256),
            wide(256, HEAD_DIM),
            wide(256, HEAD_DIM),
            wide(8, 8, 256),
            wide(8, 8, 256),
            dma((3,)),
            dma((17,)),
            dma((9, 8, 2)),
            dma((9, 8, 2)),
            dma((2, 4)),
            dma((3, 2, 2, 3, 2)),
            dma((3, 3, 4, 2)),
        ]
        + [dma((4, 8))] * 5
        + [dma((3, 2, 8)), dma((2, 8))],
        compiler_params=pltpu.CompilerParams(
            collective_id=0, has_side_effects=True, vmem_limit_bytes=63 * 2**20
        ),
        cost_estimate=pl.CostEstimate(flops=2 * 10**10, bytes_accessed=60 * 2**20, transcendentals=0),
        name="layer",
    )(owners, tokens, dy, own_gains, speeds, master)


TILE = 256


def update_kernel(rows, branch, owners, basis, gain_grad, norm_gains, gain_first, gain_second, *rest):
    (zs, gs, acts, bs, dys), olds, through, rest = rest[:5], rest[5:8], rest[8:10], rest[10:]
    news, low_new, passed, gain_news, rest = rest[:4], rest[4], rest[5:7], rest[7:11], rest[11:]
    turned_g, turned_z, wide_basis, act, old, new, z_got, g_got, block, carried, asem, osem, nsem, sems = rest
    me, line = lax.axis_index("seq"), lax.axis_index("head")
    tile, tiles = pl.program_id(0), pl.num_programs(0)
    slot = tile % 2
    a_slab, f_slab = slab_of(owners, 0, me), slab_of(owners, 1, me)

    def columns_of(t):
        return pl.ds(pl.multiple_of(t * TILE, TILE), TILE)

    def act_copy(t, kind, which):
        at = pl.ds(pl.multiple_of(lax.rem(t, HALF // TILE) * TILE, TILE), TILE)
        if kind == 3:
            part = dys.at[lax.div(t, 2), :, lax.rem(t, 2)]
        elif kind == 2:
            part = bs.at[:, lax.div(t, HALF // TILE), :, at]
        else:
            part = acts.at[kind, :, lax.div(t, HALF // TILE), :, at]
        return pltpu.make_async_copy(part, act.at[t % 2, which], asem.at[t % 2, which])

    def act_copies(t, kind, which):
        act_copy(t, kind, which).start()

    def act_wait(which):
        act_copy(tile, 2, which).wait()

    def factor_of(which):
        return act[slot, which].reshape(8 * rows, TILE)

    def fetch_acts(t):
        pl.when(a_slab < 6)(lambda: act_copies(t, 0, 0))
        pl.when(a_slab >= 6)(lambda: act_copies(t, 1, 0))
        pl.when(f_slab <= 5)(lambda: act_copies(t, 2, 1))
        pl.when(f_slab > 5)(lambda: act_copies(t, 3, 1))
        pl.when(f_slab == 5)(lambda: act_copies(t, 3, 2))

    def old_copy(i, t):
        return pltpu.make_async_copy(olds[i].at[:, 0, columns_of(t)], old.at[t % 2, i], osem.at[t % 2, i])

    def new_copy(i, t):
        return pltpu.make_async_copy(new.at[t % 2, i], news[i].at[:, 0, columns_of(t)], nsem.at[t % 2, i])

    def fetch(t):
        fetch_acts(t)
        for i in range(3):
            old_copy(i, t).start()

    @pl.when(tile == 0)
    def _():
        small = [pltpu.make_async_copy(*pair, sems.at[i]) for i, pair in enumerate(((gs, g_got), (zs, z_got)))]
        for copy in small:
            copy.start()
        fetch(0)
        for i in (0, 1):
            pltpu.make_async_copy(through[i], (block, carried)[i], sems.at[2 + i]).start()
        made = gain_grad[...]
        one = BETA_FIRST * gain_first[...] + (1.0 - BETA_FIRST) * made
        two = BETA_SECOND * gain_second[...] + (1.0 - BETA_SECOND) * made * made
        gain_news[0][...] = made
        gain_news[1][...] = one
        gain_news[2][...] = two
        gain_news[3][...] = norm_gains[...] - GAIN_RATE * (one / (1.0 - BETA_FIRST**ADAM_STEP)) / (
            jnp.sqrt(two / (1.0 - BETA_SECOND**ADAM_STEP)) + ADAM_EPS
        )
        wide_basis[...] = jnp.zeros_like(wide_basis)
        for copy in small:
            copy.wait()
        turned_g[...] = g_got[...].reshape(8 * rows, 256).T
        lane = lax.broadcasted_iota(jnp.int32, (PAD, 128), 1)
        for m in range(0, 8, 2):
            early, late = [], []
            for i in (0, 1):
                early.append(z_got[m + i, pl.ds(0, PAD), :].astype(F32))
                pair = z_got[m + i, pl.ds(PAD, PAD // 2), :].astype(F32)
                other = pltpu.roll(pair, 64, 1)
                late.append(jnp.concatenate([other, pair] if i else [pair, other], axis=0))
            shifted = pltpu.roll(early[1], 64, 1)
            made = (early[0], jnp.where(lane < 64, late[0], shifted), jnp.where(lane < 64, shifted, late[1]))
            for i in range(3):
                at = m * rows + i * 128
                turned_z[:, at : at + 128] = made[i].astype(BF16)

    pl.when(tile + 1 < tiles)(lambda: fetch(tile + 1))

    @pl.when(tile == 1)
    def _():
        for i in (0, 1):
            pltpu.make_async_copy(through[i], (block, carried)[i], sems.at[2 + i]).wait()
            pltpu.make_async_copy((block, carried)[i], passed[i], sems.at[4 + i]).start()


    @pl.when(tile >= 2)
    def _():
        for i in range(4):
            new_copy(i, tile - 2).wait()

    grad, first_new, second_new, master_new = (new.at[slot, i] for i in range(4))
    first, second, master = (old.at[slot, i] for i in range(3))

    def ffn_rows(which, start, stop):
        return jnp.dot(turned_z[start:stop, :], factor_of(which), preferred_element_type=F32)

    act_wait(0)
    factor = jnp.where(a_slab < 6, 1.0, branch)
    grad[pl.ds(0, 256), :] = factor * jnp.dot(turned_g[...], factor_of(0), preferred_element_type=F32)
    act_wait(1)
    first_of_down = 2 * UNITS - f_slab * SLAB
    edge = 2 * UNITS - 5 * SLAB
    low_edge, high_edge = edge // 16 * 16, -(-edge // 16) * 16

    @pl.when(f_slab != 5)
    def _():
        grad[pl.ds(256, SLAB), :] = ffn_rows(1, 0, PAD)[:SLAB]

    @pl.when(f_slab == 5)
    def _():
        upper = ffn_rows(1, 0, high_edge)
        act_wait(2)
        lower = ffn_rows(2, low_edge, PAD)
        row = low_edge + lax.broadcasted_iota(jnp.int32, (high_edge - low_edge, 1), 0)
        grad[pl.ds(256, low_edge), :] = upper[:low_edge]
        grad[pl.ds(256 + low_edge, high_edge - low_edge), :] = jnp.where(
            row < edge, upper[low_edge:], lower[: high_edge - low_edge]
        )
        grad[pl.ds(256 + high_edge, SLAB - high_edge), :] = lower[high_edge - low_edge : SLAB - low_edge]

    for i in range(3):
        old_copy(i, tile).wait()
    row = lax.broadcasted_iota(jnp.int32, (256 + SLAB, 1), 0)
    rate = jnp.where((row < 256) | (row - 256 < first_of_down), 0.5 * (2 * HALF) ** (-0.5), 0.5 * FF ** (-0.5))
    for b in range(TILE // HEAD_DIM):
        cut = slice(b * HEAD_DIM, (b + 1) * HEAD_DIM)
        wide_basis[cut, cut] = basis[b].astype(BF16)
    turned = jnp.dot(grad[...].astype(BF16), wide_basis[...], preferred_element_type=F32)
    one = BETA_FIRST * first[...] + (1.0 - BETA_FIRST) * turned
    two = BETA_SECOND * second[...] + (1.0 - BETA_SECOND) * turned * turned
    first_new[...] = one
    second_new[...] = two
    adam = (one / (1.0 - BETA_FIRST**ADAM_STEP)) / (jnp.sqrt(two / (1.0 - BETA_SECOND**ADAM_STEP)) + ADAM_EPS)
    back = lax.dot_general(adam.astype(BF16), wide_basis[...], NT, preferred_element_type=F32)
    before = master[...]
    after = before - rate * (back + DECAY_RATE * before)
    master_new[...] = after
    low_new[...] = after.astype(BF16)
    for i in range(4):
        new_copy(i, tile).start()

    @pl.when(tile == tiles - 1)
    def _():
        for t in (tile - 1, tile):
            for i in range(4):
                new_copy(i, t).wait()
        for i in (0, 1):
            pltpu.make_async_copy((block, carried)[i], passed[i], sems.at[4 + i]).wait()


def update(owners, basis, small, zs, gs, acts, bs, dys, olds, through, branch):
    rows = gs.shape[1]
    height, _, width = olds[0].shape

    def whole(array):
        return pl.BlockSpec(array.shape, lambda i: (0,) * array.ndim)

    tall = pl.BlockSpec((height, TILE), lambda i: (0, i))
    per = TILE // HEAD_DIM
    gains = [shape(*array.shape, F32) for array in small]
    return call(
        functools.partial(update_kernel, rows, branch),
        [jax.ShapeDtypeStruct(olds[0].shape, F32)] * 4
        + [shape(height, width)]
        + [jax.ShapeDtypeStruct(array.shape, array.dtype) for array in through]
        + gains,
        [SM, pl.BlockSpec((per, HEAD_DIM, HEAD_DIM), lambda i: (i, 0, 0))]
        + [whole(array) for array in small]
        + [HB] * 10,
        [owners, basis, *small, zs, gs, acts, bs, dys, *olds, *through],
        [
            pltpu.VMEM((256, 8 * rows), BF16),
            pltpu.VMEM((PAD, 8 * rows), BF16),
            pltpu.VMEM((TILE, TILE), BF16),
            pltpu.VMEM((2, 3, 8, rows, TILE), BF16),
            pltpu.VMEM((2, 3, height, TILE), F32),
            pltpu.VMEM((2, 4, height, TILE), F32),
            pltpu.VMEM(zs.shape, BF16),
            pltpu.VMEM(gs.shape, BF16),
            *[pltpu.VMEM(array.shape, array.dtype) for array in through],
            pltpu.SemaphoreType.DMA((2, 3)),
            pltpu.SemaphoreType.DMA((2, 3)),
            pltpu.SemaphoreType.DMA((2, 4)),
            pltpu.SemaphoreType.DMA((6,)),
        ],
        out_specs=[HB] * 4 + [tall] + [HB] * 2 + [whole(array) for array in small],
        grid=(width // TILE,),
        flops=2 * 8 * rows * height * width,
        moved=70 * 2**20,
    )


def plane_mesh(
    tokens,
    cotangent,
    owners,
    master,
    first_moment,
    second_moment,
    eigenbases,
    norm_gains,
    gain_first,
    gain_second,
):
    rows, width = tokens.shape
    scale = HEAD_DIM ** (-0.5)
    branch = (WINDOW / 3.0) ** 0.5
    half = HEAD_DIM // 2
    speeds = ROPE_BASE ** (-jnp.arange(half, dtype=F32) / half)
    speeds = jnp.concatenate([speeds, speeds])[None, :]
    tall = [array.reshape(array.shape[2], 1, width) for array in (first_moment, second_moment, master)]
    block_out, gain_grad, input_grad, acts, zs, gs, bs, dys = layer(
        owners, tokens, cotangent, norm_gains, speeds, tall[2], scale, branch
    )
    (
        grad, first_new, second_new, master_new, low_new, block_out, input_grad, gain_grad, gain_first_new,
        gain_second_new, gain_new,
    ) = update(
        owners, eigenbases[0, 0], [gain_grad, norm_gains, gain_first, gain_second], zs, gs, acts, bs, dys, tall,
        [block_out, input_grad], branch,
    )
    whole = (1, 1, *tall[0].shape[::2])
    return (
        block_out,
        input_grad,
        grad.reshape(whole),
        first_new.reshape(whole),
        second_new.reshape(whole),
        master_new.reshape(whole),
        low_new[None, None],
        gain_grad,
        gain_first_new,
        gain_second_new,
        gain_new,
    )


def solution(mesh):
    in_specs = (
        P("seq", None),
        P("seq", None),
        P(),
        P("head", "seq", None, None),
        P("head", "seq", None, None),
        P("head", "seq", None, None),
        P("head", "seq", None, None, None),
        P(None, "seq"),
        P(None, "seq"),
        P(None, "seq"),
    )
    out_specs = (
        P("seq", "head"),
        P("seq", None),
        P("head", "seq", None, None),
        P("head", "seq", None, None),
        P("head", "seq", None, None),
        P("head", "seq", None, None),
        P("head", "seq", None, None),
        P(None, "seq"),
        P(None, "seq"),
        P(None, "seq"),
        P(None, "seq"),
    )
    plane = mesh.shape["seq"] == 8 and mesh.shape["head"] == 4
    return jax.shard_map(
        plane_mesh if plane else any_mesh, mesh=mesh, in_specs=in_specs, out_specs=out_specs, check_vma=False
    )
```
